32 devices in a mesh: dp: 8 (over y, x, core), mp: 4 (over z).
Axes of the slice: x: 2, y: 2, z: 4, core: 2. Of those that a mesh axis runs over, the one named last changes fastest.
Arguments:
- tokens: bfloat16 [12288, 768], P('dp'), may hold values from -6 to 6
- alignment: int32 [24, 128], P('dp'), may hold values from 0 to 383, as said below
- segment_count: int32 [24], P('dp'), may hold values from 5 to 128, as said below
- text_mask: int32 [24, 384], P('dp'), may hold values from 0 to 1, as said below
- cotangent: bfloat16 [12288, 768], P('dp'), may hold values from -6 to 6
- attention_master: float32 [768, 4, 768], P('dp', None, 'mp')
- attention_moment: float32 [768, 4, 768], P('dp', None, 'mp')
- attention_average: float32 [768, 4, 768], P('dp', None, 'mp')
- feedforward_master: float32 [768, 2, 3072], P('dp', None, 'mp')
- feedforward_moment: float32 [768, 2, 3072], P('dp', None, 'mp')
- feedforward_average: float32 [768, 2, 3072], P('dp', None, 'mp')
- shared_master: float32 [768, 6], P('dp')
- shared_moment: float32 [768, 6], P('dp')
- shared_average: float32 [768, 6], P('dp')
- split_master: float32 [768, 6], P('mp')
- split_moment: float32 [768, 6], P('mp')
- split_average: float32 [768, 6], P('mp')
Outputs:
- layer_output: bfloat16 [12288, 768], P('dp')
- input_gradient: float32 [12288, 768], P('dp')
- attention_velocity: float32 [768, 4, 768], P('dp', None, 'mp')
- attention_updated: float32 [768, 4, 768], P('dp', None, 'mp')
- attention_averaged: float32 [768, 4, 768], P('dp', None, 'mp')
- attention_rounded: bfloat16 [768, 4, 768], P('dp', None, 'mp')
- feedforward_velocity: float32 [768, 2, 3072], P('dp', None, 'mp')
- feedforward_updated: float32 [768, 2, 3072], P('dp', None, 'mp')
- feedforward_averaged: float32 [768, 2, 3072], P('dp', None, 'mp')
- feedforward_rounded: bfloat16 [768, 2, 3072], P('dp', None, 'mp')
- shared_velocity: float32 [768, 6], P('dp')
- shared_updated: float32 [768, 6], P('dp')
- shared_averaged: float32 [768, 6], P('dp')
- shared_rounded: bfloat16 [768, 6], P('dp')
- split_velocity: float32 [768, 6], P('mp')
- split_updated: float32 [768, 6], P('mp')
- split_averaged: float32 [768, 6], P('mp')
- split_rounded: bfloat16 [768, 6], P('mp')
The draws below stay inside these ranges and needn't reach their ends.
Inputs may be any that keep to these rules, and one draw needn't show every extreme that they name: alignment[d, j] is less than the number of ones in row d of text_mask. `segment_count`: at least one document holds 128 live segment slots. `text_mask`: each row is ones followed by zeros, with at least 96 ones; some row is all ones.
All inputs are finite; a program needn't handle non-finite values.
Results may differ from the reference program's by a relative error of at most 0.02.
Values may be sent and summed in bfloat16 or wider, within the bound.
A program may use at most 128 MiB of HBM per device.

```python
import jax
import jax.numpy as jnp
from jax import lax

D = 768
HEADS = 12
HEAD_DIM = 64
FF = 3072
TEXT = 384
SEG = 128
DOC_LEN = 512
DOCS = 24
TOKENS = 12288
N_MP = 4


def text_lengths(key):
    key = jax.random.fold_in(key, 5)
    first_key, second_key = jax.random.split(key)
    lengths = jax.random.randint(first_key, (DOCS,), TEXT // 4, TEXT + 1)
    longest = jax.random.randint(second_key, (), 0, DOCS)
    return jnp.where(jnp.arange(DOCS) == longest, TEXT, lengths).astype(jnp.int32)


def draw_text_mask(key, part):
    lengths = text_lengths(key)
    return (jnp.arange(TEXT)[None, :] < lengths[:, None]).astype(jnp.int32)


def draw_alignment(key, part):
    lengths = text_lengths(key)
    key = jax.random.fold_in(key, 17)
    raw_values = jax.random.randint(key, (DOCS, SEG), 0, 1 << 20)
    picked = raw_values % lengths[:, None]
    corner = (lengths[:, None] == TEXT) & (jnp.arange(SEG)[None, :] == SEG - 1)
    return jnp.where(corner, TEXT - 1, picked).astype(jnp.int32)


def draw_segment_count(key, part):
    key = jax.random.fold_in(key, 23)
    first_key, second_key = jax.random.split(key)
    raw_values = jax.random.randint(first_key, (3, DOCS), 0, SEG - 4)
    counts = 5 + jnp.min(raw_values, axis=0)
    fullest = jax.random.randint(second_key, (), 0, DOCS)
    return jnp.where(jnp.arange(DOCS) == fullest, SEG, counts).astype(jnp.int32)


def slab_normal(key, shape, factors, slab_shape):
    return jax.random.normal(key, shape, jnp.float32) * jnp.asarray(factors, jnp.float32).reshape(slab_shape)


def attention_scales():
    base = D ** (-0.5)
    return (base, base, base, base * (TEXT / 2.0) ** 0.5)


def draw_attention_master(key, part):
    key = jax.random.fold_in(key, 31)
    return slab_normal(key, (D, 4, D), attention_scales(), (1, 4, 1))


def draw_attention_average(key, part):
    key = jax.random.fold_in(key, 32)
    return slab_normal(key, (D, 4, D), attention_scales(), (1, 4, 1))


def draw_attention_moment(key, part):
    key = jax.random.fold_in(key, 33)
    root = TOKENS ** 0.5
    return slab_normal(key, (D, 4, D), (root, root, 1.4 * root, root * (2.0 / TEXT) ** 0.5), (1, 4, 1))


def draw_feedforward_master(key, part):
    key = jax.random.fold_in(key, 41)
    return slab_normal(key, (D, 2, FF), (D ** (-0.5), FF ** (-0.5)), (1, 2, 1))


def draw_feedforward_average(key, part):
    key = jax.random.fold_in(key, 42)
    return slab_normal(key, (D, 2, FF), (D ** (-0.5), FF ** (-0.5)), (1, 2, 1))


def draw_feedforward_moment(key, part):
    key = jax.random.fold_in(key, 43)
    root = TOKENS ** 0.5
    return slab_normal(key, (D, 2, FF), (0.25 * root, 0.65 * root), (1, 2, 1))


def shared_values(key):
    first_key, second_key = jax.random.split(key)
    noise = 0.3 * jax.random.normal(first_key, (D, 6), jnp.float32)
    gains = 1.0 + jax.random.uniform(second_key, (D, 6), jnp.float32, -0.3, 0.3)
    column = jnp.arange(6)[None, :]
    return jnp.where((column == 1) | (column == 3), gains, noise)


def draw_shared_master(key, part):
    key = jax.random.fold_in(key, 51)
    return shared_values(key)


def draw_shared_average(key, part):
    key = jax.random.fold_in(key, 52)
    return shared_values(key)


def draw_shared_moment(key, part):
    key = jax.random.fold_in(key, 53)
    return 0.7 * TOKENS ** 0.5 * jax.random.normal(key, (D, 6), jnp.float32)


def draw_split_master(key, part):
    key = jax.random.fold_in(key, 61)
    return 0.3 * jax.random.normal(key, (D, 6), jnp.float32)


def draw_split_average(key, part):
    key = jax.random.fold_in(key, 62)
    return 0.3 * jax.random.normal(key, (D, 6), jnp.float32)


def draw_split_moment(key, part):
    key = jax.random.fold_in(key, 63)
    root = TOKENS ** 0.5
    return slab_normal(key, (D, 6), (root, 1.4 * root, 0.25 * root, 0.25 * root, 0.25 * root, 0.25 * root), (1, 6))


def levels(stream_key, extent, shards, least, top_value):
    loudness, own = 1.0, jax.random.fold_in(stream_key, 6)
    for dim, parts in shards:
        heights = jnp.exp(jax.random.uniform(jax.random.fold_in(own, dim), (parts,), jnp.float32, least / len(shards), top_value / len(shards)))
        loudness = loudness * jnp.repeat(heights, extent[dim] // parts).reshape([-1 if axis == dim else 1 for axis in range(len(extent))])
    return loudness


def centred(own_key, dims, width, reach, cuts=(), kind=jnp.bfloat16):
    entries = width * jax.random.normal(own_key, dims, jnp.float32)
    if cuts:
        entries = entries * levels(own_key, dims, cuts, -0.22, 0.18)
    return jnp.clip(entries, -reach, reach).astype(kind)


def setup_inputs(seed: int = 0) -> dict:
    key_list = jax.random.split(jax.random.key(seed), 18)
    tokens = centred(key_list[0], (TOKENS, D), 1.0, 6.0, ((0, 8),))
    alignment = draw_alignment(jax.random.fold_in(key_list[17], 71), 0)
    segment_count = draw_segment_count(jax.random.fold_in(key_list[17], 71), 0)
    text_mask = draw_text_mask(jax.random.fold_in(key_list[17], 71), 0)
    cotangent = centred(key_list[4], (TOKENS, D), 1.0, 6.0, ((0, 8),))
    attention_master = draw_attention_master(jax.random.fold_in(key_list[17], 71), 0)
    attention_moment = draw_attention_moment(jax.random.fold_in(key_list[17], 71), 0)
    attention_average = draw_attention_average(jax.random.fold_in(key_list[17], 71), 0)
    feedforward_master = draw_feedforward_master(jax.random.fold_in(key_list[17], 71), 0)
    feedforward_moment = draw_feedforward_moment(jax.random.fold_in(key_list[17], 71), 0)
    feedforward_average = draw_feedforward_average(jax.random.fold_in(key_list[17], 71), 0)
    shared_master = draw_shared_master(jax.random.fold_in(key_list[17], 71), 0)
    shared_moment = draw_shared_moment(jax.random.fold_in(key_list[17], 71), 0)
    shared_average = draw_shared_average(jax.random.fold_in(key_list[17], 71), 0)
    split_master = draw_split_master(jax.random.fold_in(key_list[17], 71), 0)
    split_moment = draw_split_moment(jax.random.fold_in(key_list[17], 71), 0)
    split_average = draw_split_average(jax.random.fold_in(key_list[17], 71), 0)
    return {"tokens": tokens, "alignment": alignment, "segment_count": segment_count, "text_mask": text_mask, "cotangent": cotangent, "attention_master": attention_master, "attention_moment": attention_moment, "attention_average": attention_average, "feedforward_master": feedforward_master, "feedforward_moment": feedforward_moment, "feedforward_average": feedforward_average, "shared_master": shared_master, "shared_moment": shared_moment, "shared_average": shared_average, "split_master": split_master, "split_moment": split_moment, "split_average": split_average}


@jax.custom_vjp
def low(v):
    return lax.optimization_barrier(v.astype(jnp.bfloat16)).astype(jnp.float32)

@jax.custom_vjp
def low_back(v):
    return v

def low_keep(v):
    return (low(v), None)

def low_pass(kept, grad):
    return (grad,)

def back_keep(v):
    return (v, None)

def back_low(kept, grad):
    return (low(grad),)
low.defvjp(low_keep, low_pass)
low_back.defvjp(back_keep, back_low)
EPS = 1e-05
MOMENTUM = 0.9
AVERAGE = 0.75
ATTENTION_RATES = (4e-05, 4e-05, 4e-05, 0.01)
FEEDFORWARD_RATES = (0.0002, 4e-05)
SHARED_RATE = 0.0006
SPLIT_RATES = (0.0004, 0.0003, 0.0017, 0.0017, 0.0017, 0.0017)
HIGHEST_MODE = lax.Precision.HIGHEST

def product(left, right):
    return jnp.dot(left, right, precision=HIGHEST_MODE, preferred_element_type=jnp.float32)

def layer_norm(value, gain, shift):
    center = value - lax.optimization_barrier(jnp.mean(value, axis=-1, keepdims=True))
    spread = lax.optimization_barrier(jnp.mean(center * center, axis=-1, keepdims=True))
    return center * lax.rsqrt(spread + EPS) * gain + shift

def document_attention(pieces):
    queries, key_rows, value_rows, valid_keys = pieces
    scores = jnp.einsum('qhd,khd->hqk', queries, key_rows, precision=HIGHEST_MODE) * HEAD_DIM ** (-0.5)
    scores = low_back(scores)
    scores = jnp.where(valid_keys[None, None, :], scores, -1e+30)
    row_max = lax.optimization_barrier(jnp.max(scores, axis=-1, keepdims=True))
    exponent = jnp.exp(scores - row_max)
    probability = low(exponent / lax.optimization_barrier(jnp.sum(exponent, axis=-1, keepdims=True)))
    return jnp.einsum('hqk,khd->qhd', probability, value_rows, precision=HIGHEST_MODE)

def by_heads(matrix):
    return matrix.reshape(DOCS, DOC_LEN, HEADS, HEAD_DIM)

def forward(inputs, attention, feedforward, shared, split_bias, alignment, live_slots, valid_keys):
    text_part = inputs[:, :TEXT]
    taken_rows = jnp.take_along_axis(text_part, alignment[:, :, None], axis=1)
    layer_in = jnp.concatenate([text_part, inputs[:, TEXT:] + taken_rows * live_slots[:, :, None]], axis=1).reshape(TOKENS, D)
    attention = low(attention)
    feedforward = low(feedforward)
    shared = low(shared)
    split_bias = low(split_bias)
    rows_in = low(layer_in)
    queries = low(low_back(product(rows_in, attention[:, 0]) + split_bias[:, 0]))
    key_rows = low(low_back(product(rows_in, attention[:, 1])))
    value_rows = low(low_back(product(rows_in, attention[:, 2]) + split_bias[:, 1]))
    context = lax.map(jax.checkpoint(document_attention), (by_heads(queries), by_heads(key_rows), by_heads(value_rows), valid_keys))
    context = low(low_back(context.reshape(TOKENS, D)))
    head_cols = D // N_MP
    unit_cols = FF // N_MP
    joined = jnp.zeros((TOKENS, D), jnp.float32)
    for group in range(N_MP):
        head_slice = slice(group * head_cols, (group + 1) * head_cols)
        joined = joined + low(product(context[:, head_slice], attention[:, 3, head_slice].T))
    mixed = layer_in + low_back(joined) + shared[:, 0]
    first_norm = layer_norm(mixed, shared[:, 1], shared[:, 2])
    hidden_in = low(first_norm)
    inner_pre = low_back(product(hidden_in, feedforward[:, 0]) + split_bias[:, 2:].reshape(FF))
    active = low(jax.nn.gelu(inner_pre, approximate=False))
    down_sum = jnp.zeros((TOKENS, D), jnp.float32)
    for group in range(N_MP):
        unit_slice = slice(group * unit_cols, (group + 1) * unit_cols)
        down_sum = down_sum + low(product(active[:, unit_slice], feedforward[:, 1, unit_slice].T))
    second = first_norm + low_back(down_sum) + shared[:, 5]
    return layer_norm(second, shared[:, 3], shared[:, 4])

def renew(master, moment, average, gradient, rates):
    velocity = MOMENTUM * moment + gradient
    updated = master - rates * (gradient + MOMENTUM * velocity)
    averaged = AVERAGE * average + (1.0 - AVERAGE) * updated
    return (velocity, updated, averaged, updated.astype(jnp.bfloat16))

def reference(tokens, alignment, segment_count, text_mask, cotangent, attention_master, attention_moment, attention_average, feedforward_master, feedforward_moment, feedforward_average, shared_master, shared_moment, shared_average, split_master, split_moment, split_average):
    live_mask = jnp.arange(SEG)[None, :] < segment_count[:, None]
    live_slots = live_mask.astype(jnp.float32)
    valid_keys = jnp.concatenate([text_mask > 0, live_mask], axis=1)
    inputs = tokens.astype(jnp.float32).reshape(DOCS, DOC_LEN, D)

    def wrapped(inputs, attention, feedforward, shared, split_bias):
        return forward(inputs, attention, feedforward, shared, split_bias, alignment, live_slots, valid_keys)
    output, pull = jax.vjp(wrapped, inputs, attention_master, feedforward_master, shared_master, split_master)
    grad_inputs, grad_attention, grad_feedforward, grad_shared, grad_split = pull(cotangent.astype(jnp.float32))
    attention_new = renew(attention_master, attention_moment, attention_average, grad_attention, jnp.asarray(ATTENTION_RATES, jnp.float32).reshape(1, 4, 1))
    feedforward_new = renew(feedforward_master, feedforward_moment, feedforward_average, grad_feedforward, jnp.asarray(FEEDFORWARD_RATES, jnp.float32).reshape(1, 2, 1))
    shared_new = renew(shared_master, shared_moment, shared_average, grad_shared, SHARED_RATE)
    split_new = renew(split_master, split_moment, split_average, grad_split, jnp.asarray(SPLIT_RATES, jnp.float32).reshape(1, 6))
    return (output.astype(jnp.bfloat16), grad_inputs.reshape(TOKENS, D), attention_new[0], attention_new[1], attention_new[2], attention_new[3], feedforward_new[0], feedforward_new[1], feedforward_new[2], feedforward_new[3], shared_new[0], shared_new[1], shared_new[2], shared_new[3], split_new[0], split_new[1], split_new[2], split_new[3])
```

```python
from functools import partial

import jax
import jax.numpy as jnp
from jax import lax
from jax.experimental import pallas as pl
from jax.experimental.pallas import tpu as pltpu
from jax.sharding import PartitionSpec as P

MESH = pl.DeviceIdType.MESH

HEAD_DIM = 64


EPS = 1e-05
MOMENTUM = 0.9
AVERAGE = 0.75
ATTENTION_RATES = (4e-05, 4e-05, 4e-05, 0.01)
FEEDFORWARD_RATES = (0.0002, 4e-05)
SHARED_RATE = 0.0006
SPLIT_RATES = (0.0004, 0.0003, 0.0017, 0.0017, 0.0017, 0.0017)
HIGHEST_MODE = lax.Precision.HIGHEST


def contract_last(left, right):
    return lax.dot_general(
        left, right, (((1,), (1,)), ((), ())), preferred_element_type=jnp.float32
    )


def contract_rows(left, right):
    return lax.dot_general(
        left, right, (((0,), (0,)), ((), ())), preferred_element_type=jnp.float32
    )


def layer_norm(value, gain, shift):
    center = value - jnp.mean(value, axis=-1, keepdims=True)
    factor = lax.rsqrt(jnp.mean(center * center, axis=-1, keepdims=True) + EPS)
    normed = center * factor
    return (normed * gain + shift, normed, factor)


def norm_back(incoming, normed, factor, gain):
    scaled = incoming * gain
    inner_part = (
        scaled
        - jnp.mean(scaled, axis=-1, keepdims=True)
        - normed * jnp.mean(scaled * normed, axis=-1, keepdims=True)
    )
    return (factor * inner_part, jnp.sum(incoming * normed, axis=0), jnp.sum(incoming, axis=0))


def masked_scores(queries, key_rows, valid_keys):
    scores = jnp.einsum(
        "qhd,khd->hqk", queries, key_rows, preferred_element_type=jnp.float32
    ) * HEAD_DIM ** (-0.5)
    return jnp.where(valid_keys[None, None, :], scores, -1e30)


def attend(pieces):
    queries, key_rows, value_rows, valid_keys = pieces
    scores = masked_scores(queries, key_rows, valid_keys)
    row_max = jnp.max(scores, axis=-1, keepdims=True)
    exponent = jnp.exp(scores - row_max)
    row_total = jnp.sum(exponent, axis=-1, keepdims=True)
    probability = (exponent / row_total).astype(jnp.bfloat16)
    context = jnp.einsum(
        "hqk,khd->qhd", probability, value_rows, preferred_element_type=jnp.float32
    )
    return (context.astype(jnp.bfloat16), row_max + jnp.log(row_total))


def attend_back(pieces):
    queries, key_rows, value_rows, valid_keys, upstream, logsum = pieces
    scores = masked_scores(queries, key_rows, valid_keys)
    probability = jnp.exp(scores - logsum)
    grad_values = jnp.einsum(
        "hqk,qhd->khd",
        probability.astype(jnp.bfloat16),
        upstream,
        preferred_element_type=jnp.float32,
    )
    grad_probs = jnp.einsum(
        "qhd,khd->hqk", upstream, value_rows, preferred_element_type=jnp.float32
    )
    row_delta = jnp.sum(probability * grad_probs, axis=-1, keepdims=True)
    grad_scores = (probability * (grad_probs - row_delta)).astype(jnp.bfloat16)
    grad_queries = jnp.einsum(
        "hqk,khd->qhd", grad_scores, key_rows, preferred_element_type=jnp.float32
    ) * HEAD_DIM ** (-0.5)
    grad_keys = jnp.einsum(
        "hqk,qhd->khd", grad_scores, queries, preferred_element_type=jnp.float32
    ) * HEAD_DIM ** (-0.5)
    return (
        grad_queries.astype(jnp.bfloat16),
        grad_keys.astype(jnp.bfloat16),
        grad_values.astype(jnp.bfloat16),
    )


def renew(master, moment, average, gradient, rates):
    velocity = MOMENTUM * moment + gradient
    updated = master - rates * (gradient + MOMENTUM * velocity)
    averaged = AVERAGE * average + (1.0 - AVERAGE) * updated
    return (velocity, updated, averaged, updated.astype(jnp.bfloat16))


def general_shards(
    tokens,
    alignment,
    segment_count,
    text_mask,
    cotangent,
    attention_master,
    attention_moment,
    attention_average,
    feedforward_master,
    feedforward_moment,
    feedforward_average,
    shared_master,
    shared_moment,
    shared_average,
    split_master,
    split_moment,
    split_average,
):
    documents, slot_count = alignment.shape
    text_rows = text_mask.shape[1]
    document_rows = text_rows + slot_count
    model_width = tokens.shape[1]
    local_width = split_master.shape[0]
    local_heads = local_width // HEAD_DIM
    row_count = documents * document_rows
    attention_full, feedforward_full, shared_full = (
        lax.all_gather(attention_master.astype(jnp.bfloat16), "dp", axis=0, tiled=True),
        lax.all_gather(feedforward_master.astype(jnp.bfloat16), "dp", axis=0, tiled=True),
        lax.all_gather(shared_master.astype(jnp.bfloat16), "dp", axis=0, tiled=True),
    )
    shared = shared_full.astype(jnp.float32)
    split_bias = lax.optimization_barrier(split_master.astype(jnp.bfloat16)).astype(jnp.float32)
    live_slots = (
        lax.broadcasted_iota(jnp.int32, (documents, slot_count), 1) < segment_count[:, None]
    )
    valid_keys = jnp.concatenate([text_mask > 0, live_slots], axis=1)
    text_index = lax.broadcasted_iota(jnp.int32, (documents, slot_count, text_rows), 2)
    pick_table = ((alignment[:, :, None] == text_index) & live_slots[:, :, None]).astype(
        jnp.bfloat16
    )
    inputs = tokens.reshape(documents, document_rows, model_width)
    taken_rows = jnp.einsum(
        "dst,dtw->dsw", pick_table, inputs[:, :text_rows], preferred_element_type=jnp.float32
    )
    layer_in = jnp.concatenate(
        [
            inputs[:, :text_rows].astype(jnp.float32),
            inputs[:, text_rows:].astype(jnp.float32) + taken_rows,
        ],
        axis=1,
    ).reshape(row_count, model_width)
    rows_in = layer_in.astype(jnp.bfloat16)
    project_weights = attention_full[:, :3].reshape(model_width, 3 * local_width)
    project_bias = jnp.concatenate(
        [split_bias[:, 0], jnp.zeros_like(split_bias[:, 0]), split_bias[:, 1]]
    )
    projected = (
        jnp.dot(rows_in, project_weights, preferred_element_type=jnp.float32) + project_bias
    ).astype(jnp.bfloat16)
    projected = projected.reshape(documents, document_rows, 3, local_heads, HEAD_DIM)
    queries = projected[:, :, 0]
    key_rows = projected[:, :, 1]
    value_rows = projected[:, :, 2]
    context, logsum = lax.map(attend, (queries, key_rows, value_rows, valid_keys))
    context_rows = context.reshape(row_count, local_width)
    joined = lax.psum(
        contract_last(context_rows, attention_full[:, 3]).astype(jnp.bfloat16), "mp"
    ).astype(jnp.float32)
    mixed = layer_in + joined + shared[:, 0]
    first_norm, normed_one, factor_one = layer_norm(mixed, shared[:, 1], shared[:, 2])
    hidden_in = first_norm.astype(jnp.bfloat16)
    inner_pre = jnp.dot(
        hidden_in, feedforward_full[:, 0], preferred_element_type=jnp.float32
    ) + split_bias[:, 2:].reshape(-1)
    active = jax.nn.gelu(inner_pre, approximate=False).astype(jnp.bfloat16)
    down_sum = lax.psum(
        contract_last(active, feedforward_full[:, 1]).astype(jnp.bfloat16), "mp"
    ).astype(jnp.float32)
    second = first_norm + down_sum + shared[:, 5]
    output, normed_two, factor_two = layer_norm(second, shared[:, 3], shared[:, 4])
    grad_second, grad_gain_two, grad_shift_two = norm_back(
        cotangent.astype(jnp.float32), normed_two, factor_two, shared[:, 3]
    )
    grad_down = grad_second.astype(jnp.bfloat16)
    grad_active = jnp.dot(grad_down, feedforward_full[:, 1], preferred_element_type=jnp.float32)
    gelu_value, gelu_pull = jax.vjp(partial(jax.nn.gelu, approximate=False), inner_pre)
    grad_inner = gelu_pull(grad_active)[0].astype(jnp.bfloat16)
    feedforward_grad = jnp.stack(
        [contract_rows(hidden_in, grad_inner), contract_rows(grad_down, active)], axis=1
    )
    grad_first = grad_second + lax.psum(
        contract_last(grad_inner, feedforward_full[:, 0]).astype(jnp.bfloat16), "mp"
    ).astype(jnp.float32)
    grad_mixed, grad_gain_one, grad_shift_one = norm_back(
        grad_first, normed_one, factor_one, shared[:, 1]
    )
    grad_joined = grad_mixed.astype(jnp.bfloat16)
    output_grad = contract_rows(grad_joined, context_rows)
    grad_context = jnp.dot(
        grad_joined, attention_full[:, 3], preferred_element_type=jnp.float32
    ).astype(jnp.bfloat16)
    upstream = grad_context.reshape(documents, document_rows, local_heads, HEAD_DIM)
    grad_queries, grad_keys, grad_values = lax.map(
        attend_back, (queries, key_rows, value_rows, valid_keys, upstream, logsum)
    )
    query_rows = grad_queries.reshape(row_count, local_width)
    value_grad_rows = grad_values.reshape(row_count, local_width)
    grad_project = jnp.concatenate(
        [query_rows, grad_keys.reshape(row_count, local_width), value_grad_rows], axis=1
    )
    project_grad = contract_rows(rows_in, grad_project).reshape(model_width, 3, local_width)
    attention_grad = jnp.concatenate([project_grad, output_grad[:, None, :]], axis=1)
    grad_layer_in = grad_mixed + lax.psum(
        contract_last(grad_project, project_weights).astype(jnp.bfloat16), "mp"
    ).astype(jnp.float32)
    shared_grad = jnp.stack(
        [
            jnp.sum(grad_mixed, axis=0),
            grad_gain_one,
            grad_shift_one,
            grad_gain_two,
            grad_shift_two,
            jnp.sum(grad_second, axis=0),
        ],
        axis=1,
    )
    split_grad = jnp.concatenate(
        [
            jnp.sum(query_rows, axis=0, dtype=jnp.float32)[:, None],
            jnp.sum(value_grad_rows, axis=0, dtype=jnp.float32)[:, None],
            jnp.sum(grad_inner, axis=0, dtype=jnp.float32).reshape(local_width, 4),
        ],
        axis=1,
    )
    grad_documents = grad_layer_in.reshape(documents, document_rows, model_width)
    moved_rows = jnp.einsum(
        "dst,dsw->dtw",
        pick_table.astype(jnp.float32),
        grad_documents[:, text_rows:],
        precision=HIGHEST_MODE,
        preferred_element_type=jnp.float32,
    )
    input_gradient = jnp.concatenate(
        [grad_documents[:, :text_rows] + moved_rows, grad_documents[:, text_rows:]], axis=1
    ).reshape(row_count, model_width)
    attention_sum, feedforward_sum, shared_sum = (
        lax.psum_scatter(attention_grad, "dp", scatter_dimension=0, tiled=True),
        lax.psum_scatter(feedforward_grad, "dp", scatter_dimension=0, tiled=True),
        lax.psum_scatter(shared_grad, "dp", scatter_dimension=0, tiled=True),
    )
    split_sum = lax.psum(split_grad, "dp")
    attention_new = renew(
        attention_master,
        attention_moment,
        attention_average,
        attention_sum,
        jnp.asarray(ATTENTION_RATES, jnp.float32).reshape(1, 4, 1),
    )
    feedforward_new = renew(
        feedforward_master,
        feedforward_moment,
        feedforward_average,
        feedforward_sum,
        jnp.asarray(FEEDFORWARD_RATES, jnp.float32).reshape(1, 2, 1),
    )
    shared_new = renew(shared_master, shared_moment, shared_average, shared_sum, SHARED_RATE)
    split_new = renew(
        split_master,
        split_moment,
        split_average,
        split_sum,
        jnp.asarray(SPLIT_RATES, jnp.float32).reshape(1, 6),
    )
    return (
        output.astype(jnp.bfloat16),
        input_gradient,
        attention_new[0],
        attention_new[1],
        attention_new[2],
        attention_new[3],
        feedforward_new[0],
        feedforward_new[1],
        feedforward_new[2],
        feedforward_new[3],
        shared_new[0],
        shared_new[1],
        shared_new[2],
        shared_new[3],
        split_new[0],
        split_new[1],
        split_new[2],
        split_new[3],
    )


def place():
    dp, z = lax.axis_index("dp"), lax.axis_index("mp")
    return z, lax.div(dp, 4), lax.rem(lax.div(dp, 2), 2), lax.rem(dp, 2)


def device(z, y, x, c):
    return (y * 4 + x * 2 + c, z)


def nearest_level(z, k):
    low, high = lax.rem(z, 2), lax.div(z, 2)
    if k == 0:
        return z
    if k == 1:
        return 1 + (2 * high - 1) * low
    if k == 2:
        return 2 + high * (1 - 2 * low)
    return 3 - 3 * high


def greet(z, y, x, c):
    barrier = pltpu.get_barrier_semaphore()
    partners = [device(z, y, x, 1 - c), device(z, y, 1 - x, c), device(z, 1 - y, x, c)]
    partners += [device(lax.rem(z + k, 4), y, x, c) for k in (1, 2, 3)]
    for partner in partners:
        pl.semaphore_signal(barrier, inc=1, device_id=partner, device_id_type=MESH)
    pl.semaphore_wait(barrier, len(partners))


def remote(source, target, send, recv, to):
    return pltpu.make_async_remote_copy(
        src_ref=source, dst_ref=target, send_sem=send, recv_sem=recv, device_id=to, device_id_type=MESH
    )


def when(condition, action):
    pl.when(condition)(action)


def gather_kernel(
    own_ref, small_ref, full_ref, plane_ref, line_ref,
    line_send, line_recv, first_send, first_recv, second_send, second_recv, pair_send, pair_recv,
    tiny_send, tiny_recv, own_sem, tiny_own,
):
    z, y, x, c = place()
    greet(z, y, x, c)
    up, down = device(z + 1, y, x, c), device(z - 1, y, x, c)
    across_x, across_y, pair = device(z, y, 1 - x, c), device(z, 1 - y, x, c), device(z, y, x, 1 - c)

    def line_copy(t, level, source, way):
        return remote(
            source, full_ref.at[t, level, y, x, c], line_send.at[t, level, way], line_recv.at[t, level],
            up if way == 0 else down,
        )

    own_copies = []
    for t in range(3):
        when(z < 3, lambda t=t: line_copy(t, z, own_ref.at[t], 0).start())
        when(z > 0, lambda t=t: line_copy(t, z, own_ref.at[t], 1).start())
        copy = pltpu.make_async_copy(own_ref.at[t], full_ref.at[t, z, y, x, c], own_sem.at[t])
        copy.start()
        own_copies.append(copy)

    tiny = [pltpu.make_async_copy(small_ref, plane_ref.at[y, x, c], tiny_own.at[0]),
            pltpu.make_async_copy(small_ref, line_ref.at[z], tiny_own.at[1])]
    for copy in tiny:
        copy.start()
    far = [
        remote(small_ref, line_ref.at[z], tiny_send.at[k], tiny_recv.at[k], device(lax.rem(z + k, 4), y, x, c))
        for k in (1, 2, 3)
    ]
    for copy in far:
        copy.start()
    for copy in tiny:
        copy.wait()
    tiny_steps = [
        remote(plane_ref.at[y, x, c], plane_ref.at[y, x, c], tiny_send.at[4], tiny_recv.at[4], across_x),
        remote(plane_ref.at[y, :, c], plane_ref.at[y, :, c], tiny_send.at[5], tiny_recv.at[5], across_y),
        remote(plane_ref.at[:, :, c], plane_ref.at[:, :, c], tiny_send.at[6], tiny_recv.at[6], pair),
    ]

    def first_copy(t, k):
        level = nearest_level(z, k)
        block = full_ref.at[t, level, y, x, c]
        return remote(
            own_ref.at[t] if k == 0 else block, block, first_send.at[t, k], first_recv.at[t, k],
            across_x if (t + k) % 2 == 0 else across_y,
        )

    def second_copy(t, k):
        level = nearest_level(z, k)
        if (t + k) % 2 == 0:
            block, to = full_ref.at[t, level, y, :, c], across_y
        else:
            block, to = full_ref.at[t, level, :, x, c], across_x
        return remote(block, block, second_send.at[t, k], second_recv.at[t, k], to)

    def pair_copy(t, k):
        block = full_ref.at[t, nearest_level(z, k), :, :, c]
        return remote(block, block, pair_send.at[t, k], pair_recv.at[t, k], pair)

    def arrive(t, k):
        if k > 0:
            level = nearest_level(z, k)
            block = full_ref.at[t, level, y, x, c]
            line_copy(t, level, block, 0).wait_recv()
            when((level < z) & (z < 3), lambda: line_copy(t, level, block, 0).start())
            when((level > z) & (z > 0), lambda: line_copy(t, level, block, 1).start())
        first_copy(t, k).start()

    units = [(t, k) for t in range(3) for k in range(4)]
    count = len(units)
    for step in range(count + 3):
        if step < count:
            arrive(*units[step])
        if step < 3:
            tiny_steps[step].start()
        if 0 <= step - 1 < count:
            t, k = units[step - 1]
            first_copy(t, k).wait_recv()
            if k == 0:
                own_copies[t].wait()
            second_copy(t, k).start()
        if 0 <= step - 2 < count:
            second_copy(*units[step - 2]).wait_recv()
            pair_copy(*units[step - 2]).start()
        if 0 <= step - 3 < count:
            pair_copy(*units[step - 3]).wait_recv()
        if step < 3:
            tiny_steps[step].wait_recv()
    for copy in far:
        copy.wait()
    for copy in tiny_steps:
        copy.wait_send()
    for t, k in units:
        level = nearest_level(z, k)
        block = full_ref.at[t, level, y, x, c]
        if k == 0:
            when(z < 3, lambda t=t: line_copy(t, z, own_ref.at[t], 0).wait_send())
            when(z > 0, lambda t=t: line_copy(t, z, own_ref.at[t], 1).wait_send())
        else:
            when((level < z) & (z < 3), lambda t=t, level=level, block=block: line_copy(t, level, block, 0).wait_send())
            when((level > z) & (z > 0), lambda t=t, level=level, block=block: line_copy(t, level, block, 1).wait_send())
        first_copy(t, k).wait_send()
        second_copy(t, k).wait_send()
        pair_copy(t, k).wait_send()


def gather(own, small):
    dma = pltpu.SemaphoreType.DMA
    return pl.pallas_call(
        gather_kernel,
        out_shape=(
            jax.ShapeDtypeStruct((3, 4, 2, 2, 2, 96, 768), jnp.bfloat16),
            jax.ShapeDtypeStruct((2, 2, 2, 16, 256), jnp.bfloat16),
            jax.ShapeDtypeStruct((4, 16, 256), jnp.bfloat16),
        ),
        in_specs=[pl.BlockSpec(memory_space=pl.ANY)] * 2,
        out_specs=(pl.BlockSpec(memory_space=pl.ANY),) * 3,
        scratch_shapes=[
            dma((3, 4, 2)), dma((3, 4)), dma((3, 4)), dma((3, 4)), dma((3, 4)), dma((3, 4)), dma((3, 4)), dma((3, 4)),
            dma((7,)), dma((7,)), dma((3,)), dma((2,)),
        ],
        compiler_params=pltpu.CompilerParams(collective_id=0, has_side_effects=True),
        name="gather_weights",
    )(own, small)


SOURCES = (0, 2, 3)
LEVEL_ORDER = (0, 3, 1, 2)
PIECES = 4


def reduce_kernel(
    grads_ref, small_ref, text_ref, back_ref,
    sum_ref, small_sum_ref, text_all, back_all,
    total, pair_in, first_in, second_in, line_in, small_total, small_in, line_small,
    pair_send, pair_recv, first_send, first_recv, second_send, second_recv, line_send, line_recv,
    small_send, small_recv, cast_send, cast_recv, cast_own,
):
    z, y, x, c = place()
    greet(z, y, x, c)
    up, down = device(z + 1, y, x, c), device(z - 1, y, x, c)
    across_x, across_y, pair = device(z, y, 1 - x, c), device(z, 1 - y, x, c), device(z, y, x, 1 - c)
    rows = text_ref.shape[0] // PIECES

    pieces = [(a, d, p) for p in range(PIECES) for d in range(3) for a in range(2)]
    arrays = ((text_ref, text_all), (back_ref, back_all))

    def cast_copy(a, d, p, way, first):
        part = pl.ds(p * rows, rows)
        target = arrays[a][1].at[d, part]
        source = arrays[a][0].at[part] if first else target
        return remote(
            source, target, cast_send.at[a, d, p, way], cast_recv.at[a, d, p], up if way == 0 else down
        )

    own_copies = []
    for a in range(2):
        for d, start in enumerate(SOURCES):
            copy = pltpu.make_async_copy(arrays[a][0], arrays[a][1].at[d], cast_own.at[a, d])
            own_copies.append((start, copy))
            when(z == start, lambda copy=copy: copy.start())
    for a, d, p in pieces:
        start = SOURCES[d]
        if start < 3:
            when(z == start, lambda a=a, d=d, p=p: cast_copy(a, d, p, 0, True).start())
        if start > 0:
            when(z == start, lambda a=a, d=d, p=p: cast_copy(a, d, p, 1, True).start())

    def relay(a, d, p):
        start = SOURCES[d]

        def from_below():
            cast_copy(a, d, p, 0, False).wait_recv()
            when(z < 3, lambda: cast_copy(a, d, p, 0, False).start())

        def from_above():
            cast_copy(a, d, p, 1, False).wait_recv()
            when(z > 0, lambda: cast_copy(a, d, p, 1, False).start())

        if start < 3:
            when(z > start, from_below)
        if start > 0:
            when(z < start, from_above)

    units = [(t, level) for level in LEVEL_ORDER for t in range(3)]

    def along_x(u):
        return u % 2 == 0

    def pair_copy(u):
        t, level = units[u]
        return remote(
            grads_ref.at[t, level, :, :, 1 - c], pair_in.at[u], pair_send.at[u], pair_recv.at[u], pair
        )

    def first_copy(u):
        source = total.at[u, :, 1 - x] if along_x(u) else total.at[u, 1 - y]
        return remote(
            source, first_in.at[u], first_send.at[u], first_recv.at[u], across_x if along_x(u) else across_y
        )

    def second_copy(u):
        return remote(
            total.at[u, 1 - y, x] if along_x(u) else total.at[u, y, 1 - x],
            second_in.at[u], second_send.at[u], second_recv.at[u], across_y if along_x(u) else across_x,
        )

    def line_copy(u, way):
        return remote(
            total.at[u, y, x], line_in.at[u, way], line_send.at[u], line_recv.at[u, way], up if way == 0 else down
        )

    def line_step(u):
        t, level = units[u]

        def below():
            line_copy(u, 0).wait_recv()
            total[u, y, x] = total[u, y, x] + line_in[u, 0]

        def above():
            line_copy(u, 1).wait_recv()
            total[u, y, x] = total[u, y, x] + line_in[u, 1]

        if level > 0:
            when((z <= level) & (z > 0), below)
        if level < 3:
            when((z >= level) & (z < 3), above)
        when(z < level, lambda: line_copy(u, 0).start())
        when(z > level, lambda: line_copy(u, 1).start())

        def finish():
            sum_ref[t] = total[u, y, x].astype(jnp.float32)

        when(z == level, finish)

    small_steps = [
        remote(small_total.at[i], small_in.at[i], small_send.at[i], small_recv.at[i], to)
        for i, to in enumerate((pair, across_x, across_y))
    ]
    far = [
        remote(small_total.at[3], line_small.at[z], small_send.at[2 + k], small_recv.at[2 + k], device(lax.rem(z + k, 4), y, x, c))
        for k in (1, 2, 3)
    ]
    for u in range(12):
        pair_copy(u).start()
    small_total[0] = small_ref[...]
    for step in range(12 + 3):
        if step < 12:
            t, level = units[step]
            pair_copy(step).wait_recv()
            total[step] = grads_ref[t, level, :, :, c] + pair_in[step]
            first_copy(step).start()
        if step < 3:
            small_steps[step].start()
        if 0 <= step - 1 < 12:
            u = step - 1
            first_copy(u).wait_recv()
            if along_x(u):
                total[u, :, x] = total[u, :, x] + first_in[u]
            else:
                total[u, y] = total[u, y] + first_in[u]
            second_copy(u).start()
        if 0 <= step - 2 < 12:
            u = step - 2
            second_copy(u).wait_recv()
            total[u, y, x] = total[u, y, x] + second_in[u]
        if step < 3:
            small_steps[step].wait_recv()
            small_total[step + 1] = small_total[step] + small_in[step]
            if step == 2:
                for copy in far:
                    copy.start()
                line_small[z] = small_total[3]
        if 0 <= step - 3 < 12:
            line_step(step - 3)
        for piece in pieces[2 * step : 2 * step + 2]:
            relay(*piece)
    for copy in far:
        copy.wait()
    small_sum_ref[...] = line_small[0] + line_small[1] + line_small[2] + line_small[3]
    for copy in small_steps:
        copy.wait_send()
    for start, copy in own_copies:
        when(z == start, lambda copy=copy: copy.wait())
    for u in range(12):
        t, level = units[u]
        pair_copy(u).wait_send()
        first_copy(u).wait_send()
        second_copy(u).wait_send()
        when(z < level, lambda u=u: line_copy(u, 0).wait_send())
        when(z > level, lambda u=u: line_copy(u, 1).wait_send())
    for a, d, p in pieces:
        start = SOURCES[d]
        if start < 3:
            when((z >= start) & (z < 3), lambda a=a, d=d, p=p: cast_copy(a, d, p, 0, True).wait_send())
        if start > 0:
            when((z <= start) & (z > 0), lambda a=a, d=d, p=p: cast_copy(a, d, p, 1, True).wait_send())


def reduce_all(grads, small, text, back):
    dma = pltpu.SemaphoreType.DMA
    whole = jax.ShapeDtypeStruct((3, 512, 768), jnp.bfloat16)
    vmem = pl.BlockSpec(memory_space=pltpu.VMEM)
    hbm = pl.BlockSpec(memory_space=pl.ANY)
    block = jnp.bfloat16
    return pl.pallas_call(
        reduce_kernel,
        out_shape=(
            jax.ShapeDtypeStruct((3, 96, 768), jnp.float32),
            jax.ShapeDtypeStruct((16, 768), jnp.float32),
            whole,
            whole,
        ),
        in_specs=[vmem, vmem, hbm, hbm],
        out_specs=(vmem, vmem, hbm, hbm),
        scratch_shapes=[
            pltpu.VMEM((12, 2, 2, 96, 768), block),
            pltpu.VMEM((12, 2, 2, 96, 768), block),
            pltpu.VMEM((12, 2, 96, 768), block),
            pltpu.VMEM((12, 96, 768), block),
            pltpu.VMEM((12, 2, 96, 768), block),
            pltpu.VMEM((4, 16, 768), jnp.float32),
            pltpu.VMEM((3, 16, 768), jnp.float32),
            pltpu.VMEM((4, 16, 768), jnp.float32),
            dma((12,)), dma((12,)), dma((12,)), dma((12,)), dma((12,)), dma((12,)), dma((12,)), dma((12, 2)),
            dma((6,)), dma((6,)), dma((2, 3, PIECES, 2)), dma((2, 3, PIECES)), dma((2, 3)),
        ],
        compiler_params=pltpu.CompilerParams(
            collective_id=1, has_side_effects=True, vmem_limit_bytes=58 * 2**20
        ),
        name="reduce_gradients",
    )(grads, small, text, back)


def line_shards(
    tokens,
    alignment,
    segment_count,
    text_mask,
    cotangent,
    attention_master,
    attention_moment,
    attention_average,
    feedforward_master,
    feedforward_moment,
    feedforward_average,
    shared_master,
    shared_moment,
    shared_average,
    split_master,
    split_moment,
    split_average,
):
    documents, slot_count = alignment.shape
    text_rows = text_mask.shape[1]
    rows = text_rows + slot_count
    width = tokens.shape[1]
    low = jnp.bfloat16
    level = lax.axis_index("mp")
    own = jnp.concatenate(
        [attention_master.reshape(1, 96, 768), jnp.swapaxes(feedforward_master, 0, 1)], axis=0
    ).astype(low)
    small = jnp.concatenate(
        [
            jnp.pad(shared_master.T, ((0, 0), (0, 160))),
            jnp.pad(split_master.T, ((0, 4), (0, 64))),
        ],
        axis=0,
    ).astype(low)
    full, plane_small, line_small = gather(own, small)
    shared = plane_small.reshape(8, 16, 256)[:, :6, :96].astype(jnp.float32)
    shared = jnp.swapaxes(shared, 0, 1).reshape(6, 768)
    split = jnp.swapaxes(line_small[:, 6:12, :192].astype(jnp.float32), 0, 1)
    bias_q, bias_v = split[0], split[1]
    bias_up = jnp.stack([split[2], split[3], split[4], split[5]], axis=-1).reshape(4, 768)
    weights = full.reshape(3, 4, 768, 768)
    project, w_out = weights[0, :, :, :576], weights[0, :, :, 576:]
    w_up, w_down = weights[1], weights[2]

    doc = jnp.maximum(level - 1, 0)
    inputs = lax.dynamic_slice(tokens, (doc * rows, 0), (rows, width))
    upstream = lax.dynamic_slice(cotangent, (doc * rows, 0), (rows, width)).astype(jnp.float32)
    upstream = jnp.where(level == 1, 0.0, upstream)
    slots = lax.dynamic_slice(alignment, (doc, 0), (1, slot_count))[0]
    live = jnp.arange(slot_count) < lax.dynamic_slice(segment_count, (doc,), (1,))
    valid = jnp.concatenate([lax.dynamic_slice(text_mask, (doc, 0), (1, text_rows))[0] > 0, live])
    pick = ((slots[:, None] == jnp.arange(text_rows)[None, :]) & live[:, None]).astype(low)
    taken = jnp.dot(pick, inputs[:text_rows], preferred_element_type=jnp.float32)
    layer_in = jnp.concatenate(
        [inputs[:text_rows].astype(jnp.float32), inputs[text_rows:].astype(jnp.float32) + taken], axis=0
    )
    rows_in = layer_in.astype(low)

    def mul(form, left, right):
        return jnp.einsum(form, left, right, preferred_element_type=jnp.float32)

    bias = jnp.concatenate([bias_q, jnp.zeros_like(bias_q), bias_v], axis=1)
    projected = (mul("rd,zdc->zrc", rows_in, project) + bias[:, None, :]).astype(low)
    projected = projected.reshape(4, rows, 3, 3, HEAD_DIM)
    queries, keys, values = projected[:, :, 0], projected[:, :, 1], projected[:, :, 2]
    scores = mul("zqhd,zkhd->zhqk", queries, keys) * HEAD_DIM**-0.5
    scores = jnp.where(valid, scores, -1e30)
    top = jnp.max(scores, axis=-1, keepdims=True)
    raised = jnp.exp(scores - top)
    probs = raised / jnp.sum(raised, axis=-1, keepdims=True)
    probs_low = probs.astype(low)
    context = mul("zhqk,zkhd->zqhd", probs_low, values).astype(low).reshape(4, rows, 192)
    joined = jnp.sum(mul("zrc,zoc->zro", context, w_out).astype(low).astype(jnp.float32), axis=0)
    mixed = layer_in + joined + shared[0]
    first_norm, normed_one, factor_one = layer_norm(mixed, shared[1], shared[2])
    hidden_in = first_norm.astype(low)
    inner = mul("rd,zdc->zrc", hidden_in, w_up) + bias_up[:, None, :]
    active, pull = jax.vjp(partial(jax.nn.gelu, approximate=False), inner)
    active = active.astype(low)
    down = jnp.sum(mul("zrc,zoc->zro", active, w_down).astype(low).astype(jnp.float32), axis=0)
    second = first_norm + down + shared[5]
    final, normed_two, factor_two = layer_norm(second, shared[3], shared[4])
    grad_second, grad_gain_two, grad_shift_two = norm_back(upstream, normed_two, factor_two, shared[3])
    grad_down = grad_second.astype(low)
    grad_inner = pull(mul("ro,zoc->zrc", grad_down, w_down))[0].astype(low)
    grad_up_w = mul("rd,zrc->zdc", hidden_in, grad_inner).astype(low)
    grad_down_w = mul("ro,zrc->zoc", grad_down, active).astype(low)
    grad_first = grad_second + mul("zrc,zdc->rd", grad_inner, w_up)
    grad_mixed, grad_gain_one, grad_shift_one = norm_back(grad_first, normed_one, factor_one, shared[1])
    grad_joined = grad_mixed.astype(low)
    grad_out_w = mul("ro,zrc->zoc", grad_joined, context).astype(low)
    grad_context = mul("ro,zoc->zrc", grad_joined, w_out).astype(low).reshape(4, rows, 3, HEAD_DIM)
    grad_values = mul("zhqk,zqhd->zkhd", probs_low, grad_context).astype(low)
    grad_probs = mul("zqhd,zkhd->zhqk", grad_context, values)
    delta = jnp.sum(probs * grad_probs, axis=-1, keepdims=True)
    grad_scores = (probs * (grad_probs - delta)).astype(low)
    grad_queries = (mul("zhqk,zkhd->zqhd", grad_scores, keys) * HEAD_DIM**-0.5).astype(low)
    grad_keys = (mul("zhqk,zqhd->zkhd", grad_scores, queries) * HEAD_DIM**-0.5).astype(low)
    grad_project = jnp.stack([grad_queries, grad_keys, grad_values], axis=2).reshape(4, rows, 576)
    grad_project_w = mul("rd,zrc->zdc", rows_in, grad_project).astype(low)
    grad_layer = grad_mixed + mul("zrc,zdc->rd", grad_project, project)
    moved = mul("st,sw->tw", pick, grad_layer[text_rows:].astype(low))
    back = jnp.concatenate([grad_layer[:text_rows] + moved, grad_layer[text_rows:]], axis=0).astype(low)

    attention_grad = jnp.concatenate([grad_project_w, grad_out_w], axis=2)
    grads = jnp.stack([attention_grad, grad_up_w, grad_down_w], axis=0).reshape(3, 4, 2, 2, 2, 96, 768)
    small_grad = jnp.concatenate(
        [
            jnp.stack(
                [
                    jnp.sum(grad_mixed, axis=0),
                    grad_gain_one,
                    grad_shift_one,
                    grad_gain_two,
                    grad_shift_two,
                    jnp.sum(grad_second, axis=0),
                    jnp.sum(grad_queries, axis=1, dtype=jnp.float32).reshape(768),
                    jnp.sum(grad_values, axis=1, dtype=jnp.float32).reshape(768),
                ]
            ),
            jnp.sum(grad_inner, axis=1, dtype=jnp.float32),
            jnp.zeros((4, 768), jnp.float32),
        ],
        axis=0,
    )
    sums, small_sum, text_all, back_all = reduce_all(grads, small_grad, final.astype(low), back)
    index = lax.axis_index("dp")
    shared_sum = lax.dynamic_slice(small_sum, (0, index * 96), (6, 96)).T
    split_sum = jnp.concatenate(
        [
            lax.dynamic_slice(small_sum, (6, level * 192), (2, 192)).T,
            lax.dynamic_slice(small_sum, (8 + level, 0), (1, 768)).reshape(192, 4),
        ],
        axis=1,
    )
    attention_new = renew(
        attention_master,
        attention_moment,
        attention_average,
        sums[0].reshape(96, 4, 192),
        jnp.asarray(ATTENTION_RATES, jnp.float32).reshape(1, 4, 1),
    )
    feedforward_new = renew(
        feedforward_master,
        feedforward_moment,
        feedforward_average,
        jnp.swapaxes(sums[1:], 0, 1),
        jnp.asarray(FEEDFORWARD_RATES, jnp.float32).reshape(1, 2, 1),
    )
    shared_new = renew(shared_master, shared_moment, shared_average, shared_sum, SHARED_RATE)
    split_new = renew(
        split_master,
        split_moment,
        split_average,
        split_sum,
        jnp.asarray(SPLIT_RATES, jnp.float32).reshape(1, 6),
    )
    return (
        text_all.reshape(documents * rows, width),
        back_all.reshape(documents * rows, width).astype(jnp.float32),
        *attention_new,
        *feedforward_new,
        *shared_new,
        *split_new,
    )


def solution(mesh):
    in_specs = (
        P("dp", None),
        P("dp", None),
        P("dp"),
        P("dp", None),
        P("dp", None),
        P("dp", None, "mp"),
        P("dp", None, "mp"),
        P("dp", None, "mp"),
        P("dp", None, "mp"),
        P("dp", None, "mp"),
        P("dp", None, "mp"),
        P("dp", None),
        P("dp", None),
        P("dp", None),
        P("mp", None),
        P("mp", None),
        P("mp", None),
    )
    out_specs = (
        P("dp", None),
        P("dp", None),
        P("dp", None, "mp"),
        P("dp", None, "mp"),
        P("dp", None, "mp"),
        P("dp", None, "mp"),
        P("dp", None, "mp"),
        P("dp", None, "mp"),
        P("dp", None, "mp"),
        P("dp", None, "mp"),
        P("dp", None),
        P("dp", None),
        P("dp", None),
        P("dp", None),
        P("mp", None),
        P("mp", None),
        P("mp", None),
        P("mp", None),
    )
    body = line_shards if mesh.shape["dp"] == 8 and mesh.shape["mp"] == 4 else general_shards
    return jax.shard_map(body, mesh=mesh, in_specs=in_specs, out_specs=out_specs, check_vma=False)
```

```python
from functools import partial
from types import SimpleNamespace

import jax
import jax.numpy as jnp
from jax import lax
from jax.experimental import pallas as pl
from jax.experimental.pallas import tpu as pltpu
from jax.sharding import PartitionSpec as P

MESH = pl.DeviceIdType.MESH

HEAD_DIM = 64


EPS = 1e-05
MOMENTUM = 0.9
AVERAGE = 0.75
ATTENTION_RATES = (4e-05, 4e-05, 4e-05, 0.01)
FEEDFORWARD_RATES = (0.0002, 4e-05)
SHARED_RATE = 0.0006
SPLIT_RATES = (0.0004, 0.0003, 0.0017, 0.0017, 0.0017, 0.0017)
HIGHEST_MODE = lax.Precision.HIGHEST


def contract_last(left, right):
    return lax.dot_general(
        left, right, (((1,), (1,)), ((), ())), preferred_element_type=jnp.float32
    )


def contract_rows(left, right):
    return lax.dot_general(
        left, right, (((0,), (0,)), ((), ())), preferred_element_type=jnp.float32
    )


def layer_norm(value, gain, shift):
    center = value - jnp.mean(value, axis=-1, keepdims=True)
    factor = lax.rsqrt(jnp.mean(center * center, axis=-1, keepdims=True) + EPS)
    normed = center * factor
    return (normed * gain + shift, normed, factor)


def norm_back(incoming, normed, factor, gain):
    scaled = incoming * gain
    inner_part = (
        scaled
        - jnp.mean(scaled, axis=-1, keepdims=True)
        - normed * jnp.mean(scaled * normed, axis=-1, keepdims=True)
    )
    return (factor * inner_part, jnp.sum(incoming * normed, axis=0), jnp.sum(incoming, axis=0))


def masked_scores(queries, key_rows, valid_keys):
    scores = jnp.einsum(
        "qhd,khd->hqk", queries, key_rows, preferred_element_type=jnp.float32
    ) * HEAD_DIM ** (-0.5)
    return jnp.where(valid_keys[None, None, :], scores, -1e30)


def attend(pieces):
    queries, key_rows, value_rows, valid_keys = pieces
    scores = masked_scores(queries, key_rows, valid_keys)
    row_max = jnp.max(scores, axis=-1, keepdims=True)
    exponent = jnp.exp(scores - row_max)
    row_total = jnp.sum(exponent, axis=-1, keepdims=True)
    probability = (exponent / row_total).astype(jnp.bfloat16)
    context = jnp.einsum(
        "hqk,khd->qhd", probability, value_rows, preferred_element_type=jnp.float32
    )
    return (context.astype(jnp.bfloat16), row_max + jnp.log(row_total))


def attend_back(pieces):
    queries, key_rows, value_rows, valid_keys, upstream, logsum = pieces
    scores = masked_scores(queries, key_rows, valid_keys)
    probability = jnp.exp(scores - logsum)
    grad_values = jnp.einsum(
        "hqk,qhd->khd",
        probability.astype(jnp.bfloat16),
        upstream,
        preferred_element_type=jnp.float32,
    )
    grad_probs = jnp.einsum(
        "qhd,khd->hqk", upstream, value_rows, preferred_element_type=jnp.float32
    )
    row_delta = jnp.sum(probability * grad_probs, axis=-1, keepdims=True)
    grad_scores = (probability * (grad_probs - row_delta)).astype(jnp.bfloat16)
    grad_queries = jnp.einsum(
        "hqk,khd->qhd", grad_scores, key_rows, preferred_element_type=jnp.float32
    ) * HEAD_DIM ** (-0.5)
    grad_keys = jnp.einsum(
        "hqk,qhd->khd", grad_scores, queries, preferred_element_type=jnp.float32
    ) * HEAD_DIM ** (-0.5)
    return (
        grad_queries.astype(jnp.bfloat16),
        grad_keys.astype(jnp.bfloat16),
        grad_values.astype(jnp.bfloat16),
    )


def renew(master, moment, average, gradient, rates):
    velocity = MOMENTUM * moment + gradient
    updated = master - rates * (gradient + MOMENTUM * velocity)
    averaged = AVERAGE * average + (1.0 - AVERAGE) * updated
    return (velocity, updated, averaged, updated.astype(jnp.bfloat16))


def general_shards(
    tokens,
    alignment,
    segment_count,
    text_mask,
    cotangent,
    attention_master,
    attention_moment,
    attention_average,
    feedforward_master,
    feedforward_moment,
    feedforward_average,
    shared_master,
    shared_moment,
    shared_average,
    split_master,
    split_moment,
    split_average,
):
    documents, slot_count = alignment.shape
    text_rows = text_mask.shape[1]
    document_rows = text_rows + slot_count
    model_width = tokens.shape[1]
    local_width = split_master.shape[0]
    local_heads = local_width // HEAD_DIM
    row_count = documents * document_rows
    attention_full, feedforward_full, shared_full = (
        lax.all_gather(attention_master.astype(jnp.bfloat16), "dp", axis=0, tiled=True),
        lax.all_gather(feedforward_master.astype(jnp.bfloat16), "dp", axis=0, tiled=True),
        lax.all_gather(shared_master.astype(jnp.bfloat16), "dp", axis=0, tiled=True),
    )
    shared = shared_full.astype(jnp.float32)
    split_bias = lax.optimization_barrier(split_master.astype(jnp.bfloat16)).astype(jnp.float32)
    live_slots = (
        lax.broadcasted_iota(jnp.int32, (documents, slot_count), 1) < segment_count[:, None]
    )
    valid_keys = jnp.concatenate([text_mask > 0, live_slots], axis=1)
    text_index = lax.broadcasted_iota(jnp.int32, (documents, slot_count, text_rows), 2)
    pick_table = ((alignment[:, :, None] == text_index) & live_slots[:, :, None]).astype(
        jnp.bfloat16
    )
    inputs = tokens.reshape(documents, document_rows, model_width)
    taken_rows = jnp.einsum(
        "dst,dtw->dsw", pick_table, inputs[:, :text_rows], preferred_element_type=jnp.float32
    )
    layer_in = jnp.concatenate(
        [
            inputs[:, :text_rows].astype(jnp.float32),
            inputs[:, text_rows:].astype(jnp.float32) + taken_rows,
        ],
        axis=1,
    ).reshape(row_count, model_width)
    rows_in = layer_in.astype(jnp.bfloat16)
    project_weights = attention_full[:, :3].reshape(model_width, 3 * local_width)
    project_bias = jnp.concatenate(
        [split_bias[:, 0], jnp.zeros_like(split_bias[:, 0]), split_bias[:, 1]]
    )
    projected = (
        jnp.dot(rows_in, project_weights, preferred_element_type=jnp.float32) + project_bias
    ).astype(jnp.bfloat16)
    projected = projected.reshape(documents, document_rows, 3, local_heads, HEAD_DIM)
    queries = projected[:, :, 0]
    key_rows = projected[:, :, 1]
    value_rows = projected[:, :, 2]
    context, logsum = lax.map(attend, (queries, key_rows, value_rows, valid_keys))
    context_rows = context.reshape(row_count, local_width)
    joined = lax.psum(
        contract_last(context_rows, attention_full[:, 3]).astype(jnp.bfloat16), "mp"
    ).astype(jnp.float32)
    mixed = layer_in + joined + shared[:, 0]
    first_norm, normed_one, factor_one = layer_norm(mixed, shared[:, 1], shared[:, 2])
    hidden_in = first_norm.astype(jnp.bfloat16)
    inner_pre = jnp.dot(
        hidden_in, feedforward_full[:, 0], preferred_element_type=jnp.float32
    ) + split_bias[:, 2:].reshape(-1)
    active = jax.nn.gelu(inner_pre, approximate=False).astype(jnp.bfloat16)
    down_sum = lax.psum(
        contract_last(active, feedforward_full[:, 1]).astype(jnp.bfloat16), "mp"
    ).astype(jnp.float32)
    second = first_norm + down_sum + shared[:, 5]
    output, normed_two, factor_two = layer_norm(second, shared[:, 3], shared[:, 4])
    grad_second, grad_gain_two, grad_shift_two = norm_back(
        cotangent.astype(jnp.float32), normed_two, factor_two, shared[:, 3]
    )
    grad_down = grad_second.astype(jnp.bfloat16)
    grad_active = jnp.dot(grad_down, feedforward_full[:, 1], preferred_element_type=jnp.float32)
    gelu_value, gelu_pull = jax.vjp(partial(jax.nn.gelu, approximate=False), inner_pre)
    grad_inner = gelu_pull(grad_active)[0].astype(jnp.bfloat16)
    feedforward_grad = jnp.stack(
        [contract_rows(hidden_in, grad_inner), contract_rows(grad_down, active)], axis=1
    )
    grad_first = grad_second + lax.psum(
        contract_last(grad_inner, feedforward_full[:, 0]).astype(jnp.bfloat16), "mp"
    ).astype(jnp.float32)
    grad_mixed, grad_gain_one, grad_shift_one = norm_back(
        grad_first, normed_one, factor_one, shared[:, 1]
    )
    grad_joined = grad_mixed.astype(jnp.bfloat16)
    output_grad = contract_rows(grad_joined, context_rows)
    grad_context = jnp.dot(
        grad_joined, attention_full[:, 3], preferred_element_type=jnp.float32
    ).astype(jnp.bfloat16)
    upstream = grad_context.reshape(documents, document_rows, local_heads, HEAD_DIM)
    grad_queries, grad_keys, grad_values = lax.map(
        attend_back, (queries, key_rows, value_rows, valid_keys, upstream, logsum)
    )
    query_rows = grad_queries.reshape(row_count, local_width)
    value_grad_rows = grad_values.reshape(row_count, local_width)
    grad_project = jnp.concatenate(
        [query_rows, grad_keys.reshape(row_count, local_width), value_grad_rows], axis=1
    )
    project_grad = contract_rows(rows_in, grad_project).reshape(model_width, 3, local_width)
    attention_grad = jnp.concatenate([project_grad, output_grad[:, None, :]], axis=1)
    grad_layer_in = grad_mixed + lax.psum(
        contract_last(grad_project, project_weights).astype(jnp.bfloat16), "mp"
    ).astype(jnp.float32)
    shared_grad = jnp.stack(
        [
            jnp.sum(grad_mixed, axis=0),
            grad_gain_one,
            grad_shift_one,
            grad_gain_two,
            grad_shift_two,
            jnp.sum(grad_second, axis=0),
        ],
        axis=1,
    )
    split_grad = jnp.concatenate(
        [
            jnp.sum(query_rows, axis=0, dtype=jnp.float32)[:, None],
            jnp.sum(value_grad_rows, axis=0, dtype=jnp.float32)[:, None],
            jnp.sum(grad_inner, axis=0, dtype=jnp.float32).reshape(local_width, 4),
        ],
        axis=1,
    )
    grad_documents = grad_layer_in.reshape(documents, document_rows, model_width)
    moved_rows = jnp.einsum(
        "dst,dsw->dtw",
        pick_table.astype(jnp.float32),
        grad_documents[:, text_rows:],
        precision=HIGHEST_MODE,
        preferred_element_type=jnp.float32,
    )
    input_gradient = jnp.concatenate(
        [grad_documents[:, :text_rows] + moved_rows, grad_documents[:, text_rows:]], axis=1
    ).reshape(row_count, model_width)
    attention_sum, feedforward_sum, shared_sum = (
        lax.psum_scatter(attention_grad, "dp", scatter_dimension=0, tiled=True),
        lax.psum_scatter(feedforward_grad, "dp", scatter_dimension=0, tiled=True),
        lax.psum_scatter(shared_grad, "dp", scatter_dimension=0, tiled=True),
    )
    split_sum = lax.psum(split_grad, "dp")
    attention_new = renew(
        attention_master,
        attention_moment,
        attention_average,
        attention_sum,
        jnp.asarray(ATTENTION_RATES, jnp.float32).reshape(1, 4, 1),
    )
    feedforward_new = renew(
        feedforward_master,
        feedforward_moment,
        feedforward_average,
        feedforward_sum,
        jnp.asarray(FEEDFORWARD_RATES, jnp.float32).reshape(1, 2, 1),
    )
    shared_new = renew(shared_master, shared_moment, shared_average, shared_sum, SHARED_RATE)
    split_new = renew(
        split_master,
        split_moment,
        split_average,
        split_sum,
        jnp.asarray(SPLIT_RATES, jnp.float32).reshape(1, 6),
    )
    return (
        output.astype(jnp.bfloat16),
        input_gradient,
        attention_new[0],
        attention_new[1],
        attention_new[2],
        attention_new[3],
        feedforward_new[0],
        feedforward_new[1],
        feedforward_new[2],
        feedforward_new[3],
        shared_new[0],
        shared_new[1],
        shared_new[2],
        shared_new[3],
        split_new[0],
        split_new[1],
        split_new[2],
        split_new[3],
    )


LOW = jnp.bfloat16
WIDE = jnp.float32
UNITS = [(0, 0), (1, 0), (2, 0), (0, 1), (0, 2), (0, 3)] + [(t, k) for k in range(1, 4) for t in (1, 2)]
LAG = 2
BACK_UNITS = [(t, k) for k in range(4) for t in (2, 1)] + [(0, k) for k in range(4)]
SOURCES = (0, 2, 3)
PIECES = 4
SENDS = 3
PAIRS = 4


def place():
    dp, z = lax.axis_index("dp"), lax.axis_index("mp")
    return z, lax.div(dp, 4), lax.rem(lax.div(dp, 2), 2), lax.rem(dp, 2)


def device(z, y, x, c):
    return (y * 4 + x * 2 + c, z)


def document_of(z):
    return z - lax.div(z + 2, 3)


def nearest_level(z, k):
    low, high = lax.rem(z, 2), lax.div(z, 2)
    if k == 0:
        return z
    if k == 1:
        return 1 + (2 * high - 1) * low
    if k == 2:
        return 2 + high * (1 - 2 * low)
    return 3 - 3 * high


def greet(z, y, x, c):
    barrier = pltpu.get_barrier_semaphore()
    partners = [device(z, y, x, 1 - c), device(z, y, 1 - x, c), device(z, 1 - y, x, c)]
    partners += [device(lax.rem(z + k, 4), y, x, c) for k in (1, 2, 3)]
    for partner in partners:
        pl.semaphore_signal(barrier, inc=1, device_id=partner, device_id_type=MESH)
    pl.semaphore_wait(barrier, len(partners))


def remote(source, target, send, recv, to):
    return pltpu.make_async_remote_copy(
        src_ref=source, dst_ref=target, send_sem=send, recv_sem=recv, device_id=to, device_id_type=MESH
    )


def when(condition, action):
    pl.when(condition)(action)


def mul(left, right):
    return jnp.dot(left, right, preferred_element_type=WIDE)


def gelu_parts(value):
    root = value * 0.7071067811865476
    inverse = 1.0 / (1.0 + 0.3275911 * jnp.abs(root))
    bell = jnp.exp(-root * root)
    series = 1.061405429
    for factor in (-1.453152027, 1.421413741, -0.284496736, 0.254829592):
        series = series * inverse + factor
    tail = 0.5 * series * inverse * bell
    share = jnp.where(value >= 0, 1.0 - tail, tail)
    return value * share, share + value * (bell * 0.3989422804014327)


def head_mask(head, scale, lanes=192):
    lane = lax.broadcasted_iota(jnp.int32, (1, lanes), 1)
    return jnp.where((lane >= head * HEAD_DIM) & (lane < (head + 1) * HEAD_DIM), scale, 0.0).astype(LOW)


def unit_weight(r, t, level):
    return r.full[t, level].reshape(768, 768)


class Gather:
    def __init__(self, own, small, r):
        self.own, self.small, self.r = own, small, r
        self.z, self.y, self.x, self.c = z, y, x, c = place()
        self.up, self.down = device(z + 1, y, x, c), device(z - 1, y, x, c)
        self.across_x, self.across_y = device(z, y, 1 - x, c), device(z, 1 - y, x, c)
        self.pair = device(z, y, x, 1 - c)

    def line_copy(self, t, level, source, way):
        r = self.r
        return remote(
            source, r.full.at[t, level, self.y, self.x, self.c], r.line_send.at[t, level, way],
            r.line_recv.at[t, level], self.up if way == 0 else self.down,
        )

    def first(self, u):
        t, k = UNITS[u]
        block = self.r.full.at[t, nearest_level(self.z, k), self.y, self.x, self.c]
        return remote(
            self.own.at[t] if k == 0 else block, block, self.r.first_send.at[u], self.r.first_recv.at[u],
            self.across_x if u % 2 == 0 else self.across_y,
        )

    def second(self, u):
        t, k = UNITS[u]
        level = nearest_level(self.z, k)
        if u % 2 == 0:
            block, to = self.r.full.at[t, level, self.y, :, self.c], self.across_y
        else:
            block, to = self.r.full.at[t, level, :, self.x, self.c], self.across_x
        return remote(block, block, self.r.second_send.at[u], self.r.second_recv.at[u], to)

    def paired(self, u):
        t, k = UNITS[u]
        block = self.r.full.at[t, nearest_level(self.z, k), :, :, self.c]
        return remote(block, block, self.r.pair_send.at[u], self.r.pair_recv.at[u], self.pair)

    def own_copy(self, t):
        return pltpu.make_async_copy(
            self.own.at[t], self.r.full.at[t, self.z, self.y, self.x, self.c], self.r.own_sem.at[t]
        )

    def tiny_own(self, i):
        target = self.r.plane.at[self.y, self.x, self.c] if i == 0 else self.r.line.at[self.z]
        return pltpu.make_async_copy(self.small, target, self.r.own_sem.at[3 + i])

    def tiny(self, i):
        r = self.r
        if i == 0:
            block, to = r.plane.at[self.y, self.x, self.c], self.across_x
        elif i == 1:
            block, to = r.plane.at[self.y, :, self.c], self.across_y
        elif i == 2:
            block, to = r.plane.at[:, :, self.c], self.pair
        else:
            block, to = r.line.at[self.z], device(lax.rem(self.z + i - 2, 4), self.y, self.x, self.c)
        source = self.small if i == 0 or i > 2 else block
        return remote(source, block, r.tiny_send.at[i], r.tiny_recv.at[i], to)

    def own_line(self, t, act):
        when(self.z < 3, lambda: act(self.line_copy(t, self.z, self.own.at[t], 0)))
        when(self.z > 0, lambda: act(self.line_copy(t, self.z, self.own.at[t], 1)))

    def begin(self):
        self.own_line(0, lambda copy: copy.start())
        for t in range(3):
            self.own_copy(t).start()
        for i in range(2):
            self.tiny_own(i).start()
        for i in (0, 3, 4, 5):
            self.tiny(i).start()

    def arrive(self, u):
        t, k = UNITS[u]
        if k > 0:
            level = nearest_level(self.z, k)
            block = self.r.full.at[t, level, self.y, self.x, self.c]
            self.line_copy(t, level, block, 0).wait_recv()
            when((level < self.z) & (self.z < 3), lambda: self.line_copy(t, level, block, 0).start())
            when((level > self.z) & (self.z > 0), lambda: self.line_copy(t, level, block, 1).start())
        self.first(u).start()

    def service(self, step):
        count = len(UNITS)
        if step < count:
            self.arrive(step)
        if step in (2, 3):
            self.own_line(step - 1, lambda copy: copy.start())
        u = step - LAG
        if 0 <= u < count:
            self.first(u).wait_recv()
            if UNITS[u][1] == 0:
                self.own_copy(UNITS[u][0]).wait()
            self.second(u).start()
        u = step - 2 * LAG
        if 0 <= u < count:
            self.second(u).wait_recv()
            self.paired(u).start()
        u = step - 3 * LAG
        if 0 <= u < count:
            self.paired(u).wait_recv()
        if step == 1:
            for i in range(2):
                self.tiny_own(i).wait()
        if 1 <= step <= 3:
            self.tiny(step - 1).wait_recv()
        if 1 <= step <= 2:
            self.tiny(step).start()
        if step == 4:
            for i in (3, 4, 5):
                self.tiny(i).wait_recv()

    def finish(self):
        z = self.z
        for i in range(6):
            self.tiny(i).wait_send()
        for u, (t, k) in enumerate(UNITS):
            level = nearest_level(z, k)
            block = self.r.full.at[t, level, self.y, self.x, self.c]
            if k == 0:
                self.own_line(t, lambda copy: copy.wait_send())
            else:
                when((level < z) & (z < 3), lambda t=t, v=level, b=block: self.line_copy(t, v, b, 0).wait_send())
                when((level > z) & (z > 0), lambda t=t, v=level, b=block: self.line_copy(t, v, b, 1).wait_send())
            self.first(u).wait_send()
            self.second(u).wait_send()
            self.paired(u).wait_send()


class Reduce:
    def __init__(self, sum_ref, r):
        self.sum_ref, self.r = sum_ref, r
        self.z, self.y, self.x, self.c = z, y, x, c = place()
        self.up, self.down = device(z + 1, y, x, c), device(z - 1, y, x, c)
        self.across_x, self.across_y = device(z, y, 1 - x, c), device(z, 1 - y, x, c)
        self.pair = device(z, y, x, 1 - c)

    def pair_copy(self, u):
        r = self.r
        return remote(
            r.sends.at[u % SENDS], r.pair_in.at[u % PAIRS], r.r_pair_send.at[u], r.r_pair_recv.at[u], self.pair
        )

    def first_copy(self, u):
        r = self.r
        source = r.total.at[u, :, 1 - self.x] if u % 2 == 0 else r.total.at[u, 1 - self.y]
        return remote(
            source, r.first_in.at[u], r.r_first_send.at[u], r.r_first_recv.at[u],
            self.across_x if u % 2 == 0 else self.across_y,
        )

    def second_copy(self, u):
        r, x, y = self.r, self.x, self.y
        return remote(
            r.total.at[u, 1 - y, x] if u % 2 == 0 else r.total.at[u, y, 1 - x],
            r.second_in.at[u], r.r_second_send.at[u], r.r_second_recv.at[u],
            self.across_y if u % 2 == 0 else self.across_x,
        )

    def line_copy(self, u, way):
        r = self.r
        t, k = BACK_UNITS[u]
        level = nearest_level(self.z, 3 - k)
        return remote(
            r.total.at[u, self.y, self.x], r.line_in.at[t, level, way], r.r_line_send.at[t, level],
            r.r_line_recv.at[t, level, way], self.up if way == 0 else self.down,
        )

    def produce(self, u, parts):
        r = self.r
        if u >= SENDS:
            self.pair_copy(u - SENDS).wait_send()
        for half, target in ((1 - self.c, r.sends.at[u % SENDS]), (self.c, r.total.at[u])):
            for products, lanes in parts:
                value = sum(mul(turned[:, :, half].reshape(384, 512), columns) for turned, columns in products)
                target[:, :, :, lanes] = value.astype(LOW).reshape(2, 2, 96, value.shape[1])
            if half is not self.c:
                self.pair_copy(u).start()

    def add_pair(self, u):
        r = self.r
        self.pair_copy(u).wait_recv()
        r.total[u] = r.total[u] + r.pair_in[u % PAIRS]
        self.first_copy(u).start()

    def add_first(self, u):
        r, x, y = self.r, self.x, self.y
        self.first_copy(u).wait_recv()
        if u % 2 == 0:
            r.total[u, :, x] = r.total[u, :, x] + r.first_in[u]
        else:
            r.total[u, y] = r.total[u, y] + r.first_in[u]
        self.second_copy(u).start()

    def add_second(self, u):
        r, x, y, z = self.r, self.x, self.y, self.z
        t, k = BACK_UNITS[u]
        level = nearest_level(z, 3 - k)
        self.second_copy(u).wait_recv()
        r.total[u, y, x] = r.total[u, y, x] + r.second_in[u]
        if k < 3:
            when((z == 0) | (z == 3), lambda: self.send_line(u))

    def send_line(self, u):
        level = nearest_level(self.z, 3 - BACK_UNITS[u][1])
        when(self.z < level, lambda: self.line_copy(u, 0).start())
        when(self.z > level, lambda: self.line_copy(u, 1).start())

    def take_line(self, u, way):
        r, x, y = self.r, self.x, self.y
        t, k = BACK_UNITS[u]
        level = nearest_level(self.z, 3 - k)
        self.line_copy(u, way).wait_recv()
        r.total[u, y, x] = r.total[u, y, x] + r.line_in[t, level, way]

    def add_line(self, u):
        r, z = self.r, self.z
        t, k = BACK_UNITS[u]
        level = nearest_level(z, 3 - k)
        middle = (z == 1) | (z == 2)
        if k < 3:
            when(middle & (z < level), lambda: self.take_line(u, 0))
            when(middle & (z > level), lambda: self.take_line(u, 1))
            when(middle, lambda: self.send_line(u))
        else:
            when(z > 0, lambda: self.take_line(u, 0))
            when(z < 3, lambda: self.take_line(u, 1))
            self.sum_ref[t] = r.total[u, self.y, self.x].astype(WIDE)

    def small_copy(self, i):
        r = self.r
        if i < 3:
            to = (self.pair, self.across_x, self.across_y)[i]
            return remote(r.small_total.at[i], r.small_in.at[i], r.small_send.at[i], r.small_recv.at[i], to)
        to = device(lax.rem(self.z + i - 2, 4), self.y, self.x, self.c)
        return remote(r.small_total.at[3], r.small_line.at[self.z], r.small_send.at[i], r.small_recv.at[i], to)

    def small_step(self, i):
        r = self.r
        self.small_copy(i).wait_recv()
        r.small_total[i + 1] = r.small_total[i] + r.small_in[i]
        if i < 2:
            self.small_copy(i + 1).start()
        else:
            for j in (3, 4, 5):
                self.small_copy(j).start()
            r.small_line[self.z] = r.small_total[3]

    def small_end(self, out):
        for i in (3, 4, 5):
            self.small_copy(i).wait_recv()
        line = self.r.small_line
        out[...] = line[0] + line[1] + line[2] + line[3]

    def finish(self):
        z = self.z
        for i in range(6):
            self.small_copy(i).wait_send()
        for u, (t, k) in enumerate(BACK_UNITS):
            if u >= len(BACK_UNITS) - SENDS:
                self.pair_copy(u).wait_send()
            self.first_copy(u).wait_send()
            self.second_copy(u).wait_send()
            if k < 3:
                level = nearest_level(z, 3 - k)
                when(z < level, lambda u=u: self.line_copy(u, 0).wait_send())
                when(z > level, lambda u=u: self.line_copy(u, 1).wait_send())


class Cast:
    def __init__(self, a, source, target, r):
        self.a, self.source, self.target, self.r = a, source, target, r
        self.z, y, x, c = place()
        self.up, self.down = device(self.z + 1, y, x, c), device(self.z - 1, y, x, c)

    def copy(self, d, p, way, first):
        r = self.r
        part = pl.ds(p * (512 // PIECES), 512 // PIECES)
        target = self.target.at[d, part]
        return remote(
            self.source.at[part] if first else target, target, r.cast_send.at[self.a, d, p, way],
            r.cast_recv.at[self.a, d, p], self.up if way == 0 else self.down,
        )

    def own(self, d):
        return pltpu.make_async_copy(self.source, self.target.at[d], self.r.cast_own.at[self.a, d])

    def begin(self):
        for d, start in enumerate(SOURCES):
            when(self.z == start, lambda d=d: self.own(d).start())
        for p in range(PIECES):
            for d, start in enumerate(SOURCES):
                if start < 3:
                    when(self.z == start, lambda d=d, p=p: self.copy(d, p, 0, True).start())
                if start > 0:
                    when(self.z == start, lambda d=d, p=p: self.copy(d, p, 1, True).start())

    def relay(self, d, p):
        z, start = self.z, SOURCES[d]

        def pass_on(way, go):
            self.copy(d, p, way, False).wait_recv()
            when(go, lambda: self.copy(d, p, way, False).start())

        if start < 3:
            when(z > start, lambda: pass_on(0, z < 3))
        if start > 0:
            when(z < start, lambda: pass_on(1, z > 0))

    def finish(self):
        z = self.z
        for d, start in enumerate(SOURCES):
            when(z == start, lambda d=d: self.own(d).wait())
            for p in range(PIECES):
                if start < 3:
                    when((z >= start) & (z < 3), lambda d=d, p=p: self.copy(d, p, 0, True).wait_send())
                if start > 0:
                    when((z <= start) & (z > 0), lambda d=d, p=p: self.copy(d, p, 1, True).wait_send())


def buffers():
    vmem = pltpu.VMEM
    return dict(
        full=vmem((3, 4, 2, 2, 2, 96, 768), LOW),
        plane=vmem((2, 2, 2, 16, 768), LOW),
        line=vmem((4, 16, 768), LOW),
        tok=vmem((512, 768), LOW),
        cot=vmem((512, 768), LOW),
        pick=vmem((384, 128), LOW),
        rows_in=vmem((512, 768), LOW),
        hidden_in=vmem((512, 768), LOW),
        rows_t=vmem((2, 2, 2, 96, 512), LOW),
        hidden_t=vmem((2, 2, 2, 96, 512), LOW),
        down_t=vmem((2, 2, 2, 96, 512), LOW),
        joined_t=vmem((2, 2, 2, 96, 512), LOW),
        inner=vmem((512, 768), LOW),
        project=vmem((512, 768), LOW),
        qkv=vmem((4, 512, 640), LOW),
        probs=vmem((2, 3, 512, 512), LOW),
        context=vmem((4, 512, 256), LOW),
        active=vmem((4, 512, 768), LOW),
        slope=vmem((4, 512, 768), LOW),
        mixed=vmem((512, 768), WIDE),
        normed_one=vmem((512, 768), WIDE),
        factor_one=vmem((512, 1), WIDE),
        total=vmem((12, 2, 2, 96, 768), LOW),
        sends=vmem((SENDS, 2, 2, 96, 768), LOW),
        pair_in=vmem((PAIRS, 2, 2, 96, 768), LOW),
        first_in=vmem((12, 2, 96, 768), LOW),
        second_in=vmem((12, 96, 768), LOW),
        line_in=vmem((3, 4, 2, 96, 768), LOW),
        small_total=vmem((4, 16, 768), WIDE),
        small_in=vmem((3, 16, 768), WIDE),
        small_line=vmem((4, 16, 768), WIDE),
    )


def flags():
    dma = pltpu.SemaphoreType.DMA
    return dict(
        line_send=dma((3, 4, 2)),
        line_recv=dma((3, 4)),
        first_send=dma((12,)),
        first_recv=dma((12,)),
        second_send=dma((12,)),
        second_recv=dma((12,)),
        pair_send=dma((12,)),
        pair_recv=dma((12,)),
        tiny_send=dma((6,)),
        tiny_recv=dma((6,)),
        own_sem=dma((5,)),
        load_sem=dma((6,)),
        r_pair_send=dma((12,)),
        r_pair_recv=dma((12,)),
        r_first_send=dma((12,)),
        r_first_recv=dma((12,)),
        r_second_send=dma((12,)),
        r_second_recv=dma((12,)),
        r_line_send=dma((3, 4)),
        r_line_recv=dma((3, 4, 2)),
        small_send=dma((6,)),
        small_recv=dma((6,)),
        cast_send=dma((2, 3, PIECES, 2)),
        cast_recv=dma((2, 3, PIECES)),
        cast_own=dma((2, 3)),
    )


def turn(value):
    return value.T.reshape(2, 2, 2, 96, 512)


def layer_kernel(
    own_ref, small_ref, tokens_ref, cotangent_ref, align_ref, count_ref, mask_ref,
    sum_ref, small_sum_ref, text_all, back_all, probs_out, *refs,
):
    r = SimpleNamespace(**dict(zip([*buffers(), *flags()], refs)))
    z, y, x, c = place()
    doc = document_of(z)
    tok_copy = pltpu.make_async_copy(tokens_ref.at[pl.ds(doc * 512, 512)], r.tok, r.load_sem.at[0])
    cot_copy = pltpu.make_async_copy(cotangent_ref.at[pl.ds(doc * 512, 512)], r.cot, r.load_sem.at[1])
    tok_copy.start()
    cot_copy.start()
    greet(z, y, x, c)
    net = Gather(own_ref, small_ref, r)
    net.begin()
    net.service(0)
    net.service(1)

    tok_copy.wait()
    live = lax.broadcasted_iota(jnp.int32, (1, 128), 1) < count_ref[pl.ds(doc, 1), :]
    pick = jnp.where(
        (lax.broadcasted_iota(jnp.int32, (384, 128), 0) == align_ref[pl.ds(doc, 1), :]) & live, 1.0, 0.0
    ).astype(LOW)
    r.pick[...] = pick
    text_tokens = r.tok[:384]
    taken = lax.dot_general(pick, text_tokens, (((0,), (0,)), ((), ())), preferred_element_type=WIDE)
    slot_rows = r.tok[384:].astype(WIDE) + taken
    r.mixed[:384] = text_tokens.astype(WIDE)
    r.mixed[384:] = slot_rows
    r.rows_in[:384] = text_tokens
    r.rows_in[384:] = slot_rows.astype(LOW)
    r.rows_t[...] = turn(r.rows_in[...])
    valid = jnp.concatenate([mask_ref[pl.ds(doc, 1), :] > 0, live], axis=1)
    bar = jnp.where(valid, 0.0, -1e30)
    for step in range(2, 3 * LAG):
        net.service(step)

    def spill(k):
        return pltpu.make_async_copy(r.probs.at[k % 2], probs_out.at[k % 2], r.load_sem.at[2 + k % 2])

    def attention(k):
        level = nearest_level(z, k)
        weight = unit_weight(r, 0, level)
        bias = r.line[level][6:7].astype(WIDE)
        projected = (mul(r.rows_in[...], weight[...]) + bias).astype(LOW)
        r.qkv[k] = projected[:, :640]
        queries, keys, values = projected[:, :192], projected[:, 192:384], projected[:, 384:640]
        if k >= 2:
            spill(k).wait()
        context = jnp.zeros((512, 256), WIDE)
        for head in range(3):
            scores = contract_last(queries * head_mask(head, 0.125), keys)
            scores = jnp.where(bar < 0.0, -1e30, scores)
            raised = jnp.exp(scores - jnp.max(scores, axis=-1, keepdims=True))
            probs = (raised * (1.0 / jnp.sum(raised, axis=-1, keepdims=True))).astype(LOW)
            r.probs[k % 2, head] = probs
            context = context + mul(probs, values * head_mask(head, 1.0, 256))
        context = pltpu.roll(context, 64, 1).astype(LOW)
        r.context[k] = context
        r.mixed[...] += contract_last(context, weight[:, 512:])
        if k < 2:
            spill(k).start()

    for step in range(3 * LAG, 3 * LAG + 6):
        net.service(step)
        if step - 3 * LAG not in (1, 2):
            attention(max(0, step - 3 * LAG - 2))

    shared = jnp.sum(r.plane[...].astype(WIDE).reshape(8, 16, 768), axis=0)
    mixed = r.mixed[...] + shared[0:1]
    first_norm, normed, factor = layer_norm(mixed, shared[1:2], shared[2:3])
    r.normed_one[...] = normed
    r.factor_one[...] = factor
    r.hidden_in[...] = first_norm.astype(LOW)
    r.hidden_t[...] = turn(first_norm.astype(LOW))
    r.mixed[...] = first_norm + shared[5:6]

    def feed(k):
        level = nearest_level(z, k)
        bias = r.line[level][7:8, :].astype(WIDE)
        up = unit_weight(r, 1, level)
        for part in range(3):
            lanes = slice(part * 256, (part + 1) * 256)
            inner = mul(r.hidden_in[...], up[:, lanes]) + bias[:, lanes]
            active, slope = gelu_parts(inner)
            r.active[k, :, lanes] = active.astype(LOW)
            r.slope[k, :, lanes] = slope.astype(LOW)
        r.mixed[...] += contract_last(r.active[k], unit_weight(r, 2, level))

    for k in range(4):
        if k > 0:
            net.service(5 + 2 * k + 3 * LAG - 1)
            net.service(5 + 2 * k + 3 * LAG)
        feed(k)

    text_cast = Cast(0, r.tok, text_all, r)
    back_cast = Cast(1, r.cot, back_all, r)
    red = Reduce(sum_ref, r)

    def second_norm():
        final, normed, factor = layer_norm(r.mixed[...], shared[3:4], shared[4:5])
        r.tok[...] = final.astype(LOW)
        text_cast.begin()
        cot_copy.wait()
        incoming = r.cot[...].astype(WIDE) * jnp.where(z == 1, 0.0, 1.0)
        grad, gain, shift = norm_back(incoming, normed, factor, shared[3:4])
        r.mixed[...] = grad
        low = grad.astype(LOW)
        r.rows_in[...] = low
        r.down_t[...] = turn(low)
        r.small_total[0] = jnp.zeros((16, 768), WIDE)
        r.small_total[0, 3:4] = gain[None]
        r.small_total[0, 4:5] = shift[None]
        r.small_total[0, 5:6] = jnp.sum(grad, axis=0, keepdims=True)

    def feed_back(k):
        level = nearest_level(z, 3 - k)
        grad = mul(r.rows_in[...], unit_weight(r, 2, level)) * r.slope[3 - k].astype(WIDE)
        r.inner[...] = grad.astype(LOW)
        r.small_total[0, pl.ds(12 + level, 1)] = jnp.sum(grad.astype(LOW).astype(WIDE), axis=0, keepdims=True)
        red.produce(2 * k, [([(r.down_t, r.active[3 - k])], slice(0, 768))])

    def feed_back_up(k):
        level = nearest_level(z, 3 - k)
        red.produce(2 * k + 1, [([(r.hidden_t, r.inner[...])], slice(0, 768))])
        r.mixed[...] += contract_last(r.inner[...], unit_weight(r, 1, level))

    def first_norm_back():
        grad, gain, shift = norm_back(r.mixed[...], r.normed_one[...], r.factor_one[...], shared[1:2])
        r.mixed[...] = grad
        low = grad.astype(LOW)
        r.hidden_in[...] = low
        r.joined_t[...] = turn(low)
        r.project[:, 576:] = jnp.zeros((512, 192), LOW)
        r.small_total[0, 0:1] = jnp.sum(grad, axis=0, keepdims=True)
        r.small_total[0, 1:2] = gain[None]
        r.small_total[0, 2:3] = shift[None]

    def reload(k):
        return pltpu.make_async_copy(probs_out.at[k], r.probs.at[k], r.load_sem.at[4 + k])

    def attention_back(k):
        slot = 3 - k
        level = nearest_level(z, slot)
        projected = r.qkv[slot]
        queries, keys, values = projected[:, :192], projected[:, 192:384], projected[:, 384:576]
        upstream = mul(r.hidden_in[...], unit_weight(r, 0, level)[:, 512:])[:, 64:].astype(LOW)
        if slot < 2:
            reload(slot).wait()
        grad_q = grad_k = grad_v = jnp.zeros((512, 192), WIDE)
        for head in range(3):
            probs = r.probs[slot % 2, head]
            up = upstream * head_mask(head, 1.0)
            grad_v = grad_v + contract_rows(probs, up)
            grad_probs = contract_last(up, values)
            wide = probs.astype(WIDE)
            weighed = wide * grad_probs
            grad_scores = (weighed - wide * jnp.sum(weighed, axis=-1, keepdims=True)).astype(LOW)
            grad_q = grad_q + mul(grad_scores, keys * head_mask(head, 0.125))
            grad_k = grad_k + contract_rows(grad_scores, queries * head_mask(head, 0.125))
        if slot >= 2:
            reload(slot - 2).start()
        r.project[:, :192] = grad_q.astype(LOW)
        r.project[:, 192:384] = grad_k.astype(LOW)
        r.project[:, 384:576] = grad_v.astype(LOW)
        r.small_total[0, pl.ds(8 + level, 1)] = jnp.sum(r.project[...].astype(WIDE), axis=0, keepdims=True)

    def project_back(k):
        slot = 3 - k
        level = nearest_level(z, slot)
        red.produce(
            8 + k,
            [
                ([(r.rows_t, r.project[:, :512])], slice(0, 512)),
                ([(r.rows_t, r.project[:, 512:]), (r.joined_t, r.context[slot])], slice(512, 768)),
            ],
        )
        r.mixed[...] += contract_last(r.project[...], unit_weight(r, 0, level))

    def input_back():
        grad = r.mixed[...]
        r.cot[:384] = (grad[:384] + mul(r.pick[...], grad[384:].astype(LOW))).astype(LOW)
        r.cot[384:] = grad[384:].astype(LOW)
        back_cast.begin()
        red.small_copy(0).start()

    work = [(4.0, second_norm)]
    for k in range(4):
        work += [(2.0, partial(feed_back, k)), (2.0, partial(feed_back_up, k))]
    work.append((2.5, first_norm_back))
    for k in range(4):
        work += [(4.0, partial(attention_back, k)), (2.0, partial(project_back, k))]
    work.append((2.0, input_back))
    made = [8.0 + 2.0 * u for u in range(8)] + [28.5 + 6.0 * k for k in range(4)]
    events = []
    for u in range(12):
        started = max(made[u] + 1.0, made[0] + PACE * u)
        events.append((started + 6.5, partial(red.add_first, u)))
        events.append((started + 13.0, partial(red.add_second, u)))
        events.append((started + 16.5, partial(red.add_line, u)))
    for p in range(PIECES):
        for d in range(3):
            events.append((9.0 + 8.5 * p + 2.0 * d, partial(text_cast.relay, d, p)))
            events.append((54.0 + 8.5 * p + 2.0 * d, partial(back_cast.relay, d, p)))
    for i in range(3):
        events.append((53.0 + 4.0 * i, partial(red.small_step, i)))
    events.append((68.0, lambda: red.small_end(small_sum_ref)))
    events.sort(key=lambda event: event[0])
    clock, made_units = 0.0, 0
    for length, action in work:
        while events and events[0][0] <= clock:
            events.pop(0)[1]()
        action()
        clock += length
        if action.__class__ is partial and action.func in (feed_back, feed_back_up, project_back):
            if made_units > 0:
                red.add_pair(made_units - 1)
            made_units += 1
    red.add_pair(11)
    for _, action in events:
        action()
    net.finish()
    text_cast.finish()
    back_cast.finish()
    red.finish()


PACE = 4.8


def run_layer(own, small, tokens, cotangent, align, count, mask):
    vmem = pl.BlockSpec(memory_space=pltpu.VMEM)
    hbm = pl.BlockSpec(memory_space=pl.ANY)
    whole = jax.ShapeDtypeStruct((3, 512, 768), LOW)
    return pl.pallas_call(
        layer_kernel,
        out_shape=(
            jax.ShapeDtypeStruct((3, 96, 768), WIDE),
            jax.ShapeDtypeStruct((16, 768), WIDE),
            whole,
            whole,
            jax.ShapeDtypeStruct((2, 3, 512, 512), LOW),
        ),
        in_specs=[vmem, vmem, hbm, hbm, vmem, vmem, vmem],
        out_specs=(vmem, vmem, hbm, hbm, hbm),
        scratch_shapes=[*buffers().values(), *flags().values()],
        compiler_params=pltpu.CompilerParams(
            collective_id=0, has_side_effects=True, vmem_limit_bytes=VMEM_LIMIT
        ),
        name="layer_step",
    )(own, small, tokens, cotangent, align, count, mask)


VMEM_LIMIT = 63 * 2**20


def line_shards(
    tokens,
    alignment,
    segment_count,
    text_mask,
    cotangent,
    attention_master,
    attention_moment,
    attention_average,
    feedforward_master,
    feedforward_moment,
    feedforward_average,
    shared_master,
    shared_moment,
    shared_average,
    split_master,
    split_moment,
    split_average,
):
    documents, slot_count = alignment.shape
    rows, width = tokens.shape
    level, index = lax.axis_index("mp"), lax.axis_index("dp")
    own = jnp.concatenate(
        [attention_master.reshape(1, 96, 768), jnp.swapaxes(feedforward_master, 0, 1)], axis=0
    ).astype(LOW)
    line_row = jnp.concatenate(
        [split_master[:, 0], jnp.zeros((192,), WIDE), split_master[:, 1], jnp.zeros((192,), WIDE)]
    )
    small = jnp.concatenate(
        [
            lax.dynamic_update_slice(jnp.zeros((6, 768), WIDE), shared_master.T, (0, index * 96)),
            line_row[None],
            split_master[:, 2:].reshape(1, 768),
            jnp.zeros((8, 768), WIDE),
        ],
        axis=0,
    ).astype(LOW)
    count = jnp.broadcast_to(segment_count[:, None], (documents, slot_count))
    sums, small_sum, text_all, back_all, _ = run_layer(
        own, small, tokens, cotangent, alignment, count, text_mask
    )
    shared_sum = lax.dynamic_slice(small_sum, (0, index * 96), (6, 96)).T
    bias_sum = lax.dynamic_slice(small_sum, (8 + level, 0), (1, 768))[0]
    split_sum = jnp.concatenate(
        [
            bias_sum[:192, None],
            bias_sum[384:576, None],
            lax.dynamic_slice(small_sum, (12 + level, 0), (1, 768)).reshape(192, 4),
        ],
        axis=1,
    )
    attention_new = renew(
        attention_master,
        attention_moment,
        attention_average,
        sums[0].reshape(96, 4, 192),
        jnp.asarray(ATTENTION_RATES, WIDE).reshape(1, 4, 1),
    )
    feedforward_new = renew(
        feedforward_master,
        feedforward_moment,
        feedforward_average,
        jnp.swapaxes(sums[1:], 0, 1),
        jnp.asarray(FEEDFORWARD_RATES, WIDE).reshape(1, 2, 1),
    )
    shared_new = renew(shared_master, shared_moment, shared_average, shared_sum, SHARED_RATE)
    split_new = renew(
        split_master,
        split_moment,
        split_average,
        split_sum,
        jnp.asarray(SPLIT_RATES, WIDE).reshape(1, 6),
    )
    return (
        text_all.reshape(rows, width),
        back_all.reshape(rows, width).astype(WIDE),
        *attention_new,
        *feedforward_new,
        *shared_new,
        *split_new,
    )


def solution(mesh):
    in_specs = (
        P("dp", None),
        P("dp", None),
        P("dp"),
        P("dp", None),
        P("dp", None),
        P("dp", None, "mp"),
        P("dp", None, "mp"),
        P("dp", None, "mp"),
        P("dp", None, "mp"),
        P("dp", None, "mp"),
        P("dp", None, "mp"),
        P("dp", None),
        P("dp", None),
        P("dp", None),
        P("mp", None),
        P("mp", None),
        P("mp", None),
    )
    out_specs = (
        P("dp", None),
        P("dp", None),
        P("dp", None, "mp"),
        P("dp", None, "mp"),
        P("dp", None, "mp"),
        P("dp", None, "mp"),
        P("dp", None, "mp"),
        P("dp", None, "mp"),
        P("dp", None, "mp"),
        P("dp", None, "mp"),
        P("dp", None),
        P("dp", None),
        P("dp", None),
        P("dp", None),
        P("mp", None),
        P("mp", None),
        P("mp", None),
        P("mp", None),
    )
    body = line_shards if mesh.shape["dp"] == 8 and mesh.shape["mp"] == 4 else general_shards
    return jax.shard_map(body, mesh=mesh, in_specs=in_specs, out_specs=out_specs, check_vma=False)
```

```python
from functools import partial
from types import SimpleNamespace

import jax
import jax.numpy as jnp
from jax import lax
from jax.experimental import pallas as pl
from jax.experimental.pallas import tpu as pltpu
from jax.sharding import PartitionSpec as P

MESH = pl.DeviceIdType.MESH

HEAD_DIM = 64


EPS = 1e-05
MOMENTUM = 0.9
AVERAGE = 0.75
ATTENTION_RATES = (4e-05, 4e-05, 4e-05, 0.01)
FEEDFORWARD_RATES = (0.0002, 4e-05)
SHARED_RATE = 0.0006
SPLIT_RATES = (0.0004, 0.0003, 0.0017, 0.0017, 0.0017, 0.0017)
HIGHEST_MODE = lax.Precision.HIGHEST


def contract_last(left, right):
    return lax.dot_general(
        left, right, (((1,), (1,)), ((), ())), preferred_element_type=jnp.float32
    )


def contract_rows(left, right):
    return lax.dot_general(
        left, right, (((0,), (0,)), ((), ())), preferred_element_type=jnp.float32
    )


def layer_norm(value, gain, shift):
    center = value - jnp.mean(value, axis=-1, keepdims=True)
    factor = lax.rsqrt(jnp.mean(center * center, axis=-1, keepdims=True) + EPS)
    normed = center * factor
    return (normed * gain + shift, normed, factor)


def norm_back(incoming, normed, factor, gain):
    scaled = incoming * gain
    inner_part = (
        scaled
        - jnp.mean(scaled, axis=-1, keepdims=True)
        - normed * jnp.mean(scaled * normed, axis=-1, keepdims=True)
    )
    return (factor * inner_part, jnp.sum(incoming * normed, axis=0), jnp.sum(incoming, axis=0))


def masked_scores(queries, key_rows, valid_keys):
    scores = jnp.einsum(
        "qhd,khd->hqk", queries, key_rows, preferred_element_type=jnp.float32
    ) * HEAD_DIM ** (-0.5)
    return jnp.where(valid_keys[None, None, :], scores, -1e30)


def attend(pieces):
    queries, key_rows, value_rows, valid_keys = pieces
    scores = masked_scores(queries, key_rows, valid_keys)
    row_max = jnp.max(scores, axis=-1, keepdims=True)
    exponent = jnp.exp(scores - row_max)
    row_total = jnp.sum(exponent, axis=-1, keepdims=True)
    probability = (exponent / row_total).astype(jnp.bfloat16)
    context = jnp.einsum(
        "hqk,khd->qhd", probability, value_rows, preferred_element_type=jnp.float32
    )
    return (context.astype(jnp.bfloat16), row_max + jnp.log(row_total))


def attend_back(pieces):
    queries, key_rows, value_rows, valid_keys, upstream, logsum = pieces
    scores = masked_scores(queries, key_rows, valid_keys)
    probability = jnp.exp(scores - logsum)
    grad_values = jnp.einsum(
        "hqk,qhd->khd",
        probability.astype(jnp.bfloat16),
        upstream,
        preferred_element_type=jnp.float32,
    )
    grad_probs = jnp.einsum(
        "qhd,khd->hqk", upstream, value_rows, preferred_element_type=jnp.float32
    )
    row_delta = jnp.sum(probability * grad_probs, axis=-1, keepdims=True)
    grad_scores = (probability * (grad_probs - row_delta)).astype(jnp.bfloat16)
    grad_queries = jnp.einsum(
        "hqk,khd->qhd", grad_scores, key_rows, preferred_element_type=jnp.float32
    ) * HEAD_DIM ** (-0.5)
    grad_keys = jnp.einsum(
        "hqk,qhd->khd", grad_scores, queries, preferred_element_type=jnp.float32
    ) * HEAD_DIM ** (-0.5)
    return (
        grad_queries.astype(jnp.bfloat16),
        grad_keys.astype(jnp.bfloat16),
        grad_values.astype(jnp.bfloat16),
    )


def renew(master, moment, average, gradient, rates):
    velocity = MOMENTUM * moment + gradient
    updated = master - rates * (gradient + MOMENTUM * velocity)
    averaged = AVERAGE * average + (1.0 - AVERAGE) * updated
    return (velocity, updated, averaged, updated.astype(jnp.bfloat16))


def general_shards(
    tokens,
    alignment,
    segment_count,
    text_mask,
    cotangent,
    attention_master,
    attention_moment,
    attention_average,
    feedforward_master,
    feedforward_moment,
    feedforward_average,
    shared_master,
    shared_moment,
    shared_average,
    split_master,
    split_moment,
    split_average,
):
    documents, slot_count = alignment.shape
    text_rows = text_mask.shape[1]
    document_rows = text_rows + slot_count
    model_width = tokens.shape[1]
    local_width = split_master.shape[0]
    local_heads = local_width // HEAD_DIM
    row_count = documents * document_rows
    attention_full, feedforward_full, shared_full = (
        lax.all_gather(attention_master.astype(jnp.bfloat16), "dp", axis=0, tiled=True),
        lax.all_gather(feedforward_master.astype(jnp.bfloat16), "dp", axis=0, tiled=True),
        lax.all_gather(shared_master.astype(jnp.bfloat16), "dp", axis=0, tiled=True),
    )
    shared = shared_full.astype(jnp.float32)
    split_bias = lax.optimization_barrier(split_master.astype(jnp.bfloat16)).astype(jnp.float32)
    live_slots = (
        lax.broadcasted_iota(jnp.int32, (documents, slot_count), 1) < segment_count[:, None]
    )
    valid_keys = jnp.concatenate([text_mask > 0, live_slots], axis=1)
    text_index = lax.broadcasted_iota(jnp.int32, (documents, slot_count, text_rows), 2)
    pick_table = ((alignment[:, :, None] == text_index) & live_slots[:, :, None]).astype(
        jnp.bfloat16
    )
    inputs = tokens.reshape(documents, document_rows, model_width)
    taken_rows = jnp.einsum(
        "dst,dtw->dsw", pick_table, inputs[:, :text_rows], preferred_element_type=jnp.float32
    )
    layer_in = jnp.concatenate(
        [
            inputs[:, :text_rows].astype(jnp.float32),
            inputs[:, text_rows:].astype(jnp.float32) + taken_rows,
        ],
        axis=1,
    ).reshape(row_count, model_width)
    rows_in = layer_in.astype(jnp.bfloat16)
    project_weights = attention_full[:, :3].reshape(model_width, 3 * local_width)
    project_bias = jnp.concatenate(
        [split_bias[:, 0], jnp.zeros_like(split_bias[:, 0]), split_bias[:, 1]]
    )
    projected = (
        jnp.dot(rows_in, project_weights, preferred_element_type=jnp.float32) + project_bias
    ).astype(jnp.bfloat16)
    projected = projected.reshape(documents, document_rows, 3, local_heads, HEAD_DIM)
    queries = projected[:, :, 0]
    key_rows = projected[:, :, 1]
    value_rows = projected[:, :, 2]
    context, logsum = lax.map(attend, (queries, key_rows, value_rows, valid_keys))
    context_rows = context.reshape(row_count, local_width)
    joined = lax.psum(
        contract_last(context_rows, attention_full[:, 3]).astype(jnp.bfloat16), "mp"
    ).astype(jnp.float32)
    mixed = layer_in + joined + shared[:, 0]
    first_norm, normed_one, factor_one = layer_norm(mixed, shared[:, 1], shared[:, 2])
    hidden_in = first_norm.astype(jnp.bfloat16)
    inner_pre = jnp.dot(
        hidden_in, feedforward_full[:, 0], preferred_element_type=jnp.float32
    ) + split_bias[:, 2:].reshape(-1)
    active = jax.nn.gelu(inner_pre, approximate=False).astype(jnp.bfloat16)
    down_sum = lax.psum(
        contract_last(active, feedforward_full[:, 1]).astype(jnp.bfloat16), "mp"
    ).astype(jnp.float32)
    second = first_norm + down_sum + shared[:, 5]
    output, normed_two, factor_two = layer_norm(second, shared[:, 3], shared[:, 4])
    grad_second, grad_gain_two, grad_shift_two = norm_back(
        cotangent.astype(jnp.float32), normed_two, factor_two, shared[:, 3]
    )
    grad_down = grad_second.astype(jnp.bfloat16)
    grad_active = jnp.dot(grad_down, feedforward_full[:, 1], preferred_element_type=jnp.float32)
    gelu_value, gelu_pull = jax.vjp(partial(jax.nn.gelu, approximate=False), inner_pre)
    grad_inner = gelu_pull(grad_active)[0].astype(jnp.bfloat16)
    feedforward_grad = jnp.stack(
        [contract_rows(hidden_in, grad_inner), contract_rows(grad_down, active)], axis=1
    )
    grad_first = grad_second + lax.psum(
        contract_last(grad_inner, feedforward_full[:, 0]).astype(jnp.bfloat16), "mp"
    ).astype(jnp.float32)
    grad_mixed, grad_gain_one, grad_shift_one = norm_back(
        grad_first, normed_one, factor_one, shared[:, 1]
    )
    grad_joined = grad_mixed.astype(jnp.bfloat16)
    output_grad = contract_rows(grad_joined, context_rows)
    grad_context = jnp.dot(
        grad_joined, attention_full[:, 3], preferred_element_type=jnp.float32
    ).astype(jnp.bfloat16)
    upstream = grad_context.reshape(documents, document_rows, local_heads, HEAD_DIM)
    grad_queries, grad_keys, grad_values = lax.map(
        attend_back, (queries, key_rows, value_rows, valid_keys, upstream, logsum)
    )
    query_rows = grad_queries.reshape(row_count, local_width)
    value_grad_rows = grad_values.reshape(row_count, local_width)
    grad_project = jnp.concatenate(
        [query_rows, grad_keys.reshape(row_count, local_width), value_grad_rows], axis=1
    )
    project_grad = contract_rows(rows_in, grad_project).reshape(model_width, 3, local_width)
    attention_grad = jnp.concatenate([project_grad, output_grad[:, None, :]], axis=1)
    grad_layer_in = grad_mixed + lax.psum(
        contract_last(grad_project, project_weights).astype(jnp.bfloat16), "mp"
    ).astype(jnp.float32)
    shared_grad = jnp.stack(
        [
            jnp.sum(grad_mixed, axis=0),
            grad_gain_one,
            grad_shift_one,
            grad_gain_two,
            grad_shift_two,
            jnp.sum(grad_second, axis=0),
        ],
        axis=1,
    )
    split_grad = jnp.concatenate(
        [
            jnp.sum(query_rows, axis=0, dtype=jnp.float32)[:, None],
            jnp.sum(value_grad_rows, axis=0, dtype=jnp.float32)[:, None],
            jnp.sum(grad_inner, axis=0, dtype=jnp.float32).reshape(local_width, 4),
        ],
        axis=1,
    )
    grad_documents = grad_layer_in.reshape(documents, document_rows, model_width)
    moved_rows = jnp.einsum(
        "dst,dsw->dtw",
        pick_table.astype(jnp.float32),
        grad_documents[:, text_rows:],
        precision=HIGHEST_MODE,
        preferred_element_type=jnp.float32,
    )
    input_gradient = jnp.concatenate(
        [grad_documents[:, :text_rows] + moved_rows, grad_documents[:, text_rows:]], axis=1
    ).reshape(row_count, model_width)
    attention_sum, feedforward_sum, shared_sum = (
        lax.psum_scatter(attention_grad, "dp", scatter_dimension=0, tiled=True),
        lax.psum_scatter(feedforward_grad, "dp", scatter_dimension=0, tiled=True),
        lax.psum_scatter(shared_grad, "dp", scatter_dimension=0, tiled=True),
    )
    split_sum = lax.psum(split_grad, "dp")
    attention_new = renew(
        attention_master,
        attention_moment,
        attention_average,
        attention_sum,
        jnp.asarray(ATTENTION_RATES, jnp.float32).reshape(1, 4, 1),
    )
    feedforward_new = renew(
        feedforward_master,
        feedforward_moment,
        feedforward_average,
        feedforward_sum,
        jnp.asarray(FEEDFORWARD_RATES, jnp.float32).reshape(1, 2, 1),
    )
    shared_new = renew(shared_master, shared_moment, shared_average, shared_sum, SHARED_RATE)
    split_new = renew(
        split_master,
        split_moment,
        split_average,
        split_sum,
        jnp.asarray(SPLIT_RATES, jnp.float32).reshape(1, 6),
    )
    return (
        output.astype(jnp.bfloat16),
        input_gradient,
        attention_new[0],
        attention_new[1],
        attention_new[2],
        attention_new[3],
        feedforward_new[0],
        feedforward_new[1],
        feedforward_new[2],
        feedforward_new[3],
        shared_new[0],
        shared_new[1],
        shared_new[2],
        shared_new[3],
        split_new[0],
        split_new[1],
        split_new[2],
        split_new[3],
    )


LOW = jnp.bfloat16
WIDE = jnp.float32
UNITS = [(0, 0), (1, 0), (2, 0), (0, 1), (0, 2), (0, 3)] + [(t, k) for k in range(1, 4) for t in (1, 2)]
AXES = (0, 1, 0, 1, 0, 1, 0, 0, 0, 1, 0, 1)
LINE = 4
BACK_UNITS = [(t, k) for k in range(4) for t in (2, 1)] + [(0, k) for k in range(4)]
PIECES = 8
SENDS = 3
PAIRS = 4


def place():
    dp, z = lax.axis_index("dp"), lax.axis_index("mp")
    return z, lax.div(dp, 4), lax.rem(lax.div(dp, 2), 2), lax.rem(dp, 2)


def device(z, y, x, c):
    return (y * 4 + x * 2 + c, z)


def document_of(z):
    return lax.div(z + 1, 2)


def nearest_level(z, k):
    low, high = lax.rem(z, 2), lax.div(z, 2)
    if k == 0:
        return z
    if k == 1:
        return 1 + (2 * high - 1) * low
    if k == 2:
        return 2 + high * (1 - 2 * low)
    return 3 - 3 * high


def greet(z, y, x, c):
    barrier = pltpu.get_barrier_semaphore()
    partners = [device(z, y, x, 1 - c), device(z, y, 1 - x, c), device(z, 1 - y, x, c)]
    partners += [device(lax.rem(z + k, 4), y, x, c) for k in (1, 2, 3)]
    for partner in partners:
        pl.semaphore_signal(barrier, inc=1, device_id=partner, device_id_type=MESH)
    pl.semaphore_wait(barrier, len(partners))


def remote(source, target, send, recv, to):
    return pltpu.make_async_remote_copy(
        src_ref=source, dst_ref=target, send_sem=send, recv_sem=recv, device_id=to, device_id_type=MESH
    )


def when(condition, action):
    pl.when(condition)(action)


def mul(left, right):
    return jnp.dot(left, right, preferred_element_type=WIDE)


def gelu_parts(value):
    root = value * 0.7071067811865476
    inverse = 1.0 / (1.0 + 0.3275911 * jnp.abs(root))
    bell = jnp.exp(-root * root)
    series = 1.061405429
    for factor in (-1.453152027, 1.421413741, -0.284496736, 0.254829592):
        series = series * inverse + factor
    tail = 0.5 * series * inverse * bell
    share = jnp.where(value >= 0, 1.0 - tail, tail)
    return value * share, share + value * (bell * 0.3989422804014327)


def head_mask(head, scale, lanes=192):
    lane = lax.broadcasted_iota(jnp.int32, (1, lanes), 1)
    return jnp.where((lane >= head * HEAD_DIM) & (lane < (head + 1) * HEAD_DIM), scale, 0.0).astype(LOW)


def unit_weight(r, t, level):
    return r.full[t, level].reshape(768, 768)


class Gather:
    def __init__(self, own, small, r):
        self.own, self.small, self.r = own, small, r
        self.z, self.y, self.x, self.c = z, y, x, c = place()
        self.up, self.down = device(z + 1, y, x, c), device(z - 1, y, x, c)
        self.across_x, self.across_y = device(z, y, 1 - x, c), device(z, 1 - y, x, c)
        self.pair = device(z, y, x, 1 - c)
        self.end = (z == 0) | (z == LINE - 1)

    def line_copy(self, t, level, source, way):
        r = self.r
        return remote(
            source, r.full.at[t, level, self.y, self.x, self.c], r.line_send.at[t, level, way],
            r.line_recv.at[t, level], self.up if way == 0 else self.down,
        )

    def along_x(self, u):
        return AXES[u] == 0

    def first(self, u):
        t, k = UNITS[u]
        block = self.r.full.at[t, nearest_level(self.z, k), self.y, self.x, self.c]
        return remote(
            self.own.at[t] if k == 0 else block, block, self.r.first_send.at[u], self.r.first_recv.at[u],
            self.across_x if self.along_x(u) else self.across_y,
        )

    def second(self, u):
        t, k = UNITS[u]
        level = nearest_level(self.z, k)
        if self.along_x(u):
            block, to = self.r.full.at[t, level, self.y, :, self.c], self.across_y
        else:
            block, to = self.r.full.at[t, level, :, self.x, self.c], self.across_x
        return remote(block, block, self.r.second_send.at[u], self.r.second_recv.at[u], to)

    def extra(self, u, level, part, way):
        t, y, x, c = UNITS[u][0], self.y, self.x, self.c
        if self.along_x(u):
            index = (t, level, y, 1 - x, c) if part == 0 else (t, level, 1 - y, slice(None), c)
        else:
            index = (t, level, 1 - y, x, c) if part == 0 else (t, level, slice(None), 1 - x, c)
        block = self.r.full.at[index]
        return remote(
            block, block, self.r.extra_send.at[t - 1, part, way], self.r.extra_recv.at[t - 1, level, part],
            self.up if way == 0 else self.down,
        )

    def paired(self, u):
        t, k = UNITS[u]
        block = self.r.full.at[t, nearest_level(self.z, k), :, :, self.c]
        return remote(block, block, self.r.pair_send.at[u], self.r.pair_recv.at[u], self.pair)

    def own_copy(self, t):
        return pltpu.make_async_copy(
            self.own.at[t], self.r.full.at[t, self.z, self.y, self.x, self.c], self.r.own_sem.at[t]
        )

    def tiny_own(self, i):
        target = self.r.plane.at[self.y, self.x, self.c] if i == 0 else self.r.line.at[self.z]
        return pltpu.make_async_copy(self.small, target, self.r.own_sem.at[3 + i])

    def tiny(self, i):
        r = self.r
        if i == 0:
            block, to = r.plane.at[self.y, self.x, self.c], self.across_x
        elif i == 1:
            block, to = r.plane.at[self.y, :, self.c], self.across_y
        elif i == 2:
            block, to = r.plane.at[:, :, self.c], self.pair
        else:
            block, to = r.line.at[self.z], device(lax.rem(self.z + i - 2, 4), self.y, self.x, self.c)
        source = self.small if i == 0 or i > 2 else block
        return remote(source, block, r.tiny_send.at[i], r.tiny_recv.at[i], to)

    def own_line(self, t, act):
        when(self.z < 3, lambda: act(self.line_copy(t, self.z, self.own.at[t], 0)))
        when(self.z > 0, lambda: act(self.line_copy(t, self.z, self.own.at[t], 1)))

    def own_extra(self, u, part, act):
        when(self.z < 3, lambda: act(self.extra(u, self.z, part, 0)))
        when(self.z > 0, lambda: act(self.extra(u, self.z, part, 1)))

    def begin(self):
        self.own_line(0, lambda copy: copy.start())
        for t in range(3):
            self.own_copy(t).start()
        for i in range(2):
            self.tiny_own(i).start()
        for i in (0, 3, 4, 5):
            self.tiny(i).start()

    def crosses(self, u, act):
        t, k = UNITS[u]
        if t == 0 or k in (0, 3):
            act()
        elif k == 2:
            when(self.end, act)

    def comes_whole(self, u, act):
        t, k = UNITS[u]
        if t > 0 and k == 1:
            act()
        elif t > 0 and k == 2:
            when(jnp.logical_not(self.end), act)

    def arrive(self, u):
        t, k = UNITS[u]
        if k == 0 and t > 0:
            self.own_line(t, lambda copy: copy.start())
        if k > 0:
            level = nearest_level(self.z, k)
            block = self.r.full.at[t, level, self.y, self.x, self.c]
            self.line_copy(t, level, block, 0).wait_recv()
            when((level < self.z) & (self.z < 3), lambda: self.line_copy(t, level, block, 0).start())
            when((level > self.z) & (self.z > 0), lambda: self.line_copy(t, level, block, 1).start())
        self.crosses(u, lambda: self.first(u).start())

    def cross(self, u):
        t, k = UNITS[u]

        def act():
            self.first(u).wait_recv()
            if k == 0:
                self.own_copy(t).wait()
            self.second(u).start()
            if t > 0 and k == 0:
                self.own_extra(u, 0, lambda copy: copy.start())

        self.crosses(u, act)

    def share(self, u):
        t, k = UNITS[u]
        level = nearest_level(self.z, k)

        def act():
            self.second(u).wait_recv()
            if t > 0 and k == 0:
                self.own_extra(u, 1, lambda copy: copy.start())
            self.paired(u).start()

        def act_whole():
            own = UNITS.index((t, 0))
            for part in range(2):
                self.extra(own, level, part, 0).wait_recv()
            self.paired(u).start()

        self.crosses(u, act)
        self.comes_whole(u, act_whole)

    def take(self, u):
        self.paired(u).wait_recv()

    def tiny_step(self, i):
        if i == 0:
            for j in range(2):
                self.tiny_own(j).wait()
        if i < 3:
            self.tiny(i).wait_recv()
        if i < 2:
            self.tiny(i + 1).start()
        if i == 3:
            for j in (3, 4, 5):
                self.tiny(j).wait_recv()

    def finish(self):
        z = self.z
        for i in range(6):
            self.tiny(i).wait_send()
        for u, (t, k) in enumerate(UNITS):
            level = nearest_level(z, k)
            block = self.r.full.at[t, level, self.y, self.x, self.c]
            if k == 0:
                self.own_line(t, lambda copy: copy.wait_send())
                if t > 0:
                    for part in range(2):
                        self.own_extra(u, part, lambda copy: copy.wait_send())
            else:
                when((level < z) & (z < 3), lambda t=t, v=level, b=block: self.line_copy(t, v, b, 0).wait_send())
                when((level > z) & (z > 0), lambda t=t, v=level, b=block: self.line_copy(t, v, b, 1).wait_send())

            def both(u=u):
                self.first(u).wait_send()
                self.second(u).wait_send()

            self.crosses(u, both)
            self.paired(u).wait_send()


class Reduce:
    def __init__(self, sum_ref, r):
        self.sum_ref, self.r = sum_ref, r
        self.z, self.y, self.x, self.c = z, y, x, c = place()
        self.up, self.down = device(z + 1, y, x, c), device(z - 1, y, x, c)
        self.across_x, self.across_y = device(z, y, 1 - x, c), device(z, 1 - y, x, c)
        self.pair = device(z, y, x, 1 - c)

    def pair_copy(self, u):
        r = self.r
        return remote(
            r.sends.at[u % SENDS], r.pair_in.at[u % PAIRS], r.r_pair_send.at[u], r.r_pair_recv.at[u], self.pair
        )

    def first_copy(self, u):
        r = self.r
        source = r.total.at[u, :, 1 - self.x] if u % 2 == 0 else r.total.at[u, 1 - self.y]
        return remote(
            source, r.first_in.at[u], r.r_first_send.at[u], r.r_first_recv.at[u],
            self.across_x if u % 2 == 0 else self.across_y,
        )

    def second_copy(self, u):
        r, x, y = self.r, self.x, self.y
        return remote(
            r.total.at[u, 1 - y, x] if u % 2 == 0 else r.total.at[u, y, 1 - x],
            r.second_in.at[u], r.r_second_send.at[u], r.r_second_recv.at[u],
            self.across_y if u % 2 == 0 else self.across_x,
        )

    def line_copy(self, u, way):
        r = self.r
        t, k = BACK_UNITS[u]
        level = nearest_level(self.z, 3 - k)
        return remote(
            r.total.at[u, self.y, self.x], r.line_in.at[t, level, way], r.r_line_send.at[t, level],
            r.r_line_recv.at[t, level, way], self.up if way == 0 else self.down,
        )

    def produce(self, u, parts):
        r = self.r
        if u >= SENDS:
            self.pair_copy(u - SENDS).wait_send()
        for half, target in ((1 - self.c, r.sends.at[u % SENDS]), (self.c, r.total.at[u])):
            for products, lanes in parts:
                value = sum(mul(turned[:, :, half].reshape(384, 512), columns) for turned, columns in products)
                target[:, :, :, lanes] = value.astype(LOW).reshape(2, 2, 96, value.shape[1])
            if half is not self.c:
                self.pair_copy(u).start()

    def add_pair(self, u):
        r = self.r
        self.pair_copy(u).wait_recv()
        r.total[u] = r.total[u] + r.pair_in[u % PAIRS]
        self.first_copy(u).start()

    def add_first(self, u):
        r, x, y = self.r, self.x, self.y
        self.first_copy(u).wait_recv()
        if u % 2 == 0:
            r.total[u, :, x] = r.total[u, :, x] + r.first_in[u]
        else:
            r.total[u, y] = r.total[u, y] + r.first_in[u]
        self.second_copy(u).start()

    def add_second(self, u):
        r, x, y, z = self.r, self.x, self.y, self.z
        t, k = BACK_UNITS[u]
        level = nearest_level(z, 3 - k)
        self.second_copy(u).wait_recv()
        r.total[u, y, x] = r.total[u, y, x] + r.second_in[u]
        if k < 3:
            when((z == 0) | (z == 3), lambda: self.send_line(u))

    def send_line(self, u):
        level = nearest_level(self.z, 3 - BACK_UNITS[u][1])
        when(self.z < level, lambda: self.line_copy(u, 0).start())
        when(self.z > level, lambda: self.line_copy(u, 1).start())

    def take_line(self, u, way):
        r, x, y = self.r, self.x, self.y
        t, k = BACK_UNITS[u]
        level = nearest_level(self.z, 3 - k)
        self.line_copy(u, way).wait_recv()
        r.total[u, y, x] = r.total[u, y, x] + r.line_in[t, level, way]

    def add_line(self, u):
        r, z = self.r, self.z
        t, k = BACK_UNITS[u]
        level = nearest_level(z, 3 - k)
        middle = (z == 1) | (z == 2)
        if k < 3:
            when(middle & (z < level), lambda: self.take_line(u, 0))
            when(middle & (z > level), lambda: self.take_line(u, 1))
            when(middle, lambda: self.send_line(u))
        else:
            when(z > 0, lambda: self.take_line(u, 0))
            when(z < 3, lambda: self.take_line(u, 1))
            self.sum_ref[t] = r.total[u, self.y, self.x].astype(WIDE)

    def small_copy(self, i):
        r = self.r
        if i < 3:
            to = (self.pair, self.across_x, self.across_y)[i]
            return remote(r.small_total.at[i], r.small_in.at[i], r.small_send.at[i], r.small_recv.at[i], to)
        to = device(lax.rem(self.z + i - 2, 4), self.y, self.x, self.c)
        return remote(r.small_total.at[3], r.small_line.at[self.z], r.small_send.at[i], r.small_recv.at[i], to)

    def small_step(self, i):
        r = self.r
        self.small_copy(i).wait_recv()
        r.small_total[i + 1] = r.small_total[i] + r.small_in[i]
        if i < 2:
            self.small_copy(i + 1).start()
        else:
            for j in (3, 4, 5):
                self.small_copy(j).start()
            r.small_line[self.z] = r.small_total[3]

    def small_end(self, out):
        for i in (3, 4, 5):
            self.small_copy(i).wait_recv()
        line = self.r.small_line
        out[...] = line[0] + line[1] + line[2] + line[3]

    def finish(self):
        z = self.z
        for i in range(6):
            self.small_copy(i).wait_send()
        for u, (t, k) in enumerate(BACK_UNITS):
            if u >= len(BACK_UNITS) - SENDS:
                self.pair_copy(u).wait_send()
            self.first_copy(u).wait_send()
            self.second_copy(u).wait_send()
            if k < 3:
                level = nearest_level(z, 3 - k)
                when(z < level, lambda u=u: self.line_copy(u, 0).wait_send())
                when(z > level, lambda u=u: self.line_copy(u, 1).wait_send())


class Cast:
    def __init__(self, a, source, target, r):
        self.a, self.source, self.target, self.r = a, source, target, r
        self.z, y, x, c = place()
        self.up, self.down = device(self.z + 1, y, x, c), device(self.z - 1, y, x, c)

    def copy(self, d, p, way, first):
        r = self.r
        part = pl.ds(p * (512 // PIECES), 512 // PIECES)
        target = self.target.at[d, part]
        return remote(
            self.source.at[part] if first else target, target, r.cast_send.at[self.a, d, p, way],
            r.cast_recv.at[self.a, d, p], self.up if way == 0 else self.down,
        )

    def own(self):
        return pltpu.make_async_copy(self.source, self.target.at[document_of(self.z)], self.r.cast_own.at[self.a])

    def firsts(self, p, act):
        for level, d, way in ((0, 0, 0), (1, 1, 1), (2, 1, 0), (3, 2, 1)):
            when(self.z == level, lambda d=d, way=way: act(self.copy(d, p, way, True)))

    def begin(self):
        self.own().start()
        for p in range(PIECES):
            self.firsts(p, lambda copy: copy.start())

    def pass_on(self, d, p, way):
        copy = self.copy(d, p, way, False)
        copy.wait_recv()
        copy.start()

    def near(self, p):
        when(self.z == 1, lambda: self.pass_on(0, p, 0))
        when(self.z == 2, lambda: self.pass_on(2, p, 1))

    def far(self, p):
        when(self.z == 1, lambda: self.pass_on(2, p, 1))
        when(self.z == 2, lambda: self.pass_on(0, p, 0))

    def finish(self):
        self.own().wait()
        for p in range(PIECES):
            self.firsts(p, lambda copy: copy.wait_send())
            for level in (1, 2):
                when(self.z == level, lambda p=p: self.copy(0, p, 0, False).wait_send())
                when(self.z == level, lambda p=p: self.copy(2, p, 1, False).wait_send())
            for level, d, way in ((0, 1, 1), (0, 2, 1), (3, 1, 0), (3, 0, 0)):
                when(self.z == level, lambda p=p, d=d, way=way: self.copy(d, p, way, False).wait_recv())


def buffers():
    vmem = pltpu.VMEM
    return dict(
        full=vmem((3, 4, 2, 2, 2, 96, 768), LOW),
        plane=vmem((2, 2, 2, 16, 768), LOW),
        line=vmem((4, 16, 768), LOW),
        tok=vmem((512, 768), LOW),
        cot=vmem((512, 768), LOW),
        pick=vmem((384, 128), LOW),
        rows_in=vmem((512, 768), LOW),
        hidden_in=vmem((512, 768), LOW),
        rows_t=vmem((2, 2, 2, 96, 512), LOW),
        hidden_t=vmem((2, 2, 2, 96, 512), LOW),
        down_t=vmem((2, 2, 2, 96, 512), LOW),
        joined_t=vmem((2, 2, 2, 96, 512), LOW),
        qkv=vmem((4, 512, 640), LOW),
        probs=vmem((2, 3, 512, 512), LOW),
        context=vmem((4, 512, 256), LOW),
        active=vmem((4, 512, 768), LOW),
        slope=vmem((4, 512, 768), LOW),
        mixed=vmem((512, 768), WIDE),
        normed_one=vmem((512, 768), WIDE),
        factor_one=vmem((512, 1), WIDE),
        total=vmem((12, 2, 2, 96, 768), LOW),
        sends=vmem((SENDS, 2, 2, 96, 768), LOW),
        pair_in=vmem((PAIRS, 2, 2, 96, 768), LOW),
        first_in=vmem((12, 2, 96, 768), LOW),
        second_in=vmem((12, 96, 768), LOW),
        line_in=vmem((3, 4, 2, 96, 768), LOW),
        small_total=vmem((4, 16, 768), WIDE),
        small_in=vmem((3, 16, 768), WIDE),
        small_line=vmem((4, 16, 768), WIDE),
    )


def flags():
    dma = pltpu.SemaphoreType.DMA
    return dict(
        line_send=dma((3, 4, 2)),
        line_recv=dma((3, 4)),
        first_send=dma((12,)),
        first_recv=dma((12,)),
        second_send=dma((12,)),
        second_recv=dma((12,)),
        pair_send=dma((12,)),
        pair_recv=dma((12,)),
        tiny_send=dma((6,)),
        tiny_recv=dma((6,)),
        extra_send=dma((2, 2, 2)),
        extra_recv=dma((2, 4, 2)),
        own_sem=dma((5,)),
        load_sem=dma((6,)),
        r_pair_send=dma((12,)),
        r_pair_recv=dma((12,)),
        r_first_send=dma((12,)),
        r_first_recv=dma((12,)),
        r_second_send=dma((12,)),
        r_second_recv=dma((12,)),
        r_line_send=dma((3, 4)),
        r_line_recv=dma((3, 4, 2)),
        small_send=dma((6,)),
        small_recv=dma((6,)),
        cast_send=dma((2, 3, PIECES, 2)),
        cast_recv=dma((2, 3, PIECES)),
        cast_own=dma((2,)),
    )


def turn(value, counts):
    return (value * counts.astype(LOW)).T.reshape(2, 2, 2, 96, 512)


def layer_kernel(
    own_ref, small_ref, tokens_ref, cotangent_ref, align_ref, count_ref, mask_ref,
    sum_ref, small_sum_ref, text_all, back_all, probs_out, *refs,
):
    r = SimpleNamespace(**dict(zip([*buffers(), *flags()], refs)))
    z, y, x, c = place()
    doc = document_of(z)
    counts = jnp.where(z == 2, 0.0, 1.0)
    tok_copy = pltpu.make_async_copy(tokens_ref.at[pl.ds(doc * 512, 512)], r.tok, r.load_sem.at[0])
    cot_copy = pltpu.make_async_copy(cotangent_ref.at[pl.ds(doc * 512, 512)], r.cot, r.load_sem.at[1])
    tok_copy.start()
    cot_copy.start()
    greet(z, y, x, c)
    net = Gather(own_ref, small_ref, r)
    net.begin()
    held = SimpleNamespace()

    def prologue():
        tok_copy.wait()
        live = lax.broadcasted_iota(jnp.int32, (1, 128), 1) < count_ref[pl.ds(doc, 1), :]
        pick = jnp.where(
            (lax.broadcasted_iota(jnp.int32, (384, 128), 0) == align_ref[pl.ds(doc, 1), :]) & live, 1.0, 0.0
        ).astype(LOW)
        r.pick[...] = pick
        text_tokens = r.tok[:384]
        taken = lax.dot_general(pick, text_tokens, (((0,), (0,)), ((), ())), preferred_element_type=WIDE)
        slot_rows = r.tok[384:].astype(WIDE) + taken
        r.mixed[:384] = text_tokens.astype(WIDE)
        r.mixed[384:] = slot_rows
        r.rows_in[:384] = text_tokens
        r.rows_in[384:] = slot_rows.astype(LOW)
        r.rows_t[...] = turn(r.rows_in[...], counts)
        valid = jnp.concatenate([mask_ref[pl.ds(doc, 1), :] > 0, live], axis=1)
        held.bar = jnp.where(valid, 0.0, -1e30)

    def spill(k):
        return pltpu.make_async_copy(r.probs.at[k % 2], probs_out.at[k % 2], r.load_sem.at[2 + k % 2])

    def attention(k):
        level = nearest_level(z, k)
        weight = unit_weight(r, 0, level)
        bias = r.line[level][6:7].astype(WIDE)
        projected = (mul(r.rows_in[...], weight[...]) + bias).astype(LOW)
        r.qkv[k] = projected[:, :640]
        queries, keys, values = projected[:, :192], projected[:, 192:384], projected[:, 384:640]
        if k >= 2:
            spill(k).wait()
        context = jnp.zeros((512, 256), WIDE)
        for head in range(3):
            scores = contract_last(queries * head_mask(head, 0.125), keys)
            scores = jnp.where(held.bar < 0.0, -1e30, scores)
            raised = jnp.exp(scores - jnp.max(scores, axis=-1, keepdims=True))
            probs = (raised * (1.0 / jnp.sum(raised, axis=-1, keepdims=True))).astype(LOW)
            r.probs[k % 2, head] = probs
            context = context + mul(probs, values * head_mask(head, 1.0, 256))
        context = pltpu.roll(context, 64, 1).astype(LOW)
        r.context[level] = context
        if k < 2:
            spill(k).start()

    def first_norm():
        for level in range(4):
            r.mixed[...] += contract_last(r.context[level], unit_weight(r, 0, level)[:, 512:])
        held.shared = shared = jnp.sum(r.plane[...].astype(WIDE).reshape(8, 16, 768), axis=0)
        mixed = r.mixed[...] + shared[0:1]
        first_norm, normed, factor = layer_norm(mixed, shared[1:2], shared[2:3])
        r.normed_one[...] = normed
        r.factor_one[...] = factor
        r.hidden_in[...] = first_norm.astype(LOW)
        r.hidden_t[...] = turn(first_norm.astype(LOW), counts)
        r.mixed[...] = first_norm + shared[5:6]

    def feed(k):
        level = nearest_level(z, k)
        bias = r.line[level][7:8, :].astype(WIDE)
        up = unit_weight(r, 1, level)
        for part in range(3):
            lanes = slice(part * 256, (part + 1) * 256)
            inner = mul(r.hidden_in[...], up[:, lanes]) + bias[:, lanes]
            active, slope = gelu_parts(inner)
            r.active[level, :, lanes] = active.astype(LOW)
            r.slope[level, :, lanes] = slope.astype(LOW)

    def feed_sum():
        for level in range(4):
            r.mixed[...] += contract_last(r.active[level], unit_weight(r, 2, level))

    text_cast = Cast(0, r.tok, text_all, r)
    back_cast = Cast(1, r.cot, back_all, r)
    red = Reduce(sum_ref, r)

    def second_norm():
        shared = held.shared
        final, normed, factor = layer_norm(r.mixed[...], shared[3:4], shared[4:5])
        r.tok[...] = final.astype(LOW)
        text_cast.begin()
        cot_copy.wait()
        incoming = r.cot[...].astype(WIDE)
        grad, gain, shift = norm_back(incoming, normed, factor, shared[3:4])
        r.mixed[...] = grad
        low = grad.astype(LOW)
        r.rows_in[...] = low
        r.down_t[...] = turn(low, counts)
        r.small_total[0] = jnp.zeros((16, 768), WIDE)
        r.small_total[0, 3:4] = gain[None]
        r.small_total[0, 4:5] = shift[None]
        r.small_total[0, 5:6] = jnp.sum(grad, axis=0, keepdims=True)

    def feed_back(k):
        level = nearest_level(z, 3 - k)
        grad = mul(r.rows_in[...], unit_weight(r, 2, level)) * r.slope[level].astype(WIDE)
        r.slope[level] = grad.astype(LOW)
        r.small_total[0, pl.ds(12 + level, 1)] = jnp.sum(grad.astype(LOW).astype(WIDE), axis=0, keepdims=True)
        red.produce(2 * k, [([(r.down_t, r.active[level])], slice(0, 768))])

    def feed_back_up(k):
        level = nearest_level(z, 3 - k)
        red.produce(2 * k + 1, [([(r.hidden_t, r.slope[level])], slice(0, 768))])

    def first_norm_back():
        for level in range(4):
            r.mixed[...] += contract_last(r.slope[level], unit_weight(r, 1, level))
        grad, gain, shift = norm_back(r.mixed[...], r.normed_one[...], r.factor_one[...], held.shared[1:2])
        r.mixed[...] = grad
        low = grad.astype(LOW)
        r.hidden_in[...] = low
        r.joined_t[...] = turn(low, counts)
        r.small_total[0, 0:1] = jnp.sum(grad, axis=0, keepdims=True)
        r.small_total[0, 1:2] = gain[None]
        r.small_total[0, 2:3] = shift[None]

    def reload(k):
        return pltpu.make_async_copy(probs_out.at[k], r.probs.at[k], r.load_sem.at[4 + k])

    def attention_back(k):
        slot = 3 - k
        level = nearest_level(z, slot)
        projected = r.qkv[slot]
        queries, keys, values = projected[:, :192], projected[:, 192:384], projected[:, 384:576]
        upstream = mul(r.hidden_in[...], unit_weight(r, 0, level)[:, 512:])[:, 64:].astype(LOW)
        if slot < 2:
            reload(slot).wait()
        grad_q = grad_k = grad_v = jnp.zeros((512, 192), WIDE)
        for head in range(3):
            probs = r.probs[slot % 2, head]
            up = upstream * head_mask(head, 1.0)
            grad_v = grad_v + contract_rows(probs, up)
            grad_probs = contract_last(up, values)
            wide = probs.astype(WIDE)
            weighed = wide * grad_probs
            grad_scores = (weighed - wide * jnp.sum(weighed, axis=-1, keepdims=True)).astype(LOW)
            grad_q = grad_q + mul(grad_scores, keys * head_mask(head, 0.125))
            grad_k = grad_k + contract_rows(grad_scores, queries * head_mask(head, 0.125))
        if slot >= 2:
            reload(slot - 2).start()
        r.active[level, :, :192] = grad_q.astype(LOW)
        r.active[level, :, 192:384] = grad_k.astype(LOW)
        r.active[level, :, 384:576] = grad_v.astype(LOW)
        r.active[level, :, 576:] = jnp.zeros((512, 192), LOW)
        r.small_total[0, pl.ds(8 + level, 1)] = jnp.sum(r.active[level].astype(WIDE), axis=0, keepdims=True)

    def project_back(k):
        slot = 3 - k
        level = nearest_level(z, slot)
        red.produce(
            8 + k,
            [
                ([(r.rows_t, r.active[level, :, :512])], slice(0, 512)),
                ([(r.rows_t, r.active[level, :, 512:]), (r.joined_t, r.context[level])], slice(512, 768)),
            ],
        )

    def input_back():
        for level in range(4):
            r.mixed[...] += contract_last(r.active[level], unit_weight(r, 0, level))
        grad = r.mixed[...]
        r.cot[:384] = (grad[:384] + mul(r.pick[...], grad[384:].astype(LOW))).astype(LOW)
        r.cot[384:] = grad[384:].astype(LOW)
        back_cast.begin()
        r.small_total[0] = r.small_total[0] * counts
        red.small_copy(0).start()

    steps = program_steps(net, red, text_cast, back_cast, small_sum_ref, [
        prologue, attention, first_norm, feed, feed_sum, second_norm, feed_back, feed_back_up, first_norm_back,
        attention_back, project_back, input_back,
    ])
    for i in ORDER:
        steps[i][0]()
    net.finish()
    text_cast.finish()
    back_cast.finish()
    red.finish()


def program_steps(net, red, text_cast, back_cast, small_sum_ref, work):
    steps = []

    def add(action, *after):
        steps.append((action, after))
        return len(steps) - 1

    (prologue, attention, first_norm, feed, feed_sum, second_norm, feed_back, feed_back_up, first_norm_back,
     attention_back, project_back, input_back) = work
    taken = {}
    for u, unit in enumerate(UNITS):
        step = add(partial(net.arrive, u))
        step = add(partial(net.cross, u), step)
        step = add(partial(net.share, u), step)
        taken[unit] = add(partial(net.take, u), step)
    tiny = [add(partial(net.tiny_step, 0))]
    for i in (1, 2, 3):
        tiny.append(add(partial(net.tiny_step, i), tiny[-1]))
    step = add(prologue)
    for k in range(4):
        step = add(partial(attention, k), step, taken[0, k], tiny[3])
    step = add(first_norm, step, tiny[2])
    for k in range(4):
        step = add(partial(feed, k), step, taken[1, k])
    step = add(feed_sum, step, *[taken[2, k] for k in range(4)])
    step = started = add(second_norm, step)
    made, joined = {}, {}

    def make(u, action, before):
        ahead = [joined[u - 2]] if u >= 2 else []
        made[u] = add(action, before, *ahead)
        joined[u] = add(partial(red.add_pair, u), made[u])
        return made[u]

    for k in range(4):
        step = make(2 * k, partial(feed_back, k), step)
        step = make(2 * k + 1, partial(feed_back_up, k), step)
    step = add(first_norm_back, step)
    for k in range(4):
        step = add(partial(attention_back, k), step)
        step = make(8 + k, partial(project_back, k), step)
    step = ended = add(input_back, step)
    for u in range(12):
        step = add(partial(red.add_first, u), joined[u])
        step = add(partial(red.add_second, u), step)
        add(partial(red.add_line, u), step)
    for cast, begun in ((text_cast, started), (back_cast, ended)):
        for p in range(PIECES):
            add(partial(cast.near, p), begun)
            add(partial(cast.far, p), begun)
    step = ended
    for i in range(3):
        step = add(partial(red.small_step, i), step)
    add(partial(red.small_end, small_sum_ref), step)
    return steps


ORDER = (
    4, 0, 52, 48, 12, 1, 8, 13, 16, 9, 20, 5, 2, 49, 50, 51, 24, 3, 17, 28, 14, 32, 53, 36, 21, 15, 54, 44, 18,
    40, 6, 19, 37, 33, 22, 55, 10, 41, 45, 23, 25, 56, 57, 29, 7, 11, 26, 34, 58, 42, 27, 59, 46, 35, 43, 38, 30,
    60, 47, 61, 39, 31, 62, 63, 64, 66, 65, 68, 132, 130, 67, 70, 134, 69, 72, 136, 71, 74, 94, 133, 138, 73, 76,
    97, 75, 78, 80, 140, 81, 137, 144, 77, 79, 142, 131, 139, 141, 95, 82, 84, 85, 87, 135, 143, 83, 88, 98, 86,
    90, 91, 145, 93, 115, 162, 100, 146, 118, 121, 101, 103, 148, 163, 92, 106, 150, 96, 149, 152, 89, 154, 112,
    147, 156, 151, 124, 119, 160, 153, 127, 107, 158, 102, 108, 157, 109, 99, 104, 120, 122, 155, 128, 159, 125,
    110, 111, 105, 116, 123, 126, 164, 113, 161, 114, 117, 165, 129,
)


def run_layer(own, small, tokens, cotangent, align, count, mask):
    vmem = pl.BlockSpec(memory_space=pltpu.VMEM)
    hbm = pl.BlockSpec(memory_space=pl.ANY)
    whole = jax.ShapeDtypeStruct((3, 512, 768), LOW)
    return pl.pallas_call(
        layer_kernel,
        out_shape=(
            jax.ShapeDtypeStruct((3, 96, 768), WIDE),
            jax.ShapeDtypeStruct((16, 768), WIDE),
            whole,
            whole,
            jax.ShapeDtypeStruct((2, 3, 512, 512), LOW),
        ),
        in_specs=[vmem, vmem, hbm, hbm, vmem, vmem, vmem],
        out_specs=(vmem, vmem, hbm, hbm, hbm),
        scratch_shapes=[*buffers().values(), *flags().values()],
        compiler_params=pltpu.CompilerParams(
            collective_id=0, has_side_effects=True, vmem_limit_bytes=VMEM_LIMIT
        ),
        name="layer_step",
    )(own, small, tokens, cotangent, align, count, mask)


VMEM_LIMIT = 63 * 2**20


def line_shards(
    tokens,
    alignment,
    segment_count,
    text_mask,
    cotangent,
    attention_master,
    attention_moment,
    attention_average,
    feedforward_master,
    feedforward_moment,
    feedforward_average,
    shared_master,
    shared_moment,
    shared_average,
    split_master,
    split_moment,
    split_average,
):
    documents, slot_count = alignment.shape
    rows, width = tokens.shape
    level, index = lax.axis_index("mp"), lax.axis_index("dp")
    own = jnp.concatenate(
        [attention_master.reshape(1, 96, 768), jnp.swapaxes(feedforward_master, 0, 1)], axis=0
    ).astype(LOW)
    line_row = jnp.concatenate(
        [split_master[:, 0], jnp.zeros((192,), WIDE), split_master[:, 1], jnp.zeros((192,), WIDE)]
    )
    small = jnp.concatenate(
        [
            lax.dynamic_update_slice(jnp.zeros((6, 768), WIDE), shared_master.T, (0, index * 96)),
            line_row[None],
            split_master[:, 2:].reshape(1, 768),
            jnp.zeros((8, 768), WIDE),
        ],
        axis=0,
    ).astype(LOW)
    count = jnp.broadcast_to(segment_count[:, None], (documents, slot_count))
    sums, small_sum, text_all, back_all, _ = run_layer(
        own, small, tokens, cotangent, alignment, count, text_mask
    )
    shared_sum = lax.dynamic_slice(small_sum, (0, index * 96), (6, 96)).T
    bias_sum = lax.dynamic_slice(small_sum, (8 + level, 0), (1, 768))[0]
    split_sum = jnp.concatenate(
        [
            bias_sum[:192, None],
            bias_sum[384:576, None],
            lax.dynamic_slice(small_sum, (12 + level, 0), (1, 768)).reshape(192, 4),
        ],
        axis=1,
    )
    attention_new = renew(
        attention_master,
        attention_moment,
        attention_average,
        sums[0].reshape(96, 4, 192),
        jnp.asarray(ATTENTION_RATES, WIDE).reshape(1, 4, 1),
    )
    feedforward_new = renew(
        feedforward_master,
        feedforward_moment,
        feedforward_average,
        jnp.swapaxes(sums[1:], 0, 1),
        jnp.asarray(FEEDFORWARD_RATES, WIDE).reshape(1, 2, 1),
    )
    shared_new = renew(shared_master, shared_moment, shared_average, shared_sum, SHARED_RATE)
    split_new = renew(
        split_master,
        split_moment,
        split_average,
        split_sum,
        jnp.asarray(SPLIT_RATES, WIDE).reshape(1, 6),
    )
    return (
        text_all.reshape(rows, width),
        back_all.reshape(rows, width).astype(WIDE),
        *attention_new,
        *feedforward_new,
        *shared_new,
        *split_new,
    )


def solution(mesh):
    in_specs = (
        P("dp", None),
        P("dp", None),
        P("dp"),
        P("dp", None),
        P("dp", None),
        P("dp", None, "mp"),
        P("dp", None, "mp"),
        P("dp", None, "mp"),
        P("dp", None, "mp"),
        P("dp", None, "mp"),
        P("dp", None, "mp"),
        P("dp", None),
        P("dp", None),
        P("dp", None),
        P("mp", None),
        P("mp", None),
        P("mp", None),
    )
    out_specs = (
        P("dp", None),
        P("dp", None),
        P("dp", None, "mp"),
        P("dp", None, "mp"),
        P("dp", None, "mp"),
        P("dp", None, "mp"),
        P("dp", None, "mp"),
        P("dp", None, "mp"),
        P("dp", None, "mp"),
        P("dp", None, "mp"),
        P("dp", None),
        P("dp", None),
        P("dp", None),
        P("dp", None),
        P("mp", None),
        P("mp", None),
        P("mp", None),
        P("mp", None),
    )
    body = line_shards if mesh.shape["dp"] == 8 and mesh.shape["mp"] == 4 else general_shards
    return jax.shard_map(body, mesh=mesh, in_specs=in_specs, out_specs=out_specs, check_vma=False)
```

```python
from functools import partial
from types import SimpleNamespace

import jax
import jax.numpy as jnp
from jax import lax
from jax.experimental import pallas as pl
from jax.experimental.pallas import tpu as pltpu
from jax.sharding import PartitionSpec as P

MESH = pl.DeviceIdType.MESH

HEAD_DIM = 64


EPS = 1e-05
MOMENTUM = 0.9
AVERAGE = 0.75
ATTENTION_RATES = (4e-05, 4e-05, 4e-05, 0.01)
FEEDFORWARD_RATES = (0.0002, 4e-05)
SHARED_RATE = 0.0006
SPLIT_RATES = (0.0004, 0.0003, 0.0017, 0.0017, 0.0017, 0.0017)
HIGHEST_MODE = lax.Precision.HIGHEST


def contract_last(left, right):
    return lax.dot_general(
        left, right, (((1,), (1,)), ((), ())), preferred_element_type=jnp.float32
    )


def contract_rows(left, right):
    return lax.dot_general(
        left, right, (((0,), (0,)), ((), ())), preferred_element_type=jnp.float32
    )


def layer_norm(value, gain, shift):
    center = value - jnp.mean(value, axis=-1, keepdims=True)
    factor = lax.rsqrt(jnp.mean(center * center, axis=-1, keepdims=True) + EPS)
    normed = center * factor
    return (normed * gain + shift, normed, factor)


def norm_back(incoming, normed, factor, gain):
    scaled = incoming * gain
    inner_part = (
        scaled
        - jnp.mean(scaled, axis=-1, keepdims=True)
        - normed * jnp.mean(scaled * normed, axis=-1, keepdims=True)
    )
    return (factor * inner_part, jnp.sum(incoming * normed, axis=0), jnp.sum(incoming, axis=0))


def masked_scores(queries, key_rows, valid_keys):
    scores = jnp.einsum(
        "qhd,khd->hqk", queries, key_rows, preferred_element_type=jnp.float32
    ) * HEAD_DIM ** (-0.5)
    return jnp.where(valid_keys[None, None, :], scores, -1e30)


def attend(pieces):
    queries, key_rows, value_rows, valid_keys = pieces
    scores = masked_scores(queries, key_rows, valid_keys)
    row_max = jnp.max(scores, axis=-1, keepdims=True)
    exponent = jnp.exp(scores - row_max)
    row_total = jnp.sum(exponent, axis=-1, keepdims=True)
    probability = (exponent / row_total).astype(jnp.bfloat16)
    context = jnp.einsum(
        "hqk,khd->qhd", probability, value_rows, preferred_element_type=jnp.float32
    )
    return (context.astype(jnp.bfloat16), row_max + jnp.log(row_total))


def attend_back(pieces):
    queries, key_rows, value_rows, valid_keys, upstream, logsum = pieces
    scores = masked_scores(queries, key_rows, valid_keys)
    probability = jnp.exp(scores - logsum)
    grad_values = jnp.einsum(
        "hqk,qhd->khd",
        probability.astype(jnp.bfloat16),
        upstream,
        preferred_element_type=jnp.float32,
    )
    grad_probs = jnp.einsum(
        "qhd,khd->hqk", upstream, value_rows, preferred_element_type=jnp.float32
    )
    row_delta = jnp.sum(probability * grad_probs, axis=-1, keepdims=True)
    grad_scores = (probability * (grad_probs - row_delta)).astype(jnp.bfloat16)
    grad_queries = jnp.einsum(
        "hqk,khd->qhd", grad_scores, key_rows, preferred_element_type=jnp.float32
    ) * HEAD_DIM ** (-0.5)
    grad_keys = jnp.einsum(
        "hqk,qhd->khd", grad_scores, queries, preferred_element_type=jnp.float32
    ) * HEAD_DIM ** (-0.5)
    return (
        grad_queries.astype(jnp.bfloat16),
        grad_keys.astype(jnp.bfloat16),
        grad_values.astype(jnp.bfloat16),
    )


def renew(master, moment, average, gradient, rates):
    velocity = MOMENTUM * moment + gradient
    updated = master - rates * (gradient + MOMENTUM * velocity)
    averaged = AVERAGE * average + (1.0 - AVERAGE) * updated
    return (velocity, updated, averaged, updated.astype(jnp.bfloat16))


def general_shards(
    tokens,
    alignment,
    segment_count,
    text_mask,
    cotangent,
    attention_master,
    attention_moment,
    attention_average,
    feedforward_master,
    feedforward_moment,
    feedforward_average,
    shared_master,
    shared_moment,
    shared_average,
    split_master,
    split_moment,
    split_average,
):
    documents, slot_count = alignment.shape
    text_rows = text_mask.shape[1]
    document_rows = text_rows + slot_count
    model_width = tokens.shape[1]
    local_width = split_master.shape[0]
    local_heads = local_width // HEAD_DIM
    row_count = documents * document_rows
    attention_full, feedforward_full, shared_full = (
        lax.all_gather(attention_master.astype(jnp.bfloat16), "dp", axis=0, tiled=True),
        lax.all_gather(feedforward_master.astype(jnp.bfloat16), "dp", axis=0, tiled=True),
        lax.all_gather(shared_master.astype(jnp.bfloat16), "dp", axis=0, tiled=True),
    )
    shared = shared_full.astype(jnp.float32)
    split_bias = lax.optimization_barrier(split_master.astype(jnp.bfloat16)).astype(jnp.float32)
    live_slots = (
        lax.broadcasted_iota(jnp.int32, (documents, slot_count), 1) < segment_count[:, None]
    )
    valid_keys = jnp.concatenate([text_mask > 0, live_slots], axis=1)
    text_index = lax.broadcasted_iota(jnp.int32, (documents, slot_count, text_rows), 2)
    pick_table = ((alignment[:, :, None] == text_index) & live_slots[:, :, None]).astype(
        jnp.bfloat16
    )
    inputs = tokens.reshape(documents, document_rows, model_width)
    taken_rows = jnp.einsum(
        "dst,dtw->dsw", pick_table, inputs[:, :text_rows], preferred_element_type=jnp.float32
    )
    layer_in = jnp.concatenate(
        [
            inputs[:, :text_rows].astype(jnp.float32),
            inputs[:, text_rows:].astype(jnp.float32) + taken_rows,
        ],
        axis=1,
    ).reshape(row_count, model_width)
    rows_in = layer_in.astype(jnp.bfloat16)
    project_weights = attention_full[:, :3].reshape(model_width, 3 * local_width)
    project_bias = jnp.concatenate(
        [split_bias[:, 0], jnp.zeros_like(split_bias[:, 0]), split_bias[:, 1]]
    )
    projected = (
        jnp.dot(rows_in, project_weights, preferred_element_type=jnp.float32) + project_bias
    ).astype(jnp.bfloat16)
    projected = projected.reshape(documents, document_rows, 3, local_heads, HEAD_DIM)
    queries = projected[:, :, 0]
    key_rows = projected[:, :, 1]
    value_rows = projected[:, :, 2]
    context, logsum = lax.map(attend, (queries, key_rows, value_rows, valid_keys))
    context_rows = context.reshape(row_count, local_width)
    joined = lax.psum(
        contract_last(context_rows, attention_full[:, 3]).astype(jnp.bfloat16), "mp"
    ).astype(jnp.float32)
    mixed = layer_in + joined + shared[:, 0]
    first_norm, normed_one, factor_one = layer_norm(mixed, shared[:, 1], shared[:, 2])
    hidden_in = first_norm.astype(jnp.bfloat16)
    inner_pre = jnp.dot(
        hidden_in, feedforward_full[:, 0], preferred_element_type=jnp.float32
    ) + split_bias[:, 2:].reshape(-1)
    active = jax.nn.gelu(inner_pre, approximate=False).astype(jnp.bfloat16)
    down_sum = lax.psum(
        contract_last(active, feedforward_full[:, 1]).astype(jnp.bfloat16), "mp"
    ).astype(jnp.float32)
    second = first_norm + down_sum + shared[:, 5]
    output, normed_two, factor_two = layer_norm(second, shared[:, 3], shared[:, 4])
    grad_second, grad_gain_two, grad_shift_two = norm_back(
        cotangent.astype(jnp.float32), normed_two, factor_two, shared[:, 3]
    )
    grad_down = grad_second.astype(jnp.bfloat16)
    grad_active = jnp.dot(grad_down, feedforward_full[:, 1], preferred_element_type=jnp.float32)
    gelu_value, gelu_pull = jax.vjp(partial(jax.nn.gelu, approximate=False), inner_pre)
    grad_inner = gelu_pull(grad_active)[0].astype(jnp.bfloat16)
    feedforward_grad = jnp.stack(
        [contract_rows(hidden_in, grad_inner), contract_rows(grad_down, active)], axis=1
    )
    grad_first = grad_second + lax.psum(
        contract_last(grad_inner, feedforward_full[:, 0]).astype(jnp.bfloat16), "mp"
    ).astype(jnp.float32)
    grad_mixed, grad_gain_one, grad_shift_one = norm_back(
        grad_first, normed_one, factor_one, shared[:, 1]
    )
    grad_joined = grad_mixed.astype(jnp.bfloat16)
    output_grad = contract_rows(grad_joined, context_rows)
    grad_context = jnp.dot(
        grad_joined, attention_full[:, 3], preferred_element_type=jnp.float32
    ).astype(jnp.bfloat16)
    upstream = grad_context.reshape(documents, document_rows, local_heads, HEAD_DIM)
    grad_queries, grad_keys, grad_values = lax.map(
        attend_back, (queries, key_rows, value_rows, valid_keys, upstream, logsum)
    )
    query_rows = grad_queries.reshape(row_count, local_width)
    value_grad_rows = grad_values.reshape(row_count, local_width)
    grad_project = jnp.concatenate(
        [query_rows, grad_keys.reshape(row_count, local_width), value_grad_rows], axis=1
    )
    project_grad = contract_rows(rows_in, grad_project).reshape(model_width, 3, local_width)
    attention_grad = jnp.concatenate([project_grad, output_grad[:, None, :]], axis=1)
    grad_layer_in = grad_mixed + lax.psum(
        contract_last(grad_project, project_weights).astype(jnp.bfloat16), "mp"
    ).astype(jnp.float32)
    shared_grad = jnp.stack(
        [
            jnp.sum(grad_mixed, axis=0),
            grad_gain_one,
            grad_shift_one,
            grad_gain_two,
            grad_shift_two,
            jnp.sum(grad_second, axis=0),
        ],
        axis=1,
    )
    split_grad = jnp.concatenate(
        [
            jnp.sum(query_rows, axis=0, dtype=jnp.float32)[:, None],
            jnp.sum(value_grad_rows, axis=0, dtype=jnp.float32)[:, None],
            jnp.sum(grad_inner, axis=0, dtype=jnp.float32).reshape(local_width, 4),
        ],
        axis=1,
    )
    grad_documents = grad_layer_in.reshape(documents, document_rows, model_width)
    moved_rows = jnp.einsum(
        "dst,dsw->dtw",
        pick_table.astype(jnp.float32),
        grad_documents[:, text_rows:],
        precision=HIGHEST_MODE,
        preferred_element_type=jnp.float32,
    )
    input_gradient = jnp.concatenate(
        [grad_documents[:, :text_rows] + moved_rows, grad_documents[:, text_rows:]], axis=1
    ).reshape(row_count, model_width)
    attention_sum, feedforward_sum, shared_sum = (
        lax.psum_scatter(attention_grad, "dp", scatter_dimension=0, tiled=True),
        lax.psum_scatter(feedforward_grad, "dp", scatter_dimension=0, tiled=True),
        lax.psum_scatter(shared_grad, "dp", scatter_dimension=0, tiled=True),
    )
    split_sum = lax.psum(split_grad, "dp")
    attention_new = renew(
        attention_master,
        attention_moment,
        attention_average,
        attention_sum,
        jnp.asarray(ATTENTION_RATES, jnp.float32).reshape(1, 4, 1),
    )
    feedforward_new = renew(
        feedforward_master,
        feedforward_moment,
        feedforward_average,
        feedforward_sum,
        jnp.asarray(FEEDFORWARD_RATES, jnp.float32).reshape(1, 2, 1),
    )
    shared_new = renew(shared_master, shared_moment, shared_average, shared_sum, SHARED_RATE)
    split_new = renew(
        split_master,
        split_moment,
        split_average,
        split_sum,
        jnp.asarray(SPLIT_RATES, jnp.float32).reshape(1, 6),
    )
    return (
        output.astype(jnp.bfloat16),
        input_gradient,
        attention_new[0],
        attention_new[1],
        attention_new[2],
        attention_new[3],
        feedforward_new[0],
        feedforward_new[1],
        feedforward_new[2],
        feedforward_new[3],
        shared_new[0],
        shared_new[1],
        shared_new[2],
        shared_new[3],
        split_new[0],
        split_new[1],
        split_new[2],
        split_new[3],
    )


LOW = jnp.bfloat16
WIDE = jnp.float32
UNITS = [(0, 0), (1, 0), (2, 0), (0, 1), (0, 2), (0, 3)] + [(t, k) for k in range(1, 4) for t in (1, 2)]
AXES = (0, 1, 0, 1, 0, 1, 0, 0, 0, 1, 0, 1)
LINE = 4
BACK_UNITS = [(t, k) for k in range(4) for t in (2, 1)] + [(0, k) for k in range(4)]
PIECES = 8
SENDS = 3
PAIRS = 4


def place():
    dp, z = lax.axis_index("dp"), lax.axis_index("mp")
    return z, lax.div(dp, 4), lax.rem(lax.div(dp, 2), 2), lax.rem(dp, 2)


def device(z, y, x, c):
    return (y * 4 + x * 2 + c, z)


def document_of(z):
    return lax.div(z + 1, 2)


def nearest_level(z, k):
    low, high = lax.rem(z, 2), lax.div(z, 2)
    if k == 0:
        return z
    if k == 1:
        return 1 + (2 * high - 1) * low
    if k == 2:
        return 2 + high * (1 - 2 * low)
    return 3 - 3 * high


def greet(z, y, x, c):
    barrier = pltpu.get_barrier_semaphore()
    partners = [device(z, y, x, 1 - c), device(z, y, 1 - x, c), device(z, 1 - y, x, c)]
    partners += [device(lax.rem(z + k, 4), y, x, c) for k in (1, 2, 3)]
    for partner in partners:
        pl.semaphore_signal(barrier, inc=1, device_id=partner, device_id_type=MESH)
    pl.semaphore_wait(barrier, len(partners))


def remote(source, target, send, recv, to):
    return pltpu.make_async_remote_copy(
        src_ref=source, dst_ref=target, send_sem=send, recv_sem=recv, device_id=to, device_id_type=MESH
    )


def when(condition, action):
    pl.when(condition)(action)


def mul(left, right):
    return jnp.dot(left, right, preferred_element_type=WIDE)


def gelu_parts(value):
    root = value * 0.7071067811865476
    inverse = 1.0 / (1.0 + 0.3275911 * jnp.abs(root))
    bell = jnp.exp(-root * root)
    series = 1.061405429
    for factor in (-1.453152027, 1.421413741, -0.284496736, 0.254829592):
        series = series * inverse + factor
    tail = 0.5 * series * inverse * bell
    share = jnp.where(value >= 0, 1.0 - tail, tail)
    return value * share, share + value * (bell * 0.3989422804014327)


def head_mask(head, scale, lanes=192):
    lane = lax.broadcasted_iota(jnp.int32, (1, lanes), 1)
    return jnp.where((lane >= head * HEAD_DIM) & (lane < (head + 1) * HEAD_DIM), scale, 0.0).astype(LOW)


def unit_weight(r, t, level):
    return r.full[t, level].reshape(768, 768)


class Gather:
    def __init__(self, r):
        self.own, self.small, self.r = r.own, r.small, r
        self.z, self.y, self.x, self.c = z, y, x, c = place()
        self.up, self.down = device(z + 1, y, x, c), device(z - 1, y, x, c)
        self.across_x, self.across_y = device(z, y, 1 - x, c), device(z, 1 - y, x, c)
        self.pair = device(z, y, x, 1 - c)
        self.end = (z == 0) | (z == LINE - 1)

    def line_copy(self, t, level, source, way):
        r = self.r
        return remote(
            source, r.full.at[t, level, self.y, self.x, self.c], r.line_send.at[t, level, way],
            r.line_recv.at[t, level], self.up if way == 0 else self.down,
        )

    def along_x(self, u):
        return AXES[u] == 0

    def first(self, u):
        t, k = UNITS[u]
        block = self.r.full.at[t, nearest_level(self.z, k), self.y, self.x, self.c]
        return remote(
            self.own.at[t] if k == 0 else block, block, self.r.first_send.at[u], self.r.first_recv.at[u],
            self.across_x if self.along_x(u) else self.across_y,
        )

    def second(self, u):
        t, k = UNITS[u]
        level = nearest_level(self.z, k)
        if self.along_x(u):
            block, to = self.r.full.at[t, level, self.y, :, self.c], self.across_y
        else:
            block, to = self.r.full.at[t, level, :, self.x, self.c], self.across_x
        return remote(block, block, self.r.second_send.at[u], self.r.second_recv.at[u], to)

    def extra(self, u, level, part, way):
        t, y, x, c = UNITS[u][0], self.y, self.x, self.c
        if self.along_x(u):
            index = (t, level, y, 1 - x, c) if part == 0 else (t, level, 1 - y, slice(None), c)
        else:
            index = (t, level, 1 - y, x, c) if part == 0 else (t, level, slice(None), 1 - x, c)
        block = self.r.full.at[index]
        return remote(
            block, block, self.r.extra_send.at[t - 1, part, way], self.r.extra_recv.at[t - 1, level, part],
            self.up if way == 0 else self.down,
        )

    def paired(self, u):
        t, k = UNITS[u]
        block = self.r.full.at[t, nearest_level(self.z, k), :, :, self.c]
        return remote(block, block, self.r.pair_send.at[u], self.r.pair_recv.at[u], self.pair)

    def own_copy(self, t):
        return pltpu.make_async_copy(
            self.own.at[t], self.r.full.at[t, self.z, self.y, self.x, self.c], self.r.own_sem.at[t]
        )

    def tiny_own(self, i):
        target = self.r.plane.at[self.y, self.x, self.c] if i == 0 else self.r.line.at[self.z]
        return pltpu.make_async_copy(self.small, target, self.r.own_sem.at[3 + i])

    def tiny(self, i):
        r = self.r
        if i == 0:
            block, to = r.plane.at[self.y, self.x, self.c], self.across_x
        elif i == 1:
            block, to = r.plane.at[self.y, :, self.c], self.across_y
        elif i == 2:
            block, to = r.plane.at[:, :, self.c], self.pair
        else:
            block, to = r.line.at[self.z], device(lax.rem(self.z + i - 2, 4), self.y, self.x, self.c)
        source = self.small if i == 0 or i > 2 else block
        return remote(source, block, r.tiny_send.at[i], r.tiny_recv.at[i], to)

    def own_line(self, t, act):
        when(self.z < 3, lambda: act(self.line_copy(t, self.z, self.own.at[t], 0)))
        when(self.z > 0, lambda: act(self.line_copy(t, self.z, self.own.at[t], 1)))

    def own_extra(self, u, part, act):
        when(self.z < 3, lambda: act(self.extra(u, self.z, part, 0)))
        when(self.z > 0, lambda: act(self.extra(u, self.z, part, 1)))

    def begin(self):
        self.own_line(0, lambda copy: copy.start())
        for t in range(3):
            self.own_copy(t).start()

    def begin_tiny(self):
        for i in range(2):
            self.tiny_own(i).start()
        for i in (0, 3, 4, 5):
            self.tiny(i).start()

    def crosses(self, u, act):
        t, k = UNITS[u]
        if t == 0 or k in (0, 3):
            act()
        elif k == 2:
            when(self.end, act)

    def comes_whole(self, u, act):
        t, k = UNITS[u]
        if t > 0 and k == 1:
            act()
        elif t > 0 and k == 2:
            when(jnp.logical_not(self.end), act)

    def arrive(self, u):
        t, k = UNITS[u]
        if k == 0 and t > 0:
            self.own_line(t, lambda copy: copy.start())
        if k > 0:
            level = nearest_level(self.z, k)
            block = self.r.full.at[t, level, self.y, self.x, self.c]
            self.line_copy(t, level, block, 0).wait_recv()
            when((level < self.z) & (self.z < 3), lambda: self.line_copy(t, level, block, 0).start())
            when((level > self.z) & (self.z > 0), lambda: self.line_copy(t, level, block, 1).start())
        self.crosses(u, lambda: self.first(u).start())

    def cross(self, u):
        t, k = UNITS[u]

        def act():
            self.first(u).wait_recv()
            if k == 0:
                self.own_copy(t).wait()
            self.second(u).start()
            if t > 0 and k == 0:
                self.own_extra(u, 0, lambda copy: copy.start())

        self.crosses(u, act)

    def share(self, u):
        t, k = UNITS[u]
        level = nearest_level(self.z, k)

        def act():
            self.second(u).wait_recv()
            if t > 0 and k == 0:
                self.own_extra(u, 1, lambda copy: copy.start())
            self.paired(u).start()

        def act_whole():
            own = UNITS.index((t, 0))
            for part in range(2):
                self.extra(own, level, part, 0).wait_recv()
            self.paired(u).start()

        self.crosses(u, act)
        self.comes_whole(u, act_whole)

    def take(self, u):
        self.paired(u).wait_recv()

    def tiny_step(self, i):
        if i == 0:
            for j in range(2):
                self.tiny_own(j).wait()
        if i < 3:
            self.tiny(i).wait_recv()
        if i < 2:
            self.tiny(i + 1).start()
        if i == 3:
            for j in (3, 4, 5):
                self.tiny(j).wait_recv()

    def finish(self):
        z = self.z
        for i in range(6):
            self.tiny(i).wait_send()
        for u, (t, k) in enumerate(UNITS):
            level = nearest_level(z, k)
            block = self.r.full.at[t, level, self.y, self.x, self.c]
            if k == 0:
                self.own_line(t, lambda copy: copy.wait_send())
                if t > 0:
                    for part in range(2):
                        self.own_extra(u, part, lambda copy: copy.wait_send())
            else:
                when((level < z) & (z < 3), lambda t=t, v=level, b=block: self.line_copy(t, v, b, 0).wait_send())
                when((level > z) & (z > 0), lambda t=t, v=level, b=block: self.line_copy(t, v, b, 1).wait_send())

            def both(u=u):
                self.first(u).wait_send()
                self.second(u).wait_send()

            self.crosses(u, both)
            self.paired(u).wait_send()


class Reduce:
    def __init__(self, att_sum, ff_sum, r):
        self.att_sum, self.ff_sum, self.r = att_sum, ff_sum, r
        self.z, self.y, self.x, self.c = z, y, x, c = place()
        self.up, self.down = device(z + 1, y, x, c), device(z - 1, y, x, c)
        self.across_x, self.across_y = device(z, y, 1 - x, c), device(z, 1 - y, x, c)
        self.pair = device(z, y, x, 1 - c)

    def pair_copy(self, u):
        r = self.r
        return remote(
            r.sends.at[u % SENDS], r.pair_in.at[u % PAIRS], r.r_pair_send.at[u], r.r_pair_recv.at[u], self.pair
        )

    def first_copy(self, u):
        r = self.r
        source = r.total.at[u, :, 1 - self.x] if u % 2 == 0 else r.total.at[u, 1 - self.y]
        return remote(
            source, r.first_in.at[u], r.r_first_send.at[u], r.r_first_recv.at[u],
            self.across_x if u % 2 == 0 else self.across_y,
        )

    def second_copy(self, u):
        r, x, y = self.r, self.x, self.y
        return remote(
            r.total.at[u, 1 - y, x] if u % 2 == 0 else r.total.at[u, y, 1 - x],
            r.second_in.at[u], r.r_second_send.at[u], r.r_second_recv.at[u],
            self.across_y if u % 2 == 0 else self.across_x,
        )

    def line_copy(self, u, way):
        r = self.r
        t, k = BACK_UNITS[u]
        level = nearest_level(self.z, 3 - k)
        return remote(
            r.total.at[u, self.y, self.x], r.line_in.at[t, level + 1 - way], r.r_line_send.at[t, level],
            r.r_line_recv.at[t, level, way], self.up if way == 0 else self.down,
        )

    def produce(self, u, parts):
        r = self.r
        if u >= SENDS:
            self.pair_copy(u - SENDS).wait_send()
        for half, target in ((1 - self.c, r.sends.at[u % SENDS]), (self.c, r.total.at[u])):
            for products, lanes in parts:
                value = sum(mul(turned[:, :, half].reshape(384, 512), columns) for turned, columns in products)
                target[:, :, :, lanes] = value.astype(LOW).reshape(2, 2, 96, value.shape[1])
            if half is not self.c:
                self.pair_copy(u).start()

    def add_pair(self, u):
        r = self.r
        self.pair_copy(u).wait_recv()
        r.total[u] = r.total[u] + r.pair_in[u % PAIRS]
        self.first_copy(u).start()

    def add_first(self, u):
        r, x, y = self.r, self.x, self.y
        self.first_copy(u).wait_recv()
        if u % 2 == 0:
            r.total[u, :, x] = r.total[u, :, x] + r.first_in[u]
        else:
            r.total[u, y] = r.total[u, y] + r.first_in[u]
        self.second_copy(u).start()

    def add_second(self, u):
        r, x, y, z = self.r, self.x, self.y, self.z
        t, k = BACK_UNITS[u]
        level = nearest_level(z, 3 - k)
        self.second_copy(u).wait_recv()
        r.total[u, y, x] = r.total[u, y, x] + r.second_in[u]
        if k < 3:
            when((z == 0) | (z == 3), lambda: self.send_line(u))

    def send_line(self, u):
        level = nearest_level(self.z, 3 - BACK_UNITS[u][1])
        when(self.z < level, lambda: self.line_copy(u, 0).start())
        when(self.z > level, lambda: self.line_copy(u, 1).start())

    def take_line(self, u, way):
        r, x, y = self.r, self.x, self.y
        t, k = BACK_UNITS[u]
        level = nearest_level(self.z, 3 - k)
        self.line_copy(u, way).wait_recv()
        r.total[u, y, x] = r.total[u, y, x] + r.line_in[t, level + 1 - way]

    def add_line(self, u):
        r, z = self.r, self.z
        t, k = BACK_UNITS[u]
        level = nearest_level(z, 3 - k)
        middle = (z == 1) | (z == 2)
        if k < 3:
            when(middle & (z < level), lambda: self.take_line(u, 0))
            when(middle & (z > level), lambda: self.take_line(u, 1))
            when(middle, lambda: self.send_line(u))
        else:
            when(z > 0, lambda: self.take_line(u, 0))
            when(z < 3, lambda: self.take_line(u, 1))
            self.give(t, r.total[u, self.y, self.x])

    def give(self, t, value):
        if t == 0:
            for slab in range(4):
                self.att_sum[:, slab, :] = value[:, slab * 192 : (slab + 1) * 192].astype(WIDE)
        else:
            self.ff_sum[:, t - 1, :] = value.astype(WIDE)

    def small_copy(self, i):
        r = self.r
        if i < 3:
            to = (self.pair, self.across_x, self.across_y)[i]
            return remote(r.small_total.at[i], r.small_in.at[i], r.small_send.at[i], r.small_recv.at[i], to)
        to = device(lax.rem(self.z + i - 2, 4), self.y, self.x, self.c)
        return remote(r.small_total.at[3], r.small_line.at[self.z], r.small_send.at[i], r.small_recv.at[i], to)

    def small_step(self, i):
        r = self.r
        self.small_copy(i).wait_recv()
        r.small_total[i + 1] = r.small_total[i] + r.small_in[i]
        if i < 2:
            self.small_copy(i + 1).start()
        else:
            for j in (3, 4, 5):
                self.small_copy(j).start()
            r.small_line[self.z] = r.small_total[3]

    def small_end(self, shared_sum, split_sum):
        r, z = self.r, self.z
        for i in (3, 4, 5):
            self.small_copy(i).wait_recv()
        r.small_sum[...] = r.small_line[0] + r.small_line[1] + r.small_line[2] + r.small_line[3]
        index = self.y * 4 + self.x * 2 + self.c
        shared_sum[...] = pltpu.roll(r.small_sum[:8], lax.rem(768 - index * 96, 768), 1)[:6, :96]
        biases = r.small_sum[pl.ds(8 + z, 1)]
        split_sum[0:1] = biases[:, :192]
        split_sum[1:2] = biases[:, 384:576]
        inner = r.small_sum[pl.ds(12 + z, 1)]
        for j in range(4):
            split_sum[2 + j : 3 + j] = inner[:, j * 192 : (j + 1) * 192]

    def finish(self):
        z = self.z
        for i in range(6):
            self.small_copy(i).wait_send()
        for u, (t, k) in enumerate(BACK_UNITS):
            if u >= len(BACK_UNITS) - SENDS:
                self.pair_copy(u).wait_send()
            self.first_copy(u).wait_send()
            self.second_copy(u).wait_send()
            if k < 3:
                level = nearest_level(z, 3 - k)
                when(z < level, lambda u=u: self.line_copy(u, 0).wait_send())
                when(z > level, lambda u=u: self.line_copy(u, 1).wait_send())


class Cast:
    def __init__(self, a, source, target, r):
        self.a, self.source, self.target, self.r = a, source, target, r
        self.z, y, x, c = place()
        self.up, self.down = device(self.z + 1, y, x, c), device(self.z - 1, y, x, c)

    def copy(self, d, p, way, first):
        r = self.r
        part = pl.ds(p * (512 // PIECES), 512 // PIECES)
        target = self.target.at[d, part]
        return remote(
            self.source.at[part] if first else target, target, r.cast_send.at[self.a, d, p, way],
            r.cast_recv.at[self.a, d, p], self.up if way == 0 else self.down,
        )

    def own(self):
        return pltpu.make_async_copy(self.source, self.target.at[document_of(self.z)], self.r.cast_own.at[self.a])

    def firsts(self, p, act):
        for level, d, way in ((0, 0, 0), (1, 1, 1), (2, 1, 0), (3, 2, 1)):
            when(self.z == level, lambda d=d, way=way: act(self.copy(d, p, way, True)))

    def begin(self):
        self.own().start()
        for p in range(PIECES):
            self.firsts(p, lambda copy: copy.start())

    def pass_on(self, d, p, way):
        copy = self.copy(d, p, way, False)
        copy.wait_recv()
        copy.start()

    def near(self, p):
        when(self.z == 1, lambda: self.pass_on(0, p, 0))
        when(self.z == 2, lambda: self.pass_on(2, p, 1))

    def far(self, p):
        when(self.z == 1, lambda: self.pass_on(2, p, 1))
        when(self.z == 2, lambda: self.pass_on(0, p, 0))

    def finish(self):
        self.own().wait()
        for p in range(PIECES):
            self.firsts(p, lambda copy: copy.wait_send())
            for level in (1, 2):
                when(self.z == level, lambda p=p: self.copy(0, p, 0, False).wait_send())
                when(self.z == level, lambda p=p: self.copy(2, p, 1, False).wait_send())
            for level, d, way in ((0, 1, 1), (0, 2, 1), (3, 1, 0), (3, 0, 0)):
                when(self.z == level, lambda p=p, d=d, way=way: self.copy(d, p, way, False).wait_recv())


def buffers():
    vmem = pltpu.VMEM
    return dict(
        full=vmem((3, 4, 2, 2, 2, 96, 768), LOW),
        plane=vmem((2, 2, 2, 16, 768), LOW),
        line=vmem((4, 16, 768), LOW),
        tok=vmem((512, 768), LOW),
        cot=vmem((512, 768), LOW),
        pick=vmem((384, 128), LOW),
        rows_in=vmem((512, 768), LOW),
        hidden_in=vmem((512, 768), LOW),
        rows_t=vmem((2, 2, 2, 96, 512), LOW),
        hidden_t=vmem((2, 2, 2, 96, 512), LOW),
        down_t=vmem((2, 2, 2, 96, 512), LOW),
        qkv=vmem((4, 512, 640), LOW),
        probs=vmem((2, 3, 512, 512), LOW),
        context=vmem((4, 512, 256), LOW),
        active=vmem((4, 512, 768), LOW),
        slope=vmem((4, 512, 768), LOW),
        mixed=vmem((512, 768), WIDE),
        normed_one=vmem((512, 768), WIDE),
        factor_one=vmem((512, 1), WIDE),
        total=vmem((12, 2, 2, 96, 768), LOW),
        sends=vmem((SENDS, 2, 2, 96, 768), LOW),
        pair_in=vmem((PAIRS, 2, 2, 96, 768), LOW),
        first_in=vmem((12, 2, 96, 768), LOW),
        second_in=vmem((12, 96, 768), LOW),
        line_in=vmem((3, 5, 96, 768), LOW),
        small_total=vmem((4, 16, 768), WIDE),
        small_in=vmem((3, 16, 768), WIDE),
        small_line=vmem((4, 16, 768), WIDE),
        small_sum=vmem((16, 768), WIDE),
        own=vmem((3, 96, 768), LOW),
        small=vmem((16, 768), LOW),
    )


def flags():
    dma = pltpu.SemaphoreType.DMA
    return dict(
        line_send=dma((3, 4, 2)),
        line_recv=dma((3, 4)),
        first_send=dma((12,)),
        first_recv=dma((12,)),
        second_send=dma((12,)),
        second_recv=dma((12,)),
        pair_send=dma((12,)),
        pair_recv=dma((12,)),
        tiny_send=dma((6,)),
        tiny_recv=dma((6,)),
        extra_send=dma((2, 2, 2)),
        extra_recv=dma((2, 4, 2)),
        own_sem=dma((5,)),
        load_sem=dma((6,)),
        r_pair_send=dma((12,)),
        r_pair_recv=dma((12,)),
        r_first_send=dma((12,)),
        r_first_recv=dma((12,)),
        r_second_send=dma((12,)),
        r_second_recv=dma((12,)),
        r_line_send=dma((3, 4)),
        r_line_recv=dma((3, 4, 2)),
        small_send=dma((6,)),
        small_recv=dma((6,)),
        cast_send=dma((2, 3, PIECES, 2)),
        cast_recv=dma((2, 3, PIECES)),
        cast_own=dma((2,)),
    )


def spread(j):
    unit = lax.broadcasted_iota(jnp.int32, (192, 768), 1)
    return jnp.where(unit == 4 * lax.broadcasted_iota(jnp.int32, (192, 768), 0) + j, 1.0, 0.0).astype(LOW)


def turn(value, counts):
    return (value * counts.astype(LOW)).T.reshape(2, 2, 2, 96, 512)


def layer_kernel(
    att_ref, ff_ref, shared_ref, split_ref, tokens_ref, cotangent_ref, align_ref, count_ref, mask_ref,
    att_sum, ff_sum, shared_sum, split_sum, text_all, back_all, probs_out, *refs,
):
    r = SimpleNamespace(**dict(zip([*buffers(), *flags()], refs)))
    z, y, x, c = place()
    doc = document_of(z)
    counts = jnp.where(z == 2, 0.0, 1.0)
    tok_copy = pltpu.make_async_copy(tokens_ref.at[pl.ds(doc * 512, 512)], r.tok, r.load_sem.at[0])
    cot_copy = pltpu.make_async_copy(cotangent_ref.at[pl.ds(doc * 512, 512)], r.cot, r.load_sem.at[1])
    tok_copy.start()
    cot_copy.start()
    for slab in range(4):
        r.own[0, :, slab * 192 : (slab + 1) * 192] = att_ref[:, slab, :].astype(LOW)
    for t in (1, 2):
        r.own[t] = ff_ref[:, t - 1, :].astype(LOW)
    greet(z, y, x, c)
    net = Gather(r)
    net.begin()
    held = SimpleNamespace()

    def small_start():
        r.small_sum[...] = jnp.zeros((16, 768), WIDE)
        r.small_sum[:6, :96] = shared_ref[...]
        shared = pltpu.roll(r.small_sum[:8], (y * 4 + x * 2 + c) * 96, 1)
        r.small_sum[8:14, :192] = split_ref[...]
        units = r.small_sum[8:16, :192].astype(LOW)
        inner = sum(mul(units, spread(j))[2 + j : 3 + j] for j in range(4))
        r.small_sum[:8] = shared
        r.small_sum[6:7] = jnp.zeros((1, 768), WIDE)
        r.small_sum[6:7, :192] = split_ref[0:1]
        r.small_sum[6:7, 384:576] = split_ref[1:2]
        r.small_sum[7:8] = inner
        r.small[...] = r.small_sum[...].astype(LOW)
        net.begin_tiny()

    def small_ready():
        value = r.small_total[0, 8:16]
        high = value.astype(LOW)
        rest = value - high.astype(WIDE)
        middle = rest.astype(LOW)
        last = (rest - middle.astype(WIDE)).astype(LOW)
        for j in range(4):
            packed = sum(contract_last(piece, spread(j)) for piece in (last, middle, high))
            r.small_total[0, 12:16, j * 192 : (j + 1) * 192] = packed[4:8]
        r.small_total[0] = r.small_total[0] * counts
        red.small_copy(0).start()

    def prologue():
        tok_copy.wait()
        live = lax.broadcasted_iota(jnp.int32, (1, 128), 1) < count_ref[doc]
        pick = jnp.where(
            (lax.broadcasted_iota(jnp.int32, (384, 128), 0) == align_ref[pl.ds(doc, 1), :]) & live, 1.0, 0.0
        ).astype(LOW)
        r.pick[...] = pick
        text_tokens = r.tok[:384]
        taken = lax.dot_general(pick, text_tokens, (((0,), (0,)), ((), ())), preferred_element_type=WIDE)
        slot_rows = r.tok[384:].astype(WIDE) + taken
        r.mixed[:384] = text_tokens.astype(WIDE)
        r.mixed[384:] = slot_rows
        r.rows_in[:384] = text_tokens
        r.rows_in[384:] = slot_rows.astype(LOW)
        r.rows_t[...] = turn(r.rows_in[...], counts)
        valid = jnp.concatenate([mask_ref[pl.ds(doc, 1), :] > 0, live], axis=1)
        held.bar = jnp.where(valid, 0.0, -1e30)

    def spill(k):
        return pltpu.make_async_copy(r.probs.at[k % 2], probs_out.at[k % 2], r.load_sem.at[2 + k % 2])

    def attention(k):
        level = nearest_level(z, k)
        weight = unit_weight(r, 0, level)
        bias = r.line[level][6:7].astype(WIDE)
        projected = (mul(r.rows_in[...], weight[...]) + bias).astype(LOW)
        r.qkv[k] = projected[:, :640]
        queries, keys, values = projected[:, :192], projected[:, 192:384], projected[:, 384:640]
        if k >= 2:
            spill(k).wait()
        context = jnp.zeros((512, 256), WIDE)
        for head in range(3):
            scores = contract_last(queries * head_mask(head, 0.125), keys)
            scores = jnp.where(held.bar < 0.0, -1e30, scores)
            raised = jnp.exp(scores - jnp.max(scores, axis=-1, keepdims=True))
            probs = (raised * (1.0 / jnp.sum(raised, axis=-1, keepdims=True))).astype(LOW)
            r.probs[k % 2, head] = probs
            context = context + mul(probs, values * head_mask(head, 1.0, 256))
        context = pltpu.roll(context, 64, 1).astype(LOW)
        r.context[level] = context
        if k < 2:
            spill(k).start()

    def first_norm():
        for level in range(4):
            r.mixed[...] += contract_last(r.context[level], unit_weight(r, 0, level)[:, 512:])
        held.shared = shared = jnp.sum(r.plane[...].astype(WIDE).reshape(8, 16, 768), axis=0)
        mixed = r.mixed[...] + shared[0:1]
        first_norm, normed, factor = layer_norm(mixed, shared[1:2], shared[2:3])
        r.normed_one[...] = normed
        r.factor_one[...] = factor
        r.hidden_in[...] = first_norm.astype(LOW)
        r.hidden_t[...] = turn(first_norm.astype(LOW), counts)
        r.mixed[...] = first_norm + shared[5:6]

    def feed(k):
        level = nearest_level(z, k)
        bias = r.line[level][7:8, :].astype(WIDE)
        up = unit_weight(r, 1, level)
        for part in range(3):
            lanes = slice(part * 256, (part + 1) * 256)
            inner = mul(r.hidden_in[...], up[:, lanes]) + bias[:, lanes]
            active, slope = gelu_parts(inner)
            r.active[level, :, lanes] = active.astype(LOW)
            r.slope[level, :, lanes] = slope.astype(LOW)

    def feed_sum():
        for level in range(4):
            r.mixed[...] += contract_last(r.active[level], unit_weight(r, 2, level))

    text_cast = Cast(0, r.tok, text_all, r)
    back_cast = Cast(1, r.cot, back_all, r)
    red = Reduce(att_sum, ff_sum, r)

    def second_norm():
        shared = held.shared
        final, normed, factor = layer_norm(r.mixed[...], shared[3:4], shared[4:5])
        r.tok[...] = final.astype(LOW)
        text_cast.begin()
        cot_copy.wait()
        incoming = r.cot[...].astype(WIDE)
        grad, gain, shift = norm_back(incoming, normed, factor, shared[3:4])
        r.mixed[...] = grad
        low = grad.astype(LOW)
        r.rows_in[...] = low
        r.down_t[...] = turn(low, counts)
        r.small_total[0] = jnp.zeros((16, 768), WIDE)
        r.small_total[0, 3:4] = gain[None]
        r.small_total[0, 4:5] = shift[None]
        r.small_total[0, 5:6] = jnp.sum(grad, axis=0, keepdims=True)

    def feed_back(k):
        level = nearest_level(z, 3 - k)
        grad = mul(r.rows_in[...], unit_weight(r, 2, level)) * r.slope[level].astype(WIDE)
        r.slope[level] = grad.astype(LOW)
        r.small_total[0, pl.ds(12 + level, 1)] = jnp.sum(grad.astype(LOW).astype(WIDE), axis=0, keepdims=True)
        red.produce(2 * k, [([(r.down_t, r.active[level])], slice(0, 768))])

    def feed_back_up(k):
        level = nearest_level(z, 3 - k)
        red.produce(2 * k + 1, [([(r.hidden_t, r.slope[level])], slice(0, 768))])

    def first_norm_back():
        for level in range(4):
            r.mixed[...] += contract_last(r.slope[level], unit_weight(r, 1, level))
        grad, gain, shift = norm_back(r.mixed[...], r.normed_one[...], r.factor_one[...], held.shared[1:2])
        r.mixed[...] = grad
        low = grad.astype(LOW)
        r.hidden_in[...] = low
        r.hidden_t[...] = turn(low, counts)
        r.small_total[0, 0:1] = jnp.sum(grad, axis=0, keepdims=True)
        r.small_total[0, 1:2] = gain[None]
        r.small_total[0, 2:3] = shift[None]

    def reload(k):
        return pltpu.make_async_copy(probs_out.at[k], r.probs.at[k], r.load_sem.at[4 + k])

    def attention_back(k):
        slot = 3 - k
        level = nearest_level(z, slot)
        projected = r.qkv[slot]
        queries, keys, values = projected[:, :192], projected[:, 192:384], projected[:, 384:576]
        upstream = mul(r.hidden_in[...], unit_weight(r, 0, level)[:, 512:])[:, 64:].astype(LOW)
        if slot < 2:
            reload(slot).wait()
        grad_q = grad_k = grad_v = jnp.zeros((512, 192), WIDE)
        for head in range(3):
            probs = r.probs[slot % 2, head]
            up = upstream * head_mask(head, 1.0)
            grad_v = grad_v + contract_rows(probs, up)
            grad_probs = contract_last(up, values)
            wide = probs.astype(WIDE)
            weighed = wide * grad_probs
            grad_scores = (weighed - wide * jnp.sum(weighed, axis=-1, keepdims=True)).astype(LOW)
            grad_q = grad_q + mul(grad_scores, keys * head_mask(head, 0.125))
            grad_k = grad_k + contract_rows(grad_scores, queries * head_mask(head, 0.125))
        if slot >= 2:
            reload(slot - 2).start()
        r.active[level, :, :192] = grad_q.astype(LOW)
        r.active[level, :, 192:384] = grad_k.astype(LOW)
        r.active[level, :, 384:576] = grad_v.astype(LOW)
        r.active[level, :, 576:] = jnp.zeros((512, 192), LOW)
        r.small_total[0, pl.ds(8 + level, 1)] = jnp.sum(r.active[level].astype(WIDE), axis=0, keepdims=True)

    def project_back(k):
        slot = 3 - k
        level = nearest_level(z, slot)
        red.produce(
            8 + k,
            [
                ([(r.rows_t, r.active[level, :, :512])], slice(0, 512)),
                ([(r.rows_t, r.active[level, :, 512:]), (r.hidden_t, r.context[level])], slice(512, 768)),
            ],
        )

    def input_back():
        for level in range(4):
            r.mixed[...] += contract_last(r.active[level], unit_weight(r, 0, level))
        grad = r.mixed[...]
        r.cot[:384] = (grad[:384] + mul(r.pick[...], grad[384:].astype(LOW))).astype(LOW)
        r.cot[384:] = grad[384:].astype(LOW)
        back_cast.begin()

    steps = program_steps(net, red, text_cast, back_cast, (shared_sum, split_sum), [
        small_start, small_ready, prologue, attention, first_norm, feed, feed_sum, second_norm, feed_back, feed_back_up, first_norm_back,
        attention_back, project_back, input_back,
    ])
    for i in ORDER:
        steps[i][0]()
    net.finish()
    text_cast.finish()
    back_cast.finish()
    red.finish()


def program_steps(net, red, text_cast, back_cast, small_sums, work):
    steps = []

    def add(action, *after):
        steps.append((action, after))
        return len(steps) - 1

    (small_start, small_ready, prologue, attention, first_norm, feed, feed_sum, second_norm, feed_back, feed_back_up, first_norm_back,
     attention_back, project_back, input_back) = work
    taken = {}
    for u, unit in enumerate(UNITS):
        step = add(partial(net.arrive, u))
        step = add(partial(net.cross, u), step)
        step = add(partial(net.share, u), step)
        taken[unit] = add(partial(net.take, u), step)
    step = add(small_start)
    tiny = [add(partial(net.tiny_step, 0), step)]
    for i in (1, 2, 3):
        tiny.append(add(partial(net.tiny_step, i), tiny[-1]))
    step = add(prologue)
    for k in range(4):
        step = add(partial(attention, k), step, taken[0, k], tiny[3])
    step = add(first_norm, step, tiny[2])
    for k in range(4):
        step = add(partial(feed, k), step, taken[1, k])
    step = add(feed_sum, step, *[taken[2, k] for k in range(4)])
    step = started = add(second_norm, step)
    made, joined = {}, {}

    def make(u, action, before):
        ahead = [joined[u - 2]] if u >= 2 else []
        made[u] = add(action, before, *ahead)
        joined[u] = add(partial(red.add_pair, u), made[u])
        return made[u]

    for k in range(4):
        step = make(2 * k, partial(feed_back, k), step)
        step = make(2 * k + 1, partial(feed_back_up, k), step)
    step = add(first_norm_back, step)
    for k in range(4):
        step = add(partial(attention_back, k), step)
        step = make(8 + k, partial(project_back, k), step)
    step = ended = add(input_back, step)
    for u in range(12):
        step = add(partial(red.add_first, u), joined[u])
        step = add(partial(red.add_second, u), step)
        add(partial(red.add_line, u), step)
    for cast, begun in ((text_cast, started), (back_cast, ended)):
        for p in range(PIECES):
            add(partial(cast.near, p), begun)
            add(partial(cast.far, p), begun)
    step = add(small_ready, ended)
    for i in range(3):
        step = add(partial(red.small_step, i), step)
    add(partial(red.small_end, *small_sums), step)
    return steps


ORDER = (
    0, 8, 4, 53, 12, 48, 1, 13, 16, 49, 36, 28, 20, 5, 2, 24, 50, 17, 51, 21, 32, 52, 3, 54, 44, 14, 40, 6, 29, 9,
    18, 15, 55, 22, 45, 7, 37, 19, 33, 56, 23, 41, 25, 10, 57, 26, 58, 46, 34, 27, 59, 60, 42, 47, 38, 35, 11, 30,
    61, 43, 62, 39, 31, 63, 64, 65, 67, 66, 69, 131, 68, 71, 133, 70, 73, 132, 72, 75, 135, 137, 134, 95, 74, 77,
    139, 98, 76, 79, 81, 140, 141, 78, 82, 143, 145, 138, 80, 83, 85, 142, 86, 88, 84, 89, 146, 99, 96, 144, 91,
    87, 92, 136, 94, 100, 90, 104, 163, 101, 113, 97, 119, 147, 122, 149, 93, 164, 151, 105, 153, 155, 116, 120,
    110, 150, 157, 152, 154, 125, 159, 128, 156, 148, 161, 165, 102, 107, 160, 123, 111, 121, 166, 117, 158, 103,
    126, 112, 129, 124, 108, 106, 127, 109, 114, 162, 118, 115, 167, 130,
)


def run_layer(attention, feedforward, shared, split, tokens, cotangent, align, count, mask):
    vmem = pl.BlockSpec(memory_space=pltpu.VMEM)
    smem = pl.BlockSpec(memory_space=pltpu.SMEM)
    hbm = pl.BlockSpec(memory_space=pl.ANY)
    whole = jax.ShapeDtypeStruct((3, 512, 768), LOW)
    return pl.pallas_call(
        layer_kernel,
        out_shape=(
            jax.ShapeDtypeStruct((96, 4, 192), WIDE),
            jax.ShapeDtypeStruct((96, 2, 768), WIDE),
            jax.ShapeDtypeStruct((6, 96), WIDE),
            jax.ShapeDtypeStruct((6, 192), WIDE),
            whole,
            whole,
            jax.ShapeDtypeStruct((2, 3, 512, 512), LOW),
        ),
        in_specs=[vmem, vmem, vmem, vmem, hbm, hbm, vmem, smem, vmem],
        out_specs=(vmem, vmem, vmem, vmem, hbm, hbm, hbm),
        scratch_shapes=[*buffers().values(), *flags().values()],
        compiler_params=pltpu.CompilerParams(
            collective_id=0, has_side_effects=True, vmem_limit_bytes=VMEM_LIMIT
        ),
        name="layer_step",
    )(attention, feedforward, shared, split, tokens, cotangent, align, count, mask)


VMEM_LIMIT = 63 * 2**20


def slab_rates(rates, shape):
    slab = lax.broadcasted_iota(jnp.int32, shape, 1)
    value = jnp.full(shape, rates[0], WIDE)
    for i, rate in enumerate(rates[1:]):
        value = jnp.where(slab == i + 1, rate, value)
    return value


def update_kernel(text_ref, back_ref, *refs):
    families, outs = refs[:16], refs[16:]
    outs[0][...] = text_ref[...]
    outs[1][...] = back_ref[...].astype(WIDE)
    shape = families[12].shape
    row = lax.broadcasted_iota(jnp.int32, shape, 0)
    split_rates = jnp.full(shape, SPLIT_RATES[2], WIDE)
    for i in (0, 1, 3, 4, 5):
        split_rates = jnp.where(row == i, SPLIT_RATES[i], split_rates)
    rates = (
        slab_rates(ATTENTION_RATES, families[0].shape),
        slab_rates(FEEDFORWARD_RATES, families[4].shape),
        SHARED_RATE,
        split_rates,
    )
    for i, rate in enumerate(rates):
        master, moment, average, gradient = (ref[...] for ref in families[4 * i : 4 * i + 4])
        for out, value in zip(outs[2 + 4 * i : 6 + 4 * i], renew(master, moment, average, gradient, rate)):
            out[...] = value


PARTS = 4


def run_update(text, back, families):
    rows, width = text.shape

    def split_rows(array):
        block = (array.shape[0] // PARTS, *array.shape[1:])
        return pl.BlockSpec(block, lambda i: (i,) + (0,) * (len(block) - 1))

    def at_once(array):
        return pl.BlockSpec(array.shape, lambda i: (0,) * len(array.shape))

    specs = [split_rows(text), split_rows(back)]
    shapes = [jax.ShapeDtypeStruct(text.shape, LOW), jax.ShapeDtypeStruct(back.shape, WIDE)]
    outs = list(specs)
    for i, family in enumerate(families):
        spec = split_rows(family[0]) if i < 2 else at_once(family[0])
        specs += [spec] * 4
        outs += [spec] * 4
        shapes += [jax.ShapeDtypeStruct(family[0].shape, kind) for kind in (WIDE, WIDE, WIDE, LOW)]
    return pl.pallas_call(
        update_kernel,
        grid=(PARTS,),
        in_specs=specs,
        out_specs=outs,
        out_shape=shapes,
        compiler_params=pltpu.CompilerParams(vmem_limit_bytes=VMEM_LIMIT),
        name="update_parameters",
    )(text, back, *[array for family in families for array in family])


def line_shards(
    tokens,
    alignment,
    segment_count,
    text_mask,
    cotangent,
    attention_master,
    attention_moment,
    attention_average,
    feedforward_master,
    feedforward_moment,
    feedforward_average,
    shared_master,
    shared_moment,
    shared_average,
    split_master,
    split_moment,
    split_average,
):
    rows, width = tokens.shape
    attention_sum, feedforward_sum, shared_sum, split_sum, text_all, back_all, _ = run_layer(
        attention_master, feedforward_master, shared_master.T, split_master.T,
        tokens, cotangent, alignment, segment_count, text_mask,
    )
    outs = run_update(
        text_all.reshape(rows, width),
        back_all.reshape(rows, width),
        (
            (attention_master, attention_moment, attention_average, attention_sum),
            (feedforward_master, feedforward_moment, feedforward_average, feedforward_sum),
            (shared_master.T, shared_moment.T, shared_average.T, shared_sum),
            (split_master.T, split_moment.T, split_average.T, split_sum),
        ),
    )
    return (*outs[:10], *[out.T for out in outs[10:]])


def solution(mesh):
    in_specs = (
        P("dp", None),
        P("dp", None),
        P("dp"),
        P("dp", None),
        P("dp", None),
        P("dp", None, "mp"),
        P("dp", None, "mp"),
        P("dp", None, "mp"),
        P("dp", None, "mp"),
        P("dp", None, "mp"),
        P("dp", None, "mp"),
        P("dp", None),
        P("dp", None),
        P("dp", None),
        P("mp", None),
        P("mp", None),
        P("mp", None),
    )
    out_specs = (
        P("dp", None),
        P("dp", None),
        P("dp", None, "mp"),
        P("dp", None, "mp"),
        P("dp", None, "mp"),
        P("dp", None, "mp"),
        P("dp", None, "mp"),
        P("dp", None, "mp"),
        P("dp", None, "mp"),
        P("dp", None, "mp"),
        P("dp", None),
        P("dp", None),
        P("dp", None),
        P("dp", None),
        P("mp", None),
        P("mp", None),
        P("mp", None),
        P("mp", None),
    )
    body = line_shards if mesh.shape["dp"] == 8 and mesh.shape["mp"] == 4 else general_shards
    return jax.shard_map(body, mesh=mesh, in_specs=in_specs, out_specs=out_specs, check_vma=False)
```

```python
from functools import partial
from types import SimpleNamespace

import jax
import jax.numpy as jnp
from jax import lax
from jax.experimental import pallas as pl
from jax.experimental.pallas import tpu as pltpu
from jax.sharding import PartitionSpec as P

MESH = pl.DeviceIdType.MESH

HEAD_DIM = 64


EPS = 1e-05
MOMENTUM = 0.9
AVERAGE = 0.75
ATTENTION_RATES = (4e-05, 4e-05, 4e-05, 0.01)
FEEDFORWARD_RATES = (0.0002, 4e-05)
SHARED_RATE = 0.0006
SPLIT_RATES = (0.0004, 0.0003, 0.0017, 0.0017, 0.0017, 0.0017)
HIGHEST_MODE = lax.Precision.HIGHEST


def contract_last(left, right):
    return lax.dot_general(
        left, right, (((1,), (1,)), ((), ())), preferred_element_type=jnp.float32
    )


def contract_rows(left, right):
    return lax.dot_general(
        left, right, (((0,), (0,)), ((), ())), preferred_element_type=jnp.float32
    )


def layer_norm(value, gain, shift):
    center = value - jnp.mean(value, axis=-1, keepdims=True)
    factor = lax.rsqrt(jnp.mean(center * center, axis=-1, keepdims=True) + EPS)
    normed = center * factor
    return (normed * gain + shift, normed, factor)


def norm_back(incoming, normed, factor, gain):
    scaled = incoming * gain
    inner_part = (
        scaled
        - jnp.mean(scaled, axis=-1, keepdims=True)
        - normed * jnp.mean(scaled * normed, axis=-1, keepdims=True)
    )
    return (factor * inner_part, jnp.sum(incoming * normed, axis=0), jnp.sum(incoming, axis=0))


def masked_scores(queries, key_rows, valid_keys):
    scores = jnp.einsum(
        "qhd,khd->hqk", queries, key_rows, preferred_element_type=jnp.float32
    ) * HEAD_DIM ** (-0.5)
    return jnp.where(valid_keys[None, None, :], scores, -1e30)


def attend(pieces):
    queries, key_rows, value_rows, valid_keys = pieces
    scores = masked_scores(queries, key_rows, valid_keys)
    row_max = jnp.max(scores, axis=-1, keepdims=True)
    exponent = jnp.exp(scores - row_max)
    row_total = jnp.sum(exponent, axis=-1, keepdims=True)
    probability = (exponent / row_total).astype(jnp.bfloat16)
    context = jnp.einsum(
        "hqk,khd->qhd", probability, value_rows, preferred_element_type=jnp.float32
    )
    return (context.astype(jnp.bfloat16), row_max + jnp.log(row_total))


def attend_back(pieces):
    queries, key_rows, value_rows, valid_keys, upstream, logsum = pieces
    scores = masked_scores(queries, key_rows, valid_keys)
    probability = jnp.exp(scores - logsum)
    grad_values = jnp.einsum(
        "hqk,qhd->khd",
        probability.astype(jnp.bfloat16),
        upstream,
        preferred_element_type=jnp.float32,
    )
    grad_probs = jnp.einsum(
        "qhd,khd->hqk", upstream, value_rows, preferred_element_type=jnp.float32
    )
    row_delta = jnp.sum(probability * grad_probs, axis=-1, keepdims=True)
    grad_scores = (probability * (grad_probs - row_delta)).astype(jnp.bfloat16)
    grad_queries = jnp.einsum(
        "hqk,khd->qhd", grad_scores, key_rows, preferred_element_type=jnp.float32
    ) * HEAD_DIM ** (-0.5)
    grad_keys = jnp.einsum(
        "hqk,qhd->khd", grad_scores, queries, preferred_element_type=jnp.float32
    ) * HEAD_DIM ** (-0.5)
    return (
        grad_queries.astype(jnp.bfloat16),
        grad_keys.astype(jnp.bfloat16),
        grad_values.astype(jnp.bfloat16),
    )


def renew(master, moment, average, gradient, rates):
    velocity = MOMENTUM * moment + gradient
    updated = master - rates * (gradient + MOMENTUM * velocity)
    averaged = AVERAGE * average + (1.0 - AVERAGE) * updated
    return (velocity, updated, averaged, updated.astype(jnp.bfloat16))


def general_shards(
    tokens,
    alignment,
    segment_count,
    text_mask,
    cotangent,
    attention_master,
    attention_moment,
    attention_average,
    feedforward_master,
    feedforward_moment,
    feedforward_average,
    shared_master,
    shared_moment,
    shared_average,
    split_master,
    split_moment,
    split_average,
):
    documents, slot_count = alignment.shape
    text_rows = text_mask.shape[1]
    document_rows = text_rows + slot_count
    model_width = tokens.shape[1]
    local_width = split_master.shape[0]
    local_heads = local_width // HEAD_DIM
    row_count = documents * document_rows
    attention_full, feedforward_full, shared_full = (
        lax.all_gather(attention_master.astype(jnp.bfloat16), "dp", axis=0, tiled=True),
        lax.all_gather(feedforward_master.astype(jnp.bfloat16), "dp", axis=0, tiled=True),
        lax.all_gather(shared_master.astype(jnp.bfloat16), "dp", axis=0, tiled=True),
    )
    shared = shared_full.astype(jnp.float32)
    split_bias = lax.optimization_barrier(split_master.astype(jnp.bfloat16)).astype(jnp.float32)
    live_slots = (
        lax.broadcasted_iota(jnp.int32, (documents, slot_count), 1) < segment_count[:, None]
    )
    valid_keys = jnp.concatenate([text_mask > 0, live_slots], axis=1)
    text_index = lax.broadcasted_iota(jnp.int32, (documents, slot_count, text_rows), 2)
    pick_table = ((alignment[:, :, None] == text_index) & live_slots[:, :, None]).astype(
        jnp.bfloat16
    )
    inputs = tokens.reshape(documents, document_rows, model_width)
    taken_rows = jnp.einsum(
        "dst,dtw->dsw", pick_table, inputs[:, :text_rows], preferred_element_type=jnp.float32
    )
    layer_in = jnp.concatenate(
        [
            inputs[:, :text_rows].astype(jnp.float32),
            inputs[:, text_rows:].astype(jnp.float32) + taken_rows,
        ],
        axis=1,
    ).reshape(row_count, model_width)
    rows_in = layer_in.astype(jnp.bfloat16)
    project_weights = attention_full[:, :3].reshape(model_width, 3 * local_width)
    project_bias = jnp.concatenate(
        [split_bias[:, 0], jnp.zeros_like(split_bias[:, 0]), split_bias[:, 1]]
    )
    projected = (
        jnp.dot(rows_in, project_weights, preferred_element_type=jnp.float32) + project_bias
    ).astype(jnp.bfloat16)
    projected = projected.reshape(documents, document_rows, 3, local_heads, HEAD_DIM)
    queries = projected[:, :, 0]
    key_rows = projected[:, :, 1]
    value_rows = projected[:, :, 2]
    context, logsum = lax.map(attend, (queries, key_rows, value_rows, valid_keys))
    context_rows = context.reshape(row_count, local_width)
    joined = lax.psum(
        contract_last(context_rows, attention_full[:, 3]).astype(jnp.bfloat16), "mp"
    ).astype(jnp.float32)
    mixed = layer_in + joined + shared[:, 0]
    first_norm, normed_one, factor_one = layer_norm(mixed, shared[:, 1], shared[:, 2])
    hidden_in = first_norm.astype(jnp.bfloat16)
    inner_pre = jnp.dot(
        hidden_in, feedforward_full[:, 0], preferred_element_type=jnp.float32
    ) + split_bias[:, 2:].reshape(-1)
    active = jax.nn.gelu(inner_pre, approximate=False).astype(jnp.bfloat16)
    down_sum = lax.psum(
        contract_last(active, feedforward_full[:, 1]).astype(jnp.bfloat16), "mp"
    ).astype(jnp.float32)
    second = first_norm + down_sum + shared[:, 5]
    output, normed_two, factor_two = layer_norm(second, shared[:, 3], shared[:, 4])
    grad_second, grad_gain_two, grad_shift_two = norm_back(
        cotangent.astype(jnp.float32), normed_two, factor_two, shared[:, 3]
    )
    grad_down = grad_second.astype(jnp.bfloat16)
    grad_active = jnp.dot(grad_down, feedforward_full[:, 1], preferred_element_type=jnp.float32)
    gelu_value, gelu_pull = jax.vjp(partial(jax.nn.gelu, approximate=False), inner_pre)
    grad_inner = gelu_pull(grad_active)[0].astype(jnp.bfloat16)
    feedforward_grad = jnp.stack(
        [contract_rows(hidden_in, grad_inner), contract_rows(grad_down, active)], axis=1
    )
    grad_first = grad_second + lax.psum(
        contract_last(grad_inner, feedforward_full[:, 0]).astype(jnp.bfloat16), "mp"
    ).astype(jnp.float32)
    grad_mixed, grad_gain_one, grad_shift_one = norm_back(
        grad_first, normed_one, factor_one, shared[:, 1]
    )
    grad_joined = grad_mixed.astype(jnp.bfloat16)
    output_grad = contract_rows(grad_joined, context_rows)
    grad_context = jnp.dot(
        grad_joined, attention_full[:, 3], preferred_element_type=jnp.float32
    ).astype(jnp.bfloat16)
    upstream = grad_context.reshape(documents, document_rows, local_heads, HEAD_DIM)
    grad_queries, grad_keys, grad_values = lax.map(
        attend_back, (queries, key_rows, value_rows, valid_keys, upstream, logsum)
    )
    query_rows = grad_queries.reshape(row_count, local_width)
    value_grad_rows = grad_values.reshape(row_count, local_width)
    grad_project = jnp.concatenate(
        [query_rows, grad_keys.reshape(row_count, local_width), value_grad_rows], axis=1
    )
    project_grad = contract_rows(rows_in, grad_project).reshape(model_width, 3, local_width)
    attention_grad = jnp.concatenate([project_grad, output_grad[:, None, :]], axis=1)
    grad_layer_in = grad_mixed + lax.psum(
        contract_last(grad_project, project_weights).astype(jnp.bfloat16), "mp"
    ).astype(jnp.float32)
    shared_grad = jnp.stack(
        [
            jnp.sum(grad_mixed, axis=0),
            grad_gain_one,
            grad_shift_one,
            grad_gain_two,
            grad_shift_two,
            jnp.sum(grad_second, axis=0),
        ],
        axis=1,
    )
    split_grad = jnp.concatenate(
        [
            jnp.sum(query_rows, axis=0, dtype=jnp.float32)[:, None],
            jnp.sum(value_grad_rows, axis=0, dtype=jnp.float32)[:, None],
            jnp.sum(grad_inner, axis=0, dtype=jnp.float32).reshape(local_width, 4),
        ],
        axis=1,
    )
    grad_documents = grad_layer_in.reshape(documents, document_rows, model_width)
    moved_rows = jnp.einsum(
        "dst,dsw->dtw",
        pick_table.astype(jnp.float32),
        grad_documents[:, text_rows:],
        precision=HIGHEST_MODE,
        preferred_element_type=jnp.float32,
    )
    input_gradient = jnp.concatenate(
        [grad_documents[:, :text_rows] + moved_rows, grad_documents[:, text_rows:]], axis=1
    ).reshape(row_count, model_width)
    attention_sum, feedforward_sum, shared_sum = (
        lax.psum_scatter(attention_grad, "dp", scatter_dimension=0, tiled=True),
        lax.psum_scatter(feedforward_grad, "dp", scatter_dimension=0, tiled=True),
        lax.psum_scatter(shared_grad, "dp", scatter_dimension=0, tiled=True),
    )
    split_sum = lax.psum(split_grad, "dp")
    attention_new = renew(
        attention_master,
        attention_moment,
        attention_average,
        attention_sum,
        jnp.asarray(ATTENTION_RATES, jnp.float32).reshape(1, 4, 1),
    )
    feedforward_new = renew(
        feedforward_master,
        feedforward_moment,
        feedforward_average,
        feedforward_sum,
        jnp.asarray(FEEDFORWARD_RATES, jnp.float32).reshape(1, 2, 1),
    )
    shared_new = renew(shared_master, shared_moment, shared_average, shared_sum, SHARED_RATE)
    split_new = renew(
        split_master,
        split_moment,
        split_average,
        split_sum,
        jnp.asarray(SPLIT_RATES, jnp.float32).reshape(1, 6),
    )
    return (
        output.astype(jnp.bfloat16),
        input_gradient,
        attention_new[0],
        attention_new[1],
        attention_new[2],
        attention_new[3],
        feedforward_new[0],
        feedforward_new[1],
        feedforward_new[2],
        feedforward_new[3],
        shared_new[0],
        shared_new[1],
        shared_new[2],
        shared_new[3],
        split_new[0],
        split_new[1],
        split_new[2],
        split_new[3],
    )


LOW = jnp.bfloat16
WIDE = jnp.float32
UNITS = [(0, 0), (1, 0), (2, 0), (0, 1), (0, 2), (0, 3)] + [(t, k) for k in range(1, 4) for t in (1, 2)]
AXES = (0, 1, 0, 1, 0, 1, 0, 0, 0, 1, 0, 1)
LINE = 4
BACK_UNITS = [(t, k) for k in range(4) for t in (2, 1)] + [(0, k) for k in range(4)]
PIECES = 8
SENDS = 3
ENDS_MAKE = False
PAIRS = 4


def place():
    dp, z = lax.axis_index("dp"), lax.axis_index("mp")
    return z, lax.div(dp, 4), lax.rem(lax.div(dp, 2), 2), lax.rem(dp, 2)


def device(z, y, x, c):
    return (y * 4 + x * 2 + c, z)


def document_of(z):
    return lax.div(z + 1, 2)


def nearest_level(z, k):
    low, high = lax.rem(z, 2), lax.div(z, 2)
    if k == 0:
        return z
    if k == 1:
        return 1 + (2 * high - 1) * low
    if k == 2:
        return 2 + high * (1 - 2 * low)
    return 3 - 3 * high


def greet(z, y, x, c):
    barrier = pltpu.get_barrier_semaphore()
    partners = [device(z, y, x, 1 - c), device(z, y, 1 - x, c), device(z, 1 - y, x, c)]
    partners += [device(lax.rem(z + k, 4), y, x, c) for k in (1, 2, 3)]
    for partner in partners:
        pl.semaphore_signal(barrier, inc=1, device_id=partner, device_id_type=MESH)
    pl.semaphore_wait(barrier, len(partners))


def remote(source, target, send, recv, to):
    return pltpu.make_async_remote_copy(
        src_ref=source, dst_ref=target, send_sem=send, recv_sem=recv, device_id=to, device_id_type=MESH
    )


def when(condition, action):
    pl.when(condition)(action)


def mul(left, right):
    return jnp.dot(left, right, preferred_element_type=WIDE)


def gelu_parts(value):
    root = value * 0.7071067811865476
    inverse = 1.0 / (1.0 + 0.3275911 * jnp.abs(root))
    bell = jnp.exp(-root * root)
    series = 1.061405429
    for factor in (-1.453152027, 1.421413741, -0.284496736, 0.254829592):
        series = series * inverse + factor
    tail = 0.5 * series * inverse * bell
    share = jnp.where(value >= 0, 1.0 - tail, tail)
    return value * share, share + value * (bell * 0.3989422804014327)


def head_mask(head, scale, lanes=192):
    lane = lax.broadcasted_iota(jnp.int32, (1, lanes), 1)
    return jnp.where((lane >= head * HEAD_DIM) & (lane < (head + 1) * HEAD_DIM), scale, 0.0).astype(LOW)


def wide_product(left, right, width):
    value = mul(left, right)
    if right.shape[1] < width:
        value = jnp.concatenate([value, jnp.zeros((left.shape[0], width - right.shape[1]), WIDE)], axis=1)
    return value


def unit_weight(r, t, level):
    return r.full[t, level].reshape(768, 768)


class Gather:
    def __init__(self, r):
        self.own, self.small, self.r = r.own, r.small, r
        self.z, self.y, self.x, self.c = z, y, x, c = place()
        self.up, self.down = device(z + 1, y, x, c), device(z - 1, y, x, c)
        self.across_x, self.across_y = device(z, y, 1 - x, c), device(z, 1 - y, x, c)
        self.pair = device(z, y, x, 1 - c)
        self.end = (z == 0) | (z == LINE - 1)

    def line_copy(self, t, level, source, way):
        r = self.r
        return remote(
            source, r.full.at[t, level, self.y, self.x, self.c], r.sent.at[0],
            r.line_recv.at[t, level], self.up if way == 0 else self.down,
        )

    def along_x(self, u):
        return AXES[u] == 0

    def first(self, u):
        t, k = UNITS[u]
        block = self.r.full.at[t, nearest_level(self.z, k), self.y, self.x, self.c]
        return remote(
            self.own.at[t] if k == 0 else block, block, self.r.sent.at[1], self.r.first_recv.at[u],
            self.across_x if self.along_x(u) else self.across_y,
        )

    def second(self, u):
        t, k = UNITS[u]
        level = nearest_level(self.z, k)
        if self.along_x(u):
            block, to = self.r.full.at[t, level, self.y, :, self.c], self.across_y
        else:
            block, to = self.r.full.at[t, level, :, self.x, self.c], self.across_x
        return remote(block, block, self.r.sent.at[2], self.r.second_recv.at[u], to)

    def extra(self, u, level, part, way):
        t, y, x, c = UNITS[u][0], self.y, self.x, self.c
        if self.along_x(u):
            index = (t, level, y, 1 - x, c) if part == 0 else (t, level, 1 - y, slice(None), c)
        else:
            index = (t, level, 1 - y, x, c) if part == 0 else (t, level, slice(None), 1 - x, c)
        block = self.r.full.at[index]
        return remote(
            block, block, self.r.sent.at[4], self.r.extra_recv.at[t - 1, level],
            self.up if way == 0 else self.down,
        )

    def paired(self, u):
        t, k = UNITS[u]
        block = self.r.full.at[t, nearest_level(self.z, k), :, :, self.c]
        return remote(block, block, self.r.sent.at[3], self.r.pair_recv.at[u], self.pair)

    def own_copy(self, t):
        return pltpu.make_async_copy(
            self.own.at[t], self.r.full.at[t, self.z, self.y, self.x, self.c], self.r.own_sem.at[t]
        )

    def tiny_own(self, i):
        target = self.r.plane.at[self.y, self.x, self.c] if i == 0 else self.r.line.at[self.z]
        return pltpu.make_async_copy(self.small, target, self.r.own_sem.at[3 + i])

    def tiny(self, i):
        r = self.r
        if i == 0:
            block, to = r.plane.at[self.y, self.x, self.c], self.across_x
        elif i == 1:
            block, to = r.plane.at[self.y, :, self.c], self.across_y
        elif i == 2:
            block, to = r.plane.at[:, :, self.c], self.pair
        else:
            block, to = r.line.at[self.z], device(lax.rem(self.z + i - 2, 4), self.y, self.x, self.c)
        source = self.small if i == 0 or i > 2 else block
        return remote(source, block, r.tiny_send.at[i], r.tiny_recv.at[i], to)

    def own_line(self, t, act):
        when(self.z < 3, lambda: act(self.line_copy(t, self.z, self.own.at[t], 0)))
        when(self.z > 0, lambda: act(self.line_copy(t, self.z, self.own.at[t], 1)))

    def own_extra(self, u, part, act):
        when(self.z < 3, lambda: act(self.extra(u, self.z, part, 0)))
        when(self.z > 0, lambda: act(self.extra(u, self.z, part, 1)))

    def begin(self):
        self.own_line(0, lambda copy: copy.start())
        for t in range(3):
            self.own_copy(t).start()

    def begin_tiny(self):
        for i in range(2):
            self.tiny_own(i).start()
        for i in (0, 3, 4, 5):
            self.tiny(i).start()

    def crosses(self, u, act):
        t, k = UNITS[u]
        if t == 0 or k in (0, 3):
            act()
        elif k == 2:
            when(self.end, act)

    def comes_whole(self, u, act):
        t, k = UNITS[u]
        if t > 0 and k == 1:
            act()
        elif t > 0 and k == 2:
            when(jnp.logical_not(self.end), act)

    def relay(self, u):
        t, k = UNITS[u]
        level = nearest_level(self.z, k)
        block = self.r.full.at[t, level, self.y, self.x, self.c]

        def act():
            self.line_copy(t, level, block, 0).wait_recv()
            when(level < self.z, lambda: self.line_copy(t, level, block, 0).start())
            when(level > self.z, lambda: self.line_copy(t, level, block, 1).start())

        when(jnp.logical_not(self.end), act)

    def arrive(self, u):
        t, k = UNITS[u]
        if k == 0 and t > 0:
            self.own_line(t, lambda copy: copy.start())
        if k > 0:
            level = nearest_level(self.z, k)
            block = self.r.full.at[t, level, self.y, self.x, self.c]
            when(self.end, lambda: self.line_copy(t, level, block, 0).wait_recv())
        self.crosses(u, lambda: self.first(u).start())

    def cross(self, u):
        t, k = UNITS[u]

        def act():
            self.first(u).wait_recv()
            if k == 0:
                self.own_copy(t).wait()
            self.second(u).start()
            if t > 0 and k == 0:
                self.own_extra(u, 0, lambda copy: copy.start())

        self.crosses(u, act)

    def share(self, u):
        t, k = UNITS[u]
        level = nearest_level(self.z, k)

        def act():
            self.second(u).wait_recv()
            if t > 0 and k == 0:
                self.own_extra(u, 1, lambda copy: copy.start())
            self.paired(u).start()

        def act_whole():
            blocks = self.r.second_in.at[pl.ds(0, 3)]
            remote(blocks, blocks, self.r.sent.at[4], self.r.extra_recv.at[t - 1, level], self.up).wait_recv()
            self.paired(u).start()

        self.crosses(u, act)
        self.comes_whole(u, act_whole)

    def take(self, u):
        self.paired(u).wait_recv()

    def tiny_step(self, i):
        if i == 0:
            for j in range(2):
                self.tiny_own(j).wait()
        if i < 3:
            self.tiny(i).wait_recv()
        if i < 2:
            self.tiny(i + 1).start()
        if i == 3:
            for j in (3, 4, 5):
                self.tiny(j).wait_recv()

    def finish(self):
        r = self.r
        for i in range(6):
            self.tiny(i).wait_send()

        def all_sent(*counts):
            for i, count in enumerate(counts):
                if count == 15:
                    blocks = r.line_in
                elif count == 48:
                    blocks = r.total
                elif count in (16, 20):
                    blocks = r.first_in.at[pl.ds(0, count // 2)]
                else:
                    blocks = r.second_in.at[pl.ds(0, count)]
                remote(blocks, blocks, r.sent.at[i], r.pair_recv.at[0], self.pair).wait_send()

        when(self.end, lambda: all_sent(3, 10, 20, 48, 6))
        when(jnp.logical_not(self.end), lambda: all_sent(15, 8, 16, 48, 12))


class Reduce:
    def __init__(self, att_sum, ff_sum, r):
        self.att_sum, self.ff_sum, self.r = att_sum, ff_sum, r
        self.z, self.y, self.x, self.c = z, y, x, c = place()
        self.up, self.down = device(z + 1, y, x, c), device(z - 1, y, x, c)
        self.across_x, self.across_y = device(z, y, 1 - x, c), device(z, 1 - y, x, c)
        self.pair = device(z, y, x, 1 - c)

    def pair_copy(self, u):
        r = self.r
        return remote(
            r.sends.at[u % SENDS], r.pair_in.at[u % PAIRS], r.r_pair_send.at[u % SENDS], r.r_pair_recv.at[u % PAIRS],
            self.pair,
        )

    def first_copy(self, u):
        r = self.r
        source = r.total.at[u, :, 1 - self.x] if u % 2 == 0 else r.total.at[u, 1 - self.y]
        return remote(
            source, r.first_in.at[u], r.sent.at[5], r.r_first_recv.at[u],
            self.across_x if u % 2 == 0 else self.across_y,
        )

    def second_copy(self, u):
        r, x, y = self.r, self.x, self.y
        return remote(
            r.total.at[u, 1 - y, x] if u % 2 == 0 else r.total.at[u, y, 1 - x],
            r.second_in.at[u], r.sent.at[6], r.r_second_recv.at[u],
            self.across_y if u % 2 == 0 else self.across_x,
        )

    def line_copy(self, u, way):
        r = self.r
        t, k = BACK_UNITS[u]
        level = nearest_level(self.z, 3 - k)
        return remote(
            r.total.at[u, self.y, self.x], r.line_in.at[t, level + 1 - way], r.sent.at[7],
            r.r_line_recv.at[t, level + 1 - way], self.up if way == 0 else self.down,
        )

    def produce(self, u, parts):
        r = self.r
        if u >= SENDS:
            self.pair_copy(u - SENDS).wait_send()
        for half, target in ((1 - self.c, r.sends.at[u % SENDS]), (self.c, r.total.at[u])):
            for products, lanes in parts:
                width = lanes.stop - lanes.start
                value = sum(wide_product(turned[:, :, half].reshape(384, 512), columns, width) for turned, columns in products)
                target[:, :, :, lanes] = value.astype(LOW).reshape(2, 2, 96, width)
            if half is not self.c:
                self.pair_copy(u).start()

    def add_pair(self, u):
        r = self.r
        self.pair_copy(u).wait_recv()
        r.total[u] = r.total[u] + r.pair_in[u % PAIRS]
        self.first_copy(u).start()

    def add_first(self, u):
        r, x, y = self.r, self.x, self.y
        self.first_copy(u).wait_recv()
        if u % 2 == 0:
            r.total[u, :, x] = r.total[u, :, x] + r.first_in[u]
        else:
            r.total[u, y] = r.total[u, y] + r.first_in[u]
        self.second_copy(u).start()

    def add_second(self, u):
        r, x, y, z = self.r, self.x, self.y, self.z
        t, k = BACK_UNITS[u]
        level = nearest_level(z, 3 - k)
        self.second_copy(u).wait_recv()
        r.total[u, y, x] = r.total[u, y, x] + r.second_in[u]
        if k < 3:
            when((z == 0) | (z == 3), lambda: self.send_line(u))

    def send_line(self, u):
        level = nearest_level(self.z, 3 - BACK_UNITS[u][1])
        when(self.z < level, lambda: self.line_copy(u, 0).start())
        when(self.z > level, lambda: self.line_copy(u, 1).start())

    def take_line(self, u, way):
        r, x, y = self.r, self.x, self.y
        t, k = BACK_UNITS[u]
        level = nearest_level(self.z, 3 - k)
        self.line_copy(u, way).wait_recv()
        r.total[u, y, x] = r.total[u, y, x] + r.line_in[t, level + 1 - way]

    def add_line(self, u):
        r, z = self.r, self.z
        t, k = BACK_UNITS[u]
        level = nearest_level(z, 3 - k)
        middle = (z == 1) | (z == 2)
        if k < 3:
            when(middle & (z < level), lambda: self.take_line(u, 0))
            when(middle & (z > level), lambda: self.take_line(u, 1))
            when(middle, lambda: self.send_line(u))
        else:
            when(z > 0, lambda: self.take_line(u, 0))
            when(z < 3, lambda: self.take_line(u, 1))
            self.give(t, r.total[u, self.y, self.x])

    def give(self, t, value):
        r = self.r
        if t == 0:
            for slab in range(4):
                r.att_in[:, slab, :] = value[:, slab * 192 : (slab + 1) * 192].astype(WIDE)
            self.given(0).start()
        else:
            r.ff_in[:, t - 1, :] = value.astype(WIDE)

    def given(self, i):
        source, target = ((self.r.att_in, self.att_sum), (self.r.ff_in, self.ff_sum))[i]
        return pltpu.make_async_copy(source, target, self.r.load_sem.at[6 + i])

    def small_copy(self, i):
        r = self.r
        if i < 3:
            to = (self.pair, self.across_x, self.across_y)[i]
            return remote(r.small_total.at[i], r.small_in.at[i], r.small_send.at[i], r.small_recv.at[i], to)
        to = device(lax.rem(self.z + i - 2, 4), self.y, self.x, self.c)
        return remote(r.small_total.at[3], r.small_line.at[self.z], r.small_send.at[i], r.small_recv.at[i], to)

    def small_step(self, i):
        r = self.r
        self.small_copy(i).wait_recv()
        r.small_total[i + 1] = r.small_total[i] + r.small_in[i]
        if i < 2:
            self.small_copy(i + 1).start()
        else:
            for j in (3, 4, 5):
                self.small_copy(j).start()
            r.small_line[self.z] = r.small_total[3]

    def small_end(self, shared_sum, split_sum):
        r, z = self.r, self.z
        for i in (3, 4, 5):
            self.small_copy(i).wait_recv()
        r.small_sum[...] = r.small_line[0] + r.small_line[1] + r.small_line[2] + r.small_line[3]
        index = self.y * 4 + self.x * 2 + self.c
        shared_sum[...] = pltpu.roll(r.small_sum[:8], lax.rem(768 - index * 96, 768), 1)[:6, :96]
        biases = r.small_sum[pl.ds(8 + z, 1)]
        split_sum[0:1] = biases[:, :192]
        split_sum[1:2] = biases[:, 384:576]
        inner = r.small_sum[pl.ds(12 + z, 1)]
        for j in range(4):
            split_sum[2 + j : 3 + j] = inner[:, j * 192 : (j + 1) * 192]

    def finish(self):
        for i in range(6):
            self.small_copy(i).wait_send()
        for u in range(len(BACK_UNITS) - SENDS, len(BACK_UNITS)):
            self.pair_copy(u).wait_send()
        r = self.r
        for i, blocks in ((5, r.first_in), (6, r.second_in), (7, r.second_in.at[pl.ds(0, 9)])):
            remote(blocks, blocks, r.sent.at[i], r.r_pair_recv.at[0], self.pair).wait_send()


class Cast:
    def __init__(self, a, source, target, r):
        self.a, self.source, self.target, self.r = a, source, target, r
        self.z, y, x, c = place()
        self.up, self.down = device(self.z + 1, y, x, c), device(self.z - 1, y, x, c)

    def copy(self, d, p, way, first):
        r = self.r
        part = pl.ds(p * (512 // PIECES), 512 // PIECES)
        target = self.target.at[d, part]
        return remote(
            self.source.at[part] if first else target, target, r.cast_send.at[self.a],
            r.cast_recv.at[self.a, 16 if d == 1 else d * 4 + p], self.up if way == 0 else self.down,
        )

    def own(self):
        return pltpu.make_async_copy(self.source, self.target.at[document_of(self.z)], self.r.cast_own.at[self.a])

    def firsts(self, p, act):
        for level, d, way in ((0, 0, 0), (1, 1, 1), (2, 1, 0), (3, 2, 1))[:: 3 if self.a == 0 and ENDS_MAKE else 1]:
            when(self.z == level, lambda d=d, way=way: act(self.copy(d, p, way, True)))

    def begin(self):
        self.own().start()
        for p in range(PIECES):
            self.firsts(p, lambda copy: copy.start())

    def pass_on(self, d, p, way):
        copy = self.copy(d, p, way, False)
        copy.wait_recv()
        copy.start()

    def near(self, p):
        when(self.z == 1, lambda: self.pass_on(0, p, 0))
        when(self.z == 2, lambda: self.pass_on(2, p, 1))

    def far(self, p):
        when(self.z == 1, lambda: self.pass_on(2, p, 1))
        when(self.z == 2, lambda: self.pass_on(0, p, 0))

    def finish(self):
        r = self.r
        self.own().wait()
        for level, d, way in ((0, 2, 1), (3, 0, 0)):
            for p in range(PIECES):
                when(self.z == level, lambda p=p, d=d, way=way: self.copy(d, p, way, False).wait_recv())

        def wait(blocks, act):
            act(remote(blocks, blocks, r.cast_send.at[self.a], r.cast_recv.at[self.a, 16], self.up))

        end = (self.z == 0) | (self.z == 3)
        if self.a == 1 or not ENDS_MAKE:
            when(end, lambda: wait(self.target.at[1], lambda copy: copy.wait_recv()))
        when(end, lambda: wait(self.source, lambda copy: copy.wait_send()))
        when(jnp.logical_not(end), lambda: wait(self.target, lambda copy: copy.wait_send()))


def buffers():
    vmem = pltpu.VMEM
    return dict(
        full=vmem((3, 4, 2, 2, 2, 96, 768), LOW),
        plane=vmem((2, 2, 2, 16, 768), LOW),
        line=vmem((4, 16, 768), LOW),
        tok=vmem((512, 768), LOW),
        cot=vmem((512, 768), LOW),
        pick=vmem((384, 128), LOW),
        rows_in=vmem((512, 768), LOW),
        hidden_in=vmem((512, 768), LOW),
        rows_t=vmem((2, 2, 2, 96, 512), LOW),
        hidden_t=vmem((2, 2, 2, 96, 512), LOW),
        down_t=vmem((2, 2, 2, 96, 512), LOW),
        joined_t=vmem((2, 2, 2, 96, 512), LOW),
        qkv=vmem((4, 512, 640), LOW),
        probs=vmem((2, 3, 512, 512), LOW),
        context=vmem((4, 512, 256), LOW),
        active=vmem((4, 512, 768), LOW),
        slope=vmem((4, 512, 768), LOW),
        mixed=vmem((512, 768), WIDE),
        bar=vmem((1, 512), WIDE),
        normed_one=vmem((512, 768), WIDE),
        factor_one=vmem((512, 1), WIDE),
        total=vmem((12, 2, 2, 96, 768), LOW),
        sends=vmem((SENDS, 2, 2, 96, 768), LOW),
        pair_in=vmem((PAIRS, 2, 2, 96, 768), LOW),
        first_in=vmem((12, 2, 96, 768), LOW),
        second_in=vmem((12, 96, 768), LOW),
        line_in=vmem((3, 5, 96, 768), LOW),
        small_total=vmem((4, 16, 768), WIDE),
        small_in=vmem((3, 16, 768), WIDE),
        small_line=vmem((4, 16, 768), WIDE),
        small_sum=vmem((16, 768), WIDE),
        shared=vmem((16, 768), WIDE),
        own=vmem((3, 96, 768), LOW),
        att_in=vmem((96, 4, 192), WIDE),
        ff_in=vmem((96, 2, 768), WIDE),
        shared_in=vmem((6, 96), WIDE),
        split_in=vmem((6, 192), WIDE),
        align_in=vmem((3, 128), jnp.int32),
        mask_in=vmem((3, 384), jnp.int32),
        small=vmem((16, 768), LOW),
    )


def flags():
    dma = pltpu.SemaphoreType.DMA
    return dict(
        sent=dma((8,)),
        line_recv=dma((3, 4)),
        first_recv=dma((12,)),
        second_recv=dma((12,)),
        pair_recv=dma((12,)),
        tiny_send=dma((6,)),
        tiny_recv=dma((6,)),
        extra_recv=dma((2, 4)),
        own_sem=dma((5,)),
        load_sem=dma((12,)),
        r_pair_send=dma((SENDS,)),
        r_pair_recv=dma((PAIRS,)),
        r_first_recv=dma((12,)),
        r_second_recv=dma((12,)),
        r_line_recv=dma((3, 5)),
        small_send=dma((6,)),
        small_recv=dma((6,)),
        cast_send=dma((2,)),
        cast_recv=dma((2, 17)),
        cast_own=dma((2,)),
    )


def spread(j):
    unit = lax.broadcasted_iota(jnp.int32, (192, 768), 1)
    return jnp.where(unit == 4 * lax.broadcasted_iota(jnp.int32, (192, 768), 0) + j, 1.0, 0.0).astype(LOW)


def turn(value, counts):
    return (value * counts.astype(LOW)).T.reshape(2, 2, 2, 96, 512)


def layer_kernel(
    att_ref, ff_ref, shared_ref, split_ref, tokens_ref, cotangent_ref, align_ref, count_ref, mask_ref,
    att_sum, ff_sum, shared_sum, split_sum, text_all, back_all, probs_out, *refs,
):
    r = SimpleNamespace(**dict(zip([*buffers(), *flags()], refs)))
    z, y, x, c = place()
    doc = document_of(z)
    counts = jnp.where(z == 2, 0.0, 1.0)
    tok_copy = pltpu.make_async_copy(tokens_ref.at[pl.ds(doc * 512, 512)], r.tok, r.load_sem.at[0])
    cot_copy = pltpu.make_async_copy(cotangent_ref.at[pl.ds(doc * 512, 512)], r.cot, r.load_sem.at[1])
    tok_copy.start()
    cot_copy.start()
    operands = (
        (att_ref, r.att_in), (ff_ref, r.ff_in), (shared_ref, r.shared_in), (split_ref, r.split_in),
        (align_ref, r.align_in), (mask_ref, r.mask_in),
    )
    loads = [pltpu.make_async_copy(source, target, r.load_sem.at[6 + i]) for i, (source, target) in enumerate(operands)]
    for copy in loads:
        copy.start()
    greet(z, y, x, c)
    net = Gather(r)
    loads[0].wait()
    for slab in range(4):
        r.own[0, :, slab * 192 : (slab + 1) * 192] = r.att_in[:, slab, :].astype(LOW)
    loads[1].wait()
    for t in (1, 2):
        r.own[t] = r.ff_in[:, t - 1, :].astype(LOW)
    for copy in loads[2:]:
        copy.wait()
    net.begin()

    def small_start():
        r.small_sum[...] = jnp.zeros((16, 768), WIDE)
        r.small_sum[:6, :96] = r.shared_in[...]
        shared = pltpu.roll(r.small_sum[:8], (y * 4 + x * 2 + c) * 96, 1)
        r.small_sum[8:14, :192] = r.split_in[...]
        units = r.small_sum[8:16, :192].astype(LOW)
        inner = sum(mul(units, spread(j))[2 + j : 3 + j] for j in range(4))
        r.small_sum[:8] = shared
        r.small_sum[6:7] = jnp.zeros((1, 768), WIDE)
        r.small_sum[6:7, :192] = r.split_in[0:1]
        r.small_sum[6:7, 384:576] = r.split_in[1:2]
        r.small_sum[7:8] = inner
        r.small[...] = r.small_sum[...].astype(LOW)
        net.begin_tiny()

    def small_ready():
        value = r.small_total[0, 8:16]
        high = value.astype(LOW)
        rest = value - high.astype(WIDE)
        middle = rest.astype(LOW)
        last = (rest - middle.astype(WIDE)).astype(LOW)
        for j in range(4):
            packed = sum(contract_last(piece, spread(j)) for piece in (last, middle, high))
            r.small_total[0, 12:16, j * 192 : (j + 1) * 192] = packed[4:8]
        r.small_total[0] = r.small_total[0] * counts
        red.small_copy(0).start()

    def input_rows(tok, document):
        live = lax.broadcasted_iota(jnp.int32, (1, 128), 1) < count_ref[document]
        pick = jnp.where(
            (lax.broadcasted_iota(jnp.int32, (384, 128), 0) == r.align_in[pl.ds(document, 1), :]) & live, 1.0, 0.0
        ).astype(LOW)
        text_tokens = tok[:384]
        taken = lax.dot_general(pick, text_tokens, (((0,), (0,)), ((), ())), preferred_element_type=WIDE)
        slot_rows = tok[384:].astype(WIDE) + taken
        r.mixed[:384] = text_tokens.astype(WIDE)
        r.mixed[384:] = slot_rows
        r.rows_in[:384] = text_tokens
        r.rows_in[384:] = slot_rows.astype(LOW)
        r.bar[...] = jnp.where(jnp.concatenate([r.mask_in[pl.ds(document, 1), :] > 0, live], axis=1), 0.0, -1e30)
        return pick

    def prologue():
        tok_copy.wait()
        r.pick[...] = input_rows(r.tok, doc)
        r.rows_t[...] = turn(r.rows_in[...], counts)

    def spill(k):
        return pltpu.make_async_copy(r.probs.at[k % 2], probs_out.at[k % 2], r.load_sem.at[2 + k % 2])

    def projected_rows(level):
        bias = r.line[level][6:7].astype(WIDE)
        return (mul(r.rows_in[...], unit_weight(r, 0, level)) + bias).astype(LOW)

    def attend_level(projected, level, keep):
        queries, keys, values = projected[:, :192], projected[:, 192:384], projected[:, 384:640]
        context = jnp.zeros((512, 256), WIDE)
        for head in range(3):
            scores = contract_last(queries * head_mask(head, 0.125), keys)
            scores = jnp.where(r.bar[...] < 0.0, -1e30, scores)
            raised = jnp.exp(scores - jnp.max(scores, axis=-1, keepdims=True))
            probs = (raised * (1.0 / jnp.sum(raised, axis=-1, keepdims=True))).astype(LOW)
            keep[head] = probs
            context = context + mul(probs, values * head_mask(head, 1.0, 256))
        r.context[level] = pltpu.roll(context, 64, 1).astype(LOW)

    def attention(k):
        level = nearest_level(z, k)
        projected = projected_rows(level)
        r.qkv[level] = projected[:, :640]
        if k >= 2:
            spill(k).wait()
        attend_level(projected, level, r.probs.at[k % 2])
        if k < 2:
            spill(k).start()

    def norm_rows():
        for level in range(4):
            r.mixed[...] += contract_last(r.context[level], unit_weight(r, 0, level)[:, 512:])
        shared = r.shared[...]
        rows, normed, factor = layer_norm(r.mixed[...] + shared[0:1], shared[1:2], shared[2:3])
        r.hidden_in[...] = rows.astype(LOW)
        r.mixed[...] = rows + shared[5:6]
        return normed, factor

    def first_norm():
        r.shared[...] = jnp.sum(r.plane[...].astype(WIDE).reshape(8, 16, 768), axis=0)
        normed, factor = norm_rows()
        r.normed_one[...] = normed
        r.factor_one[...] = factor
        r.hidden_t[...] = turn(r.hidden_in[...], counts)

    def feed_level(level, keep_slope):
        bias = r.line[level][7:8, :].astype(WIDE)
        up = unit_weight(r, 1, level)
        for part in range(3):
            lanes = slice(part * 256, (part + 1) * 256)
            inner = mul(r.hidden_in[...], up[:, lanes]) + bias[:, lanes]
            active, slope = gelu_parts(inner)
            r.active[level, :, lanes] = active.astype(LOW)
            if keep_slope:
                r.slope[level, :, lanes] = slope.astype(LOW)

    def feed(k):
        feed_level(nearest_level(z, k), True)

    def feed_sum(k):
        level = jnp.where(net.end, nearest_level(z, k), (1, 2, 0, 3)[k])
        r.mixed[...] += contract_last(r.active[level], unit_weight(r, 2, level))

    end = (z == 0) | (z == 3)

    def next_tokens():
        return pltpu.make_async_copy(tokens_ref.at[pl.ds(512, 512)], r.slope.at[0], r.load_sem.at[0])

    def next_text():
        return pltpu.make_async_copy(r.slope.at[1], text_all.at[1], r.load_sem.at[1])

    def next_input():
        next_tokens().wait()
        input_rows(r.slope.at[0], 1)

    def next_attention(level):
        attend_level(projected_rows(level), level, r.probs.at[level % 2])

    def next_norm():
        norm_rows()

    def next_feed(level):
        feed_level(level, False)

    def next_end():
        for k in range(4):
            feed_sum(k)
        shared = r.shared[...]
        r.slope[1] = layer_norm(r.mixed[...], shared[3:4], shared[4:5])[0].astype(LOW)
        next_text().start()

    def at_ends(action, *args):
        when(end, lambda: action(*args))

    text_cast = Cast(0, r.tok, text_all, r)
    back_cast = Cast(1, r.cot, back_all, r)
    red = Reduce(att_sum, ff_sum, r)

    def second_norm():
        shared = r.shared[...]
        final, normed, factor = layer_norm(r.mixed[...], shared[3:4], shared[4:5])
        r.tok[...] = final.astype(LOW)
        text_cast.begin()
        cot_copy.wait()
        incoming = r.cot[...].astype(WIDE)
        grad, gain, shift = norm_back(incoming, normed, factor, shared[3:4])
        r.mixed[...] = grad
        low = grad.astype(LOW)
        r.rows_in[...] = low
        r.down_t[...] = turn(low, counts)
        r.small_total[0] = jnp.zeros((16, 768), WIDE)
        r.small_total[0, 3:4] = gain[None]
        r.small_total[0, 4:5] = shift[None]
        r.small_total[0, 5:6] = jnp.sum(grad, axis=0, keepdims=True)

    def inner_back(k):
        level = nearest_level(z, 3 - k)
        grad = (mul(r.rows_in[...], unit_weight(r, 2, level)) * r.slope[level].astype(WIDE)).astype(LOW)
        r.slope[level] = grad
        r.small_total[0, pl.ds(12 + level, 1)] = jnp.sum(grad.astype(WIDE), axis=0, keepdims=True)

    def make_down(k):
        level = nearest_level(z, 3 - k)
        red.produce(2 * k, [([(r.down_t, r.active[level])], slice(0, 768))])

    def make_up(k):
        level = nearest_level(z, 3 - k)
        red.produce(2 * k + 1, [([(r.hidden_t, r.slope[level])], slice(0, 768))])

    def first_norm_back():
        for level in range(4):
            r.mixed[...] += contract_last(r.slope[level], unit_weight(r, 1, level))
        grad, gain, shift = norm_back(r.mixed[...], r.normed_one[...], r.factor_one[...], r.shared[1:2])
        r.mixed[...] = grad
        low = grad.astype(LOW)
        r.hidden_in[...] = low
        r.joined_t[...] = turn(low, counts)
        r.small_total[0, 0:1] = jnp.sum(grad, axis=0, keepdims=True)
        r.small_total[0, 1:2] = gain[None]
        r.small_total[0, 2:3] = shift[None]

    def reload(k):
        return pltpu.make_async_copy(probs_out.at[k], r.probs.at[k], r.load_sem.at[4 + k])

    def attention_back(k):
        slot = 3 - k
        level = nearest_level(z, slot)
        queries, keys, values = r.qkv[level, :, :192], r.qkv[level, :, 192:384], r.qkv[level, :, 384:576]
        upstream = mul(r.hidden_in[...], unit_weight(r, 0, level)[:, 512:])[:, 64:].astype(LOW)
        if slot < 2:
            reload(slot).wait()
        grad_q = grad_k = grad_v = jnp.zeros((512, 192), WIDE)
        for head in range(3):
            probs = r.probs[slot % 2, head]
            up = upstream * head_mask(head, 1.0)
            grad_v = grad_v + contract_rows(probs, up)
            grad_probs = contract_last(up, values)
            wide = probs.astype(WIDE)
            weighed = wide * grad_probs
            grad_scores = (weighed - wide * jnp.sum(weighed, axis=-1, keepdims=True)).astype(LOW)
            grad_q = grad_q + mul(grad_scores, keys * head_mask(head, 0.125))
            grad_k = grad_k + contract_rows(grad_scores, queries * head_mask(head, 0.125))
        if slot >= 2:
            reload(slot - 2).start()
        r.qkv[level, :, :192] = grad_q.astype(LOW)
        r.qkv[level, :, 192:384] = grad_k.astype(LOW)
        r.qkv[level, :, 384:576] = grad_v.astype(LOW)
        r.qkv[level, :, 576:] = jnp.zeros((512, 64), LOW)
        r.small_total[0, pl.ds(8 + level, 1), :640] = jnp.sum(r.qkv[level].astype(WIDE), axis=0, keepdims=True)

    def make_project(k):
        level = nearest_level(z, 3 - k)
        red.produce(8 + k, [
            ([(r.rows_t, r.qkv[level, :, :512])], slice(0, 512)),
            ([(r.rows_t, r.qkv[level, :, 512:]), (r.joined_t, r.context[level])], slice(512, 768)),
        ])

    def input_back():
        for level in range(4):
            r.mixed[...] += contract_last(r.qkv[level], unit_weight(r, 0, level)[:, :640])
        grad = r.mixed[...]
        r.cot[:384] = (grad[:384] + mul(r.pick[...], grad[384:].astype(LOW))).astype(LOW)
        r.cot[384:] = grad[384:].astype(LOW)
        back_cast.begin()
        if ENDS_MAKE:
            when(end, lambda: next_tokens().start())

    steps = program_steps(net, red, text_cast, back_cast, (shared_sum, split_sum), [
        small_start, small_ready, prologue, attention, first_norm, feed, feed_sum, second_norm, inner_back, make_down, make_up, first_norm_back,
        attention_back, make_project, input_back,
        *[partial(at_ends, action) for action in (next_input, next_attention, next_norm, next_feed, next_end)],
    ])
    for i in ORDER:
        steps[i][0]()
    if ENDS_MAKE:
        when(end, lambda: next_text().wait())
    red.given(1).start()
    net.finish()
    text_cast.finish()
    back_cast.finish()
    red.finish()
    for i in range(2):
        red.given(i).wait()


def program_steps(net, red, text_cast, back_cast, small_sums, work):
    steps = []

    def add(action, *after):
        steps.append((action, after))
        return len(steps) - 1

    (small_start, small_ready, prologue, attention, first_norm, feed, feed_sum, second_norm, inner_back, make_down, make_up,
     first_norm_back, attention_back, make_project, input_back, next_input, next_attention, next_norm, next_feed, next_end) = work
    taken = {}
    for u, unit in enumerate(UNITS):
        step = [add(partial(net.relay, u))] if unit[1] else []
        step = add(partial(net.arrive, u), *step)
        step = add(partial(net.cross, u), step)
        step = add(partial(net.share, u), step)
        taken[unit] = add(partial(net.take, u), step)
    step = add(small_start)
    tiny = [add(partial(net.tiny_step, 0), step)]
    for i in (1, 2, 3):
        tiny.append(add(partial(net.tiny_step, i), tiny[-1]))
    step = add(prologue)
    for k in range(4):
        step = add(partial(attention, k), step, taken[0, k], tiny[3])
    step = add(first_norm, step, tiny[2])
    fed = []
    for k in range(4):
        step = add(partial(feed, k), step, taken[1, k])
        fed.append(step)
    for k in range(4):
        needs = [taken[2, i] for i in range(min(k + 2, 4))]
        step = add(partial(feed_sum, k), fed[min(k + 1, 3)], *needs, *[step] * (k > 0))
    step = started = add(second_norm, step, fed[3])
    made, joined = {}, {}

    def make(u, action, before):
        ahead = [made[u - 1], joined[u - 2]] if u >= 2 else [made[0]] if u else []
        made[u] = add(action, before, *ahead)
        joined[u] = add(partial(red.add_pair, u), made[u])

    inner = []
    for k in range(4):
        inner.append(add(partial(inner_back, k), started))
        make(2 * k, partial(make_down, k), started)
        make(2 * k + 1, partial(make_up, k), inner[k])
    step = add(first_norm_back, *inner)
    for k in range(4):
        step = add(partial(attention_back, k), step)
        make(8 + k, partial(make_project, k), step)
    ended = add(input_back, step)
    for u in range(12):
        step = add(partial(red.add_first, u), joined[u])
        step = add(partial(red.add_second, u), step)
        add(partial(red.add_line, u), step)
    for cast, begun in ((text_cast, started), (back_cast, ended)):
        for p in range(PIECES):
            add(partial(cast.near, p), begun)
            add(partial(cast.far, p), begun)
    if ENDS_MAKE:
        step = add(next_input, ended, *made.values())
        for level in range(4):
            step = add(partial(next_attention, level), step)
        step = add(next_norm, step)
        for level in range(4):
            step = add(partial(next_feed, level), step)
        add(next_end, step)
    step = add(small_ready, ended)
    for i in range(3):
        step = add(partial(red.small_step, i), step)
    add(partial(red.small_end, *small_sums), step)
    return steps


ORDER = (
    4, 57, 0, 58, 12, 13, 17, 1, 8, 14, 22, 27, 18, 37, 9, 2, 23, 32, 42, 59, 5, 15, 62, 19, 3, 38, 60, 61, 33,
    47, 16, 28, 63, 43, 52, 24, 6, 64, 20, 7, 10, 39, 48, 44, 53, 25, 21, 65, 49, 26, 66, 29, 40, 30, 54, 67, 68,
    31, 41, 45, 34, 35, 69, 50, 70, 55, 11, 46, 36, 72, 73, 51, 71, 56, 74, 75, 76, 78, 82, 77, 80, 87, 92, 97,
    147, 81, 79, 83, 85, 149, 151, 98, 84, 148, 153, 88, 150, 155, 101, 111, 157, 86, 152, 154, 89, 159, 104, 156,
    158, 107, 117, 160, 112, 110, 114, 90, 93, 123, 120, 161, 91, 94, 113, 162, 118, 95, 99, 165, 163, 115, 96,
    102, 100, 105, 126, 167, 171, 103, 108, 175, 164, 169, 168, 179, 180, 177, 166, 135, 173, 106, 172, 116, 124,
    176, 109, 170, 127, 181, 136, 138, 174, 178, 132, 119, 121, 125, 141, 137, 129, 122, 128, 139, 182, 144, 140,
    142, 143, 133, 134, 183, 145, 130, 131, 146,
)


def run_layer(attention, feedforward, shared, split, tokens, cotangent, align, count, mask):
    vmem = pl.BlockSpec(memory_space=pltpu.VMEM)
    smem = pl.BlockSpec(memory_space=pltpu.SMEM)
    hbm = pl.BlockSpec(memory_space=pl.ANY)
    whole = jax.ShapeDtypeStruct((3, 512, 768), LOW)
    return pl.pallas_call(
        layer_kernel,
        out_shape=(
            jax.ShapeDtypeStruct((96, 4, 192), WIDE),
            jax.ShapeDtypeStruct((96, 2, 768), WIDE),
            jax.ShapeDtypeStruct((6, 96), WIDE),
            jax.ShapeDtypeStruct((6, 192), WIDE),
            whole,
            whole,
            jax.ShapeDtypeStruct((2, 3, 512, 512), LOW),
        ),
        in_specs=[hbm, hbm, hbm, hbm, hbm, hbm, hbm, smem, hbm],
        out_specs=(hbm, hbm, vmem, vmem, hbm, hbm, hbm),
        scratch_shapes=[*buffers().values(), *flags().values()],
        compiler_params=pltpu.CompilerParams(
            collective_id=0, has_side_effects=True, vmem_limit_bytes=VMEM_LIMIT
        ),
        name="layer_step",
    )(attention, feedforward, shared, split, tokens, cotangent, align, count, mask)


VMEM_LIMIT = 63 * 2**20


def slab_rates(rates, shape):
    slab = lax.broadcasted_iota(jnp.int32, shape, 1)
    value = jnp.full(shape, rates[0], WIDE)
    for i, rate in enumerate(rates[1:]):
        value = jnp.where(slab == i + 1, rate, value)
    return value


def update_kernel(text_ref, back_ref, *refs):
    families, outs = refs[:16], refs[16:]
    outs[0][...] = text_ref[...]
    outs[1][...] = back_ref[...].astype(WIDE)
    shape = families[12].shape
    row = lax.broadcasted_iota(jnp.int32, shape, 0)
    split_rates = jnp.full(shape, SPLIT_RATES[2], WIDE)
    for i in (0, 1, 3, 4, 5):
        split_rates = jnp.where(row == i, SPLIT_RATES[i], split_rates)
    rates = (
        slab_rates(ATTENTION_RATES, families[0].shape),
        slab_rates(FEEDFORWARD_RATES, families[4].shape),
        SHARED_RATE,
        split_rates,
    )
    for i, rate in enumerate(rates):
        master, moment, average, gradient = (ref[...] for ref in families[4 * i : 4 * i + 4])
        for out, value in zip(outs[2 + 4 * i : 6 + 4 * i], renew(master, moment, average, gradient, rate)):
            out[...] = value


PARTS = 4


def run_update(text, back, families):
    rows, width = text.shape

    def split_rows(array):
        block = (array.shape[0] // PARTS, *array.shape[1:])
        return pl.BlockSpec(block, lambda i: (i,) + (0,) * (len(block) - 1))

    def at_once(array):
        return pl.BlockSpec(array.shape, lambda i: (0,) * len(array.shape))

    specs = [split_rows(text), split_rows(back)]
    shapes = [jax.ShapeDtypeStruct(text.shape, LOW), jax.ShapeDtypeStruct(back.shape, WIDE)]
    outs = list(specs)
    for i, family in enumerate(families):
        spec = split_rows(family[0]) if i < 2 else at_once(family[0])
        specs += [spec] * 4
        outs += [spec] * 4
        shapes += [jax.ShapeDtypeStruct(family[0].shape, kind) for kind in (WIDE, WIDE, WIDE, LOW)]
    return pl.pallas_call(
        update_kernel,
        grid=(PARTS,),
        in_specs=specs,
        out_specs=outs,
        out_shape=shapes,
        compiler_params=pltpu.CompilerParams(vmem_limit_bytes=VMEM_LIMIT),
        name="update_parameters",
    )(text, back, *[array for family in families for array in family])


def line_shards(
    tokens,
    alignment,
    segment_count,
    text_mask,
    cotangent,
    attention_master,
    attention_moment,
    attention_average,
    feedforward_master,
    feedforward_moment,
    feedforward_average,
    shared_master,
    shared_moment,
    shared_average,
    split_master,
    split_moment,
    split_average,
):
    rows, width = tokens.shape
    attention_sum, feedforward_sum, shared_sum, split_sum, text_all, back_all, _ = run_layer(
        attention_master, feedforward_master, shared_master.T, split_master.T,
        tokens, cotangent, alignment, segment_count, text_mask,
    )
    outs = run_update(
        text_all.reshape(rows, width),
        back_all.reshape(rows, width),
        (
            (attention_master, attention_moment, attention_average, attention_sum),
            (feedforward_master, feedforward_moment, feedforward_average, feedforward_sum),
            (shared_master.T, shared_moment.T, shared_average.T, shared_sum),
            (split_master.T, split_moment.T, split_average.T, split_sum),
        ),
    )
    return (*outs[:10], *[out.T for out in outs[10:]])


def solution(mesh):
    in_specs = (
        P("dp", None),
        P("dp", None),
        P("dp"),
        P("dp", None),
        P("dp", None),
        P("dp", None, "mp"),
        P("dp", None, "mp"),
        P("dp", None, "mp"),
        P("dp", None, "mp"),
        P("dp", None, "mp"),
        P("dp", None, "mp"),
        P("dp", None),
        P("dp", None),
        P("dp", None),
        P("mp", None),
        P("mp", None),
        P("mp", None),
    )
    out_specs = (
        P("dp", None),
        P("dp", None),
        P("dp", None, "mp"),
        P("dp", None, "mp"),
        P("dp", None, "mp"),
        P("dp", None, "mp"),
        P("dp", None, "mp"),
        P("dp", None, "mp"),
        P("dp", None, "mp"),
        P("dp", None, "mp"),
        P("dp", None),
        P("dp", None),
        P("dp", None),
        P("dp", None),
        P("mp", None),
        P("mp", None),
        P("mp", None),
        P("mp", None),
    )
    body = line_shards if mesh.shape["dp"] == 8 and mesh.shape["mp"] == 4 else general_shards
    return jax.shard_map(body, mesh=mesh, in_specs=in_specs, out_specs=out_specs, check_vma=False)
```

```python
from functools import partial
from types import SimpleNamespace

import jax
import jax.numpy as jnp
from jax import lax
from jax.experimental import pallas as pl
from jax.experimental.pallas import tpu as pltpu
from jax.sharding import PartitionSpec as P

MESH = pl.DeviceIdType.MESH

HEAD_DIM = 64


EPS = 1e-05
MOMENTUM = 0.9
AVERAGE = 0.75
ATTENTION_RATES = (4e-05, 4e-05, 4e-05, 0.01)
FEEDFORWARD_RATES = (0.0002, 4e-05)
SHARED_RATE = 0.0006
SPLIT_RATES = (0.0004, 0.0003, 0.0017, 0.0017, 0.0017, 0.0017)
HIGHEST_MODE = lax.Precision.HIGHEST


def contract_last(left, right):
    return lax.dot_general(
        left, right, (((1,), (1,)), ((), ())), preferred_element_type=jnp.float32
    )


def contract_rows(left, right):
    return lax.dot_general(
        left, right, (((0,), (0,)), ((), ())), preferred_element_type=jnp.float32
    )


def layer_norm(value, gain, shift):
    center = value - jnp.mean(value, axis=-1, keepdims=True)
    factor = lax.rsqrt(jnp.mean(center * center, axis=-1, keepdims=True) + EPS)
    normed = center * factor
    return (normed * gain + shift, normed, factor)


def norm_back(incoming, normed, factor, gain):
    scaled = incoming * gain
    inner_part = (
        scaled
        - jnp.mean(scaled, axis=-1, keepdims=True)
        - normed * jnp.mean(scaled * normed, axis=-1, keepdims=True)
    )
    return (factor * inner_part, jnp.sum(incoming * normed, axis=0), jnp.sum(incoming, axis=0))


def masked_scores(queries, key_rows, valid_keys):
    scores = jnp.einsum(
        "qhd,khd->hqk", queries, key_rows, preferred_element_type=jnp.float32
    ) * HEAD_DIM ** (-0.5)
    return jnp.where(valid_keys[None, None, :], scores, -1e30)


def attend(pieces):
    queries, key_rows, value_rows, valid_keys = pieces
    scores = masked_scores(queries, key_rows, valid_keys)
    row_max = jnp.max(scores, axis=-1, keepdims=True)
    exponent = jnp.exp(scores - row_max)
    row_total = jnp.sum(exponent, axis=-1, keepdims=True)
    probability = (exponent / row_total).astype(jnp.bfloat16)
    context = jnp.einsum(
        "hqk,khd->qhd", probability, value_rows, preferred_element_type=jnp.float32
    )
    return (context.astype(jnp.bfloat16), row_max + jnp.log(row_total))


def attend_back(pieces):
    queries, key_rows, value_rows, valid_keys, upstream, logsum = pieces
    scores = masked_scores(queries, key_rows, valid_keys)
    probability = jnp.exp(scores - logsum)
    grad_values = jnp.einsum(
        "hqk,qhd->khd",
        probability.astype(jnp.bfloat16),
        upstream,
        preferred_element_type=jnp.float32,
    )
    grad_probs = jnp.einsum(
        "qhd,khd->hqk", upstream, value_rows, preferred_element_type=jnp.float32
    )
    row_delta = jnp.sum(probability * grad_probs, axis=-1, keepdims=True)
    grad_scores = (probability * (grad_probs - row_delta)).astype(jnp.bfloat16)
    grad_queries = jnp.einsum(
        "hqk,khd->qhd", grad_scores, key_rows, preferred_element_type=jnp.float32
    ) * HEAD_DIM ** (-0.5)
    grad_keys = jnp.einsum(
        "hqk,qhd->khd", grad_scores, queries, preferred_element_type=jnp.float32
    ) * HEAD_DIM ** (-0.5)
    return (
        grad_queries.astype(jnp.bfloat16),
        grad_keys.astype(jnp.bfloat16),
        grad_values.astype(jnp.bfloat16),
    )


def renew(master, moment, average, gradient, rates):
    velocity = MOMENTUM * moment + gradient
    updated = master - rates * (gradient + MOMENTUM * velocity)
    averaged = AVERAGE * average + (1.0 - AVERAGE) * updated
    return (velocity, updated, averaged, updated.astype(jnp.bfloat16))


def general_shards(
    tokens,
    alignment,
    segment_count,
    text_mask,
    cotangent,
    attention_master,
    attention_moment,
    attention_average,
    feedforward_master,
    feedforward_moment,
    feedforward_average,
    shared_master,
    shared_moment,
    shared_average,
    split_master,
    split_moment,
    split_average,
):
    documents, slot_count = alignment.shape
    text_rows = text_mask.shape[1]
    document_rows = text_rows + slot_count
    model_width = tokens.shape[1]
    local_width = split_master.shape[0]
    local_heads = local_width // HEAD_DIM
    row_count = documents * document_rows
    attention_full, feedforward_full, shared_full = (
        lax.all_gather(attention_master.astype(jnp.bfloat16), "dp", axis=0, tiled=True),
        lax.all_gather(feedforward_master.astype(jnp.bfloat16), "dp", axis=0, tiled=True),
        lax.all_gather(shared_master.astype(jnp.bfloat16), "dp", axis=0, tiled=True),
    )
    shared = shared_full.astype(jnp.float32)
    split_bias = lax.optimization_barrier(split_master.astype(jnp.bfloat16)).astype(jnp.float32)
    live_slots = (
        lax.broadcasted_iota(jnp.int32, (documents, slot_count), 1) < segment_count[:, None]
    )
    valid_keys = jnp.concatenate([text_mask > 0, live_slots], axis=1)
    text_index = lax.broadcasted_iota(jnp.int32, (documents, slot_count, text_rows), 2)
    pick_table = ((alignment[:, :, None] == text_index) & live_slots[:, :, None]).astype(
        jnp.bfloat16
    )
    inputs = tokens.reshape(documents, document_rows, model_width)
    taken_rows = jnp.einsum(
        "dst,dtw->dsw", pick_table, inputs[:, :text_rows], preferred_element_type=jnp.float32
    )
    layer_in = jnp.concatenate(
        [
            inputs[:, :text_rows].astype(jnp.float32),
            inputs[:, text_rows:].astype(jnp.float32) + taken_rows,
        ],
        axis=1,
    ).reshape(row_count, model_width)
    rows_in = layer_in.astype(jnp.bfloat16)
    project_weights = attention_full[:, :3].reshape(model_width, 3 * local_width)
    project_bias = jnp.concatenate(
        [split_bias[:, 0], jnp.zeros_like(split_bias[:, 0]), split_bias[:, 1]]
    )
    projected = (
        jnp.dot(rows_in, project_weights, preferred_element_type=jnp.float32) + project_bias
    ).astype(jnp.bfloat16)
    projected = projected.reshape(documents, document_rows, 3, local_heads, HEAD_DIM)
    queries = projected[:, :, 0]
    key_rows = projected[:, :, 1]
    value_rows = projected[:, :, 2]
    context, logsum = lax.map(attend, (queries, key_rows, value_rows, valid_keys))
    context_rows = context.reshape(row_count, local_width)
    joined = lax.psum(
        contract_last(context_rows, attention_full[:, 3]).astype(jnp.bfloat16), "mp"
    ).astype(jnp.float32)
    mixed = layer_in + joined + shared[:, 0]
    first_norm, normed_one, factor_one = layer_norm(mixed, shared[:, 1], shared[:, 2])
    hidden_in = first_norm.astype(jnp.bfloat16)
    inner_pre = jnp.dot(
        hidden_in, feedforward_full[:, 0], preferred_element_type=jnp.float32
    ) + split_bias[:, 2:].reshape(-1)
    active = jax.nn.gelu(inner_pre, approximate=False).astype(jnp.bfloat16)
    down_sum = lax.psum(
        contract_last(active, feedforward_full[:, 1]).astype(jnp.bfloat16), "mp"
    ).astype(jnp.float32)
    second = first_norm + down_sum + shared[:, 5]
    output, normed_two, factor_two = layer_norm(second, shared[:, 3], shared[:, 4])
    grad_second, grad_gain_two, grad_shift_two = norm_back(
        cotangent.astype(jnp.float32), normed_two, factor_two, shared[:, 3]
    )
    grad_down = grad_second.astype(jnp.bfloat16)
    grad_active = jnp.dot(grad_down, feedforward_full[:, 1], preferred_element_type=jnp.float32)
    gelu_value, gelu_pull = jax.vjp(partial(jax.nn.gelu, approximate=False), inner_pre)
    grad_inner = gelu_pull(grad_active)[0].astype(jnp.bfloat16)
    feedforward_grad = jnp.stack(
        [contract_rows(hidden_in, grad_inner), contract_rows(grad_down, active)], axis=1
    )
    grad_first = grad_second + lax.psum(
        contract_last(grad_inner, feedforward_full[:, 0]).astype(jnp.bfloat16), "mp"
    ).astype(jnp.float32)
    grad_mixed, grad_gain_one, grad_shift_one = norm_back(
        grad_first, normed_one, factor_one, shared[:, 1]
    )
    grad_joined = grad_mixed.astype(jnp.bfloat16)
    output_grad = contract_rows(grad_joined, context_rows)
    grad_context = jnp.dot(
        grad_joined, attention_full[:, 3], preferred_element_type=jnp.float32
    ).astype(jnp.bfloat16)
    upstream = grad_context.reshape(documents, document_rows, local_heads, HEAD_DIM)
    grad_queries, grad_keys, grad_values = lax.map(
        attend_back, (queries, key_rows, value_rows, valid_keys, upstream, logsum)
    )
    query_rows = grad_queries.reshape(row_count, local_width)
    value_grad_rows = grad_values.reshape(row_count, local_width)
    grad_project = jnp.concatenate(
        [query_rows, grad_keys.reshape(row_count, local_width), value_grad_rows], axis=1
    )
    project_grad = contract_rows(rows_in, grad_project).reshape(model_width, 3, local_width)
    attention_grad = jnp.concatenate([project_grad, output_grad[:, None, :]], axis=1)
    grad_layer_in = grad_mixed + lax.psum(
        contract_last(grad_project, project_weights).astype(jnp.bfloat16), "mp"
    ).astype(jnp.float32)
    shared_grad = jnp.stack(
        [
            jnp.sum(grad_mixed, axis=0),
            grad_gain_one,
            grad_shift_one,
            grad_gain_two,
            grad_shift_two,
            jnp.sum(grad_second, axis=0),
        ],
        axis=1,
    )
    split_grad = jnp.concatenate(
        [
            jnp.sum(query_rows, axis=0, dtype=jnp.float32)[:, None],
            jnp.sum(value_grad_rows, axis=0, dtype=jnp.float32)[:, None],
            jnp.sum(grad_inner, axis=0, dtype=jnp.float32).reshape(local_width, 4),
        ],
        axis=1,
    )
    grad_documents = grad_layer_in.reshape(documents, document_rows, model_width)
    moved_rows = jnp.einsum(
        "dst,dsw->dtw",
        pick_table.astype(jnp.float32),
        grad_documents[:, text_rows:],
        precision=HIGHEST_MODE,
        preferred_element_type=jnp.float32,
    )
    input_gradient = jnp.concatenate(
        [grad_documents[:, :text_rows] + moved_rows, grad_documents[:, text_rows:]], axis=1
    ).reshape(row_count, model_width)
    attention_sum, feedforward_sum, shared_sum = (
        lax.psum_scatter(attention_grad, "dp", scatter_dimension=0, tiled=True),
        lax.psum_scatter(feedforward_grad, "dp", scatter_dimension=0, tiled=True),
        lax.psum_scatter(shared_grad, "dp", scatter_dimension=0, tiled=True),
    )
    split_sum = lax.psum(split_grad, "dp")
    attention_new = renew(
        attention_master,
        attention_moment,
        attention_average,
        attention_sum,
        jnp.asarray(ATTENTION_RATES, jnp.float32).reshape(1, 4, 1),
    )
    feedforward_new = renew(
        feedforward_master,
        feedforward_moment,
        feedforward_average,
        feedforward_sum,
        jnp.asarray(FEEDFORWARD_RATES, jnp.float32).reshape(1, 2, 1),
    )
    shared_new = renew(shared_master, shared_moment, shared_average, shared_sum, SHARED_RATE)
    split_new = renew(
        split_master,
        split_moment,
        split_average,
        split_sum,
        jnp.asarray(SPLIT_RATES, jnp.float32).reshape(1, 6),
    )
    return (
        output.astype(jnp.bfloat16),
        input_gradient,
        attention_new[0],
        attention_new[1],
        attention_new[2],
        attention_new[3],
        feedforward_new[0],
        feedforward_new[1],
        feedforward_new[2],
        feedforward_new[3],
        shared_new[0],
        shared_new[1],
        shared_new[2],
        shared_new[3],
        split_new[0],
        split_new[1],
        split_new[2],
        split_new[3],
    )


LOW = jnp.bfloat16
WIDE = jnp.float32
UNITS = [(0, 0), (1, 0), (2, 0), (0, 1), (0, 2), (0, 3)] + [(t, k) for k in range(1, 4) for t in (1, 2)]
AXES = (0, 1, 0, 1, 0, 1, 0, 0, 0, 1, 0, 1)
LINE = 4
INNER_LEVELS = (1, 2, 0, 3)
BACK_UNITS = [(t, k) for k in range(4) for t in (2, 1)] + [(0, k) for k in range(4)]
PIECES = 8
SENDS = 3
PAIRS = 4


def place():
    dp, z = lax.axis_index("dp"), lax.axis_index("mp")
    return z, lax.div(dp, 4), lax.rem(lax.div(dp, 2), 2), lax.rem(dp, 2)


def device(z, y, x, c):
    return (y * 4 + x * 2 + c, z)


def document_of(z):
    return lax.div(z + 1, 2)


def nearest_level(z, k):
    low, high = lax.rem(z, 2), lax.div(z, 2)
    if k == 0:
        return z
    if k == 1:
        return 1 + (2 * high - 1) * low
    if k == 2:
        return 2 + high * (1 - 2 * low)
    return 3 - 3 * high


def greet(z, y, x, c, meanwhile):
    barrier = pltpu.get_barrier_semaphore()
    partners = [device(z, y, x, 1 - c), device(z, y, 1 - x, c), device(z, 1 - y, x, c)]
    partners += [device(lax.rem(z + k, 4), y, x, c) for k in (1, 2, 3)]
    for partner in partners:
        pl.semaphore_signal(barrier, inc=1, device_id=partner, device_id_type=MESH)
    meanwhile()
    pl.semaphore_wait(barrier, len(partners))


def remote(source, target, send, recv, to):
    return pltpu.make_async_remote_copy(
        src_ref=source, dst_ref=target, send_sem=send, recv_sem=recv, device_id=to, device_id_type=MESH
    )


def when(condition, action):
    pl.when(condition)(action)


def mul(left, right):
    return jnp.dot(left, right, preferred_element_type=WIDE)


def gelu_parts(value):
    root = value * 0.7071067811865476
    inverse = 1.0 / (1.0 + 0.3275911 * jnp.abs(root))
    bell = jnp.exp(-root * root)
    series = 1.061405429
    for factor in (-1.453152027, 1.421413741, -0.284496736, 0.254829592):
        series = series * inverse + factor
    tail = 0.5 * series * inverse * bell
    share = jnp.where(value >= 0, 1.0 - tail, tail)
    return value * share, share + value * (bell * 0.3989422804014327)


def head_mask(head, scale, lanes=192):
    lane = lax.broadcasted_iota(jnp.int32, (1, lanes), 1)
    return jnp.where((lane >= head * HEAD_DIM) & (lane < (head + 1) * HEAD_DIM), scale, 0.0).astype(LOW)


def wide_product(left, right, width):
    value = mul(left, right)
    if right.shape[1] < width:
        value = jnp.concatenate([value, jnp.zeros((left.shape[0], width - right.shape[1]), WIDE)], axis=1)
    return value


def unit_weight(r, t, level):
    return r.full[t, level].reshape(768, 768)


class Gather:
    def __init__(self, r):
        self.own, self.small, self.r = r.own, r.small, r
        self.z, self.y, self.x, self.c = z, y, x, c = place()
        self.up, self.down = device(z + 1, y, x, c), device(z - 1, y, x, c)
        self.across_x, self.across_y = device(z, y, 1 - x, c), device(z, 1 - y, x, c)
        self.pair = device(z, y, x, 1 - c)
        self.end = (z == 0) | (z == LINE - 1)

    def line_copy(self, t, level, source, way):
        r = self.r
        return remote(
            source, r.full.at[t, level, self.y, self.x, self.c], r.sent.at[0],
            r.line_recv.at[t, level], self.up if way == 0 else self.down,
        )

    def along_x(self, u):
        return AXES[u] == 0

    def first(self, u):
        t, k = UNITS[u]
        block = self.r.full.at[t, nearest_level(self.z, k), self.y, self.x, self.c]
        return remote(
            self.own.at[t] if k == 0 else block, block, self.r.sent.at[1], self.r.first_recv.at[u],
            self.across_x if self.along_x(u) else self.across_y,
        )

    def second(self, u):
        t, k = UNITS[u]
        level = nearest_level(self.z, k)
        if self.along_x(u):
            block, to = self.r.full.at[t, level, self.y, :, self.c], self.across_y
        else:
            block, to = self.r.full.at[t, level, :, self.x, self.c], self.across_x
        return remote(block, block, self.r.sent.at[2], self.r.second_recv.at[u], to)

    def extra(self, u, level, part, way):
        t, y, x, c = UNITS[u][0], self.y, self.x, self.c
        if self.along_x(u):
            index = (t, level, y, 1 - x, c) if part == 0 else (t, level, 1 - y, slice(None), c)
        else:
            index = (t, level, 1 - y, x, c) if part == 0 else (t, level, slice(None), 1 - x, c)
        block = self.r.full.at[index]
        return remote(
            block, block, self.r.sent.at[4], self.r.extra_recv.at[t - 1, level],
            self.up if way == 0 else self.down,
        )

    def paired(self, u):
        t, k = UNITS[u]
        block = self.r.full.at[t, nearest_level(self.z, k), :, :, self.c]
        return remote(block, block, self.r.sent.at[3], self.r.pair_recv.at[u], self.pair)

    def own_copy(self, t):
        return pltpu.make_async_copy(
            self.own.at[t], self.r.full.at[t, self.z, self.y, self.x, self.c], self.r.own_sem.at[t]
        )

    def tiny_own(self, i):
        target = self.r.plane.at[self.y, self.x, self.c] if i == 0 else self.r.line.at[self.z]
        return pltpu.make_async_copy(self.small, target, self.r.own_sem.at[3 + i])

    def tiny(self, i):
        r = self.r
        if i == 0:
            block, to = r.plane.at[self.y, self.x, self.c], self.across_x
        elif i == 1:
            block, to = r.plane.at[self.y, :, self.c], self.across_y
        elif i == 2:
            block, to = r.plane.at[:, :, self.c], self.pair
        else:
            block, to = r.line.at[self.z], device(lax.rem(self.z + i - 2, 4), self.y, self.x, self.c)
        source = self.small if i == 0 or i > 2 else block
        return remote(source, block, r.tiny_send.at[i], r.tiny_recv.at[i], to)

    def own_line(self, t, act):
        when(self.z < 3, lambda: act(self.line_copy(t, self.z, self.own.at[t], 0)))
        when(self.z > 0, lambda: act(self.line_copy(t, self.z, self.own.at[t], 1)))

    def own_extra(self, u, part, act):
        when(self.z < 3, lambda: act(self.extra(u, self.z, part, 0)))
        when(self.z > 0, lambda: act(self.extra(u, self.z, part, 1)))

    def begin(self):
        self.own_line(0, lambda copy: copy.start())
        for t in range(3):
            self.own_copy(t).start()

    def begin_tiny(self):
        for i in range(2):
            self.tiny_own(i).start()
        for i in (0, 3, 4, 5):
            self.tiny(i).start()

    def crosses(self, u, act):
        t, k = UNITS[u]
        if t == 0 or k in (0, 3):
            act()
        elif k == 2:
            when(self.end, act)

    def comes_whole(self, u, act):
        t, k = UNITS[u]
        if t > 0 and k == 1:
            act()
        elif t > 0 and k == 2:
            when(jnp.logical_not(self.end), act)

    def relay(self, u):
        t, k = UNITS[u]
        level = nearest_level(self.z, k)
        block = self.r.full.at[t, level, self.y, self.x, self.c]

        def act():
            self.line_copy(t, level, block, 0).wait_recv()
            when(level < self.z, lambda: self.line_copy(t, level, block, 0).start())
            when(level > self.z, lambda: self.line_copy(t, level, block, 1).start())

        when(jnp.logical_not(self.end), act)

    def arrive(self, u):
        t, k = UNITS[u]
        if k == 0 and t > 0:
            self.own_line(t, lambda copy: copy.start())
        if k > 0:
            level = nearest_level(self.z, k)
            block = self.r.full.at[t, level, self.y, self.x, self.c]
            when(self.end, lambda: self.line_copy(t, level, block, 0).wait_recv())
        self.crosses(u, lambda: self.first(u).start())

    def cross(self, u):
        t, k = UNITS[u]

        def act():
            self.first(u).wait_recv()
            if k == 0:
                self.own_copy(t).wait()
            self.second(u).start()
            if t > 0 and k == 0:
                self.own_extra(u, 0, lambda copy: copy.start())

        self.crosses(u, act)

    def share(self, u):
        t, k = UNITS[u]
        level = nearest_level(self.z, k)

        def act():
            self.second(u).wait_recv()
            if t > 0 and k == 0:
                self.own_extra(u, 1, lambda copy: copy.start())
            self.paired(u).start()

        def act_whole():
            blocks = self.r.second_in.at[pl.ds(0, 3)]
            remote(blocks, blocks, self.r.sent.at[4], self.r.extra_recv.at[t - 1, level], self.up).wait_recv()
            self.paired(u).start()

        self.crosses(u, act)
        self.comes_whole(u, act_whole)

    def take(self, u):
        self.paired(u).wait_recv()

    def tiny_step(self, i):
        if i == 0:
            for j in range(2):
                self.tiny_own(j).wait()
        if i < 3:
            self.tiny(i).wait_recv()
        if i < 2:
            self.tiny(i + 1).start()
        if i == 3:
            for j in (3, 4, 5):
                self.tiny(j).wait_recv()

    def finish(self):
        r = self.r
        for i in range(6):
            self.tiny(i).wait_send()

        def all_sent(*counts):
            for i, count in enumerate(counts):
                if count == 15:
                    blocks = r.line_in
                elif count == 48:
                    blocks = r.total
                elif count in (16, 20):
                    blocks = r.first_in.at[pl.ds(0, count // 2)]
                else:
                    blocks = r.second_in.at[pl.ds(0, count)]
                remote(blocks, blocks, r.sent.at[i], r.pair_recv.at[0], self.pair).wait_send()

        when(self.end, lambda: all_sent(3, 10, 20, 48, 6))
        when(jnp.logical_not(self.end), lambda: all_sent(15, 8, 16, 48, 12))


class Reduce:
    def __init__(self, att_sum, ff_sum, r):
        self.att_sum, self.ff_sum, self.r = att_sum, ff_sum, r
        self.z, self.y, self.x, self.c = z, y, x, c = place()
        self.up, self.down = device(z + 1, y, x, c), device(z - 1, y, x, c)
        self.across_x, self.across_y = device(z, y, 1 - x, c), device(z, 1 - y, x, c)
        self.pair = device(z, y, x, 1 - c)

    def pair_copy(self, u):
        r = self.r
        return remote(
            r.sends.at[u % SENDS], r.pair_in.at[u % PAIRS], r.r_pair_send.at[u % SENDS], r.r_pair_recv.at[u % PAIRS],
            self.pair,
        )

    def first_copy(self, u):
        r = self.r
        source = r.total.at[u, :, 1 - self.x] if u % 2 == 0 else r.total.at[u, 1 - self.y]
        return remote(
            source, r.first_in.at[u], r.sent.at[5], r.r_first_recv.at[u],
            self.across_x if u % 2 == 0 else self.across_y,
        )

    def second_copy(self, u):
        r, x, y = self.r, self.x, self.y
        return remote(
            r.total.at[u, 1 - y, x] if u % 2 == 0 else r.total.at[u, y, 1 - x],
            r.second_in.at[u], r.sent.at[6], r.r_second_recv.at[u],
            self.across_y if u % 2 == 0 else self.across_x,
        )

    def line_copy(self, u, way):
        r = self.r
        t, k = BACK_UNITS[u]
        level = nearest_level(self.z, 3 - k)
        return remote(
            r.total.at[u, self.y, self.x], r.line_in.at[t, level + 1 - way], r.sent.at[7],
            r.r_line_recv.at[t, level + 1 - way], self.up if way == 0 else self.down,
        )

    def produce(self, u, parts):
        r = self.r
        if u >= SENDS:
            self.pair_copy(u - SENDS).wait_send()
        for half, target in ((1 - self.c, r.sends.at[u % SENDS]), (self.c, r.total.at[u])):
            for products, lanes in parts:
                width = lanes.stop - lanes.start
                value = sum(wide_product(turned[:, :, half].reshape(384, 512), columns, width) for turned, columns in products)
                target[:, :, :, lanes] = value.astype(LOW).reshape(2, 2, 96, width)
            if half is not self.c:
                self.pair_copy(u).start()

    def add_pair(self, u):
        r = self.r
        self.pair_copy(u).wait_recv()
        r.total[u] = r.total[u] + r.pair_in[u % PAIRS]
        self.first_copy(u).start()

    def add_first(self, u):
        r, x, y = self.r, self.x, self.y
        self.first_copy(u).wait_recv()
        if u % 2 == 0:
            r.total[u, :, x] = r.total[u, :, x] + r.first_in[u]
        else:
            r.total[u, y] = r.total[u, y] + r.first_in[u]
        self.second_copy(u).start()

    def add_second(self, u):
        r, x, y, z = self.r, self.x, self.y, self.z
        t, k = BACK_UNITS[u]
        level = nearest_level(z, 3 - k)
        self.second_copy(u).wait_recv()
        r.total[u, y, x] = r.total[u, y, x] + r.second_in[u]
        if k < 3:
            when((z == 0) | (z == 3), lambda: self.send_line(u))

    def send_line(self, u):
        level = nearest_level(self.z, 3 - BACK_UNITS[u][1])
        when(self.z < level, lambda: self.line_copy(u, 0).start())
        when(self.z > level, lambda: self.line_copy(u, 1).start())

    def take_line(self, u, way):
        r, x, y = self.r, self.x, self.y
        t, k = BACK_UNITS[u]
        level = nearest_level(self.z, 3 - k)
        self.line_copy(u, way).wait_recv()
        r.total[u, y, x] = r.total[u, y, x] + r.line_in[t, level + 1 - way]

    def add_line(self, u):
        r, z = self.r, self.z
        t, k = BACK_UNITS[u]
        level = nearest_level(z, 3 - k)
        middle = (z == 1) | (z == 2)
        if k < 3:
            when(middle & (z < level), lambda: self.take_line(u, 0))
            when(middle & (z > level), lambda: self.take_line(u, 1))
            when(middle, lambda: self.send_line(u))
        else:
            when(z > 0, lambda: self.take_line(u, 0))
            when(z < 3, lambda: self.take_line(u, 1))
            self.give(t, r.total[u, self.y, self.x])

    def give(self, t, value):
        r = self.r
        if t == 0:
            for slab in range(4):
                r.att_in[:, slab, :] = value[:, slab * 192 : (slab + 1) * 192].astype(WIDE)
            self.given(0).start()
        else:
            r.ff_in[:, t - 1, :] = value.astype(WIDE)

    def given(self, i):
        source, target = ((self.r.att_in, self.att_sum), (self.r.ff_in, self.ff_sum))[i]
        return pltpu.make_async_copy(source, target, self.r.load_sem.at[6 + i])

    def small_copy(self, i):
        r = self.r
        if i < 3:
            to = (self.pair, self.across_x, self.across_y)[i]
            return remote(r.small_total.at[i], r.small_in.at[i], r.small_send.at[i], r.small_recv.at[i], to)
        to = device(lax.rem(self.z + i - 2, 4), self.y, self.x, self.c)
        return remote(r.small_total.at[3], r.small_line.at[self.z], r.small_send.at[i], r.small_recv.at[i], to)

    def small_step(self, i):
        r = self.r
        self.small_copy(i).wait_recv()
        r.small_total[i + 1] = r.small_total[i] + r.small_in[i]
        if i < 2:
            self.small_copy(i + 1).start()
        else:
            for j in (3, 4, 5):
                self.small_copy(j).start()
            r.small_line[self.z] = r.small_total[3]

    def small_end(self, shared_sum, split_sum):
        r, z = self.r, self.z
        for i in (3, 4, 5):
            self.small_copy(i).wait_recv()
        r.small_sum[...] = r.small_line[0] + r.small_line[1] + r.small_line[2] + r.small_line[3]
        index = self.y * 4 + self.x * 2 + self.c
        shared_sum[...] = pltpu.roll(r.small_sum[:8], lax.rem(768 - index * 96, 768), 1)[:6, :96]
        biases = r.small_sum[pl.ds(8 + z, 1)]
        split_sum[0:1] = biases[:, :192]
        split_sum[1:2] = biases[:, 384:576]
        inner = r.small_sum[pl.ds(12 + z, 1)]
        for j in range(4):
            split_sum[2 + j : 3 + j] = inner[:, j * 192 : (j + 1) * 192]

    def finish(self):
        for i in range(6):
            self.small_copy(i).wait_send()
        for u in range(len(BACK_UNITS) - SENDS, len(BACK_UNITS)):
            self.pair_copy(u).wait_send()
        r = self.r
        for i, blocks in ((5, r.first_in), (6, r.second_in), (7, r.second_in.at[pl.ds(0, 9)])):
            remote(blocks, blocks, r.sent.at[i], r.r_pair_recv.at[0], self.pair).wait_send()


class Cast:
    def __init__(self, a, source, target, r):
        self.a, self.source, self.target, self.r = a, source, target, r
        self.z, y, x, c = place()
        self.up, self.down = device(self.z + 1, y, x, c), device(self.z - 1, y, x, c)

    def copy(self, d, p, way, first):
        r = self.r
        part = pl.ds(p * (512 // PIECES), 512 // PIECES)
        target = self.target.at[d, part]
        return remote(
            self.source.at[part] if first else target, target, r.cast_send.at[self.a],
            r.cast_recv.at[self.a, 16 if d == 1 else d * 4 + p], self.up if way == 0 else self.down,
        )

    def own(self):
        return pltpu.make_async_copy(self.source, self.target.at[document_of(self.z)], self.r.cast_own.at[self.a])

    def firsts(self, p, act):
        for level, d, way in ((0, 0, 0), (1, 1, 1), (2, 1, 0), (3, 2, 1)):
            when(self.z == level, lambda d=d, way=way: act(self.copy(d, p, way, True)))

    def begin(self):
        self.own().start()
        for p in range(PIECES):
            self.firsts(p, lambda copy: copy.start())

    def pass_on(self, d, p, way):
        copy = self.copy(d, p, way, False)
        copy.wait_recv()
        copy.start()

    def near(self, p):
        when(self.z == 1, lambda: self.pass_on(0, p, 0))
        when(self.z == 2, lambda: self.pass_on(2, p, 1))

    def far(self, p):
        when(self.z == 1, lambda: self.pass_on(2, p, 1))
        when(self.z == 2, lambda: self.pass_on(0, p, 0))

    def finish(self):
        r = self.r
        self.own().wait()
        for level, d, way in ((0, 2, 1), (3, 0, 0)):
            for p in range(PIECES):
                when(self.z == level, lambda p=p, d=d, way=way: self.copy(d, p, way, False).wait_recv())

        def wait(blocks, act):
            act(remote(blocks, blocks, r.cast_send.at[self.a], r.cast_recv.at[self.a, 16], self.up))

        end = (self.z == 0) | (self.z == 3)
        when(end, lambda: wait(self.target.at[1], lambda copy: copy.wait_recv()))
        when(end, lambda: wait(self.source, lambda copy: copy.wait_send()))
        when(jnp.logical_not(end), lambda: wait(self.target, lambda copy: copy.wait_send()))


def buffers():
    vmem = pltpu.VMEM
    return dict(
        full=vmem((3, 4, 2, 2, 2, 96, 768), LOW),
        plane=vmem((2, 2, 2, 16, 768), LOW),
        line=vmem((4, 16, 768), LOW),
        tok=vmem((512, 768), LOW),
        cot=vmem((512, 768), LOW),
        pick=vmem((384, 128), LOW),
        rows_in=vmem((512, 768), LOW),
        hidden_in=vmem((512, 768), LOW),
        rows_t=vmem((2, 2, 2, 96, 512), LOW),
        hidden_t=vmem((2, 2, 2, 96, 512), LOW),
        down_t=vmem((2, 2, 2, 96, 512), LOW),
        joined_t=vmem((2, 2, 2, 96, 512), LOW),
        qkv=vmem((4, 512, 640), LOW),
        probs=vmem((2, 3, 512, 512), LOW),
        context=vmem((4, 512, 256), LOW),
        active=vmem((4, 512, 768), LOW),
        slope=vmem((4, 512, 768), LOW),
        mixed=vmem((512, 768), WIDE),
        bar=vmem((1, 512), WIDE),
        normed_one=vmem((512, 768), WIDE),
        factor_one=vmem((512, 1), WIDE),
        total=vmem((12, 2, 2, 96, 768), LOW),
        sends=vmem((SENDS, 2, 2, 96, 768), LOW),
        pair_in=vmem((PAIRS, 2, 2, 96, 768), LOW),
        first_in=vmem((12, 2, 96, 768), LOW),
        second_in=vmem((12, 96, 768), LOW),
        line_in=vmem((3, 5, 96, 768), LOW),
        small_total=vmem((4, 16, 768), WIDE),
        small_in=vmem((3, 16, 768), WIDE),
        small_line=vmem((4, 16, 768), WIDE),
        small_sum=vmem((16, 768), WIDE),
        shared=vmem((16, 768), WIDE),
        own=vmem((3, 96, 768), LOW),
        att_in=vmem((96, 4, 192), WIDE),
        ff_in=vmem((96, 2, 768), WIDE),
        shared_in=vmem((6, 96), WIDE),
        split_in=vmem((6, 192), WIDE),
        align_in=vmem((3, 128), jnp.int32),
        mask_in=vmem((3, 384), jnp.int32),
        small=vmem((16, 768), LOW),
    )


def flags():
    dma = pltpu.SemaphoreType.DMA
    return dict(
        sent=dma((8,)),
        line_recv=dma((3, 4)),
        first_recv=dma((12,)),
        second_recv=dma((12,)),
        pair_recv=dma((12,)),
        tiny_send=dma((6,)),
        tiny_recv=dma((6,)),
        extra_recv=dma((2, 4)),
        own_sem=dma((5,)),
        load_sem=dma((12,)),
        r_pair_send=dma((SENDS,)),
        r_pair_recv=dma((PAIRS,)),
        r_first_recv=dma((12,)),
        r_second_recv=dma((12,)),
        r_line_recv=dma((3, 5)),
        small_send=dma((6,)),
        small_recv=dma((6,)),
        cast_send=dma((2,)),
        cast_recv=dma((2, 17)),
        cast_own=dma((2,)),
    )


def spread(j):
    unit = lax.broadcasted_iota(jnp.int32, (192, 768), 1)
    return jnp.where(unit == 4 * lax.broadcasted_iota(jnp.int32, (192, 768), 0) + j, 1.0, 0.0).astype(LOW)


def turn(value, counts):
    return (value * counts.astype(LOW)).T.reshape(2, 2, 2, 96, 512)


def layer_kernel(
    att_ref, ff_ref, shared_ref, split_ref, tokens_ref, cotangent_ref, align_ref, count_ref, mask_ref,
    att_sum, ff_sum, shared_sum, split_sum, text_all, back_all, probs_out, *refs,
):
    r = SimpleNamespace(**dict(zip([*buffers(), *flags()], refs)))
    z, y, x, c = place()
    doc = document_of(z)
    counts = jnp.where(z == 2, 0.0, 1.0)
    tok_copy = pltpu.make_async_copy(tokens_ref.at[pl.ds(doc * 512, 512)], r.tok, r.load_sem.at[0])
    cot_copy = pltpu.make_async_copy(cotangent_ref.at[pl.ds(doc * 512, 512)], r.cot, r.load_sem.at[1])
    tok_copy.start()
    cot_copy.start()
    operands = (
        (att_ref, r.att_in), (ff_ref, r.ff_in), (shared_ref, r.shared_in), (split_ref, r.split_in),
        (align_ref, r.align_in), (mask_ref, r.mask_in),
    )
    loads = [pltpu.make_async_copy(source, target, r.load_sem.at[6 + i]) for i, (source, target) in enumerate(operands)]
    for copy in loads:
        copy.start()

    def cast_own():
        loads[0].wait()
        for slab in range(4):
            r.own[0, :, slab * 192 : (slab + 1) * 192] = r.att_in[:, slab, :].astype(LOW)
        loads[1].wait()
        for t in (1, 2):
            r.own[t] = r.ff_in[:, t - 1, :].astype(LOW)
        for copy in loads[2:]:
            copy.wait()

    greet(z, y, x, c, cast_own)
    net = Gather(r)
    net.begin()

    def small_start():
        r.small_sum[...] = jnp.zeros((16, 768), WIDE)
        r.small_sum[:6, :96] = r.shared_in[...]
        shared = pltpu.roll(r.small_sum[:8], (y * 4 + x * 2 + c) * 96, 1)
        r.small_sum[8:14, :192] = r.split_in[...]
        units = r.small_sum[8:16, :192].astype(LOW)
        inner = sum(mul(units, spread(j))[2 + j : 3 + j] for j in range(4))
        r.small_sum[:8] = shared
        r.small_sum[6:7] = jnp.zeros((1, 768), WIDE)
        r.small_sum[6:7, :192] = r.split_in[0:1]
        r.small_sum[6:7, 384:576] = r.split_in[1:2]
        r.small_sum[7:8] = inner
        r.small[...] = r.small_sum[...].astype(LOW)
        net.begin_tiny()

    def small_ready():
        value = r.small_total[0, 8:16]
        high = value.astype(LOW)
        rest = value - high.astype(WIDE)
        middle = rest.astype(LOW)
        last = (rest - middle.astype(WIDE)).astype(LOW)
        for j in range(4):
            packed = sum(contract_last(piece, spread(j)) for piece in (last, middle, high))
            r.small_total[0, 12:16, j * 192 : (j + 1) * 192] = packed[4:8]
        r.small_total[0] = r.small_total[0] * counts
        red.small_copy(0).start()

    def input_rows(tok, document):
        live = lax.broadcasted_iota(jnp.int32, (1, 128), 1) < count_ref[document]
        pick = jnp.where(
            (lax.broadcasted_iota(jnp.int32, (384, 128), 0) == r.align_in[pl.ds(document, 1), :]) & live, 1.0, 0.0
        ).astype(LOW)
        text_tokens = tok[:384]
        taken = lax.dot_general(pick, text_tokens, (((0,), (0,)), ((), ())), preferred_element_type=WIDE)
        slot_rows = tok[384:].astype(WIDE) + taken
        r.mixed[:384] = text_tokens.astype(WIDE)
        r.mixed[384:] = slot_rows
        r.rows_in[:384] = text_tokens
        r.rows_in[384:] = slot_rows.astype(LOW)
        r.bar[...] = jnp.where(jnp.concatenate([r.mask_in[pl.ds(document, 1), :] > 0, live], axis=1), 0.0, -1e30)
        return pick

    def prologue():
        tok_copy.wait()
        r.pick[...] = input_rows(r.tok, doc)
        r.rows_t[...] = turn(r.rows_in[...], counts)

    def spill(k):
        return pltpu.make_async_copy(r.probs.at[k % 2], probs_out.at[k % 2], r.load_sem.at[2 + k % 2])

    def projected_rows(level):
        bias = r.line[level][6:7].astype(WIDE)
        return (mul(r.rows_in[...], unit_weight(r, 0, level)) + bias).astype(LOW)

    def attend_level(projected, level, keep):
        queries, keys, values = projected[:, :192], projected[:, 192:384], projected[:, 384:640]
        context = jnp.zeros((512, 256), WIDE)
        for head in range(3):
            scores = contract_last(queries * head_mask(head, 0.125), keys)
            scores = jnp.where(r.bar[...] < 0.0, -1e30, scores)
            raised = jnp.exp(scores - jnp.max(scores, axis=-1, keepdims=True))
            probs = (raised * (1.0 / jnp.sum(raised, axis=-1, keepdims=True))).astype(LOW)
            keep[head] = probs
            context = context + mul(probs, values * head_mask(head, 1.0, 256))
        r.context[level] = pltpu.roll(context, 64, 1).astype(LOW)

    def attention(k):
        level = nearest_level(z, k)
        projected = projected_rows(level)
        r.qkv[level] = projected[:, :640]
        if k >= 2:
            spill(k).wait()
        attend_level(projected, level, r.probs.at[k % 2])
        if k < 2:
            spill(k).start()

    def norm_rows():
        for level in range(4):
            r.mixed[...] += contract_last(r.context[level], unit_weight(r, 0, level)[:, 512:])
        shared = r.shared[...]
        rows, normed, factor = layer_norm(r.mixed[...] + shared[0:1], shared[1:2], shared[2:3])
        r.hidden_in[...] = rows.astype(LOW)
        r.mixed[...] = rows + shared[5:6]
        return normed, factor

    def first_norm():
        r.shared[...] = jnp.sum(r.plane[...].astype(WIDE).reshape(8, 16, 768), axis=0)
        normed, factor = norm_rows()
        r.normed_one[...] = normed
        r.factor_one[...] = factor
        r.hidden_t[...] = turn(r.hidden_in[...], counts)

    def feed_level(level, keep_slope):
        bias = r.line[level][7:8, :].astype(WIDE)
        up = unit_weight(r, 1, level)
        for part in range(3):
            lanes = slice(part * 256, (part + 1) * 256)
            inner = mul(r.hidden_in[...], up[:, lanes]) + bias[:, lanes]
            active, slope = gelu_parts(inner)
            r.active[level, :, lanes] = active.astype(LOW)
            if keep_slope:
                r.slope[level, :, lanes] = slope.astype(LOW)

    def feed(k):
        feed_level(nearest_level(z, k), True)

    def feed_sum(k):
        level = jnp.where(net.end, nearest_level(z, k), INNER_LEVELS[k])
        r.mixed[...] += contract_last(r.active[level], unit_weight(r, 2, level))

    text_cast = Cast(0, r.tok, text_all, r)
    back_cast = Cast(1, r.cot, back_all, r)
    red = Reduce(att_sum, ff_sum, r)

    def second_norm():
        shared = r.shared[...]
        final, normed, factor = layer_norm(r.mixed[...], shared[3:4], shared[4:5])
        r.tok[...] = final.astype(LOW)
        text_cast.begin()
        cot_copy.wait()
        incoming = r.cot[...].astype(WIDE)
        grad, gain, shift = norm_back(incoming, normed, factor, shared[3:4])
        r.mixed[...] = grad
        low = grad.astype(LOW)
        r.rows_in[...] = low
        r.down_t[...] = turn(low, counts)
        r.small_total[0] = jnp.zeros((16, 768), WIDE)
        r.small_total[0, 3:4] = gain[None]
        r.small_total[0, 4:5] = shift[None]
        r.small_total[0, 5:6] = jnp.sum(grad, axis=0, keepdims=True)

    def inner_back(k):
        level = nearest_level(z, 3 - k)
        grad = (mul(r.rows_in[...], unit_weight(r, 2, level)) * r.slope[level].astype(WIDE)).astype(LOW)
        r.slope[level] = grad
        r.small_total[0, pl.ds(12 + level, 1)] = jnp.sum(grad.astype(WIDE), axis=0, keepdims=True)

    def make_down(k):
        level = nearest_level(z, 3 - k)
        red.produce(2 * k, [([(r.down_t, r.active[level])], slice(0, 768))])

    def make_up(k):
        level = nearest_level(z, 3 - k)
        red.produce(2 * k + 1, [([(r.hidden_t, r.slope[level])], slice(0, 768))])

    def first_norm_back():
        for level in range(4):
            r.mixed[...] += contract_last(r.slope[level], unit_weight(r, 1, level))
        grad, gain, shift = norm_back(r.mixed[...], r.normed_one[...], r.factor_one[...], r.shared[1:2])
        r.mixed[...] = grad
        low = grad.astype(LOW)
        r.hidden_in[...] = low
        r.joined_t[...] = turn(low, counts)
        r.small_total[0, 0:1] = jnp.sum(grad, axis=0, keepdims=True)
        r.small_total[0, 1:2] = gain[None]
        r.small_total[0, 2:3] = shift[None]

    def reload(k):
        return pltpu.make_async_copy(probs_out.at[k], r.probs.at[k], r.load_sem.at[4 + k])

    def attention_back(k):
        slot = 3 - k
        level = nearest_level(z, slot)
        queries, keys, values = r.qkv[level, :, :192], r.qkv[level, :, 192:384], r.qkv[level, :, 384:576]
        upstream = mul(r.hidden_in[...], unit_weight(r, 0, level)[:, 512:])[:, 64:].astype(LOW)
        if slot < 2:
            reload(slot).wait()
        grad_q = grad_k = grad_v = jnp.zeros((512, 192), WIDE)
        for head in range(3):
            probs = r.probs[slot % 2, head]
            up = upstream * head_mask(head, 1.0)
            grad_v = grad_v + contract_rows(probs, up)
            grad_probs = contract_last(up, values)
            wide = probs.astype(WIDE)
            weighed = wide * grad_probs
            grad_scores = (weighed - wide * jnp.sum(weighed, axis=-1, keepdims=True)).astype(LOW)
            grad_q = grad_q + mul(grad_scores, keys * head_mask(head, 0.125))
            grad_k = grad_k + contract_rows(grad_scores, queries * head_mask(head, 0.125))
        if slot >= 2:
            reload(slot - 2).start()
        r.qkv[level, :, :192] = grad_q.astype(LOW)
        r.qkv[level, :, 192:384] = grad_k.astype(LOW)
        r.qkv[level, :, 384:576] = grad_v.astype(LOW)
        r.qkv[level, :, 576:] = jnp.zeros((512, 64), LOW)
        r.small_total[0, pl.ds(8 + level, 1), :640] = jnp.sum(r.qkv[level].astype(WIDE), axis=0, keepdims=True)

    def make_project(k):
        level = nearest_level(z, 3 - k)
        red.produce(8 + k, [
            ([(r.rows_t, r.qkv[level, :, :512])], slice(0, 512)),
            ([(r.rows_t, r.qkv[level, :, 512:]), (r.joined_t, r.context[level])], slice(512, 768)),
        ])

    def input_back():
        for level in range(4):
            r.mixed[...] += contract_last(r.qkv[level], unit_weight(r, 0, level)[:, :640])
        grad = r.mixed[...]
        r.cot[:384] = (grad[:384] + mul(r.pick[...], grad[384:].astype(LOW))).astype(LOW)
        r.cot[384:] = grad[384:].astype(LOW)
        back_cast.begin()

    steps = program_steps(net, red, text_cast, back_cast, (shared_sum, split_sum), [
        small_start, small_ready, prologue, attention, first_norm, feed, feed_sum, second_norm, inner_back, make_down, make_up, first_norm_back,
        attention_back, make_project, input_back,
    ])
    for i in ORDER:
        steps[i][0]()
    red.given(1).start()
    net.finish()
    text_cast.finish()
    back_cast.finish()
    red.finish()
    for i in range(2):
        red.given(i).wait()


def program_steps(net, red, text_cast, back_cast, small_sums, work):
    steps = []

    def add(action, *after):
        steps.append((action, [i for group in after for i in (group if isinstance(group, tuple) else (group,))]))
        return len(steps) - 1

    inner = jnp.logical_not(net.end)

    def add_each(action, *after):
        def side(i):
            return [group[i] if isinstance(group, tuple) else group for group in after]

        return (
            add(partial(when, net.end, action), *side(0)),
            add(partial(when, inner, action), *side(1)),
        )

    (small_start, small_ready, prologue, attention, first_norm, feed, feed_sum, second_norm, inner_back, make_down, make_up,
     first_norm_back, attention_back, make_project, input_back) = work
    taken = {}
    for u, unit in enumerate(UNITS):
        step = [add(partial(net.relay, u))] if unit[1] else []
        step = add_each(partial(net.arrive, u), *step)
        step = add_each(partial(net.cross, u), step)
        step = add_each(partial(net.share, u), step)
        taken[unit] = add_each(partial(net.take, u), step)
    step = add(small_start)
    tiny = [add(partial(net.tiny_step, 0), step)]
    for i in (1, 2, 3):
        tiny.append(add(partial(net.tiny_step, i), tiny[-1]))
    step = add(prologue)
    for k in range(4):
        step = add(partial(attention, k), step, taken[0, k], tiny[3])
    step = add(first_norm, step, tiny[2])
    fed = []
    for k in range(4):
        step = add(partial(feed, k), step, taken[1, k])
        fed.append(step)
    for k in range(4):
        needs = [taken[2, i] for i in range(min(k + 2, 4))]
        step = add(partial(feed_sum, k), fed[min(k + 1, 3)], *needs, *[step] * (k > 0))
    step = started = add(second_norm, step, fed[3])
    made, joined = {}, {}

    def make(u, action, before):
        ahead = [made[u - 1], joined[u - 2]] if u >= 2 else [made[0]] if u else []
        made[u] = add(action, before, *ahead)
        joined[u] = add_each(partial(red.add_pair, u), made[u])

    inners = []
    for k in range(4):
        inners.append(add(partial(inner_back, k), started))
        make(2 * k, partial(make_down, k), started)
        make(2 * k + 1, partial(make_up, k), inners[k])
    step = add(first_norm_back, *inners)
    for k in range(4):
        step = add(partial(attention_back, k), step)
        make(8 + k, partial(make_project, k), step)
    ended = add(input_back, step)
    for u in range(12):
        step = add_each(partial(red.add_first, u), joined[u])
        step = add_each(partial(red.add_second, u), step)
        add_each(partial(red.add_line, u), step)
    for cast, begun in ((text_cast, started), (back_cast, ended)):
        for p in range(PIECES):
            add(partial(cast.near, p), begun)
            add(partial(cast.far, p), begun)
    step = add(small_ready, ended)
    for i in range(3):
        step = add(partial(red.small_step, i), step)
    add(partial(red.small_end, *small_sums), step)
    return steps


ORDER = (
    8, 9, 105, 0, 1, 106, 24, 26, 25, 16, 33, 35, 107, 17, 3, 28, 42, 69, 44, 10, 51, 2, 34, 18, 71, 60, 27, 78,
    43, 5, 4, 12, 36, 11, 52, 37, 110, 46, 70, 87, 62, 6, 30, 45, 108, 96, 29, 64, 19, 79, 98, 109, 61, 7, 111,
    32, 31, 14, 89, 39, 13, 20, 53, 63, 54, 88, 72, 38, 112, 47, 97, 41, 81, 40, 113, 48, 21, 55, 80, 100, 15, 73,
    91, 75, 49, 57, 90, 50, 114, 23, 115, 82, 84, 56, 59, 77, 99, 22, 74, 66, 83, 116, 102, 93, 58, 117, 65, 76,
    92, 118, 101, 67, 104, 68, 95, 86, 120, 85, 121, 94, 119, 103, 122, 123, 124, 139, 125, 126, 129, 146, 132,
    153, 128, 127, 133, 130, 243, 154, 245, 134, 135, 131, 247, 136, 244, 140, 249, 158, 246, 251, 138, 171, 248,
    253, 137, 162, 250, 141, 255, 178, 252, 166, 254, 173, 184, 177, 142, 143, 183, 172, 257, 256, 170, 144, 275,
    175, 189, 145, 147, 150, 190, 174, 176, 276, 196, 149, 261, 148, 155, 259, 151, 152, 159, 202, 277, 258, 157,
    156, 185, 163, 265, 267, 260, 160, 269, 161, 179, 186, 164, 219, 191, 167, 262, 263, 195, 187, 180, 273, 278,
    168, 270, 165, 268, 266, 214, 220, 274, 182, 221, 271, 231, 225, 201, 207, 169, 264, 197, 213, 227, 198, 203,
    193, 188, 200, 226, 237, 272, 204, 232, 222, 224, 192, 216, 233, 194, 228, 199, 238, 215, 217, 208, 206, 279,
    234, 236, 235, 230, 210, 212, 209, 211, 229, 239, 218, 181, 240, 223, 205, 242, 241,
)


def run_layer(attention, feedforward, shared, split, tokens, cotangent, align, count, mask):
    vmem = pl.BlockSpec(memory_space=pltpu.VMEM)
    smem = pl.BlockSpec(memory_space=pltpu.SMEM)
    hbm = pl.BlockSpec(memory_space=pl.ANY)
    whole = jax.ShapeDtypeStruct((3, 512, 768), LOW)
    return pl.pallas_call(
        layer_kernel,
        out_shape=(
            jax.ShapeDtypeStruct((96, 4, 192), WIDE),
            jax.ShapeDtypeStruct((96, 2, 768), WIDE),
            jax.ShapeDtypeStruct((6, 96), WIDE),
            jax.ShapeDtypeStruct((6, 192), WIDE),
            whole,
            whole,
            jax.ShapeDtypeStruct((2, 3, 512, 512), LOW),
        ),
        in_specs=[hbm, hbm, hbm, hbm, hbm, hbm, hbm, smem, hbm],
        out_specs=(hbm, hbm, vmem, vmem, hbm, hbm, hbm),
        scratch_shapes=[*buffers().values(), *flags().values()],
        compiler_params=pltpu.CompilerParams(
            collective_id=0, has_side_effects=True, vmem_limit_bytes=VMEM_LIMIT
        ),
        name="layer_step",
    )(attention, feedforward, shared, split, tokens, cotangent, align, count, mask)


VMEM_LIMIT = 63 * 2**20


def slab_rates(rates, shape):
    slab = lax.broadcasted_iota(jnp.int32, shape, 1)
    value = jnp.full(shape, rates[0], WIDE)
    for i, rate in enumerate(rates[1:]):
        value = jnp.where(slab == i + 1, rate, value)
    return value


def update_kernel(text_ref, back_ref, *refs):
    families, outs = refs[:16], refs[16:]
    outs[0][...] = text_ref[...]
    outs[1][...] = back_ref[...].astype(WIDE)
    shape = families[12].shape
    row = lax.broadcasted_iota(jnp.int32, shape, 0)
    split_rates = jnp.full(shape, SPLIT_RATES[2], WIDE)
    for i in (0, 1, 3, 4, 5):
        split_rates = jnp.where(row == i, SPLIT_RATES[i], split_rates)
    rates = (
        slab_rates(ATTENTION_RATES, families[0].shape),
        slab_rates(FEEDFORWARD_RATES, families[4].shape),
        SHARED_RATE,
        split_rates,
    )
    for i, rate in enumerate(rates):
        master, moment, average, gradient = (ref[...] for ref in families[4 * i : 4 * i + 4])
        for out, value in zip(outs[2 + 4 * i : 6 + 4 * i], renew(master, moment, average, gradient, rate)):
            out[...] = value


PARTS = 4


def run_update(text, back, families):
    rows, width = text.shape

    def split_rows(array):
        block = (array.shape[0] // PARTS, *array.shape[1:])
        return pl.BlockSpec(block, lambda i: (i,) + (0,) * (len(block) - 1))

    def at_once(array):
        return pl.BlockSpec(array.shape, lambda i: (0,) * len(array.shape))

    specs = [split_rows(text), split_rows(back)]
    shapes = [jax.ShapeDtypeStruct(text.shape, LOW), jax.ShapeDtypeStruct(back.shape, WIDE)]
    outs = list(specs)
    for i, family in enumerate(families):
        spec = split_rows(family[0]) if i < 2 else at_once(family[0])
        specs += [spec] * 4
        outs += [spec] * 4
        shapes += [jax.ShapeDtypeStruct(family[0].shape, kind) for kind in (WIDE, WIDE, WIDE, LOW)]
    return pl.pallas_call(
        update_kernel,
        grid=(PARTS,),
        in_specs=specs,
        out_specs=outs,
        out_shape=shapes,
        compiler_params=pltpu.CompilerParams(vmem_limit_bytes=VMEM_LIMIT),
        name="update_parameters",
    )(text, back, *[array for family in families for array in family])


def line_shards(
    tokens,
    alignment,
    segment_count,
    text_mask,
    cotangent,
    attention_master,
    attention_moment,
    attention_average,
    feedforward_master,
    feedforward_moment,
    feedforward_average,
    shared_master,
    shared_moment,
    shared_average,
    split_master,
    split_moment,
    split_average,
):
    rows, width = tokens.shape
    attention_sum, feedforward_sum, shared_sum, split_sum, text_all, back_all, _ = run_layer(
        attention_master, feedforward_master, shared_master.T, split_master.T,
        tokens, cotangent, alignment, segment_count, text_mask,
    )
    outs = run_update(
        text_all.reshape(rows, width),
        back_all.reshape(rows, width),
        (
            (attention_master, attention_moment, attention_average, attention_sum),
            (feedforward_master, feedforward_moment, feedforward_average, feedforward_sum),
            (shared_master.T, shared_moment.T, shared_average.T, shared_sum),
            (split_master.T, split_moment.T, split_average.T, split_sum),
        ),
    )
    return (*outs[:10], *[out.T for out in outs[10:]])


def solution(mesh):
    in_specs = (
        P("dp", None),
        P("dp", None),
        P("dp"),
        P("dp", None),
        P("dp", None),
        P("dp", None, "mp"),
        P("dp", None, "mp"),
        P("dp", None, "mp"),
        P("dp", None, "mp"),
        P("dp", None, "mp"),
        P("dp", None, "mp"),
        P("dp", None),
        P("dp", None),
        P("dp", None),
        P("mp", None),
        P("mp", None),
        P("mp", None),
    )
    out_specs = (
        P("dp", None),
        P("dp", None),
        P("dp", None, "mp"),
        P("dp", None, "mp"),
        P("dp", None, "mp"),
        P("dp", None, "mp"),
        P("dp", None, "mp"),
        P("dp", None, "mp"),
        P("dp", None, "mp"),
        P("dp", None, "mp"),
        P("dp", None),
        P("dp", None),
        P("dp", None),
        P("dp", None),
        P("mp", None),
        P("mp", None),
        P("mp", None),
        P("mp", None),
    )
    body = line_shards if mesh.shape["dp"] == 8 and mesh.shape["mp"] == 4 else general_shards
    return jax.shard_map(body, mesh=mesh, in_specs=in_specs, out_specs=out_specs, check_vma=False)
```

```python
from functools import partial
from types import SimpleNamespace

import jax
import jax.numpy as jnp
from jax import lax
from jax.experimental import pallas as pl
from jax.experimental.pallas import tpu as pltpu
from jax.sharding import PartitionSpec as P

MESH = pl.DeviceIdType.MESH

HEAD_DIM = 64


EPS = 1e-05
MOMENTUM = 0.9
AVERAGE = 0.75
ATTENTION_RATES = (4e-05, 4e-05, 4e-05, 0.01)
FEEDFORWARD_RATES = (0.0002, 4e-05)
SHARED_RATE = 0.0006
SPLIT_RATES = (0.0004, 0.0003, 0.0017, 0.0017, 0.0017, 0.0017)
HIGHEST_MODE = lax.Precision.HIGHEST


def contract_last(left, right):
    return lax.dot_general(
        left, right, (((1,), (1,)), ((), ())), preferred_element_type=jnp.float32
    )


def contract_rows(left, right):
    return lax.dot_general(
        left, right, (((0,), (0,)), ((), ())), preferred_element_type=jnp.float32
    )


def layer_norm(value, gain, shift):
    center = value - jnp.mean(value, axis=-1, keepdims=True)
    factor = lax.rsqrt(jnp.mean(center * center, axis=-1, keepdims=True) + EPS)
    normed = center * factor
    return (normed * gain + shift, normed, factor)


def norm_back(incoming, normed, factor, gain):
    scaled = incoming * gain
    inner_part = (
        scaled
        - jnp.mean(scaled, axis=-1, keepdims=True)
        - normed * jnp.mean(scaled * normed, axis=-1, keepdims=True)
    )
    return (factor * inner_part, jnp.sum(incoming * normed, axis=0), jnp.sum(incoming, axis=0))


def masked_scores(queries, key_rows, valid_keys):
    scores = jnp.einsum(
        "qhd,khd->hqk", queries, key_rows, preferred_element_type=jnp.float32
    ) * HEAD_DIM ** (-0.5)
    return jnp.where(valid_keys[None, None, :], scores, -1e30)


def attend(pieces):
    queries, key_rows, value_rows, valid_keys = pieces
    scores = masked_scores(queries, key_rows, valid_keys)
    row_max = jnp.max(scores, axis=-1, keepdims=True)
    exponent = jnp.exp(scores - row_max)
    row_total = jnp.sum(exponent, axis=-1, keepdims=True)
    probability = (exponent / row_total).astype(jnp.bfloat16)
    context = jnp.einsum(
        "hqk,khd->qhd", probability, value_rows, preferred_element_type=jnp.float32
    )
    return (context.astype(jnp.bfloat16), row_max + jnp.log(row_total))


def attend_back(pieces):
    queries, key_rows, value_rows, valid_keys, upstream, logsum = pieces
    scores = masked_scores(queries, key_rows, valid_keys)
    probability = jnp.exp(scores - logsum)
    grad_values = jnp.einsum(
        "hqk,qhd->khd",
        probability.astype(jnp.bfloat16),
        upstream,
        preferred_element_type=jnp.float32,
    )
    grad_probs = jnp.einsum(
        "qhd,khd->hqk", upstream, value_rows, preferred_element_type=jnp.float32
    )
    row_delta = jnp.sum(probability * grad_probs, axis=-1, keepdims=True)
    grad_scores = (probability * (grad_probs - row_delta)).astype(jnp.bfloat16)
    grad_queries = jnp.einsum(
        "hqk,khd->qhd", grad_scores, key_rows, preferred_element_type=jnp.float32
    ) * HEAD_DIM ** (-0.5)
    grad_keys = jnp.einsum(
        "hqk,qhd->khd", grad_scores, queries, preferred_element_type=jnp.float32
    ) * HEAD_DIM ** (-0.5)
    return (
        grad_queries.astype(jnp.bfloat16),
        grad_keys.astype(jnp.bfloat16),
        grad_values.astype(jnp.bfloat16),
    )


def renew(master, moment, average, gradient, rates):
    velocity = MOMENTUM * moment + gradient
    updated = master - rates * (gradient + MOMENTUM * velocity)
    averaged = AVERAGE * average + (1.0 - AVERAGE) * updated
    return (velocity, updated, averaged, updated.astype(jnp.bfloat16))


def general_shards(
    tokens,
    alignment,
    segment_count,
    text_mask,
    cotangent,
    attention_master,
    attention_moment,
    attention_average,
    feedforward_master,
    feedforward_moment,
    feedforward_average,
    shared_master,
    shared_moment,
    shared_average,
    split_master,
    split_moment,
    split_average,
):
    documents, slot_count = alignment.shape
    text_rows = text_mask.shape[1]
    document_rows = text_rows + slot_count
    model_width = tokens.shape[1]
    local_width = split_master.shape[0]
    local_heads = local_width // HEAD_DIM
    row_count = documents * document_rows
    attention_full, feedforward_full, shared_full = (
        lax.all_gather(attention_master.astype(jnp.bfloat16), "dp", axis=0, tiled=True),
        lax.all_gather(feedforward_master.astype(jnp.bfloat16), "dp", axis=0, tiled=True),
        lax.all_gather(shared_master.astype(jnp.bfloat16), "dp", axis=0, tiled=True),
    )
    shared = shared_full.astype(jnp.float32)
    split_bias = lax.optimization_barrier(split_master.astype(jnp.bfloat16)).astype(jnp.float32)
    live_slots = (
        lax.broadcasted_iota(jnp.int32, (documents, slot_count), 1) < segment_count[:, None]
    )
    valid_keys = jnp.concatenate([text_mask > 0, live_slots], axis=1)
    text_index = lax.broadcasted_iota(jnp.int32, (documents, slot_count, text_rows), 2)
    pick_table = ((alignment[:, :, None] == text_index) & live_slots[:, :, None]).astype(
        jnp.bfloat16
    )
    inputs = tokens.reshape(documents, document_rows, model_width)
    taken_rows = jnp.einsum(
        "dst,dtw->dsw", pick_table, inputs[:, :text_rows], preferred_element_type=jnp.float32
    )
    layer_in = jnp.concatenate(
        [
            inputs[:, :text_rows].astype(jnp.float32),
            inputs[:, text_rows:].astype(jnp.float32) + taken_rows,
        ],
        axis=1,
    ).reshape(row_count, model_width)
    rows_in = layer_in.astype(jnp.bfloat16)
    project_weights = attention_full[:, :3].reshape(model_width, 3 * local_width)
    project_bias = jnp.concatenate(
        [split_bias[:, 0], jnp.zeros_like(split_bias[:, 0]), split_bias[:, 1]]
    )
    projected = (
        jnp.dot(rows_in, project_weights, preferred_element_type=jnp.float32) + project_bias
    ).astype(jnp.bfloat16)
    projected = projected.reshape(documents, document_rows, 3, local_heads, HEAD_DIM)
    queries = projected[:, :, 0]
    key_rows = projected[:, :, 1]
    value_rows = projected[:, :, 2]
    context, logsum = lax.map(attend, (queries, key_rows, value_rows, valid_keys))
    context_rows = context.reshape(row_count, local_width)
    joined = lax.psum(
        contract_last(context_rows, attention_full[:, 3]).astype(jnp.bfloat16), "mp"
    ).astype(jnp.float32)
    mixed = layer_in + joined + shared[:, 0]
    first_norm, normed_one, factor_one = layer_norm(mixed, shared[:, 1], shared[:, 2])
    hidden_in = first_norm.astype(jnp.bfloat16)
    inner_pre = jnp.dot(
        hidden_in, feedforward_full[:, 0], preferred_element_type=jnp.float32
    ) + split_bias[:, 2:].reshape(-1)
    active = jax.nn.gelu(inner_pre, approximate=False).astype(jnp.bfloat16)
    down_sum = lax.psum(
        contract_last(active, feedforward_full[:, 1]).astype(jnp.bfloat16), "mp"
    ).astype(jnp.float32)
    second = first_norm + down_sum + shared[:, 5]
    output, normed_two, factor_two = layer_norm(second, shared[:, 3], shared[:, 4])
    grad_second, grad_gain_two, grad_shift_two = norm_back(
        cotangent.astype(jnp.float32), normed_two, factor_two, shared[:, 3]
    )
    grad_down = grad_second.astype(jnp.bfloat16)
    grad_active = jnp.dot(grad_down, feedforward_full[:, 1], preferred_element_type=jnp.float32)
    gelu_value, gelu_pull = jax.vjp(partial(jax.nn.gelu, approximate=False), inner_pre)
    grad_inner = gelu_pull(grad_active)[0].astype(jnp.bfloat16)
    feedforward_grad = jnp.stack(
        [contract_rows(hidden_in, grad_inner), contract_rows(grad_down, active)], axis=1
    )
    grad_first = grad_second + lax.psum(
        contract_last(grad_inner, feedforward_full[:, 0]).astype(jnp.bfloat16), "mp"
    ).astype(jnp.float32)
    grad_mixed, grad_gain_one, grad_shift_one = norm_back(
        grad_first, normed_one, factor_one, shared[:, 1]
    )
    grad_joined = grad_mixed.astype(jnp.bfloat16)
    output_grad = contract_rows(grad_joined, context_rows)
    grad_context = jnp.dot(
        grad_joined, attention_full[:, 3], preferred_element_type=jnp.float32
    ).astype(jnp.bfloat16)
    upstream = grad_context.reshape(documents, document_rows, local_heads, HEAD_DIM)
    grad_queries, grad_keys, grad_values = lax.map(
        attend_back, (queries, key_rows, value_rows, valid_keys, upstream, logsum)
    )
    query_rows = grad_queries.reshape(row_count, local_width)
    value_grad_rows = grad_values.reshape(row_count, local_width)
    grad_project = jnp.concatenate(
        [query_rows, grad_keys.reshape(row_count, local_width), value_grad_rows], axis=1
    )
    project_grad = contract_rows(rows_in, grad_project).reshape(model_width, 3, local_width)
    attention_grad = jnp.concatenate([project_grad, output_grad[:, None, :]], axis=1)
    grad_layer_in = grad_mixed + lax.psum(
        contract_last(grad_project, project_weights).astype(jnp.bfloat16), "mp"
    ).astype(jnp.float32)
    shared_grad = jnp.stack(
        [
            jnp.sum(grad_mixed, axis=0),
            grad_gain_one,
            grad_shift_one,
            grad_gain_two,
            grad_shift_two,
            jnp.sum(grad_second, axis=0),
        ],
        axis=1,
    )
    split_grad = jnp.concatenate(
        [
            jnp.sum(query_rows, axis=0, dtype=jnp.float32)[:, None],
            jnp.sum(value_grad_rows, axis=0, dtype=jnp.float32)[:, None],
            jnp.sum(grad_inner, axis=0, dtype=jnp.float32).reshape(local_width, 4),
        ],
        axis=1,
    )
    grad_documents = grad_layer_in.reshape(documents, document_rows, model_width)
    moved_rows = jnp.einsum(
        "dst,dsw->dtw",
        pick_table.astype(jnp.float32),
        grad_documents[:, text_rows:],
        precision=HIGHEST_MODE,
        preferred_element_type=jnp.float32,
    )
    input_gradient = jnp.concatenate(
        [grad_documents[:, :text_rows] + moved_rows, grad_documents[:, text_rows:]], axis=1
    ).reshape(row_count, model_width)
    attention_sum, feedforward_sum, shared_sum = (
        lax.psum_scatter(attention_grad, "dp", scatter_dimension=0, tiled=True),
        lax.psum_scatter(feedforward_grad, "dp", scatter_dimension=0, tiled=True),
        lax.psum_scatter(shared_grad, "dp", scatter_dimension=0, tiled=True),
    )
    split_sum = lax.psum(split_grad, "dp")
    attention_new = renew(
        attention_master,
        attention_moment,
        attention_average,
        attention_sum,
        jnp.asarray(ATTENTION_RATES, jnp.float32).reshape(1, 4, 1),
    )
    feedforward_new = renew(
        feedforward_master,
        feedforward_moment,
        feedforward_average,
        feedforward_sum,
        jnp.asarray(FEEDFORWARD_RATES, jnp.float32).reshape(1, 2, 1),
    )
    shared_new = renew(shared_master, shared_moment, shared_average, shared_sum, SHARED_RATE)
    split_new = renew(
        split_master,
        split_moment,
        split_average,
        split_sum,
        jnp.asarray(SPLIT_RATES, jnp.float32).reshape(1, 6),
    )
    return (
        output.astype(jnp.bfloat16),
        input_gradient,
        attention_new[0],
        attention_new[1],
        attention_new[2],
        attention_new[3],
        feedforward_new[0],
        feedforward_new[1],
        feedforward_new[2],
        feedforward_new[3],
        shared_new[0],
        shared_new[1],
        shared_new[2],
        shared_new[3],
        split_new[0],
        split_new[1],
        split_new[2],
        split_new[3],
    )


LOW = jnp.bfloat16
WIDE = jnp.float32
UNITS = [(0, 0), (1, 0), (2, 0), (0, 1), (0, 2), (0, 3)] + [(t, k) for k in range(1, 4) for t in (1, 2)]
AXES = (0, 1, 0, 1, 0, 1, 0, 0, 0, 1, 0, 1)
LINE = 4
INNER_LEVELS = (1, 2, 0, 3)
BACK_UNITS = [(t, k) for k in range(4) for t in (2, 1)] + [(0, k) for k in range(4)]
PIECES = 8
SENDS = 3
PAIRS = 4


def place():
    dp, z = lax.axis_index("dp"), lax.axis_index("mp")
    return z, lax.div(dp, 4), lax.rem(lax.div(dp, 2), 2), lax.rem(dp, 2)


def device(z, y, x, c):
    return (y * 4 + x * 2 + c, z)


def document_of(z):
    return lax.div(z + 1, 2)


def nearest_level(z, k):
    low, high = lax.rem(z, 2), lax.div(z, 2)
    if k == 0:
        return z
    if k == 1:
        return 1 + (2 * high - 1) * low
    if k == 2:
        return 2 + high * (1 - 2 * low)
    return 3 - 3 * high


def greet(z, y, x, c, meanwhile):
    barrier = pltpu.get_barrier_semaphore()
    partners = [device(z, y, x, 1 - c), device(z, y, 1 - x, c), device(z, 1 - y, x, c)]
    partners += [device(lax.rem(z + k, 4), y, x, c) for k in (1, 2, 3)]
    for partner in partners:
        pl.semaphore_signal(barrier, inc=1, device_id=partner, device_id_type=MESH)
    meanwhile()
    pl.semaphore_wait(barrier, len(partners))


def remote(source, target, send, recv, to):
    return pltpu.make_async_remote_copy(
        src_ref=source, dst_ref=target, send_sem=send, recv_sem=recv, device_id=to, device_id_type=MESH
    )


def when(condition, action):
    pl.when(condition)(action)


def mul(left, right):
    return jnp.dot(left, right, preferred_element_type=WIDE)


def gelu_parts(value):
    root = value * 0.7071067811865476
    inverse = 1.0 / (1.0 + 0.3275911 * jnp.abs(root))
    bell = jnp.exp(-root * root)
    series = 1.061405429
    for factor in (-1.453152027, 1.421413741, -0.284496736, 0.254829592):
        series = series * inverse + factor
    tail = 0.5 * series * inverse * bell
    share = jnp.where(value >= 0, 1.0 - tail, tail)
    return value * share, share + value * (bell * 0.3989422804014327)


def head_mask(head, scale, lanes=192):
    lane = lax.broadcasted_iota(jnp.int32, (1, lanes), 1)
    return jnp.where((lane >= head * HEAD_DIM) & (lane < (head + 1) * HEAD_DIM), scale, 0.0).astype(LOW)


def wide_product(left, right, width):
    value = mul(left, right)
    if right.shape[1] < width:
        value = jnp.concatenate([value, jnp.zeros((left.shape[0], width - right.shape[1]), WIDE)], axis=1)
    return value


def unit_weight(r, t, level):
    return r.full[t, level].reshape(768, 768)


class Gather:
    def __init__(self, r):
        self.own, self.small, self.r = r.own, r.small, r
        self.z, self.y, self.x, self.c = z, y, x, c = place()
        self.up, self.down = device(z + 1, y, x, c), device(z - 1, y, x, c)
        self.across_x, self.across_y = device(z, y, 1 - x, c), device(z, 1 - y, x, c)
        self.pair = device(z, y, x, 1 - c)
        self.end = (z == 0) | (z == LINE - 1)

    def line_copy(self, t, level, source, way):
        r = self.r
        return remote(
            source, r.full.at[t, level, self.y, self.x, self.c], r.sent.at[0],
            r.line_recv.at[t, level], self.up if way == 0 else self.down,
        )

    def along_x(self, u):
        return AXES[u] == 0

    def first(self, u):
        t, k = UNITS[u]
        block = self.r.full.at[t, nearest_level(self.z, k), self.y, self.x, self.c]
        return remote(
            self.own.at[t] if k == 0 else block, block, self.r.sent.at[1], self.r.first_recv.at[u],
            self.across_x if self.along_x(u) else self.across_y,
        )

    def second(self, u):
        t, k = UNITS[u]
        level = nearest_level(self.z, k)
        if self.along_x(u):
            block, to = self.r.full.at[t, level, self.y, :, self.c], self.across_y
        else:
            block, to = self.r.full.at[t, level, :, self.x, self.c], self.across_x
        return remote(block, block, self.r.sent.at[2], self.r.second_recv.at[u], to)

    def extra(self, u, level, part, way):
        t, y, x, c = UNITS[u][0], self.y, self.x, self.c
        if self.along_x(u):
            index = (t, level, y, 1 - x, c) if part == 0 else (t, level, 1 - y, slice(None), c)
        else:
            index = (t, level, 1 - y, x, c) if part == 0 else (t, level, slice(None), 1 - x, c)
        block = self.r.full.at[index]
        return remote(
            block, block, self.r.sent.at[4], self.r.extra_recv.at[t - 1, level],
            self.up if way == 0 else self.down,
        )

    def paired(self, u):
        t, k = UNITS[u]
        block = self.r.full.at[t, nearest_level(self.z, k), :, :, self.c]
        return remote(block, block, self.r.sent.at[3], self.r.pair_recv.at[u], self.pair)

    def own_copy(self, t):
        return pltpu.make_async_copy(
            self.own.at[t], self.r.full.at[t, self.z, self.y, self.x, self.c], self.r.own_sem.at[t]
        )

    def tiny_own(self, i):
        target = self.r.plane.at[self.y, self.x, self.c] if i == 0 else self.r.line.at[self.z]
        return pltpu.make_async_copy(self.small, target, self.r.own_sem.at[3 + i])

    def tiny(self, i):
        r = self.r
        if i == 0:
            block, to = r.plane.at[self.y, self.x, self.c], self.across_x
        elif i == 1:
            block, to = r.plane.at[self.y, :, self.c], self.across_y
        elif i == 2:
            block, to = r.plane.at[:, :, self.c], self.pair
        else:
            block, to = r.line.at[self.z], device(lax.rem(self.z + i - 2, 4), self.y, self.x, self.c)
        source = self.small if i == 0 or i > 2 else block
        return remote(source, block, r.tiny_send.at[i], r.tiny_recv.at[i], to)

    def own_line(self, t, act):
        when(self.z < 3, lambda: act(self.line_copy(t, self.z, self.own.at[t], 0)))
        when(self.z > 0, lambda: act(self.line_copy(t, self.z, self.own.at[t], 1)))

    def own_extra(self, u, part, act):
        when(self.z < 3, lambda: act(self.extra(u, self.z, part, 0)))
        when(self.z > 0, lambda: act(self.extra(u, self.z, part, 1)))

    def begin(self):
        self.own_line(0, lambda copy: copy.start())
        for t in range(3):
            self.own_copy(t).start()

    def begin_tiny(self):
        for i in range(2):
            self.tiny_own(i).start()
        for i in (0, 3, 4, 5):
            self.tiny(i).start()

    def crosses(self, u, act):
        t, k = UNITS[u]
        if t == 0 or k in (0, 3):
            act()
        elif k == 2:
            when(self.end, act)

    def comes_whole(self, u, act):
        t, k = UNITS[u]
        if t > 0 and k == 1:
            act()
        elif t > 0 and k == 2:
            when(jnp.logical_not(self.end), act)

    def relay(self, u):
        t, k = UNITS[u]
        level = nearest_level(self.z, k)
        block = self.r.full.at[t, level, self.y, self.x, self.c]

        def act():
            self.line_copy(t, level, block, 0).wait_recv()
            when(level < self.z, lambda: self.line_copy(t, level, block, 0).start())
            when(level > self.z, lambda: self.line_copy(t, level, block, 1).start())

        when(jnp.logical_not(self.end), act)

    def arrive(self, u):
        t, k = UNITS[u]
        if k == 0 and t > 0:
            self.own_line(t, lambda copy: copy.start())
        if k > 0:
            level = nearest_level(self.z, k)
            block = self.r.full.at[t, level, self.y, self.x, self.c]
            when(self.end, lambda: self.line_copy(t, level, block, 0).wait_recv())
        self.crosses(u, lambda: self.first(u).start())

    def cross(self, u):
        t, k = UNITS[u]

        def act():
            self.first(u).wait_recv()
            if k == 0:
                self.own_copy(t).wait()
            self.second(u).start()
            if t > 0 and k == 0:
                self.own_extra(u, 0, lambda copy: copy.start())

        self.crosses(u, act)

    def share(self, u):
        t, k = UNITS[u]
        level = nearest_level(self.z, k)

        def act():
            self.second(u).wait_recv()
            if t > 0 and k == 0:
                self.own_extra(u, 1, lambda copy: copy.start())
            self.paired(u).start()

        def act_whole():
            blocks = self.r.second_in.at[pl.ds(0, 3)]
            remote(blocks, blocks, self.r.sent.at[4], self.r.extra_recv.at[t - 1, level], self.up).wait_recv()
            self.paired(u).start()

        self.crosses(u, act)
        self.comes_whole(u, act_whole)

    def take(self, u):
        self.paired(u).wait_recv()

    def tiny_step(self, i):
        if i == 0:
            for j in range(2):
                self.tiny_own(j).wait()
        if i < 3:
            self.tiny(i).wait_recv()
        if i < 2:
            self.tiny(i + 1).start()
        if i == 3:
            for j in (3, 4, 5):
                self.tiny(j).wait_recv()

    def finish(self):
        r = self.r
        for i in range(6):
            self.tiny(i).wait_send()

        def all_sent(*counts):
            for i, count in enumerate(counts):
                if count == 15:
                    blocks = r.line_in
                elif count == 48:
                    blocks = r.total
                elif count in (16, 20):
                    blocks = r.first_in.at[pl.ds(0, count // 2)]
                else:
                    blocks = r.second_in.at[pl.ds(0, count)]
                remote(blocks, blocks, r.sent.at[i], r.pair_recv.at[0], self.pair).wait_send()

        when(self.end, lambda: all_sent(3, 10, 20, 48, 6))
        when(jnp.logical_not(self.end), lambda: all_sent(15, 8, 16, 48, 12))


class Reduce:
    def __init__(self, att_sum, ff_sum, r):
        self.att_sum, self.ff_sum, self.r = att_sum, ff_sum, r
        self.z, self.y, self.x, self.c = z, y, x, c = place()
        self.up, self.down = device(z + 1, y, x, c), device(z - 1, y, x, c)
        self.across_x, self.across_y = device(z, y, 1 - x, c), device(z, 1 - y, x, c)
        self.pair = device(z, y, x, 1 - c)

    def pair_copy(self, u):
        r = self.r
        return remote(
            r.sends.at[u % SENDS], r.pair_in.at[u % PAIRS], r.r_pair_send.at[u % SENDS], r.r_pair_recv.at[u % PAIRS],
            self.pair,
        )

    def first_copy(self, u):
        r = self.r
        source = r.total.at[u, :, 1 - self.x] if u % 2 == 0 else r.total.at[u, 1 - self.y]
        return remote(
            source, r.first_in.at[u], r.sent.at[5], r.r_first_recv.at[u],
            self.across_x if u % 2 == 0 else self.across_y,
        )

    def second_copy(self, u):
        r, x, y = self.r, self.x, self.y
        return remote(
            r.total.at[u, 1 - y, x] if u % 2 == 0 else r.total.at[u, y, 1 - x],
            r.second_in.at[u], r.sent.at[6], r.r_second_recv.at[u],
            self.across_y if u % 2 == 0 else self.across_x,
        )

    def line_copy(self, u, way):
        r = self.r
        t, k = BACK_UNITS[u]
        level = nearest_level(self.z, 3 - k)
        return remote(
            r.total.at[u, self.y, self.x], r.line_in.at[t, level + 1 - way], r.sent.at[7],
            r.r_line_recv.at[t, level + 1 - way], self.up if way == 0 else self.down,
        )

    def produce(self, u, parts):
        r = self.r
        if u >= SENDS:
            self.pair_copy(u - SENDS).wait_send()
        for half, target in ((1 - self.c, r.sends.at[u % SENDS]), (self.c, r.total.at[u])):
            for products, lanes in parts:
                width = lanes.stop - lanes.start
                value = sum(wide_product(turned[:, :, half].reshape(384, 512), columns, width) for turned, columns in products)
                target[:, :, :, lanes] = value.astype(LOW).reshape(2, 2, 96, width)
            if half is not self.c:
                self.pair_copy(u).start()

    def add_pair(self, u):
        r = self.r
        self.pair_copy(u).wait_recv()
        r.total[u] = r.total[u] + r.pair_in[u % PAIRS]
        self.first_copy(u).start()

    def add_first(self, u):
        r, x, y = self.r, self.x, self.y
        self.first_copy(u).wait_recv()
        if u % 2 == 0:
            r.total[u, :, x] = r.total[u, :, x] + r.first_in[u]
        else:
            r.total[u, y] = r.total[u, y] + r.first_in[u]
        self.second_copy(u).start()

    def add_second(self, u):
        r, x, y, z = self.r, self.x, self.y, self.z
        t, k = BACK_UNITS[u]
        level = nearest_level(z, 3 - k)
        self.second_copy(u).wait_recv()
        r.total[u, y, x] = r.total[u, y, x] + r.second_in[u]
        if k < 3:
            when((z == 0) | (z == 3), lambda: self.send_line(u))

    def send_line(self, u):
        level = nearest_level(self.z, 3 - BACK_UNITS[u][1])
        when(self.z < level, lambda: self.line_copy(u, 0).start())
        when(self.z > level, lambda: self.line_copy(u, 1).start())

    def take_line(self, u, way):
        r, x, y = self.r, self.x, self.y
        t, k = BACK_UNITS[u]
        level = nearest_level(self.z, 3 - k)
        self.line_copy(u, way).wait_recv()
        r.total[u, y, x] = r.total[u, y, x] + r.line_in[t, level + 1 - way]

    def add_line(self, u):
        r, z = self.r, self.z
        t, k = BACK_UNITS[u]
        level = nearest_level(z, 3 - k)
        middle = (z == 1) | (z == 2)
        if k < 3:
            when(middle & (z < level), lambda: self.take_line(u, 0))
            when(middle & (z > level), lambda: self.take_line(u, 1))
            when(middle, lambda: self.send_line(u))
        else:
            when(z > 0, lambda: self.take_line(u, 0))
            when(z < 3, lambda: self.take_line(u, 1))
            self.give(t, r.total[u, self.y, self.x])

    def give(self, t, value):
        r = self.r
        if t == 0:
            for slab in range(4):
                r.att_in[:, slab, :] = value[:, slab * 192 : (slab + 1) * 192].astype(WIDE)
            self.given(0).start()
        else:
            r.ff_in[:, t - 1, :] = value.astype(WIDE)

    def given(self, i):
        source, target = ((self.r.att_in, self.att_sum), (self.r.ff_in, self.ff_sum))[i]
        return pltpu.make_async_copy(source, target, self.r.load_sem.at[6 + i])

    def small_copy(self, i):
        r = self.r
        if i < 3:
            to = (self.pair, self.across_x, self.across_y)[i]
            return remote(r.small_total.at[i], r.small_in.at[i], r.small_send.at[i], r.small_recv.at[i], to)
        to = device(lax.rem(self.z + i - 2, 4), self.y, self.x, self.c)
        return remote(r.small_total.at[3], r.small_line.at[self.z], r.small_send.at[i], r.small_recv.at[i], to)

    def small_step(self, i):
        r = self.r
        self.small_copy(i).wait_recv()
        r.small_total[i + 1] = r.small_total[i] + r.small_in[i]
        if i < 2:
            self.small_copy(i + 1).start()
        else:
            for j in (3, 4, 5):
                self.small_copy(j).start()
            r.small_line[self.z] = r.small_total[3]

    def small_end(self, shared_sum, split_sum):
        r, z = self.r, self.z
        for i in (3, 4, 5):
            self.small_copy(i).wait_recv()
        r.small_sum[...] = r.small_line[0] + r.small_line[1] + r.small_line[2] + r.small_line[3]
        index = self.y * 4 + self.x * 2 + self.c
        shared_sum[...] = pltpu.roll(r.small_sum[:8], lax.rem(768 - index * 96, 768), 1)[:6, :96]
        biases = r.small_sum[pl.ds(8 + z, 1)]
        split_sum[0:1] = biases[:, :192]
        split_sum[1:2] = biases[:, 384:576]
        inner = r.small_sum[pl.ds(12 + z, 1)]
        for j in range(4):
            split_sum[2 + j : 3 + j] = inner[:, j * 192 : (j + 1) * 192]

    def finish(self):
        for i in range(6):
            self.small_copy(i).wait_send()
        for u in range(len(BACK_UNITS) - SENDS, len(BACK_UNITS)):
            self.pair_copy(u).wait_send()
        r = self.r
        for i, blocks in ((5, r.first_in), (6, r.second_in), (7, r.second_in.at[pl.ds(0, 9)])):
            remote(blocks, blocks, r.sent.at[i], r.r_pair_recv.at[0], self.pair).wait_send()


class Cast:
    def __init__(self, a, source, target, r):
        self.a, self.source, self.target, self.r = a, source, target, r
        self.z, y, x, c = place()
        self.up, self.down = device(self.z + 1, y, x, c), device(self.z - 1, y, x, c)

    def copy(self, d, p, way, first):
        r = self.r
        part = pl.ds(p * (512 // PIECES), 512 // PIECES)
        target = self.target.at[d, part]
        return remote(
            self.source.at[part] if first else target, target, r.cast_send.at[self.a],
            r.cast_recv.at[self.a, 16 if d == 1 else d * 4 + p], self.up if way == 0 else self.down,
        )

    def own(self):
        return pltpu.make_async_copy(self.source, self.target.at[document_of(self.z)], self.r.cast_own.at[self.a])

    def firsts(self, p, act):
        for level, d, way in ((0, 0, 0), (1, 1, 1), (2, 1, 0), (3, 2, 1)):
            when(self.z == level, lambda d=d, way=way: act(self.copy(d, p, way, True)))

    def begin(self):
        self.own().start()
        for p in range(PIECES):
            self.firsts(p, lambda copy: copy.start())

    def pass_on(self, d, p, way):
        copy = self.copy(d, p, way, False)
        copy.wait_recv()
        copy.start()

    def near(self, p):
        when(self.z == 1, lambda: self.pass_on(0, p, 0))
        when(self.z == 2, lambda: self.pass_on(2, p, 1))

    def far(self, p):
        when(self.z == 1, lambda: self.pass_on(2, p, 1))
        when(self.z == 2, lambda: self.pass_on(0, p, 0))

    def finish(self):
        r = self.r
        self.own().wait()
        for level, d, way in ((0, 2, 1), (3, 0, 0)):
            for p in range(PIECES):
                when(self.z == level, lambda p=p, d=d, way=way: self.copy(d, p, way, False).wait_recv())

        def wait(blocks, act):
            act(remote(blocks, blocks, r.cast_send.at[self.a], r.cast_recv.at[self.a, 16], self.up))

        end = (self.z == 0) | (self.z == 3)
        when(end, lambda: wait(self.target.at[1], lambda copy: copy.wait_recv()))
        when(end, lambda: wait(self.source, lambda copy: copy.wait_send()))
        when(jnp.logical_not(end), lambda: wait(self.target, lambda copy: copy.wait_send()))


def buffers():
    vmem = pltpu.VMEM
    return dict(
        full=vmem((3, 4, 2, 2, 2, 96, 768), LOW),
        plane=vmem((2, 2, 2, 16, 768), LOW),
        line=vmem((4, 16, 768), LOW),
        tok=vmem((512, 768), LOW),
        cot=vmem((512, 768), LOW),
        pick=vmem((384, 128), LOW),
        rows_in=vmem((512, 768), LOW),
        hidden_in=vmem((512, 768), LOW),
        rows_t=vmem((2, 2, 2, 96, 512), LOW),
        hidden_t=vmem((2, 2, 2, 96, 512), LOW),
        down_t=vmem((2, 2, 2, 96, 512), LOW),
        joined_t=vmem((2, 2, 2, 96, 512), LOW),
        qkv=vmem((4, 512, 640), LOW),
        probs=vmem((2, 3, 512, 512), LOW),
        context=vmem((4, 512, 256), LOW),
        active=vmem((4, 512, 768), LOW),
        slope=vmem((4, 512, 768), LOW),
        mixed=vmem((512, 768), WIDE),
        bar=vmem((1, 512), WIDE),
        normed_one=vmem((512, 768), WIDE),
        factor_one=vmem((512, 1), WIDE),
        total=vmem((12, 2, 2, 96, 768), LOW),
        sends=vmem((SENDS, 2, 2, 96, 768), LOW),
        pair_in=vmem((PAIRS, 2, 2, 96, 768), LOW),
        first_in=vmem((12, 2, 96, 768), LOW),
        second_in=vmem((12, 96, 768), LOW),
        line_in=vmem((3, 5, 96, 768), LOW),
        small_total=vmem((4, 16, 768), WIDE),
        small_in=vmem((3, 16, 768), WIDE),
        small_line=vmem((4, 16, 768), WIDE),
        small_sum=vmem((16, 768), WIDE),
        shared=vmem((16, 768), WIDE),
        own=vmem((3, 96, 768), LOW),
        att_in=vmem((96, 4, 192), WIDE),
        ff_in=vmem((96, 2, 768), WIDE),
        shared_in=vmem((6, 96), WIDE),
        split_in=vmem((6, 192), WIDE),
        align_in=vmem((3, 128), jnp.int32),
        mask_in=vmem((3, 384), jnp.int32),
        small=vmem((16, 768), LOW),
    )


def flags():
    dma = pltpu.SemaphoreType.DMA
    return dict(
        sent=dma((8,)),
        line_recv=dma((3, 4)),
        first_recv=dma((12,)),
        second_recv=dma((12,)),
        pair_recv=dma((12,)),
        tiny_send=dma((6,)),
        tiny_recv=dma((6,)),
        extra_recv=dma((2, 4)),
        own_sem=dma((5,)),
        load_sem=dma((12,)),
        r_pair_send=dma((SENDS,)),
        r_pair_recv=dma((PAIRS,)),
        r_first_recv=dma((12,)),
        r_second_recv=dma((12,)),
        r_line_recv=dma((3, 5)),
        small_send=dma((6,)),
        small_recv=dma((6,)),
        cast_send=dma((2,)),
        cast_recv=dma((2, 17)),
        cast_own=dma((2,)),
    )


def spread(j):
    unit = lax.broadcasted_iota(jnp.int32, (192, 768), 1)
    return jnp.where(unit == 4 * lax.broadcasted_iota(jnp.int32, (192, 768), 0) + j, 1.0, 0.0).astype(LOW)


def turn(value, counts):
    return (value * counts.astype(LOW)).T.reshape(2, 2, 2, 96, 512)


def layer_kernel(
    att_ref, ff_ref, shared_ref, split_ref, tokens_ref, cotangent_ref, align_ref, count_ref, mask_ref,
    att_sum, ff_sum, shared_sum, split_sum, text_all, back_all, probs_out, *refs,
):
    r = SimpleNamespace(**dict(zip([*buffers(), *flags()], refs)))
    z, y, x, c = place()
    doc = document_of(z)
    counts = jnp.where(z == 2, 0.0, 1.0)
    tok_copy = pltpu.make_async_copy(tokens_ref.at[pl.ds(doc * 512, 512)], r.tok, r.load_sem.at[0])
    cot_copy = pltpu.make_async_copy(cotangent_ref.at[pl.ds(doc * 512, 512)], r.cot, r.load_sem.at[1])
    tok_copy.start()
    cot_copy.start()
    operands = (
        (att_ref, r.att_in), (ff_ref, r.ff_in), (shared_ref, r.shared_in), (split_ref, r.split_in),
        (align_ref, r.align_in), (mask_ref, r.mask_in),
    )
    loads = [pltpu.make_async_copy(source, target, r.load_sem.at[6 + i]) for i, (source, target) in enumerate(operands)]
    for copy in loads:
        copy.start()

    def cast_own():
        loads[0].wait()
        for slab in range(4):
            r.own[0, :, slab * 192 : (slab + 1) * 192] = r.att_in[:, slab, :].astype(LOW)
        loads[1].wait()
        for t in (1, 2):
            r.own[t] = r.ff_in[:, t - 1, :].astype(LOW)
        for copy in loads[2:]:
            copy.wait()

    greet(z, y, x, c, cast_own)
    net = Gather(r)
    net.begin()

    def small_start():
        r.small_sum[...] = jnp.zeros((16, 768), WIDE)
        r.small_sum[:6, :96] = r.shared_in[...]
        shared = pltpu.roll(r.small_sum[:8], (y * 4 + x * 2 + c) * 96, 1)
        r.small_sum[8:14, :192] = r.split_in[...]
        units = r.small_sum[8:16, :192].astype(LOW)
        inner = sum(mul(units, spread(j))[2 + j : 3 + j] for j in range(4))
        r.small_sum[:8] = shared
        r.small_sum[6:7] = jnp.zeros((1, 768), WIDE)
        r.small_sum[6:7, :192] = r.split_in[0:1]
        r.small_sum[6:7, 384:576] = r.split_in[1:2]
        r.small_sum[7:8] = inner
        r.small[...] = r.small_sum[...].astype(LOW)
        net.begin_tiny()

    def small_ready():
        value = r.small_total[0, 8:16]
        high = value.astype(LOW)
        rest = value - high.astype(WIDE)
        middle = rest.astype(LOW)
        last = (rest - middle.astype(WIDE)).astype(LOW)
        for j in range(4):
            packed = sum(contract_last(piece, spread(j)) for piece in (last, middle, high))
            r.small_total[0, 12:16, j * 192 : (j + 1) * 192] = packed[4:8]
        r.small_total[0] = r.small_total[0] * counts
        red.small_copy(0).start()

    def input_rows(tok, document):
        live = lax.broadcasted_iota(jnp.int32, (1, 128), 1) < count_ref[document]
        pick = jnp.where(
            (lax.broadcasted_iota(jnp.int32, (384, 128), 0) == r.align_in[pl.ds(document, 1), :]) & live, 1.0, 0.0
        ).astype(LOW)
        text_tokens = tok[:384]
        taken = lax.dot_general(pick, text_tokens, (((0,), (0,)), ((), ())), preferred_element_type=WIDE)
        slot_rows = tok[384:].astype(WIDE) + taken
        r.mixed[:384] = text_tokens.astype(WIDE)
        r.mixed[384:] = slot_rows
        r.rows_in[:384] = text_tokens
        r.rows_in[384:] = slot_rows.astype(LOW)
        r.bar[...] = jnp.where(jnp.concatenate([r.mask_in[pl.ds(document, 1), :] > 0, live], axis=1), 0.0, -1e30)
        return pick

    def prologue():
        tok_copy.wait()
        r.pick[...] = input_rows(r.tok, doc)
        r.rows_t[...] = turn(r.rows_in[...], counts)

    def spill(k):
        return pltpu.make_async_copy(r.probs.at[k % 2], probs_out.at[k % 2], r.load_sem.at[2 + k % 2])

    def projected_rows(level):
        bias = r.line[level][6:7].astype(WIDE)
        return (mul(r.rows_in[...], unit_weight(r, 0, level)) + bias).astype(LOW)

    def attend_level(projected, level, keep):
        queries, keys, values = projected[:, :192], projected[:, 192:384], projected[:, 384:640]
        halves = (slice(0, 256), slice(256, 512))
        context = [jnp.zeros((256, 256), WIDE)] * 2
        for head in range(3):
            left, right = queries * head_mask(head, 0.125), values * head_mask(head, 1.0, 256)
            for i, rows in enumerate(halves):
                scores = jnp.where(r.bar[...] < 0.0, -1e30, contract_last(left[rows], keys))
                raised = jnp.exp(scores - jnp.max(scores, axis=-1, keepdims=True))
                probs = (raised * (1.0 / jnp.sum(raised, axis=-1, keepdims=True))).astype(LOW)
                keep[head, rows] = probs
                context[i] = context[i] + mul(probs, right)
        for i, rows in enumerate(halves):
            r.context[level, rows] = pltpu.roll(context[i], 64, 1).astype(LOW)

    def attention(k):
        level = nearest_level(z, k)
        projected = projected_rows(level)
        r.qkv[level] = projected[:, :640]
        if k >= 2:
            spill(k).wait()
        attend_level(projected, level, r.probs.at[k % 2])
        if k < 2:
            spill(k).start()

    def norm_rows():
        for level in range(4):
            r.mixed[...] += contract_last(r.context[level], unit_weight(r, 0, level)[:, 512:])
        shared = r.shared[...]
        rows, normed, factor = layer_norm(r.mixed[...] + shared[0:1], shared[1:2], shared[2:3])
        r.hidden_in[...] = rows.astype(LOW)
        r.mixed[...] = rows + shared[5:6]
        return normed, factor

    def first_norm():
        r.shared[...] = jnp.sum(r.plane[...].astype(WIDE).reshape(8, 16, 768), axis=0)
        normed, factor = norm_rows()
        r.normed_one[...] = normed
        r.factor_one[...] = factor
        r.hidden_t[...] = turn(r.hidden_in[...], counts)

    def feed_level(level, keep_slope):
        bias = r.line[level][7:8, :].astype(WIDE)
        up = unit_weight(r, 1, level)
        for block in range(4):
            rows = slice(block * 128, (block + 1) * 128)
            for part in range(3):
                lanes = slice(part * 256, (part + 1) * 256)
                inner = mul(r.hidden_in[rows], up[:, lanes]) + bias[:, lanes]
                active, slope = gelu_parts(inner)
                r.active[level, rows, lanes] = active.astype(LOW)
                if keep_slope:
                    r.slope[level, rows, lanes] = slope.astype(LOW)

    def feed(k):
        feed_level(nearest_level(z, k), True)

    def feed_sum(k):
        level = jnp.where(net.end, nearest_level(z, k), INNER_LEVELS[k])
        r.mixed[...] += contract_last(r.active[level], unit_weight(r, 2, level))

    text_cast = Cast(0, r.tok, text_all, r)
    back_cast = Cast(1, r.cot, back_all, r)
    red = Reduce(att_sum, ff_sum, r)

    def second_norm():
        shared = r.shared[...]
        final, normed, factor = layer_norm(r.mixed[...], shared[3:4], shared[4:5])
        r.tok[...] = final.astype(LOW)
        text_cast.begin()
        cot_copy.wait()
        incoming = r.cot[...].astype(WIDE)
        grad, gain, shift = norm_back(incoming, normed, factor, shared[3:4])
        r.mixed[...] = grad
        low = grad.astype(LOW)
        r.rows_in[...] = low
        r.down_t[...] = turn(low, counts)
        r.small_total[0] = jnp.zeros((16, 768), WIDE)
        r.small_total[0, 3:4] = gain[None]
        r.small_total[0, 4:5] = shift[None]
        r.small_total[0, 5:6] = jnp.sum(grad, axis=0, keepdims=True)

    def inner_back(k):
        level = nearest_level(z, 3 - k)
        grad = (mul(r.rows_in[...], unit_weight(r, 2, level)) * r.slope[level].astype(WIDE)).astype(LOW)
        r.slope[level] = grad
        r.small_total[0, pl.ds(12 + level, 1)] = jnp.sum(grad.astype(WIDE), axis=0, keepdims=True)

    def make_down(k):
        level = nearest_level(z, 3 - k)
        red.produce(2 * k, [([(r.down_t, r.active[level])], slice(0, 768))])

    def make_up(k):
        level = nearest_level(z, 3 - k)
        red.produce(2 * k + 1, [([(r.hidden_t, r.slope[level])], slice(0, 768))])

    def first_norm_back():
        for level in range(4):
            r.mixed[...] += contract_last(r.slope[level], unit_weight(r, 1, level))
        grad, gain, shift = norm_back(r.mixed[...], r.normed_one[...], r.factor_one[...], r.shared[1:2])
        r.mixed[...] = grad
        low = grad.astype(LOW)
        r.hidden_in[...] = low
        r.joined_t[...] = turn(low, counts)
        r.small_total[0, 0:1] = jnp.sum(grad, axis=0, keepdims=True)
        r.small_total[0, 1:2] = gain[None]
        r.small_total[0, 2:3] = shift[None]

    def reload(k):
        return pltpu.make_async_copy(probs_out.at[k], r.probs.at[k], r.load_sem.at[4 + k])

    def attention_back(k):
        slot = 3 - k
        level = nearest_level(z, slot)
        queries, keys, values = r.qkv[level, :, :192], r.qkv[level, :, 192:384], r.qkv[level, :, 384:576]
        upstream = mul(r.hidden_in[...], unit_weight(r, 0, level)[:, 512:])[:, 64:].astype(LOW)
        if slot < 2:
            reload(slot).wait()
        grad_q = grad_k = grad_v = jnp.zeros((512, 192), WIDE)
        for head in range(3):
            probs = r.probs[slot % 2, head]
            up = upstream * head_mask(head, 1.0)
            grad_v = grad_v + contract_rows(probs, up)
            grad_probs = contract_last(up, values)
            wide = probs.astype(WIDE)
            weighed = wide * grad_probs
            grad_scores = (weighed - wide * jnp.sum(weighed, axis=-1, keepdims=True)).astype(LOW)
            grad_q = grad_q + mul(grad_scores, keys * head_mask(head, 0.125))
            grad_k = grad_k + contract_rows(grad_scores, queries * head_mask(head, 0.125))
        if slot >= 2:
            reload(slot - 2).start()
        r.qkv[level, :, :192] = grad_q.astype(LOW)
        r.qkv[level, :, 192:384] = grad_k.astype(LOW)
        r.qkv[level, :, 384:576] = grad_v.astype(LOW)
        r.qkv[level, :, 576:] = jnp.zeros((512, 64), LOW)
        r.small_total[0, pl.ds(8 + level, 1), :640] = jnp.sum(r.qkv[level].astype(WIDE), axis=0, keepdims=True)

    def make_project(k):
        level = nearest_level(z, 3 - k)
        red.produce(8 + k, [
            ([(r.rows_t, r.qkv[level, :, :512])], slice(0, 512)),
            ([(r.rows_t, r.qkv[level, :, 512:]), (r.joined_t, r.context[level])], slice(512, 768)),
        ])

    def input_back():
        for level in range(4):
            r.mixed[...] += contract_last(r.qkv[level], unit_weight(r, 0, level)[:, :640])
        grad = r.mixed[...]
        r.cot[:384] = (grad[:384] + mul(r.pick[...], grad[384:].astype(LOW))).astype(LOW)
        r.cot[384:] = grad[384:].astype(LOW)
        back_cast.begin()

    steps = program_steps(net, red, text_cast, back_cast, (shared_sum, split_sum), [
        small_start, small_ready, prologue, attention, first_norm, feed, feed_sum, second_norm, inner_back, make_down, make_up, first_norm_back,
        attention_back, make_project, input_back,
    ])
    for i in ORDER:
        steps[i][0]()
    red.given(1).start()
    net.finish()
    text_cast.finish()
    back_cast.finish()
    red.finish()
    for i in range(2):
        red.given(i).wait()


def program_steps(net, red, text_cast, back_cast, small_sums, work):
    steps = []

    def add(action, *after):
        steps.append((action, [i for group in after for i in (group if isinstance(group, tuple) else (group,))]))
        return len(steps) - 1

    inner = jnp.logical_not(net.end)

    def add_each(action, *after):
        def side(i):
            return [group[i] if isinstance(group, tuple) else group for group in after]

        return (
            add(partial(when, net.end, action), *side(0)),
            add(partial(when, inner, action), *side(1)),
        )

    (small_start, small_ready, prologue, attention, first_norm, feed, feed_sum, second_norm, inner_back, make_down, make_up,
     first_norm_back, attention_back, make_project, input_back) = work
    taken = {}
    for u, unit in enumerate(UNITS):
        step = [add(partial(net.relay, u))] if unit[1] else []
        step = add_each(partial(net.arrive, u), *step)
        step = add_each(partial(net.cross, u), step)
        step = add_each(partial(net.share, u), step)
        taken[unit] = add_each(partial(net.take, u), step)
    step = add(small_start)
    tiny = [add(partial(net.tiny_step, 0), step)]
    for i in (1, 2, 3):
        tiny.append(add(partial(net.tiny_step, i), tiny[-1]))
    step = add(prologue)
    for k in range(4):
        step = add(partial(attention, k), step, taken[0, k], tiny[3])
    step = add(first_norm, step, tiny[2])
    fed = []
    for k in range(4):
        step = add(partial(feed, k), step, taken[1, k])
        fed.append(step)
    for k in range(4):
        needs = [taken[2, i] for i in range(min(k + 2, 4))]
        step = add(partial(feed_sum, k), fed[min(k + 1, 3)], *needs, *[step] * (k > 0))
    step = started = add(second_norm, step, fed[3])
    made, joined = {}, {}

    def make(u, action, before):
        ahead = [made[u - 1], joined[u - 2]] if u >= 2 else [made[0]] if u else []
        made[u] = add(action, before, *ahead)
        joined[u] = add_each(partial(red.add_pair, u), made[u])

    inners = []
    for k in range(4):
        inners.append(add(partial(inner_back, k), started))
        make(2 * k, partial(make_down, k), started)
        make(2 * k + 1, partial(make_up, k), inners[k])
    step = add(first_norm_back, *inners)
    for k in range(4):
        step = add(partial(attention_back, k), step)
        make(8 + k, partial(make_project, k), step)
    ended = add(input_back, step)
    for u in range(12):
        step = add_each(partial(red.add_first, u), joined[u])
        step = add_each(partial(red.add_second, u), step)
        add_each(partial(red.add_line, u), step)
    for cast, begun in ((text_cast, started), (back_cast, ended)):
        for p in range(PIECES):
            add(partial(cast.near, p), begun)
            add(partial(cast.far, p), begun)
    step = add(small_ready, ended)
    for i in range(3):
        step = add(partial(red.small_step, i), step)
    add(partial(red.small_end, *small_sums), step)
    return steps


ORDER = (
    8, 9, 105, 0, 1, 106, 24, 26, 25, 16, 33, 35, 107, 17, 3, 28, 42, 69, 44, 10, 51, 2, 34, 18, 71, 60, 27, 78,
    43, 5, 4, 12, 36, 11, 52, 37, 110, 46, 70, 87, 62, 6, 30, 45, 108, 96, 29, 64, 19, 79, 98, 109, 61, 7, 111,
    32, 31, 14, 89, 39, 13, 20, 53, 63, 54, 88, 72, 38, 112, 47, 97, 41, 81, 40, 113, 48, 21, 55, 80, 100, 15, 73,
    91, 75, 49, 57, 90, 50, 114, 23, 115, 82, 84, 56, 59, 77, 99, 22, 74, 66, 83, 116, 102, 93, 58, 117, 65, 76,
    92, 118, 101, 67, 104, 68, 95, 86, 120, 85, 121, 94, 119, 103, 122, 123, 124, 139, 125, 126, 129, 146, 132,
    153, 128, 127, 133, 130, 243, 154, 245, 134, 135, 131, 247, 136, 244, 140, 249, 158, 246, 251, 138, 171, 248,
    253, 137, 162, 250, 141, 255, 178, 252, 166, 254, 173, 184, 177, 142, 143, 183, 172, 257, 256, 170, 144, 275,
    175, 189, 145, 147, 150, 190, 174, 176, 276, 196, 149, 261, 148, 155, 259, 151, 152, 159, 202, 277, 258, 157,
    156, 185, 163, 265, 267, 260, 160, 269, 161, 179, 186, 164, 219, 191, 167, 262, 263, 195, 187, 180, 273, 278,
    168, 270, 165, 268, 266, 214, 220, 274, 182, 221, 271, 231, 225, 201, 207, 169, 264, 197, 213, 227, 198, 203,
    193, 188, 200, 226, 237, 272, 204, 232, 222, 224, 192, 216, 233, 194, 228, 199, 238, 215, 217, 208, 206, 279,
    234, 236, 235, 230, 210, 212, 209, 211, 229, 239, 218, 181, 240, 223, 205, 242, 241,
)


def run_layer(attention, feedforward, shared, split, tokens, cotangent, align, count, mask):
    vmem = pl.BlockSpec(memory_space=pltpu.VMEM)
    smem = pl.BlockSpec(memory_space=pltpu.SMEM)
    hbm = pl.BlockSpec(memory_space=pl.ANY)
    whole = jax.ShapeDtypeStruct((3, 512, 768), LOW)
    return pl.pallas_call(
        layer_kernel,
        out_shape=(
            jax.ShapeDtypeStruct((96, 4, 192), WIDE),
            jax.ShapeDtypeStruct((96, 2, 768), WIDE),
            jax.ShapeDtypeStruct((6, 96), WIDE),
            jax.ShapeDtypeStruct((6, 192), WIDE),
            whole,
            whole,
            jax.ShapeDtypeStruct((2, 3, 512, 512), LOW),
        ),
        in_specs=[hbm, hbm, hbm, hbm, hbm, hbm, hbm, smem, hbm],
        out_specs=(hbm, hbm, vmem, vmem, hbm, hbm, hbm),
        scratch_shapes=[*buffers().values(), *flags().values()],
        compiler_params=pltpu.CompilerParams(
            collective_id=0, has_side_effects=True, vmem_limit_bytes=VMEM_LIMIT
        ),
        name="layer_step",
    )(attention, feedforward, shared, split, tokens, cotangent, align, count, mask)


VMEM_LIMIT = 63 * 2**20


def slab_rates(rates, shape):
    slab = lax.broadcasted_iota(jnp.int32, shape, 1)
    value = jnp.full(shape, rates[0], WIDE)
    for i, rate in enumerate(rates[1:]):
        value = jnp.where(slab == i + 1, rate, value)
    return value


def update_kernel(*refs):
    text_ref, back_ref, families = refs[0], refs[1], refs[2:18]
    text_out, back_out, outs = refs[18], refs[19], refs[20:36]
    back_in, back_wide, text_in, ins, news = refs[36], refs[37], refs[38], refs[39:55], refs[55:71]
    load_sem, store_sem = refs[71:]

    def part(i):
        size = back_in.shape[0] // PARTS
        return pl.ds(i * size, size)

    text_loads = [
        pltpu.make_async_copy(text_ref.at[part(i)], text_in.at[part(i)], load_sem.at[16 + PARTS + i]) for i in range(PARTS)
    ]
    text_stores = [
        pltpu.make_async_copy(text_in.at[part(i)], text_out.at[part(i)], store_sem.at[16 + i]) for i in range(PARTS)
    ]
    back_loads = [
        pltpu.make_async_copy(back_ref.at[part(i)], back_in.at[part(i)], load_sem.at[16 + i]) for i in range(PARTS)
    ]
    back_stores = [
        pltpu.make_async_copy(back_wide.at[part(i)], back_out.at[part(i)], store_sem.at[16 + PARTS + i])
        for i in range(PARTS)
    ]
    loads = [pltpu.make_async_copy(families[i], ins[i], load_sem.at[i]) for i in range(16)]
    stores = [pltpu.make_async_copy(news[i], outs[i], store_sem.at[i]) for i in range(16)]

    def widen(i):
        back_loads[i].wait()
        back_wide[part(i)] = back_in[part(i)].astype(WIDE)
        back_stores[i].start()

    def update(i, rate):
        for j in range(4 * i, 4 * i + 4):
            loads[j].wait()
        master, moment, average, gradient = (ref[...] for ref in ins[4 * i : 4 * i + 4])
        for j, value in enumerate(renew(master, moment, average, gradient, rate)):
            news[4 * i + j][...] = value
            stores[4 * i + j].start()

    back_loads[0].start()
    back_loads[1].start()
    for copy in loads:
        copy.start()
    for copy in back_loads[2:]:
        copy.start()
    for copy in text_loads:
        copy.start()
    widen(0)
    widen(1)
    update(0, slab_rates(ATTENTION_RATES, ins[0].shape))
    update(1, slab_rates(FEEDFORWARD_RATES, ins[4].shape))
    row = lax.broadcasted_iota(jnp.int32, ins[12].shape, 0)
    split_rates = jnp.full(ins[12].shape, SPLIT_RATES[2], WIDE)
    for i in (0, 1, 3, 4, 5):
        split_rates = jnp.where(row == i, SPLIT_RATES[i], split_rates)
    update(2, SHARED_RATE)
    update(3, split_rates)
    for i in range(2, PARTS):
        widen(i)
    for load, store in zip(text_loads, text_stores):
        load.wait()
        store.start()
    for copy in (*text_stores, *back_stores, *stores):
        copy.wait()


PARTS = 2


def run_update(text, back, families):
    arrays = [array for family in families for array in family]
    shapes = [jax.ShapeDtypeStruct(text.shape, LOW), jax.ShapeDtypeStruct(back.shape, WIDE)]
    for family in families:
        shapes += [jax.ShapeDtypeStruct(family[0].shape, kind) for kind in (WIDE, WIDE, WIDE, LOW)]
    hbm = pl.BlockSpec(memory_space=pl.ANY)
    return pl.pallas_call(
        update_kernel,
        in_specs=[hbm] * 18,
        out_specs=[hbm] * 18,
        out_shape=shapes,
        scratch_shapes=[
            pltpu.VMEM(back.shape, LOW),
            pltpu.VMEM(back.shape, WIDE),
            pltpu.VMEM(text.shape, LOW),
            *[pltpu.VMEM(array.shape, WIDE) for array in arrays],
            *[pltpu.VMEM(shape.shape, shape.dtype) for shape in shapes[2:]],
            pltpu.SemaphoreType.DMA((16 + 2 * PARTS,)),
            pltpu.SemaphoreType.DMA((16 + 2 * PARTS,)),
        ],
        compiler_params=pltpu.CompilerParams(vmem_limit_bytes=VMEM_LIMIT),
        name="update_parameters",
    )(text, back, *arrays)


def line_shards(
    tokens,
    alignment,
    segment_count,
    text_mask,
    cotangent,
    attention_master,
    attention_moment,
    attention_average,
    feedforward_master,
    feedforward_moment,
    feedforward_average,
    shared_master,
    shared_moment,
    shared_average,
    split_master,
    split_moment,
    split_average,
):
    rows, width = tokens.shape
    attention_sum, feedforward_sum, shared_sum, split_sum, text_all, back_all, _ = run_layer(
        attention_master, feedforward_master, shared_master.T, split_master.T,
        tokens, cotangent, alignment, segment_count, text_mask,
    )
    outs = run_update(
        text_all.reshape(rows, width),
        back_all.reshape(rows, width),
        (
            (attention_master, attention_moment, attention_average, attention_sum),
            (feedforward_master, feedforward_moment, feedforward_average, feedforward_sum),
            (shared_master.T, shared_moment.T, shared_average.T, shared_sum),
            (split_master.T, split_moment.T, split_average.T, split_sum),
        ),
    )
    return (*outs[:10], *[out.T for out in outs[10:]])


def solution(mesh):
    in_specs = (
        P("dp", None),
        P("dp", None),
        P("dp"),
        P("dp", None),
        P("dp", None),
        P("dp", None, "mp"),
        P("dp", None, "mp"),
        P("dp", None, "mp"),
        P("dp", None, "mp"),
        P("dp", None, "mp"),
        P("dp", None, "mp"),
        P("dp", None),
        P("dp", None),
        P("dp", None),
        P("mp", None),
        P("mp", None),
        P("mp", None),
    )
    out_specs = (
        P("dp", None),
        P("dp", None),
        P("dp", None, "mp"),
        P("dp", None, "mp"),
        P("dp", None, "mp"),
        P("dp", None, "mp"),
        P("dp", None, "mp"),
        P("dp", None, "mp"),
        P("dp", None, "mp"),
        P("dp", None, "mp"),
        P("dp", None),
        P("dp", None),
        P("dp", None),
        P("dp", None),
        P("mp", None),
        P("mp", None),
        P("mp", None),
        P("mp", None),
    )
    body = line_shards if mesh.shape["dp"] == 8 and mesh.shape["mp"] == 4 else general_shards
    return jax.shard_map(body, mesh=mesh, in_specs=in_specs, out_specs=out_specs, check_vma=False)
```

```python
from functools import partial
from types import SimpleNamespace

import jax
import jax.numpy as jnp
from jax import lax
from jax.experimental import pallas as pl
from jax.experimental.pallas import tpu as pltpu
from jax.sharding import PartitionSpec as P

MESH = pl.DeviceIdType.MESH

HEAD_DIM = 64


EPS = 1e-05
MOMENTUM = 0.9
AVERAGE = 0.75
ATTENTION_RATES = (4e-05, 4e-05, 4e-05, 0.01)
FEEDFORWARD_RATES = (0.0002, 4e-05)
SHARED_RATE = 0.0006
SPLIT_RATES = (0.0004, 0.0003, 0.0017, 0.0017, 0.0017, 0.0017)
HIGHEST_MODE = lax.Precision.HIGHEST


def contract_last(left, right):
    return lax.dot_general(
        left, right, (((1,), (1,)), ((), ())), preferred_element_type=jnp.float32
    )


def contract_rows(left, right):
    return lax.dot_general(
        left, right, (((0,), (0,)), ((), ())), preferred_element_type=jnp.float32
    )


def layer_norm(value, gain, shift):
    center = value - jnp.mean(value, axis=-1, keepdims=True)
    factor = lax.rsqrt(jnp.mean(center * center, axis=-1, keepdims=True) + EPS)
    normed = center * factor
    return (normed * gain + shift, normed, factor)


def norm_back(incoming, normed, factor, gain):
    scaled = incoming * gain
    inner_part = (
        scaled
        - jnp.mean(scaled, axis=-1, keepdims=True)
        - normed * jnp.mean(scaled * normed, axis=-1, keepdims=True)
    )
    return (factor * inner_part, jnp.sum(incoming * normed, axis=0), jnp.sum(incoming, axis=0))


def masked_scores(queries, key_rows, valid_keys):
    scores = jnp.einsum(
        "qhd,khd->hqk", queries, key_rows, preferred_element_type=jnp.float32
    ) * HEAD_DIM ** (-0.5)
    return jnp.where(valid_keys[None, None, :], scores, -1e30)


def attend(pieces):
    queries, key_rows, value_rows, valid_keys = pieces
    scores = masked_scores(queries, key_rows, valid_keys)
    row_max = jnp.max(scores, axis=-1, keepdims=True)
    exponent = jnp.exp(scores - row_max)
    row_total = jnp.sum(exponent, axis=-1, keepdims=True)
    probability = (exponent / row_total).astype(jnp.bfloat16)
    context = jnp.einsum(
        "hqk,khd->qhd", probability, value_rows, preferred_element_type=jnp.float32
    )
    return (context.astype(jnp.bfloat16), row_max + jnp.log(row_total))


def attend_back(pieces):
    queries, key_rows, value_rows, valid_keys, upstream, logsum = pieces
    scores = masked_scores(queries, key_rows, valid_keys)
    probability = jnp.exp(scores - logsum)
    grad_values = jnp.einsum(
        "hqk,qhd->khd",
        probability.astype(jnp.bfloat16),
        upstream,
        preferred_element_type=jnp.float32,
    )
    grad_probs = jnp.einsum(
        "qhd,khd->hqk", upstream, value_rows, preferred_element_type=jnp.float32
    )
    row_delta = jnp.sum(probability * grad_probs, axis=-1, keepdims=True)
    grad_scores = (probability * (grad_probs - row_delta)).astype(jnp.bfloat16)
    grad_queries = jnp.einsum(
        "hqk,khd->qhd", grad_scores, key_rows, preferred_element_type=jnp.float32
    ) * HEAD_DIM ** (-0.5)
    grad_keys = jnp.einsum(
        "hqk,qhd->khd", grad_scores, queries, preferred_element_type=jnp.float32
    ) * HEAD_DIM ** (-0.5)
    return (
        grad_queries.astype(jnp.bfloat16),
        grad_keys.astype(jnp.bfloat16),
        grad_values.astype(jnp.bfloat16),
    )


def renew(master, moment, average, gradient, rates):
    velocity = MOMENTUM * moment + gradient
    updated = master - rates * (gradient + MOMENTUM * velocity)
    averaged = AVERAGE * average + (1.0 - AVERAGE) * updated
    return (velocity, updated, averaged, updated.astype(jnp.bfloat16))


def general_shards(
    tokens,
    alignment,
    segment_count,
    text_mask,
    cotangent,
    attention_master,
    attention_moment,
    attention_average,
    feedforward_master,
    feedforward_moment,
    feedforward_average,
    shared_master,
    shared_moment,
    shared_average,
    split_master,
    split_moment,
    split_average,
):
    documents, slot_count = alignment.shape
    text_rows = text_mask.shape[1]
    document_rows = text_rows + slot_count
    model_width = tokens.shape[1]
    local_width = split_master.shape[0]
    local_heads = local_width // HEAD_DIM
    row_count = documents * document_rows
    attention_full, feedforward_full, shared_full = (
        lax.all_gather(attention_master.astype(jnp.bfloat16), "dp", axis=0, tiled=True),
        lax.all_gather(feedforward_master.astype(jnp.bfloat16), "dp", axis=0, tiled=True),
        lax.all_gather(shared_master.astype(jnp.bfloat16), "dp", axis=0, tiled=True),
    )
    shared = shared_full.astype(jnp.float32)
    split_bias = lax.optimization_barrier(split_master.astype(jnp.bfloat16)).astype(jnp.float32)
    live_slots = (
        lax.broadcasted_iota(jnp.int32, (documents, slot_count), 1) < segment_count[:, None]
    )
    valid_keys = jnp.concatenate([text_mask > 0, live_slots], axis=1)
    text_index = lax.broadcasted_iota(jnp.int32, (documents, slot_count, text_rows), 2)
    pick_table = ((alignment[:, :, None] == text_index) & live_slots[:, :, None]).astype(
        jnp.bfloat16
    )
    inputs = tokens.reshape(documents, document_rows, model_width)
    taken_rows = jnp.einsum(
        "dst,dtw->dsw", pick_table, inputs[:, :text_rows], preferred_element_type=jnp.float32
    )
    layer_in = jnp.concatenate(
        [
            inputs[:, :text_rows].astype(jnp.float32),
            inputs[:, text_rows:].astype(jnp.float32) + taken_rows,
        ],
        axis=1,
    ).reshape(row_count, model_width)
    rows_in = layer_in.astype(jnp.bfloat16)
    project_weights = attention_full[:, :3].reshape(model_width, 3 * local_width)
    project_bias = jnp.concatenate(
        [split_bias[:, 0], jnp.zeros_like(split_bias[:, 0]), split_bias[:, 1]]
    )
    projected = (
        jnp.dot(rows_in, project_weights, preferred_element_type=jnp.float32) + project_bias
    ).astype(jnp.bfloat16)
    projected = projected.reshape(documents, document_rows, 3, local_heads, HEAD_DIM)
    queries = projected[:, :, 0]
    key_rows = projected[:, :, 1]
    value_rows = projected[:, :, 2]
    context, logsum = lax.map(attend, (queries, key_rows, value_rows, valid_keys))
    context_rows = context.reshape(row_count, local_width)
    joined = lax.psum(
        contract_last(context_rows, attention_full[:, 3]).astype(jnp.bfloat16), "mp"
    ).astype(jnp.float32)
    mixed = layer_in + joined + shared[:, 0]
    first_norm, normed_one, factor_one = layer_norm(mixed, shared[:, 1], shared[:, 2])
    hidden_in = first_norm.astype(jnp.bfloat16)
    inner_pre = jnp.dot(
        hidden_in, feedforward_full[:, 0], preferred_element_type=jnp.float32
    ) + split_bias[:, 2:].reshape(-1)
    active = jax.nn.gelu(inner_pre, approximate=False).astype(jnp.bfloat16)
    down_sum = lax.psum(
        contract_last(active, feedforward_full[:, 1]).astype(jnp.bfloat16), "mp"
    ).astype(jnp.float32)
    second = first_norm + down_sum + shared[:, 5]
    output, normed_two, factor_two = layer_norm(second, shared[:, 3], shared[:, 4])
    grad_second, grad_gain_two, grad_shift_two = norm_back(
        cotangent.astype(jnp.float32), normed_two, factor_two, shared[:, 3]
    )
    grad_down = grad_second.astype(jnp.bfloat16)
    grad_active = jnp.dot(grad_down, feedforward_full[:, 1], preferred_element_type=jnp.float32)
    gelu_value, gelu_pull = jax.vjp(partial(jax.nn.gelu, approximate=False), inner_pre)
    grad_inner = gelu_pull(grad_active)[0].astype(jnp.bfloat16)
    feedforward_grad = jnp.stack(
        [contract_rows(hidden_in, grad_inner), contract_rows(grad_down, active)], axis=1
    )
    grad_first = grad_second + lax.psum(
        contract_last(grad_inner, feedforward_full[:, 0]).astype(jnp.bfloat16), "mp"
    ).astype(jnp.float32)
    grad_mixed, grad_gain_one, grad_shift_one = norm_back(
        grad_first, normed_one, factor_one, shared[:, 1]
    )
    grad_joined = grad_mixed.astype(jnp.bfloat16)
    output_grad = contract_rows(grad_joined, context_rows)
    grad_context = jnp.dot(
        grad_joined, attention_full[:, 3], preferred_element_type=jnp.float32
    ).astype(jnp.bfloat16)
    upstream = grad_context.reshape(documents, document_rows, local_heads, HEAD_DIM)
    grad_queries, grad_keys, grad_values = lax.map(
        attend_back, (queries, key_rows, value_rows, valid_keys, upstream, logsum)
    )
    query_rows = grad_queries.reshape(row_count, local_width)
    value_grad_rows = grad_values.reshape(row_count, local_width)
    grad_project = jnp.concatenate(
        [query_rows, grad_keys.reshape(row_count, local_width), value_grad_rows], axis=1
    )
    project_grad = contract_rows(rows_in, grad_project).reshape(model_width, 3, local_width)
    attention_grad = jnp.concatenate([project_grad, output_grad[:, None, :]], axis=1)
    grad_layer_in = grad_mixed + lax.psum(
        contract_last(grad_project, project_weights).astype(jnp.bfloat16), "mp"
    ).astype(jnp.float32)
    shared_grad = jnp.stack(
        [
            jnp.sum(grad_mixed, axis=0),
            grad_gain_one,
            grad_shift_one,
            grad_gain_two,
            grad_shift_two,
            jnp.sum(grad_second, axis=0),
        ],
        axis=1,
    )
    split_grad = jnp.concatenate(
        [
            jnp.sum(query_rows, axis=0, dtype=jnp.float32)[:, None],
            jnp.sum(value_grad_rows, axis=0, dtype=jnp.float32)[:, None],
            jnp.sum(grad_inner, axis=0, dtype=jnp.float32).reshape(local_width, 4),
        ],
        axis=1,
    )
    grad_documents = grad_layer_in.reshape(documents, document_rows, model_width)
    moved_rows = jnp.einsum(
        "dst,dsw->dtw",
        pick_table.astype(jnp.float32),
        grad_documents[:, text_rows:],
        precision=HIGHEST_MODE,
        preferred_element_type=jnp.float32,
    )
    input_gradient = jnp.concatenate(
        [grad_documents[:, :text_rows] + moved_rows, grad_documents[:, text_rows:]], axis=1
    ).reshape(row_count, model_width)
    attention_sum, feedforward_sum, shared_sum = (
        lax.psum_scatter(attention_grad, "dp", scatter_dimension=0, tiled=True),
        lax.psum_scatter(feedforward_grad, "dp", scatter_dimension=0, tiled=True),
        lax.psum_scatter(shared_grad, "dp", scatter_dimension=0, tiled=True),
    )
    split_sum = lax.psum(split_grad, "dp")
    attention_new = renew(
        attention_master,
        attention_moment,
        attention_average,
        attention_sum,
        jnp.asarray(ATTENTION_RATES, jnp.float32).reshape(1, 4, 1),
    )
    feedforward_new = renew(
        feedforward_master,
        feedforward_moment,
        feedforward_average,
        feedforward_sum,
        jnp.asarray(FEEDFORWARD_RATES, jnp.float32).reshape(1, 2, 1),
    )
    shared_new = renew(shared_master, shared_moment, shared_average, shared_sum, SHARED_RATE)
    split_new = renew(
        split_master,
        split_moment,
        split_average,
        split_sum,
        jnp.asarray(SPLIT_RATES, jnp.float32).reshape(1, 6),
    )
    return (
        output.astype(jnp.bfloat16),
        input_gradient,
        attention_new[0],
        attention_new[1],
        attention_new[2],
        attention_new[3],
        feedforward_new[0],
        feedforward_new[1],
        feedforward_new[2],
        feedforward_new[3],
        shared_new[0],
        shared_new[1],
        shared_new[2],
        shared_new[3],
        split_new[0],
        split_new[1],
        split_new[2],
        split_new[3],
    )


LOW = jnp.bfloat16
WIDE = jnp.float32
UNITS = [(0, 0), (1, 0), (2, 0), (0, 1), (0, 2), (0, 3)] + [(t, k) for k in range(1, 4) for t in (1, 2)]
AXES = (0, 1, 0, 1, 0, 1, 0, 0, 0, 1, 0, 1)
LINE = 4
INNER_LEVELS = (1, 2, 0, 3)
BACK_UNITS = [(t, k) for k in range(4) for t in (2, 1)] + [(0, k) for k in range(4)]
PIECES = 8
SENDS = 3
PAIRS = 4


def place():
    dp, z = lax.axis_index("dp"), lax.axis_index("mp")
    return z, lax.div(dp, 4), lax.rem(lax.div(dp, 2), 2), lax.rem(dp, 2)


def device(z, y, x, c):
    return (y * 4 + x * 2 + c, z)


def document_of(z):
    return lax.div(z + 1, 2)


def nearest_level(z, k):
    low, high = lax.rem(z, 2), lax.div(z, 2)
    if k == 0:
        return z
    if k == 1:
        return 1 + (2 * high - 1) * low
    if k == 2:
        return 2 + high * (1 - 2 * low)
    return 3 - 3 * high


def greet(z, y, x, c, meanwhile):
    barrier = pltpu.get_barrier_semaphore()
    partners = [device(z, y, x, 1 - c), device(z, y, 1 - x, c), device(z, 1 - y, x, c)]
    partners += [device(lax.rem(z + k, 4), y, x, c) for k in (1, 2, 3)]
    for partner in partners:
        pl.semaphore_signal(barrier, inc=1, device_id=partner, device_id_type=MESH)
    meanwhile()
    pl.semaphore_wait(barrier, len(partners))


def remote(source, target, send, recv, to):
    return pltpu.make_async_remote_copy(
        src_ref=source, dst_ref=target, send_sem=send, recv_sem=recv, device_id=to, device_id_type=MESH
    )


def when(condition, action):
    pl.when(condition)(action)


def mul(left, right):
    return jnp.dot(left, right, preferred_element_type=WIDE)


def gelu_parts(value):
    root = value * 0.7071067811865476
    inverse = 1.0 / (1.0 + 0.3275911 * jnp.abs(root))
    bell = jnp.exp(-root * root)
    series = 1.061405429
    for factor in (-1.453152027, 1.421413741, -0.284496736, 0.254829592):
        series = series * inverse + factor
    tail = 0.5 * series * inverse * bell
    share = jnp.where(value >= 0, 1.0 - tail, tail)
    return value * share, share + value * (bell * 0.3989422804014327)


def head_mask(head, scale, lanes=192):
    lane = lax.broadcasted_iota(jnp.int32, (1, lanes), 1)
    return jnp.where((lane >= head * HEAD_DIM) & (lane < (head + 1) * HEAD_DIM), scale, 0.0).astype(LOW)


def wide_product(left, right, width):
    value = mul(left, right)
    if right.shape[1] < width:
        value = jnp.concatenate([value, jnp.zeros((left.shape[0], width - right.shape[1]), WIDE)], axis=1)
    return value


def unit_weight(r, t, level):
    return r.full[t, level].reshape(768, 768)


class Gather:
    def __init__(self, r):
        self.own, self.small, self.r = r.own, r.small, r
        self.z, self.y, self.x, self.c = z, y, x, c = place()
        self.up, self.down = device(z + 1, y, x, c), device(z - 1, y, x, c)
        self.across_x, self.across_y = device(z, y, 1 - x, c), device(z, 1 - y, x, c)
        self.pair = device(z, y, x, 1 - c)
        self.end = (z == 0) | (z == LINE - 1)

    def line_copy(self, t, level, source, way):
        r = self.r
        return remote(
            source, r.full.at[t, level, self.y, self.x, self.c], r.sent.at[0],
            r.line_recv.at[t, level], self.up if way == 0 else self.down,
        )

    def along_x(self, u):
        return AXES[u] == 0

    def first(self, u):
        t, k = UNITS[u]
        block = self.r.full.at[t, nearest_level(self.z, k), self.y, self.x, self.c]
        return remote(
            self.own.at[t] if k == 0 else block, block, self.r.sent.at[1], self.r.first_recv.at[u],
            self.across_x if self.along_x(u) else self.across_y,
        )

    def second(self, u):
        t, k = UNITS[u]
        level = nearest_level(self.z, k)
        if self.along_x(u):
            block, to = self.r.full.at[t, level, self.y, :, self.c], self.across_y
        else:
            block, to = self.r.full.at[t, level, :, self.x, self.c], self.across_x
        return remote(block, block, self.r.sent.at[2], self.r.second_recv.at[u], to)

    def extra(self, u, level, part, way):
        t, y, x, c = UNITS[u][0], self.y, self.x, self.c
        if self.along_x(u):
            index = (t, level, y, 1 - x, c) if part == 0 else (t, level, 1 - y, slice(None), c)
        else:
            index = (t, level, 1 - y, x, c) if part == 0 else (t, level, slice(None), 1 - x, c)
        block = self.r.full.at[index]
        return remote(
            block, block, self.r.sent.at[4], self.r.extra_recv.at[t - 1, level],
            self.up if way == 0 else self.down,
        )

    def paired(self, u):
        t, k = UNITS[u]
        block = self.r.full.at[t, nearest_level(self.z, k), :, :, self.c]
        return remote(block, block, self.r.sent.at[3], self.r.pair_recv.at[u], self.pair)

    def own_copy(self, t):
        return pltpu.make_async_copy(
            self.own.at[t], self.r.full.at[t, self.z, self.y, self.x, self.c], self.r.own_sem.at[t]
        )

    def tiny_own(self, i):
        target = self.r.plane.at[self.y, self.x, self.c] if i == 0 else self.r.line.at[self.z]
        return pltpu.make_async_copy(self.small, target, self.r.own_sem.at[3 + i])

    def tiny(self, i):
        r = self.r
        if i == 0:
            block, to = r.plane.at[self.y, self.x, self.c], self.across_x
        elif i == 1:
            block, to = r.plane.at[self.y, :, self.c], self.across_y
        elif i == 2:
            block, to = r.plane.at[:, :, self.c], self.pair
        else:
            block, to = r.line.at[self.z], device(lax.rem(self.z + i - 2, 4), self.y, self.x, self.c)
        source = self.small if i == 0 or i > 2 else block
        return remote(source, block, r.tiny_send.at[i], r.tiny_recv.at[i], to)

    def own_line(self, t, act):
        when(self.z < 3, lambda: act(self.line_copy(t, self.z, self.own.at[t], 0)))
        when(self.z > 0, lambda: act(self.line_copy(t, self.z, self.own.at[t], 1)))

    def own_extra(self, u, part, act):
        when(self.z < 3, lambda: act(self.extra(u, self.z, part, 0)))
        when(self.z > 0, lambda: act(self.extra(u, self.z, part, 1)))

    def begin(self):
        self.own_line(0, lambda copy: copy.start())
        for t in range(3):
            self.own_copy(t).start()

    def begin_tiny(self):
        for i in range(2):
            self.tiny_own(i).start()
        for i in (0, 3, 4, 5):
            self.tiny(i).start()

    def crosses(self, u, act):
        t, k = UNITS[u]
        if t == 0 or k in (0, 3):
            act()
        elif k == 2:
            when(self.end, act)

    def comes_whole(self, u, act):
        t, k = UNITS[u]
        if t > 0 and k == 1:
            act()
        elif t > 0 and k == 2:
            when(jnp.logical_not(self.end), act)

    def relay(self, u):
        t, k = UNITS[u]
        level = nearest_level(self.z, k)
        block = self.r.full.at[t, level, self.y, self.x, self.c]

        def act():
            self.line_copy(t, level, block, 0).wait_recv()
            when(level < self.z, lambda: self.line_copy(t, level, block, 0).start())
            when(level > self.z, lambda: self.line_copy(t, level, block, 1).start())

        when(jnp.logical_not(self.end), act)

    def arrive(self, u):
        t, k = UNITS[u]
        if k == 0 and t > 0:
            self.own_line(t, lambda copy: copy.start())
        if k > 0:
            level = nearest_level(self.z, k)
            block = self.r.full.at[t, level, self.y, self.x, self.c]
            when(self.end, lambda: self.line_copy(t, level, block, 0).wait_recv())
        self.crosses(u, lambda: self.first(u).start())

    def cross(self, u):
        t, k = UNITS[u]

        def act():
            self.first(u).wait_recv()
            if k == 0:
                self.own_copy(t).wait()
            self.second(u).start()
            if t > 0 and k == 0:
                self.own_extra(u, 0, lambda copy: copy.start())

        self.crosses(u, act)

    def share(self, u):
        t, k = UNITS[u]
        level = nearest_level(self.z, k)

        def act():
            self.second(u).wait_recv()
            if t > 0 and k == 0:
                self.own_extra(u, 1, lambda copy: copy.start())
            self.paired(u).start()

        def act_whole():
            blocks = self.r.second_in.at[pl.ds(0, 3)]
            remote(blocks, blocks, self.r.sent.at[4], self.r.extra_recv.at[t - 1, level], self.up).wait_recv()
            self.paired(u).start()

        self.crosses(u, act)
        self.comes_whole(u, act_whole)

    def take(self, u):
        self.paired(u).wait_recv()

    def tiny_step(self, i):
        if i == 0:
            for j in range(2):
                self.tiny_own(j).wait()
        if i < 3:
            self.tiny(i).wait_recv()
        if i < 2:
            self.tiny(i + 1).start()
        if i == 3:
            for j in (3, 4, 5):
                self.tiny(j).wait_recv()

    def finish(self):
        r = self.r
        for i in range(6):
            self.tiny(i).wait_send()

        def all_sent(*counts):
            for i, count in enumerate(counts):
                if count == 15:
                    blocks = r.line_in
                elif count == 48:
                    blocks = r.total
                elif count in (16, 20):
                    blocks = r.first_in.at[pl.ds(0, count // 2)]
                else:
                    blocks = r.second_in.at[pl.ds(0, count)]
                remote(blocks, blocks, r.sent.at[i], r.pair_recv.at[0], self.pair).wait_send()

        when(self.end, lambda: all_sent(3, 10, 20, 48, 6))
        when(jnp.logical_not(self.end), lambda: all_sent(15, 8, 16, 48, 12))


class Reduce:
    def __init__(self, att_sum, ff_sum, r):
        self.att_sum, self.ff_sum, self.r = att_sum, ff_sum, r
        self.z, self.y, self.x, self.c = z, y, x, c = place()
        self.up, self.down = device(z + 1, y, x, c), device(z - 1, y, x, c)
        self.across_x, self.across_y = device(z, y, 1 - x, c), device(z, 1 - y, x, c)
        self.pair = device(z, y, x, 1 - c)

    def pair_copy(self, u):
        r = self.r
        return remote(
            r.sends.at[u % SENDS], r.pair_in.at[u % PAIRS], r.r_pair_send.at[u % SENDS], r.r_pair_recv.at[u % PAIRS],
            self.pair,
        )

    def first_copy(self, u):
        r = self.r
        source = r.total.at[u, :, 1 - self.x] if u % 2 == 0 else r.total.at[u, 1 - self.y]
        return remote(
            source, r.first_in.at[u], r.sent.at[5], r.r_first_recv.at[u],
            self.across_x if u % 2 == 0 else self.across_y,
        )

    def second_copy(self, u):
        r, x, y = self.r, self.x, self.y
        return remote(
            r.total.at[u, 1 - y, x] if u % 2 == 0 else r.total.at[u, y, 1 - x],
            r.second_in.at[u], r.sent.at[6], r.r_second_recv.at[u],
            self.across_y if u % 2 == 0 else self.across_x,
        )

    def line_copy(self, u, way):
        r = self.r
        t, k = BACK_UNITS[u]
        level = nearest_level(self.z, 3 - k)
        return remote(
            r.total.at[u, self.y, self.x], r.line_in.at[t, level + 1 - way], r.sent.at[7],
            r.r_line_recv.at[t, level + 1 - way], self.up if way == 0 else self.down,
        )

    def produce(self, u, parts):
        r = self.r
        if u >= SENDS:
            self.pair_copy(u - SENDS).wait_send()
        for half, target in ((1 - self.c, r.sends.at[u % SENDS]), (self.c, r.total.at[u])):
            for products, lanes in parts:
                width = lanes.stop - lanes.start
                value = sum(wide_product(turned[:, :, half].reshape(384, 512), columns, width) for turned, columns in products)
                target[:, :, :, lanes] = value.astype(LOW).reshape(2, 2, 96, width)
            if half is not self.c:
                self.pair_copy(u).start()

    def add_pair(self, u):
        r = self.r
        self.pair_copy(u).wait_recv()
        r.total[u] = r.total[u] + r.pair_in[u % PAIRS]
        self.first_copy(u).start()

    def add_first(self, u):
        r, x, y = self.r, self.x, self.y
        self.first_copy(u).wait_recv()
        if u % 2 == 0:
            r.total[u, :, x] = r.total[u, :, x] + r.first_in[u]
        else:
            r.total[u, y] = r.total[u, y] + r.first_in[u]
        self.second_copy(u).start()

    def add_second(self, u):
        r, x, y, z = self.r, self.x, self.y, self.z
        t, k = BACK_UNITS[u]
        level = nearest_level(z, 3 - k)
        self.second_copy(u).wait_recv()
        r.total[u, y, x] = r.total[u, y, x] + r.second_in[u]
        if k < 3:
            when((z == 0) | (z == 3), lambda: self.send_line(u))

    def send_line(self, u):
        level = nearest_level(self.z, 3 - BACK_UNITS[u][1])
        when(self.z < level, lambda: self.line_copy(u, 0).start())
        when(self.z > level, lambda: self.line_copy(u, 1).start())

    def take_line(self, u, way):
        r, x, y = self.r, self.x, self.y
        t, k = BACK_UNITS[u]
        level = nearest_level(self.z, 3 - k)
        self.line_copy(u, way).wait_recv()
        r.total[u, y, x] = r.total[u, y, x] + r.line_in[t, level + 1 - way]

    def add_line(self, u):
        r, z = self.r, self.z
        t, k = BACK_UNITS[u]
        level = nearest_level(z, 3 - k)
        middle = (z == 1) | (z == 2)
        if k < 3:
            when(middle & (z < level), lambda: self.take_line(u, 0))
            when(middle & (z > level), lambda: self.take_line(u, 1))
            when(middle, lambda: self.send_line(u))
        else:
            when(z > 0, lambda: self.take_line(u, 0))
            when(z < 3, lambda: self.take_line(u, 1))
            self.give(t, r.total[u, self.y, self.x])

    def give(self, t, value):
        r = self.r
        if t == 0:
            for slab in range(4):
                r.att_in[:, slab, :] = value[:, slab * 192 : (slab + 1) * 192].astype(WIDE)
            self.given(0).start()
        else:
            r.ff_in[:, t - 1, :] = value.astype(WIDE)

    def given(self, i):
        source, target = ((self.r.att_in, self.att_sum), (self.r.ff_in, self.ff_sum))[i]
        return pltpu.make_async_copy(source, target, self.r.load_sem.at[6 + i])

    def small_copy(self, i):
        r = self.r
        if i < 3:
            to = (self.pair, self.across_x, self.across_y)[i]
            return remote(r.small_total.at[i], r.small_in.at[i], r.small_send.at[i], r.small_recv.at[i], to)
        to = device(lax.rem(self.z + i - 2, 4), self.y, self.x, self.c)
        return remote(r.small_total.at[3], r.small_line.at[self.z], r.small_send.at[i], r.small_recv.at[i], to)

    def small_step(self, i):
        r = self.r
        self.small_copy(i).wait_recv()
        r.small_total[i + 1] = r.small_total[i] + r.small_in[i]
        if i < 2:
            self.small_copy(i + 1).start()
        else:
            for j in (3, 4, 5):
                self.small_copy(j).start()
            r.small_line[self.z] = r.small_total[3]

    def small_end(self, shared_sum, split_sum):
        r, z = self.r, self.z
        for i in (3, 4, 5):
            self.small_copy(i).wait_recv()
        r.small_sum[...] = r.small_line[0] + r.small_line[1] + r.small_line[2] + r.small_line[3]
        index = self.y * 4 + self.x * 2 + self.c
        shared_sum[...] = pltpu.roll(r.small_sum[:8], lax.rem(768 - index * 96, 768), 1)[:6, :96]
        biases = r.small_sum[pl.ds(8 + z, 1)]
        split_sum[0:1] = biases[:, :192]
        split_sum[1:2] = biases[:, 384:576]
        inner = r.small_sum[pl.ds(12 + z, 1)]
        for j in range(4):
            split_sum[2 + j : 3 + j] = inner[:, j * 192 : (j + 1) * 192]

    def finish(self):
        for i in range(6):
            self.small_copy(i).wait_send()
        for u in range(len(BACK_UNITS) - SENDS, len(BACK_UNITS)):
            self.pair_copy(u).wait_send()
        r = self.r
        for i, blocks in ((5, r.first_in), (6, r.second_in), (7, r.second_in.at[pl.ds(0, 9)])):
            remote(blocks, blocks, r.sent.at[i], r.r_pair_recv.at[0], self.pair).wait_send()


class Cast:
    def __init__(self, a, source, target, r):
        self.a, self.source, self.target, self.r = a, source, target, r
        self.z, y, x, c = place()
        self.up, self.down = device(self.z + 1, y, x, c), device(self.z - 1, y, x, c)

    def copy(self, d, p, way, first):
        r = self.r
        part = pl.ds(p * (512 // PIECES), 512 // PIECES)
        target = self.target.at[d, part]
        return remote(
            self.source.at[part] if first else target, target, r.cast_send.at[self.a],
            r.cast_recv.at[self.a, 16 if d == 1 else d * 4 + p], self.up if way == 0 else self.down,
        )

    def own(self):
        return pltpu.make_async_copy(self.source, self.target.at[document_of(self.z)], self.r.cast_own.at[self.a])

    def firsts(self, p, act):
        for level, d, way in ((0, 0, 0), (1, 1, 1), (2, 1, 0), (3, 2, 1)):
            when(self.z == level, lambda d=d, way=way: act(self.copy(d, p, way, True)))

    def begin(self):
        self.own().start()
        for p in range(PIECES):
            self.firsts(p, lambda copy: copy.start())

    def pass_on(self, d, p, way):
        copy = self.copy(d, p, way, False)
        copy.wait_recv()
        copy.start()

    def near(self, p):
        when(self.z == 1, lambda: self.pass_on(0, p, 0))
        when(self.z == 2, lambda: self.pass_on(2, p, 1))

    def far(self, p):
        when(self.z == 1, lambda: self.pass_on(2, p, 1))
        when(self.z == 2, lambda: self.pass_on(0, p, 0))

    def finish(self):
        r = self.r
        self.own().wait()
        for level, d, way in ((0, 2, 1), (3, 0, 0)):
            for p in range(PIECES):
                when(self.z == level, lambda p=p, d=d, way=way: self.copy(d, p, way, False).wait_recv())

        def wait(blocks, act):
            act(remote(blocks, blocks, r.cast_send.at[self.a], r.cast_recv.at[self.a, 16], self.up))

        end = (self.z == 0) | (self.z == 3)
        when(end, lambda: wait(self.target.at[1], lambda copy: copy.wait_recv()))
        when(end, lambda: wait(self.source, lambda copy: copy.wait_send()))
        when(jnp.logical_not(end), lambda: wait(self.target, lambda copy: copy.wait_send()))


def buffers():
    vmem = pltpu.VMEM
    return dict(
        full=vmem((3, 4, 2, 2, 2, 96, 768), LOW),
        plane=vmem((2, 2, 2, 16, 768), LOW),
        line=vmem((4, 16, 768), LOW),
        tok=vmem((512, 768), LOW),
        cot=vmem((512, 768), LOW),
        pick=vmem((384, 128), LOW),
        rows_in=vmem((512, 768), LOW),
        hidden_in=vmem((512, 768), LOW),
        rows_t=vmem((2, 2, 2, 96, 512), LOW),
        hidden_t=vmem((2, 2, 2, 96, 512), LOW),
        down_t=vmem((2, 2, 2, 96, 512), LOW),
        joined_t=vmem((2, 2, 2, 96, 512), LOW),
        qkv=vmem((4, 512, 640), LOW),
        probs=vmem((2, 3, 512, 512), LOW),
        context=vmem((4, 512, 256), LOW),
        active=vmem((4, 512, 768), LOW),
        slope=vmem((4, 512, 768), LOW),
        mixed=vmem((512, 768), WIDE),
        bar=vmem((1, 512), WIDE),
        normed_one=vmem((512, 768), WIDE),
        factor_one=vmem((512, 1), WIDE),
        total=vmem((12, 2, 2, 96, 768), LOW),
        sends=vmem((SENDS, 2, 2, 96, 768), LOW),
        pair_in=vmem((PAIRS, 2, 2, 96, 768), LOW),
        first_in=vmem((12, 2, 96, 768), LOW),
        second_in=vmem((12, 96, 768), LOW),
        line_in=vmem((3, 5, 96, 768), LOW),
        small_total=vmem((4, 16, 768), WIDE),
        small_in=vmem((3, 16, 768), WIDE),
        small_line=vmem((4, 16, 768), WIDE),
        small_sum=vmem((16, 768), WIDE),
        shared=vmem((16, 768), WIDE),
        own=vmem((3, 96, 768), LOW),
        att_in=vmem((96, 4, 192), WIDE),
        ff_in=vmem((96, 2, 768), WIDE),
        shared_in=vmem((6, 96), WIDE),
        split_in=vmem((6, 192), WIDE),
        align_in=vmem((3, 128), jnp.int32),
        mask_in=vmem((3, 384), jnp.int32),
        small=vmem((16, 768), LOW),
    )


def flags():
    dma = pltpu.SemaphoreType.DMA
    return dict(
        sent=dma((8,)),
        line_recv=dma((3, 4)),
        first_recv=dma((12,)),
        second_recv=dma((12,)),
        pair_recv=dma((12,)),
        tiny_send=dma((6,)),
        tiny_recv=dma((6,)),
        extra_recv=dma((2, 4)),
        own_sem=dma((5,)),
        load_sem=dma((12,)),
        r_pair_send=dma((SENDS,)),
        r_pair_recv=dma((PAIRS,)),
        r_first_recv=dma((12,)),
        r_second_recv=dma((12,)),
        r_line_recv=dma((3, 5)),
        small_send=dma((6,)),
        small_recv=dma((6,)),
        cast_send=dma((2,)),
        cast_recv=dma((2, 17)),
        cast_own=dma((2,)),
    )


def spread(j):
    unit = lax.broadcasted_iota(jnp.int32, (192, 768), 1)
    return jnp.where(unit == 4 * lax.broadcasted_iota(jnp.int32, (192, 768), 0) + j, 1.0, 0.0).astype(LOW)


def turn(value, counts):
    return (value * counts.astype(LOW)).T.reshape(2, 2, 2, 96, 512)


def layer_kernel(
    att_ref, ff_ref, shared_ref, split_ref, tokens_ref, cotangent_ref, align_ref, count_ref, mask_ref,
    att_sum, ff_sum, shared_sum, split_sum, text_all, back_all, probs_out, *refs,
):
    r = SimpleNamespace(**dict(zip([*buffers(), *flags()], refs)))
    z, y, x, c = place()
    doc = document_of(z)
    counts = jnp.where(z == 2, 0.0, 1.0)
    tok_copy = pltpu.make_async_copy(tokens_ref.at[pl.ds(doc * 512, 512)], r.tok, r.load_sem.at[0])
    cot_copy = pltpu.make_async_copy(cotangent_ref.at[pl.ds(doc * 512, 512)], r.cot, r.load_sem.at[1])
    tok_copy.start()
    cot_copy.start()
    operands = (
        (att_ref, r.att_in), (ff_ref, r.ff_in), (shared_ref, r.shared_in), (split_ref, r.split_in),
        (align_ref, r.align_in), (mask_ref, r.mask_in),
    )
    loads = [pltpu.make_async_copy(source, target, r.load_sem.at[6 + i]) for i, (source, target) in enumerate(operands)]
    for copy in loads:
        copy.start()

    def cast_own():
        loads[0].wait()
        for slab in range(4):
            r.own[0, :, slab * 192 : (slab + 1) * 192] = r.att_in[:, slab, :].astype(LOW)
        loads[1].wait()
        for t in (1, 2):
            r.own[t] = r.ff_in[:, t - 1, :].astype(LOW)
        for copy in loads[2:]:
            copy.wait()

    greet(z, y, x, c, cast_own)
    net = Gather(r)
    net.begin()

    def small_start():
        r.small_sum[...] = jnp.zeros((16, 768), WIDE)
        r.small_sum[:6, :96] = r.shared_in[...]
        shared = pltpu.roll(r.small_sum[:8], (y * 4 + x * 2 + c) * 96, 1)
        r.small_sum[8:14, :192] = r.split_in[...]
        units = r.small_sum[8:16, :192].astype(LOW)
        inner = sum(mul(units, spread(j))[2 + j : 3 + j] for j in range(4))
        r.small_sum[:8] = shared
        r.small_sum[6:7] = jnp.zeros((1, 768), WIDE)
        r.small_sum[6:7, :192] = r.split_in[0:1]
        r.small_sum[6:7, 384:576] = r.split_in[1:2]
        r.small_sum[7:8] = inner
        r.small[...] = r.small_sum[...].astype(LOW)
        net.begin_tiny()

    def small_ready():
        value = r.small_total[0, 8:16]
        high = value.astype(LOW)
        rest = value - high.astype(WIDE)
        middle = rest.astype(LOW)
        last = (rest - middle.astype(WIDE)).astype(LOW)
        for j in range(4):
            packed = sum(contract_last(piece, spread(j)) for piece in (last, middle, high))
            r.small_total[0, 12:16, j * 192 : (j + 1) * 192] = packed[4:8]
        r.small_total[0] = r.small_total[0] * counts
        red.small_copy(0).start()

    def input_rows(tok, document):
        live = lax.broadcasted_iota(jnp.int32, (1, 128), 1) < count_ref[document]
        pick = jnp.where(
            (lax.broadcasted_iota(jnp.int32, (384, 128), 0) == r.align_in[pl.ds(document, 1), :]) & live, 1.0, 0.0
        ).astype(LOW)
        text_tokens = tok[:384]
        taken = lax.dot_general(pick, text_tokens, (((0,), (0,)), ((), ())), preferred_element_type=WIDE)
        slot_rows = tok[384:].astype(WIDE) + taken
        r.mixed[:384] = text_tokens.astype(WIDE)
        r.mixed[384:] = slot_rows
        r.rows_in[:384] = text_tokens
        r.rows_in[384:] = slot_rows.astype(LOW)
        r.bar[...] = jnp.where(jnp.concatenate([r.mask_in[pl.ds(document, 1), :] > 0, live], axis=1), 0.0, -1e30)
        return pick

    def prologue():
        tok_copy.wait()
        r.pick[...] = input_rows(r.tok, doc)
        r.rows_t[...] = turn(r.rows_in[...], counts)

    def spill(k):
        return pltpu.make_async_copy(r.probs.at[k % 2], probs_out.at[k % 2], r.load_sem.at[2 + k % 2])

    def projected_rows(level):
        bias = r.line[level][6:7].astype(WIDE)
        return (mul(r.rows_in[...], unit_weight(r, 0, level)) + bias).astype(LOW)

    def attend_level(projected, level, keep):
        queries, keys, values = projected[:, :192], projected[:, 192:384], projected[:, 384:640]
        halves = (slice(0, 256), slice(256, 512))
        context = [jnp.zeros((256, 256), WIDE)] * 2
        for head in range(3):
            left, right = queries * head_mask(head, 0.125), values * head_mask(head, 1.0, 256)
            for i, rows in enumerate(halves):
                scores = jnp.where(r.bar[...] < 0.0, -1e30, contract_last(left[rows], keys))
                raised = jnp.exp(scores - jnp.max(scores, axis=-1, keepdims=True))
                probs = (raised * (1.0 / jnp.sum(raised, axis=-1, keepdims=True))).astype(LOW)
                keep[head, rows] = probs
                context[i] = context[i] + mul(probs, right)
        for i, rows in enumerate(halves):
            r.context[level, rows] = pltpu.roll(context[i], 64, 1).astype(LOW)

    def attention(k):
        level = nearest_level(z, k)
        projected = projected_rows(level)
        r.qkv[level] = projected[:, :640]
        if k >= 2:
            spill(k).wait()
        attend_level(projected, level, r.probs.at[k % 2])
        if k < 2:
            spill(k).start()

    def norm_rows():
        for level in range(4):
            r.mixed[...] += contract_last(r.context[level], unit_weight(r, 0, level)[:, 512:])
        shared = r.shared[...]
        rows, normed, factor = layer_norm(r.mixed[...] + shared[0:1], shared[1:2], shared[2:3])
        r.hidden_in[...] = rows.astype(LOW)
        r.mixed[...] = rows + shared[5:6]
        return normed, factor

    def first_norm():
        r.shared[...] = jnp.sum(r.plane[...].astype(WIDE).reshape(8, 16, 768), axis=0)
        normed, factor = norm_rows()
        r.normed_one[...] = normed
        r.factor_one[...] = factor
        r.hidden_t[...] = turn(r.hidden_in[...], counts)

    def feed_level(level, keep_slope):
        bias = r.line[level][7:8, :].astype(WIDE)
        up = unit_weight(r, 1, level)
        for block in range(4):
            rows = slice(block * 128, (block + 1) * 128)
            for part in range(3):
                lanes = slice(part * 256, (part + 1) * 256)
                inner = mul(r.hidden_in[rows], up[:, lanes]) + bias[:, lanes]
                active, slope = gelu_parts(inner)
                r.active[level, rows, lanes] = active.astype(LOW)
                if keep_slope:
                    r.slope[level, rows, lanes] = slope.astype(LOW)

    def feed(k):
        feed_level(nearest_level(z, k), True)

    def feed_sum(k):
        level = jnp.where(net.end, nearest_level(z, k), INNER_LEVELS[k])
        r.mixed[...] += contract_last(r.active[level], unit_weight(r, 2, level))

    text_cast = Cast(0, r.tok, text_all, r)
    back_cast = Cast(1, r.cot, back_all, r)
    red = Reduce(att_sum, ff_sum, r)

    def second_norm():
        shared = r.shared[...]
        final, normed, factor = layer_norm(r.mixed[...], shared[3:4], shared[4:5])
        r.tok[...] = final.astype(LOW)
        text_cast.begin()
        cot_copy.wait()
        incoming = r.cot[...].astype(WIDE)
        grad, gain, shift = norm_back(incoming, normed, factor, shared[3:4])
        r.mixed[...] = grad
        low = grad.astype(LOW)
        r.rows_in[...] = low
        r.down_t[...] = turn(low, counts)
        r.small_total[0] = jnp.zeros((16, 768), WIDE)
        r.small_total[0, 3:4] = gain[None]
        r.small_total[0, 4:5] = shift[None]
        r.small_total[0, 5:6] = jnp.sum(grad, axis=0, keepdims=True)

    def inner_back(k):
        level = nearest_level(z, 3 - k)
        weight = unit_weight(r, 2, level)
        total = jnp.zeros((1, 768), WIDE)
        for block in range(4):
            rows = slice(block * 128, (block + 1) * 128)
            grad = (mul(r.rows_in[rows], weight) * r.slope[level, rows].astype(WIDE)).astype(LOW)
            r.slope[level, rows] = grad
            total = total + jnp.sum(grad.astype(WIDE), axis=0, keepdims=True)
        r.small_total[0, pl.ds(12 + level, 1)] = total

    def make_down(k):
        level = nearest_level(z, 3 - k)
        red.produce(2 * k, [([(r.down_t, r.active[level])], slice(0, 768))])

    def make_up(k):
        level = nearest_level(z, 3 - k)
        red.produce(2 * k + 1, [([(r.hidden_t, r.slope[level])], slice(0, 768))])

    def first_norm_back():
        for level in range(4):
            r.mixed[...] += contract_last(r.slope[level], unit_weight(r, 1, level))
        grad, gain, shift = norm_back(r.mixed[...], r.normed_one[...], r.factor_one[...], r.shared[1:2])
        r.mixed[...] = grad
        low = grad.astype(LOW)
        r.hidden_in[...] = low
        r.joined_t[...] = turn(low, counts)
        r.small_total[0, 0:1] = jnp.sum(grad, axis=0, keepdims=True)
        r.small_total[0, 1:2] = gain[None]
        r.small_total[0, 2:3] = shift[None]

    def reload(k):
        return pltpu.make_async_copy(probs_out.at[k], r.probs.at[k], r.load_sem.at[4 + k])

    def attention_back(k):
        slot = 3 - k
        level = nearest_level(z, slot)
        queries, keys, values = r.qkv[level, :, :192], r.qkv[level, :, 192:384], r.qkv[level, :, 384:576]
        upstream = mul(r.hidden_in[...], unit_weight(r, 0, level)[:, 512:])[:, 64:].astype(LOW)
        if slot < 2:
            reload(slot).wait()
        grad_q = grad_k = grad_v = jnp.zeros((512, 192), WIDE)
        for head in range(3):
            probs = r.probs[slot % 2, head]
            up = upstream * head_mask(head, 1.0)
            grad_v = grad_v + contract_rows(probs, up)
            grad_probs = contract_last(up, values)
            wide = probs.astype(WIDE)
            weighed = wide * grad_probs
            grad_scores = (weighed - wide * jnp.sum(weighed, axis=-1, keepdims=True)).astype(LOW)
            grad_q = grad_q + mul(grad_scores, keys * head_mask(head, 0.125))
            grad_k = grad_k + contract_rows(grad_scores, queries * head_mask(head, 0.125))
        if slot >= 2:
            reload(slot - 2).start()
        r.qkv[level, :, :192] = grad_q.astype(LOW)
        r.qkv[level, :, 192:384] = grad_k.astype(LOW)
        r.qkv[level, :, 384:576] = grad_v.astype(LOW)
        r.qkv[level, :, 576:] = jnp.zeros((512, 64), LOW)
        r.small_total[0, pl.ds(8 + level, 1), :640] = jnp.sum(r.qkv[level].astype(WIDE), axis=0, keepdims=True)

    def make_project(k):
        level = nearest_level(z, 3 - k)
        red.produce(8 + k, [
            ([(r.rows_t, r.qkv[level, :, :512])], slice(0, 512)),
            ([(r.rows_t, r.qkv[level, :, 512:]), (r.joined_t, r.context[level])], slice(512, 768)),
        ])

    def input_back():
        for level in range(4):
            r.mixed[...] += contract_last(r.qkv[level], unit_weight(r, 0, level)[:, :640])
        grad = r.mixed[...]
        r.cot[:384] = (grad[:384] + mul(r.pick[...], grad[384:].astype(LOW))).astype(LOW)
        r.cot[384:] = grad[384:].astype(LOW)
        back_cast.begin()

    steps = program_steps(net, red, text_cast, back_cast, (shared_sum, split_sum), [
        small_start, small_ready, prologue, attention, first_norm, feed, feed_sum, second_norm, inner_back, make_down, make_up, first_norm_back,
        attention_back, make_project, input_back,
    ])
    for i in ORDER:
        steps[i][0]()
    red.given(1).start()
    net.finish()
    text_cast.finish()
    back_cast.finish()
    red.finish()
    for i in range(2):
        red.given(i).wait()


def program_steps(net, red, text_cast, back_cast, small_sums, work):
    steps = []

    def add(action, *after):
        steps.append((action, [i for group in after for i in (group if isinstance(group, tuple) else (group,))]))
        return len(steps) - 1

    inner = jnp.logical_not(net.end)

    def add_each(action, *after):
        def side(i):
            return [group[i] if isinstance(group, tuple) else group for group in after]

        return (
            add(partial(when, net.end, action), *side(0)),
            add(partial(when, inner, action), *side(1)),
        )

    (small_start, small_ready, prologue, attention, first_norm, feed, feed_sum, second_norm, inner_back, make_down, make_up,
     first_norm_back, attention_back, make_project, input_back) = work
    taken = {}
    for u, unit in enumerate(UNITS):
        step = [add(partial(net.relay, u))] if unit[1] else []
        step = add_each(partial(net.arrive, u), *step)
        step = add_each(partial(net.cross, u), step)
        step = add_each(partial(net.share, u), step)
        taken[unit] = add_each(partial(net.take, u), step)
    step = add(small_start)
    tiny = [add(partial(net.tiny_step, 0), step)]
    for i in (1, 2, 3):
        tiny.append(add(partial(net.tiny_step, i), tiny[-1]))
    step = add(prologue)
    for k in range(4):
        step = add(partial(attention, k), step, taken[0, k], tiny[3])
    step = add(first_norm, step, tiny[2])
    fed = []
    for k in range(4):
        step = add(partial(feed, k), step, taken[1, k])
        fed.append(step)
    for k in range(4):
        needs = [taken[2, i] for i in range(min(k + 2, 4))]
        step = add(partial(feed_sum, k), fed[min(k + 1, 3)], *needs, *[step] * (k > 0))
    step = started = add(second_norm, step, fed[3])
    made, joined = {}, {}

    def make(u, action, before):
        ahead = [made[u - 1], joined[u - 2]] if u >= 2 else [made[0]] if u else []
        made[u] = add(action, before, *ahead)
        joined[u] = add_each(partial(red.add_pair, u), made[u])

    inners = []
    for k in range(4):
        inners.append(add(partial(inner_back, k), started))
        make(2 * k, partial(make_down, k), started)
        make(2 * k + 1, partial(make_up, k), inners[k])
    step = add(first_norm_back, *inners)
    for k in range(4):
        step = add(partial(attention_back, k), step)
        make(8 + k, partial(make_project, k), step)
    ended = add(input_back, step)
    for u in range(12):
        step = add_each(partial(red.add_first, u), joined[u])
        step = add_each(partial(red.add_second, u), step)
        add_each(partial(red.add_line, u), step)
    for cast, begun in ((text_cast, started), (back_cast, ended)):
        for p in range(PIECES):
            add(partial(cast.near, p), begun)
            add(partial(cast.far, p), begun)
    step = add(small_ready, ended)
    for i in range(3):
        step = add(partial(red.small_step, i), step)
    add(partial(red.small_end, *small_sums), step)
    return steps


ORDER = (
    8, 9, 105, 0, 1, 106, 24, 26, 25, 16, 33, 35, 107, 17, 3, 28, 42, 69, 44, 10, 51, 2, 34, 18, 71, 60, 27, 78,
    43, 5, 4, 12, 36, 11, 52, 37, 110, 46, 70, 87, 62, 6, 30, 45, 108, 96, 29, 64, 19, 79, 98, 109, 61, 7, 111,
    32, 31, 14, 89, 39, 13, 20, 53, 63, 54, 88, 72, 38, 112, 47, 97, 41, 81, 40, 113, 48, 21, 55, 80, 100, 15, 73,
    91, 75, 49, 57, 90, 50, 114, 23, 115, 82, 84, 56, 59, 77, 99, 22, 74, 66, 83, 116, 102, 93, 58, 117, 65, 76,
    92, 118, 101, 67, 104, 68, 95, 86, 120, 85, 121, 94, 119, 103, 122, 123, 124, 139, 125, 126, 129, 146, 132,
    153, 128, 127, 133, 130, 243, 154, 245, 134, 135, 131, 247, 136, 244, 140, 249, 158, 246, 251, 138, 171, 248,
    253, 137, 162, 250, 141, 255, 178, 252, 166, 254, 173, 184, 177, 142, 143, 183, 172, 257, 256, 170, 144, 275,
    175, 189, 145, 147, 150, 190, 174, 176, 276, 196, 149, 261, 148, 155, 259, 151, 152, 159, 202, 277, 258, 157,
    156, 185, 163, 265, 267, 260, 160, 269, 161, 179, 186, 164, 219, 191, 167, 262, 263, 195, 187, 180, 273, 278,
    168, 270, 165, 268, 266, 214, 220, 274, 182, 221, 271, 231, 225, 201, 207, 169, 264, 197, 213, 227, 198, 203,
    193, 188, 200, 226, 237, 272, 204, 232, 222, 224, 192, 216, 233, 194, 228, 199, 238, 215, 217, 208, 206, 279,
    234, 236, 235, 230, 210, 212, 209, 211, 229, 239, 218, 181, 240, 223, 205, 242, 241,
)


def run_layer(attention, feedforward, shared, split, tokens, cotangent, align, count, mask):
    vmem = pl.BlockSpec(memory_space=pltpu.VMEM)
    smem = pl.BlockSpec(memory_space=pltpu.SMEM)
    hbm = pl.BlockSpec(memory_space=pl.ANY)
    whole = jax.ShapeDtypeStruct((3, 512, 768), LOW)
    return pl.pallas_call(
        layer_kernel,
        out_shape=(
            jax.ShapeDtypeStruct((96, 4, 192), WIDE),
            jax.ShapeDtypeStruct((96, 2, 768), WIDE),
            jax.ShapeDtypeStruct((6, 96), WIDE),
            jax.ShapeDtypeStruct((6, 192), WIDE),
            whole,
            whole,
            jax.ShapeDtypeStruct((2, 3, 512, 512), LOW),
        ),
        in_specs=[hbm, hbm, hbm, hbm, hbm, hbm, hbm, smem, hbm],
        out_specs=(hbm, hbm, vmem, vmem, hbm, hbm, hbm),
        scratch_shapes=[*buffers().values(), *flags().values()],
        compiler_params=pltpu.CompilerParams(
            collective_id=0, has_side_effects=True, vmem_limit_bytes=VMEM_LIMIT
        ),
        name="layer_step",
    )(attention, feedforward, shared, split, tokens, cotangent, align, count, mask)


VMEM_LIMIT = 63 * 2**20


def slab_rates(rates, shape):
    slab = lax.broadcasted_iota(jnp.int32, shape, 1)
    value = jnp.full(shape, rates[0], WIDE)
    for i, rate in enumerate(rates[1:]):
        value = jnp.where(slab == i + 1, rate, value)
    return value


def update_kernel(*refs):
    text_ref, back_ref, families = refs[0], refs[1], refs[2:18]
    text_out, back_out, outs = refs[18], refs[19], refs[20:36]
    back_in, back_wide, text_in, ins, news = refs[36], refs[37], refs[38], refs[39:55], refs[55:71]
    load_sem, store_sem = refs[71:]

    def part(i):
        size = back_in.shape[0] // PARTS
        return pl.ds(i * size, size)

    text_loads = [
        pltpu.make_async_copy(text_ref.at[part(i)], text_in.at[part(i)], load_sem.at[16 + PARTS + i]) for i in range(PARTS)
    ]
    text_stores = [
        pltpu.make_async_copy(text_in.at[part(i)], text_out.at[part(i)], store_sem.at[16 + i]) for i in range(PARTS)
    ]
    back_loads = [
        pltpu.make_async_copy(back_ref.at[part(i)], back_in.at[part(i)], load_sem.at[16 + i]) for i in range(PARTS)
    ]
    back_stores = [
        pltpu.make_async_copy(back_wide.at[part(i)], back_out.at[part(i)], store_sem.at[16 + PARTS + i])
        for i in range(PARTS)
    ]
    loads = [pltpu.make_async_copy(families[i], ins[i], load_sem.at[i]) for i in range(16)]
    stores = [pltpu.make_async_copy(news[i], outs[i], store_sem.at[i]) for i in range(16)]

    def widen(i):
        back_loads[i].wait()
        back_wide[part(i)] = back_in[part(i)].astype(WIDE)
        back_stores[i].start()

    def update(i, rate):
        for j in range(4 * i, 4 * i + 4):
            loads[j].wait()
        master, moment, average, gradient = (ref[...] for ref in ins[4 * i : 4 * i + 4])
        for j, value in enumerate(renew(master, moment, average, gradient, rate)):
            news[4 * i + j][...] = value
            stores[4 * i + j].start()

    back_loads[0].start()
    back_loads[1].start()
    for copy in loads:
        copy.start()
    for copy in back_loads[2:]:
        copy.start()
    for copy in text_loads:
        copy.start()
    widen(0)
    widen(1)
    update(0, slab_rates(ATTENTION_RATES, ins[0].shape))
    update(1, slab_rates(FEEDFORWARD_RATES, ins[4].shape))
    row = lax.broadcasted_iota(jnp.int32, ins[12].shape, 0)
    split_rates = jnp.full(ins[12].shape, SPLIT_RATES[2], WIDE)
    for i in (0, 1, 3, 4, 5):
        split_rates = jnp.where(row == i, SPLIT_RATES[i], split_rates)
    update(2, SHARED_RATE)
    update(3, split_rates)
    for i in range(2, PARTS):
        widen(i)
    for load, store in zip(text_loads, text_stores):
        load.wait()
        store.start()
    for copy in (*text_stores, *back_stores, *stores):
        copy.wait()


PARTS = 2


def run_update(text, back, families):
    arrays = [array for family in families for array in family]
    shapes = [jax.ShapeDtypeStruct(text.shape, LOW), jax.ShapeDtypeStruct(back.shape, WIDE)]
    for family in families:
        shapes += [jax.ShapeDtypeStruct(family[0].shape, kind) for kind in (WIDE, WIDE, WIDE, LOW)]
    hbm = pl.BlockSpec(memory_space=pl.ANY)
    return pl.pallas_call(
        update_kernel,
        in_specs=[hbm] * 18,
        out_specs=[hbm] * 18,
        out_shape=shapes,
        scratch_shapes=[
            pltpu.VMEM(back.shape, LOW),
            pltpu.VMEM(back.shape, WIDE),
            pltpu.VMEM(text.shape, LOW),
            *[pltpu.VMEM(array.shape, WIDE) for array in arrays],
            *[pltpu.VMEM(shape.shape, shape.dtype) for shape in shapes[2:]],
            pltpu.SemaphoreType.DMA((16 + 2 * PARTS,)),
            pltpu.SemaphoreType.DMA((16 + 2 * PARTS,)),
        ],
        compiler_params=pltpu.CompilerParams(vmem_limit_bytes=VMEM_LIMIT),
        name="update_parameters",
    )(text, back, *arrays)


def line_shards(
    tokens,
    alignment,
    segment_count,
    text_mask,
    cotangent,
    attention_master,
    attention_moment,
    attention_average,
    feedforward_master,
    feedforward_moment,
    feedforward_average,
    shared_master,
    shared_moment,
    shared_average,
    split_master,
    split_moment,
    split_average,
):
    rows, width = tokens.shape
    attention_sum, feedforward_sum, shared_sum, split_sum, text_all, back_all, _ = run_layer(
        attention_master, feedforward_master, shared_master.T, split_master.T,
        tokens, cotangent, alignment, segment_count, text_mask,
    )
    outs = run_update(
        text_all.reshape(rows, width),
        back_all.reshape(rows, width),
        (
            (attention_master, attention_moment, attention_average, attention_sum),
            (feedforward_master, feedforward_moment, feedforward_average, feedforward_sum),
            (shared_master.T, shared_moment.T, shared_average.T, shared_sum),
            (split_master.T, split_moment.T, split_average.T, split_sum),
        ),
    )
    return (*outs[:10], *[out.T for out in outs[10:]])


def solution(mesh):
    in_specs = (
        P("dp", None),
        P("dp", None),
        P("dp"),
        P("dp", None),
        P("dp", None),
        P("dp", None, "mp"),
        P("dp", None, "mp"),
        P("dp", None, "mp"),
        P("dp", None, "mp"),
        P("dp", None, "mp"),
        P("dp", None, "mp"),
        P("dp", None),
        P("dp", None),
        P("dp", None),
        P("mp", None),
        P("mp", None),
        P("mp", None),
    )
    out_specs = (
        P("dp", None),
        P("dp", None),
        P("dp", None, "mp"),
        P("dp", None, "mp"),
        P("dp", None, "mp"),
        P("dp", None, "mp"),
        P("dp", None, "mp"),
        P("dp", None, "mp"),
        P("dp", None, "mp"),
        P("dp", None, "mp"),
        P("dp", None),
        P("dp", None),
        P("dp", None),
        P("dp", None),
        P("mp", None),
        P("mp", None),
        P("mp", None),
        P("mp", None),
    )
    body = line_shards if mesh.shape["dp"] == 8 and mesh.shape["mp"] == 4 else general_shards
    return jax.shard_map(body, mesh=mesh, in_specs=in_specs, out_specs=out_specs, check_vma=False)
```
